32 devices in a mesh: dp: 4 (over z), seq: 8 (over y, x, core).
Axes of the slice: x: 2, y: 2, z: 4, core: 2. Of those that a mesh axis runs over, the one named last changes fastest.
Arguments:
- tokens: bfloat16 [4, 1024, 2048], P('dp', 'seq'), may hold values from -6 to 6
- segments: int32 [4, 1024], P('dp'), may hold values from 0 to 7, as said below
- exit_layer: int32 [4, 1024], P('dp', 'seq'), may hold values from 1 to 24, as said below
- first_gain: bfloat16 [2048], P(('dp', 'seq')), may hold values from 0.25 to 1.75
- first_shift: bfloat16 [2048], P(('dp', 'seq')), may hold values from -4 to 4
- query_weight: bfloat16 [2048, 2048], P(('dp', 'seq')), may hold values from -0.125 to 0.125
- query_bias: bfloat16 [2048], P(('dp', 'seq')), may hold values from -4 to 4
- key_weight: bfloat16 [2048, 2048], P(('dp', 'seq')), may hold values from -0.125 to 0.125
- value_weight: bfloat16 [2048, 2048], P(('dp', 'seq')), may hold values from -0.125 to 0.125
- value_bias: bfloat16 [2048], P(('dp', 'seq')), may hold values from -4 to 4
- output_weight: bfloat16 [2048, 2048], P(('dp', 'seq')), may hold values from -0.5 to 0.5
- output_bias: bfloat16 [2048], P(('dp', 'seq')), may hold values from -4 to 4
- second_gain: bfloat16 [2048], P(('dp', 'seq')), may hold values from 0.25 to 1.75
- second_shift: bfloat16 [2048], P(('dp', 'seq')), may hold values from -4 to 4
- up_weight: bfloat16 [2048, 8192], P(('dp', 'seq')), may hold values from -0.125 to 0.125
- up_bias: bfloat16 [8192], P(('dp', 'seq')), may hold values from -4 to 4
- down_weight: bfloat16 [8192, 2048], P(('dp', 'seq')), may hold values from -0.09375 to 0.09375
- down_bias: bfloat16 [2048], P(('dp', 'seq')), may hold values from -4 to 4
- cotangent: bfloat16 [4, 1024, 2048], P('dp', 'seq'), may hold values from -8 to 8
Outputs:
- layer_out: bfloat16 [4, 1024, 2048], P('dp', 'seq')
- tokens_gradient: bfloat16 [4, 1024, 2048], P('dp', 'seq')
- first_gain_gradient: float32 [2048], P(('dp', 'seq'))
- first_shift_gradient: float32 [2048], P(('dp', 'seq'))
- query_weight_gradient: float32 [2048, 2048], P(('dp', 'seq'))
- query_bias_gradient: float32 [2048], P(('dp', 'seq'))
- key_weight_gradient: float32 [2048, 2048], P(('dp', 'seq'))
- value_weight_gradient: float32 [2048, 2048], P(('dp', 'seq'))
- value_bias_gradient: float32 [2048], P(('dp', 'seq'))
- output_weight_gradient: float32 [2048, 2048], P(('dp', 'seq'))
- output_bias_gradient: float32 [2048], P(('dp', 'seq'))
- second_gain_gradient: float32 [2048], P(('dp', 'seq'))
- second_shift_gradient: float32 [2048], P(('dp', 'seq'))
- up_weight_gradient: float32 [2048, 8192], P(('dp', 'seq'))
- up_bias_gradient: float32 [8192], P(('dp', 'seq'))
- down_weight_gradient: float32 [8192, 2048], P(('dp', 'seq'))
- down_bias_gradient: float32 [2048], P(('dp', 'seq'))
The draws below stay inside these ranges and needn't reach their ends.
Inputs may be any that keep to these rules, and one draw needn't show every extreme that they name: `segments`: in each sequence the document numbers start at 0, never fall, and every one of the 8 documents holds at least one position; one document of each sequence starts within the first 128 positions and ends within the last 128. `exit_layer`: within each document the exit layers never rise, so the tokens that exceed 12 form a prefix of the document; the first token of every document exceeds 12, and all tokens of the document that spans the sequence do.
All inputs are finite; a program needn't handle non-finite values.
Results may differ from the reference program's by a relative error of at most 0.03.
Values may be sent and summed in bfloat16 or wider, within the bound.
A program may use at most 576 MiB of HBM per device.

```python
import jax
import jax.numpy as jnp
from jax import lax

D = 2048
HEADS = 32
FF = 8192
NLAYERS = 24
HEAD_DIM = 64
LAYER = 12
NDOCS = 8
SEQS = 1
PIECE = 128
SEQ_LEN = 1024
BATCH = 4


def layout(key):
    base = jax.random.fold_in(key, 7301)
    length_key, active_key, long_key, head_key, tail_key = jax.random.split(base, 5)
    powers = jax.random.randint(length_key, (BATCH, NDOCS), 0, 7)
    weights = jnp.power(2, powers).astype(jnp.int32)
    docs = jnp.arange(NDOCS, dtype=jnp.int32)[None, :]
    longest = jax.random.randint(long_key, (BATCH, 1), 0, NDOCS)
    after_count = NDOCS - 1 - longest
    head_room = jax.random.randint(head_key, (BATCH, 1), 0, PIECE - NDOCS + 1)
    tail_room = jax.random.randint(tail_key, (BATCH, 1), 0, PIECE - NDOCS + 1)
    head_size = longest + (longest > 0).astype(jnp.int32) * head_room
    tail_size = after_count + (after_count > 0).astype(jnp.int32) * tail_room
    long_end = SEQ_LEN - tail_size
    early = (docs < longest).astype(jnp.int32)
    late = (docs > longest).astype(jnp.int32)
    early_w = weights * early
    late_w = weights * late
    early_total = jnp.maximum(jnp.sum(early_w, axis=1, keepdims=True), 1)
    late_total = jnp.maximum(jnp.sum(late_w, axis=1, keepdims=True), 1)
    early_before = jnp.cumsum(early_w, axis=1) - early_w
    late_before = jnp.cumsum(late_w, axis=1) - late_w
    early_start = docs + (head_size - longest) * early_before // early_total
    late_start = long_end + (docs - longest - 1) + (tail_size - after_count) * late_before // late_total
    starts = jnp.where(docs < longest, early_start, jnp.where(docs == longest, head_size, late_start)).astype(jnp.int32)
    ends = jnp.concatenate([starts[:, 1:], jnp.full((BATCH, 1), SEQ_LEN, jnp.int32)], axis=1)
    lengths = ends - starts
    ratio = jax.random.randint(active_key, (BATCH, NDOCS), 2, 8)
    active = jnp.maximum(1, lengths * ratio // 8)
    active = jnp.where(docs == longest, lengths, active)
    position = jnp.arange(SEQ_LEN, dtype=jnp.int32)
    inside = (position[None, :, None] >= starts[:, None, :]).astype(jnp.int32)
    seg = jnp.sum(inside, axis=2) - 1
    onehot = (seg[:, :, None] == jnp.arange(NDOCS, dtype=jnp.int32)[None, None, :]).astype(jnp.int32)
    start_tok = jnp.sum(onehot * starts[:, None, :], axis=2)
    active_tok = jnp.sum(onehot * active[:, None, :], axis=2)
    length_tok = jnp.sum(onehot * lengths[:, None, :], axis=2)
    offset = position[None, :] - start_tok
    upper = NLAYERS - offset * (NLAYERS - LAYER - 1) // active_tok
    lower = LAYER - (offset - active_tok + 1) * (LAYER - 1) // jnp.maximum(length_tok - active_tok, 1)
    exits = jnp.where(offset < active_tok, upper, lower)
    return (seg.astype(jnp.int32), exits.astype(jnp.int32))


def draw_segments(key, part):
    seg, exits = layout(key)
    return seg


def draw_exit_layer(key, part):
    seg, exits = layout(key)
    return exits


def with_spikes(values, own_key, source, target, parts, factor):
    def block_of(axis_at):
        return (jnp.arange(values.shape[axis_at]) // (values.shape[axis_at] // parts)).reshape((-1,) + (1,) * (values.ndim - 1 - axis_at))

    near = jax.random.permutation(own_key, parts)[block_of(target)]
    other_side = (block_of(target) + parts // 2) % parts
    return jnp.where((block_of(source) == near) | (block_of(source) == other_side), factor * values, values)


def block_levels(key, shape, cuts, least, high):
    level, own = 1.0, jax.random.fold_in(key, 6)
    for dim, shards_of in cuts:
        steps = jnp.exp(jax.random.uniform(jax.random.fold_in(own, dim), (shards_of,), jnp.float32, least / len(cuts), high / len(cuts)))
        level = level * jnp.repeat(steps, shape[dim] // shards_of).reshape([-1 if axis == dim else 1 for axis in range(len(shape))])
    return level


def normal_values(stream_key, dims, scale, reach, pieces=(), held_as=jnp.bfloat16):
    entries = scale * jax.random.normal(stream_key, dims, jnp.float32)
    if pieces:
        entries = entries * block_levels(stream_key, dims, pieces, -0.22, 0.18)
    return jnp.clip(entries, -reach, reach).astype(held_as)


def noise_with(key, shape, scale, most, cuts, heavy, kind=jnp.bfloat16):
    entries = scale * jax.random.normal(key, shape, jnp.float32)
    if cuts:
        entries = entries * block_levels(key, shape, cuts, -0.22, 0.18)
    return jnp.clip(with_spikes(entries, jax.random.fold_in(key, 3), *heavy), -most, most).astype(kind)


def setup_inputs(seed: int = 0) -> dict:
    streams_of = jax.random.split(jax.random.key(seed), 20)
    tokens = normal_values(streams_of[0], (BATCH, SEQ_LEN, D), 1.0, 6.0, ((0, 4), (1, 8)))
    segments = draw_segments(jax.random.fold_in(streams_of[19], 71), 0)
    exit_layer = draw_exit_layer(jax.random.fold_in(streams_of[19], 71), 0)
    first_gain = jnp.clip(1.0 + 0.15 * jax.random.normal(streams_of[3], (D,), jnp.float32), 0.25, 1.75).astype(jnp.bfloat16)
    first_shift = normal_values(streams_of[4], (D,), 0.3, 4.0, ((0, 32),))
    query_weight = normal_values(streams_of[5], (D, D), D ** -0.5, 0.125, ((0, 32),))
    query_bias = normal_values(streams_of[6], (D,), 0.3, 4.0, ((0, 32),))
    key_weight = normal_values(streams_of[7], (D, D), D ** -0.5, 0.125, ((0, 32),))
    value_weight = normal_values(streams_of[8], (D, D), D ** -0.5, 0.125, ((0, 32),))
    value_bias = normal_values(streams_of[9], (D,), 0.3, 4.0, ((0, 32),))
    output_weight = normal_values(streams_of[10], (D, D), (D // 16) ** -0.5, 0.5, ((0, 32),))
    output_bias = normal_values(streams_of[11], (D,), 0.3, 4.0, ((0, 32),))
    second_gain = jnp.clip(1.0 + 0.15 * jax.random.normal(streams_of[12], (D,), jnp.float32), 0.25, 1.75).astype(jnp.bfloat16)
    second_shift = normal_values(streams_of[13], (D,), 0.3, 4.0, ((0, 32),))
    up_weight = normal_values(streams_of[14], (D, FF), D ** -0.5, 0.125, ((0, 32),))
    up_bias = normal_values(streams_of[15], (FF,), 0.3, 4.0, ((0, 32),))
    down_weight = normal_values(streams_of[16], (FF, D), (FF // 2) ** -0.5, 0.09375, ((0, 32),))
    down_bias = normal_values(streams_of[17], (D,), 0.3, 4.0, ((0, 32),))
    cotangent = noise_with(streams_of[18], (BATCH, SEQ_LEN, D), 1.0, 8.0, ((0, 4), (1, 8)), (1, 2, 8, 2.0))
    return dict(tokens=tokens, segments=segments, exit_layer=exit_layer, first_gain=first_gain, first_shift=first_shift, query_weight=query_weight, query_bias=query_bias, key_weight=key_weight, value_weight=value_weight, value_bias=value_bias, output_weight=output_weight, output_bias=output_bias, second_gain=second_gain, second_shift=second_shift, up_weight=up_weight, up_bias=up_bias, down_weight=down_weight, down_bias=down_bias, cotangent=cotangent)


EPS = 1e-05
NEG = -1e+30

@jax.custom_vjp
def low(v):
    return lax.optimization_barrier(v.astype(jnp.bfloat16)).astype(jnp.float32)

@jax.custom_vjp
def low_back(v):
    return v

def low_keep(v):
    return (low(v), None)

def low_pass(kept, grad):
    return (grad,)

def back_keep(v):
    return (v, None)

def back_low(kept, grad):
    return (low(grad),)
low.defvjp(low_keep, low_pass)
low_back.defvjp(back_keep, back_low)

def activate(value):
    return jax.nn.gelu(value, approximate=True)

def layer_norm(value, gain, shift):
    mean = lax.optimization_barrier(jnp.mean(value, axis=-1, keepdims=True))
    centred = value - mean
    spread = lax.optimization_barrier(jnp.mean(centred * centred, axis=-1, keepdims=True))
    return centred * lax.rsqrt(spread + EPS) * gain + shift

def project(left, matrix):
    return jnp.einsum('gtd,de->gte', left, matrix, precision=lax.Precision.HIGHEST)

def attend(queries, keys, values, segs):
    length = queries.shape[0]
    block = min(length, 512)
    where_key = jnp.arange(length, dtype=jnp.int32)
    scale = HEAD_DIM ** (-0.5)

    def one(index):
        start = (index * block).astype(jnp.int32)
        query_rows = lax.dynamic_slice_in_dim(queries, start, block, 0)
        query_pos = start + jnp.arange(block, dtype=jnp.int32)
        query_seg = lax.dynamic_slice_in_dim(segs, start, block, 0)
        allowed = jnp.logical_and(query_seg[:, None] == segs[None, :], where_key[None, :] <= query_pos[:, None])
        scores = low_back(jnp.einsum('qhd,khd->hqk', query_rows, keys, precision=lax.Precision.HIGHEST) * scale)
        scores = jnp.where(allowed[None], scores, NEG)
        total = jax.nn.logsumexp(scores, axis=-1, keepdims=True)
        probs = low(jnp.exp(scores - total))
        return jnp.einsum('hqk,khd->qhd', probs, values, precision=lax.Precision.HIGHEST)
    mixed = lax.map(jax.checkpoint(one), jnp.arange(length // block, dtype=jnp.int32))
    return mixed.reshape(length, HEADS, HEAD_DIM)

def forward(params, inputs, segs, keep):
    first_gain, first_shift, query_weight, query_bias, key_weight, value_weight, value_bias, output_weight, output_bias, second_gain, second_shift, up_weight, up_bias, down_weight, down_bias = params
    groups, length, width = inputs.shape
    normed_one = low(layer_norm(inputs, first_gain, first_shift))
    queries = low(low_back(project(normed_one, query_weight) + query_bias))
    keys = low(low_back(project(normed_one, key_weight)))
    values = low(low_back(project(normed_one, value_weight) + value_bias))
    shaped = (groups, length, HEADS, HEAD_DIM)
    mixed = jax.vmap(attend)(queries.reshape(shaped), keys.reshape(shaped), values.reshape(shaped), segs)
    mixed = low(low_back(mixed.reshape(groups, length, width)))
    attention = low_back(project(mixed, output_weight) + output_bias)
    middle = inputs + keep * attention
    normed_two = low(layer_norm(middle, second_gain, second_shift))
    before = low_back(project(normed_two, up_weight) + up_bias)
    hidden = low(activate(before))
    branch = low_back(project(hidden, down_weight) + down_bias)
    return middle + keep * branch

def reference(tokens, segments, exit_layer, first_gain, first_shift, query_weight, query_bias, key_weight, value_weight, value_bias, output_weight, output_bias, second_gain, second_shift, up_weight, up_bias, down_weight, down_bias, cotangent):
    params = tuple((p.astype(jnp.float32) for p in (first_gain, first_shift, query_weight, query_bias, key_weight, value_weight, value_bias, output_weight, output_bias, second_gain, second_shift, up_weight, up_bias, down_weight, down_bias)))
    groups = BATCH // SEQS
    inputs = tokens.astype(jnp.float32).reshape(groups, SEQS, SEQ_LEN, D)
    segs = segments.reshape(groups, SEQS, SEQ_LEN)
    keep = (exit_layer > LAYER).astype(jnp.float32).reshape(groups, SEQS, SEQ_LEN, 1)
    upstream = cotangent.astype(jnp.float32).reshape(groups, SEQS, SEQ_LEN, D)

    def step(acc, item):
        group_in, group_seg, group_keep, group_up = item
        result, pull = jax.vjp(lambda p, v: forward(p, v, group_seg, group_keep), params, group_in)
        param_grads, input_grad = pull(group_up)
        acc = jax.tree.map(lambda a, b: a + b, acc, param_grads)
        return (acc, (result.astype(jnp.bfloat16), input_grad.astype(jnp.bfloat16)))
    zeros = tuple((jnp.zeros(p.shape, jnp.float32) for p in params))
    grads, (results, input_grads) = lax.scan(step, zeros, (inputs, segs, keep, upstream))
    layer_out = results.reshape(BATCH, SEQ_LEN, D)
    tokens_gradient = input_grads.reshape(BATCH, SEQ_LEN, D)
    return (layer_out, tokens_gradient, grads[0], grads[1], grads[2], grads[3], grads[4], grads[5], grads[6], grads[7], grads[8], grads[9], grads[10], grads[11], grads[12], grads[13], grads[14])
```

```python
import functools
import math

import jax
import jax.numpy as jnp
from jax import lax
from jax.experimental import pallas as pl
from jax.experimental.pallas import tpu as pltpu
from jax.sharding import PartitionSpec as P

HEADS = 32
LAYER = 12


EPS = 1e-05
NEG = -1e30


def activate(value):
    return jax.nn.gelu(value, approximate=True)


def layer_norm(value, gain, shift):
    mean = jnp.mean(value, axis=-1, keepdims=True)
    centred = value - mean
    spread = jnp.mean(centred * centred, axis=-1, keepdims=True)
    return centred * lax.rsqrt(spread + EPS) * gain + shift


def transposed(left, right):
    return lax.dot_general(
        left, right, (((1,), (1,)), ((), ())), preferred_element_type=jnp.float32
    )


def leading(left, right):
    return lax.dot_general(
        left, right, (((0,), (0,)), ((), ())), preferred_element_type=jnp.float32
    )


def visible(query_seg, query_pos, key_seg, key_pos):
    same = query_seg[:, :, None] == key_seg[:, None, :]
    return jnp.logical_and(same, key_pos[None, None, :] <= query_pos[None, :, None])


def by_blocks(step, carry, piece):
    length = jax.tree.leaves(piece)[0].shape[1]
    size = math.gcd(length, 128)

    def one(index, state):
        offset = index * size
        block = jax.tree.map(lambda part: lax.dynamic_slice_in_dim(part, offset, size, 1), piece)
        return step(state, block, offset)

    return lax.fori_loop(0, length // size, one, carry)


def on_device(
    tokens,
    segments,
    exit_layer,
    first_gain,
    first_shift,
    query_weight,
    query_bias,
    key_weight,
    value_weight,
    value_bias,
    output_weight,
    output_bias,
    second_gain,
    second_shift,
    up_weight,
    up_bias,
    down_weight,
    down_bias,
    cotangent,
):
    nseq, piece_len, width = tokens.shape
    head_count = HEADS
    head_size = width // head_count
    scale = head_size ** (-0.5)
    rows = nseq * piece_len
    own_first = lax.axis_index("seq") * piece_len
    own_pos = own_first + jnp.arange(piece_len, dtype=jnp.int32)
    own_seg = lax.dynamic_slice_in_dim(segments, own_first, piece_len, 1)
    keep = (exit_layer > LAYER).astype(jnp.float32).reshape(rows, 1)
    (
        gain_one,
        shift_one,
        query_full,
        query_shift,
        key_full,
        value_full,
        value_shift,
        output_full,
        output_shift,
        gain_two,
        shift_two,
        up_shift,
        down_shift,
    ) = (
        lax.all_gather(first_gain, ("dp", "seq"), axis=0, tiled=True),
        lax.all_gather(first_shift, ("dp", "seq"), axis=0, tiled=True),
        lax.all_gather(query_weight, ("dp", "seq"), axis=0, tiled=True),
        lax.all_gather(query_bias, ("dp", "seq"), axis=0, tiled=True),
        lax.all_gather(key_weight, ("dp", "seq"), axis=0, tiled=True),
        lax.all_gather(value_weight, ("dp", "seq"), axis=0, tiled=True),
        lax.all_gather(value_bias, ("dp", "seq"), axis=0, tiled=True),
        lax.all_gather(output_weight, ("dp", "seq"), axis=0, tiled=True),
        lax.all_gather(output_bias, ("dp", "seq"), axis=0, tiled=True),
        lax.all_gather(second_gain, ("dp", "seq"), axis=0, tiled=True),
        lax.all_gather(second_shift, ("dp", "seq"), axis=0, tiled=True),
        lax.all_gather(up_bias, ("dp", "seq"), axis=0, tiled=True),
        lax.all_gather(down_bias, ("dp", "seq"), axis=0, tiled=True),
    )
    gain_one = gain_one.astype(jnp.float32)
    shift_one = shift_one.astype(jnp.float32)
    gain_two = gain_two.astype(jnp.float32)
    shift_two = shift_two.astype(jnp.float32)
    inputs = tokens.astype(jnp.float32).reshape(rows, width)
    normed_one = layer_norm(inputs, gain_one, shift_one).astype(jnp.bfloat16)
    queries = (
        jnp.dot(normed_one, query_full, preferred_element_type=jnp.float32)
        + query_shift.astype(jnp.float32)
    ).astype(jnp.bfloat16)
    keys = jnp.dot(normed_one, key_full, preferred_element_type=jnp.float32).astype(jnp.bfloat16)
    values = (
        jnp.dot(normed_one, value_full, preferred_element_type=jnp.float32)
        + value_shift.astype(jnp.float32)
    ).astype(jnp.bfloat16)
    query_heads = queries.reshape(nseq, piece_len, head_count, head_size)
    key_heads = keys.reshape(nseq, piece_len, head_count, head_size)
    value_heads = values.reshape(nseq, piece_len, head_count, head_size)
    key_local = keys.reshape(nseq, piece_len, width)
    pair_local = jnp.concatenate([keys, values], axis=1).reshape(nseq, piece_len, 2 * width)

    def key_mask(start, length):
        key_pos = start + jnp.arange(length, dtype=jnp.int32)
        key_seg = lax.dynamic_slice_in_dim(segments, start, length, 1)
        return visible(own_seg, own_pos, key_seg, key_pos)[:, None]

    def local_scores(key_block):
        keyed = key_block.reshape(nseq, key_block.shape[1], head_count, head_size)
        return (
            jnp.einsum("sqhd,skhd->shqk", query_heads, keyed, preferred_element_type=jnp.float32)
            * scale
        )

    def norm_step(carry, block, start):
        top, total = carry
        allowed = key_mask(start, block.shape[1])
        scores = jnp.where(allowed, local_scores(block), NEG)
        new_top = jnp.maximum(top, jnp.max(scores, axis=-1))
        weights = jnp.where(allowed, jnp.exp(scores - new_top[..., None]), 0.0)
        return (new_top, total * jnp.exp(top - new_top) + jnp.sum(weights, axis=-1))

    start_norm = (
        jnp.full((nseq, head_count, piece_len), NEG, jnp.float32),
        jnp.zeros((nseq, head_count, piece_len), jnp.float32),
    )
    top, total = by_blocks(
        norm_step, start_norm, lax.all_gather(key_local, "seq", axis=1, tiled=True)
    )
    lse = top + jnp.log(total)

    def mix_step(acc, block, start):
        length = block.shape[1]
        allowed = key_mask(start, length)
        scores = local_scores(block[:, :, :width])
        probs = jnp.where(allowed, jnp.exp(scores - lse[..., None]), 0.0).astype(jnp.bfloat16)
        valued = block[:, :, width:].reshape(nseq, length, head_count, head_size)
        return acc + jnp.einsum(
            "shqk,skhd->sqhd", probs, valued, preferred_element_type=jnp.float32
        )

    empty_heads = jnp.zeros((nseq, piece_len, head_count, head_size), jnp.float32)
    mixed_heads = by_blocks(
        mix_step, empty_heads, lax.all_gather(pair_local, "seq", axis=1, tiled=True)
    )
    mixed = mixed_heads.reshape(rows, width).astype(jnp.bfloat16)
    attention = jnp.dot(
        mixed, output_full, preferred_element_type=jnp.float32
    ) + output_shift.astype(jnp.float32)
    middle = inputs + keep * attention
    normed_two = layer_norm(middle, gain_two, shift_two).astype(jnp.bfloat16)
    columns = normed_two
    before = jnp.dot(
        columns,
        lax.all_gather(up_weight, ("dp", "seq"), axis=0, tiled=True),
        preferred_element_type=jnp.float32,
    )
    pre_active = before + up_shift.astype(jnp.float32)
    hidden = activate(pre_active).astype(jnp.bfloat16)
    columns = hidden
    branch = jnp.dot(
        columns,
        lax.all_gather(down_weight, ("dp", "seq"), axis=0, tiled=True),
        preferred_element_type=jnp.float32,
    )
    branch = branch + down_shift.astype(jnp.float32)
    layer_out = (middle + keep * branch).astype(jnp.bfloat16).reshape(nseq, piece_len, width)
    upstream = cotangent.astype(jnp.float32).reshape(rows, width)
    branch_back = (keep * upstream).astype(jnp.bfloat16)
    down_shift_sum = jnp.sum(branch_back.astype(jnp.float32), axis=0)
    hidden_back = transposed(
        branch_back, lax.all_gather(down_weight, ("dp", "seq"), axis=0, tiled=True)
    )
    active_value, pull_active = jax.vjp(activate, pre_active)
    pre_back = pull_active(hidden_back)[0].astype(jnp.bfloat16)
    up_shift_sum = jnp.sum(pre_back.astype(jnp.float32), axis=0)
    down_gradient = lax.psum_scatter(
        leading(hidden, branch_back), ("dp", "seq"), scatter_dimension=0, tiled=True
    )
    normed_two_back = transposed(
        pre_back, lax.all_gather(up_weight, ("dp", "seq"), axis=0, tiled=True)
    )
    norm_result, pull_two = jax.vjp(layer_norm, middle, gain_two, shift_two)
    middle_part, gain_two_sum, shift_two_sum = pull_two(normed_two_back)
    middle_back = upstream + middle_part
    attention_back = (keep * middle_back).astype(jnp.bfloat16)
    output_shift_sum = jnp.sum(attention_back.astype(jnp.float32), axis=0)
    mixed_back = transposed(attention_back, output_full).astype(jnp.bfloat16)
    mixed_heads_back = mixed_back.reshape(nseq, piece_len, head_count, head_size)
    delta_rows = jnp.sum(mixed_heads_back.astype(jnp.float32) * mixed_heads, axis=-1)
    delta = delta_rows.transpose(0, 2, 1)
    lse_rows = lse.transpose(0, 2, 1)

    def query_step(acc, block, start):
        length = block.shape[1]
        allowed = key_mask(start, length)
        scores = local_scores(block[:, :, :width])
        probs = jnp.where(allowed, jnp.exp(scores - lse[..., None]), 0.0)
        valued = block[:, :, width:].reshape(nseq, length, head_count, head_size)
        keyed = block[:, :, :width].reshape(nseq, length, head_count, head_size)
        prob_back = jnp.einsum(
            "sqhd,skhd->shqk", mixed_heads_back, valued, preferred_element_type=jnp.float32
        )
        score_back = (probs * (prob_back - delta[..., None])).astype(jnp.bfloat16)
        return acc + jnp.einsum(
            "shqk,skhd->sqhd", score_back, keyed, preferred_element_type=jnp.float32
        )

    query_sum = by_blocks(
        query_step, empty_heads, lax.all_gather(pair_local, "seq", axis=1, tiled=True)
    )
    queries_back = (query_sum * scale).reshape(rows, width).astype(jnp.bfloat16)

    def key_step(carry, block, start):
        key_acc, value_acc = carry
        query_block, back_block, norm_block, delta_block = block
        length = query_block.shape[1]
        query_pos = start + jnp.arange(length, dtype=jnp.int32)
        query_seg = lax.dynamic_slice_in_dim(segments, start, length, 1)
        allowed = visible(query_seg, query_pos, own_seg, own_pos)[:, None]
        remote_query = query_block.astype(jnp.bfloat16).reshape(nseq, length, head_count, head_size)
        remote_back = back_block.astype(jnp.bfloat16).reshape(nseq, length, head_count, head_size)
        scores = (
            jnp.einsum(
                "sqhd,skhd->shqk", remote_query, key_heads, preferred_element_type=jnp.float32
            )
            * scale
        )
        probs = jnp.where(allowed, jnp.exp(scores - norm_block.transpose(0, 2, 1)[..., None]), 0.0)
        value_acc = value_acc + jnp.einsum(
            "shqk,sqhd->skhd",
            probs.astype(jnp.bfloat16),
            remote_back,
            preferred_element_type=jnp.float32,
        )
        prob_back = jnp.einsum(
            "sqhd,skhd->shqk", remote_back, value_heads, preferred_element_type=jnp.float32
        )
        score_back = (probs * (prob_back - delta_block.transpose(0, 2, 1)[..., None])).astype(
            jnp.bfloat16
        )
        key_acc = key_acc + jnp.einsum(
            "shqk,sqhd->skhd", score_back, remote_query, preferred_element_type=jnp.float32
        )
        return (key_acc, value_acc)

    query_send = queries.astype(jnp.float32).reshape(nseq, piece_len, width)
    back_send = mixed_back.astype(jnp.float32).reshape(nseq, piece_len, width)
    key_sum, value_sum = by_blocks(
        key_step,
        (empty_heads, empty_heads),
        (
            lax.all_gather(query_send.astype(jnp.bfloat16), "seq", axis=1, tiled=True).astype(
                jnp.float32
            ),
            lax.all_gather(back_send.astype(jnp.bfloat16), "seq", axis=1, tiled=True).astype(
                jnp.float32
            ),
            lax.all_gather(lse_rows.astype(jnp.bfloat16), "seq", axis=1, tiled=True).astype(
                jnp.float32
            ),
            lax.all_gather(delta_rows.astype(jnp.bfloat16), "seq", axis=1, tiled=True).astype(
                jnp.float32
            ),
        ),
    )
    keys_back = (key_sum * scale).reshape(rows, width).astype(jnp.bfloat16)
    values_back = value_sum.reshape(rows, width).astype(jnp.bfloat16)
    query_shift_sum = jnp.sum(queries_back.astype(jnp.float32), axis=0)
    value_shift_sum = jnp.sum(values_back.astype(jnp.float32), axis=0)
    normed_one_back = (
        transposed(queries_back, query_full)
        + transposed(keys_back, key_full)
        + transposed(values_back, value_full)
    )
    norm_first, pull_one = jax.vjp(layer_norm, inputs, gain_one, shift_one)
    inputs_part, gain_one_sum, shift_one_sum = pull_one(normed_one_back)
    tokens_gradient = (
        (middle_back + inputs_part).astype(jnp.bfloat16).reshape(nseq, piece_len, width)
    )
    stacked_back = jnp.concatenate([queries_back, keys_back, values_back], axis=1)
    row_gradient = lax.psum_scatter(
        jnp.concatenate(
            [
                leading(normed_one, stacked_back),
                leading(mixed, attention_back),
                leading(normed_two, pre_back),
            ],
            axis=1,
        ),
        ("dp", "seq"),
        scatter_dimension=0,
        tiled=True,
    )
    (
        gain_one_part,
        shift_one_part,
        query_shift_part,
        value_shift_part,
        output_shift_part,
        gain_two_part,
        shift_two_part,
        up_shift_part,
        down_shift_part,
    ) = (
        lax.psum_scatter(gain_one_sum, ("dp", "seq"), scatter_dimension=0, tiled=True),
        lax.psum_scatter(shift_one_sum, ("dp", "seq"), scatter_dimension=0, tiled=True),
        lax.psum_scatter(query_shift_sum, ("dp", "seq"), scatter_dimension=0, tiled=True),
        lax.psum_scatter(value_shift_sum, ("dp", "seq"), scatter_dimension=0, tiled=True),
        lax.psum_scatter(output_shift_sum, ("dp", "seq"), scatter_dimension=0, tiled=True),
        lax.psum_scatter(gain_two_sum, ("dp", "seq"), scatter_dimension=0, tiled=True),
        lax.psum_scatter(shift_two_sum, ("dp", "seq"), scatter_dimension=0, tiled=True),
        lax.psum_scatter(up_shift_sum, ("dp", "seq"), scatter_dimension=0, tiled=True),
        lax.psum_scatter(down_shift_sum, ("dp", "seq"), scatter_dimension=0, tiled=True),
    )
    return (
        layer_out,
        tokens_gradient,
        gain_one_part,
        shift_one_part,
        row_gradient[:, :width],
        query_shift_part,
        row_gradient[:, width : 2 * width],
        row_gradient[:, 2 * width : 3 * width],
        value_shift_part,
        row_gradient[:, 3 * width : 4 * width],
        output_shift_part,
        gain_two_part,
        shift_two_part,
        row_gradient[:, 4 * width :],
        up_shift_part,
        down_gradient,
        down_shift_part,
    )


MESH = pl.DeviceIdType.MESH
ORDERS = ("xyz", "yzx", "zxy")
CANON = "zyx"

def place():
    d = lax.axis_index("dp"); s = lax.axis_index("seq")
    half = lax.axis_size("dp") // 2
    far = d // half
    z = d + far * (2 * half - 1 - 2 * d)
    return dict(d=d, s=s, g=far, z=z, y=s // 4, x=(s // 2) % 2, c=s % 2)

def beside(w, dim):
    if dim == "z":
        return (w["d"] + 1 - 2 * (w["d"] % 2), w["s"])
    step = {"c": 1, "x": 2, "y": 4}[dim]
    return (w["d"], w["s"] + step * (1 - 2 * w[dim]))

def greet(ids):
    bar = pltpu.get_barrier_semaphore()
    for i in ids:
        pl.semaphore_signal(bar, inc=1, device_id=i, device_id_type=MESH)
    pl.semaphore_wait(bar, len(ids))

def column_parts(width):
    unit = width // 128
    cuts = [unit - 2 * (unit // 3), unit // 3, unit // 3]
    out, at = [], 0
    for c in cuts:
        out.append(pl.ds(at * 128, c * 128)); at += c
    return out

def box(w, open_dims, other=()):
    return tuple(pl.ds(0, 2) if q in open_dims else (1 - w[q] if q in other else w[q]) for q in CANON)

def gather_kernel(src, out, send, recv, csend, crecv, lsem):
    w = place()
    rows = src.shape[0]
    parts = column_parts(src.shape[1])
    greet([beside(w, q) for q in "cxyz"])
    def remote(a, b, ss, rs, dim):
        return pltpu.make_async_remote_copy(src_ref=a, dst_ref=b, send_sem=ss, recv_sem=rs, device_id=beside(w, dim), device_id_type=MESH)
    own = (w["z"], w["y"], w["x"], w["c"])
    everything = []
    links = {}
    for p, cols in enumerate(parts):
        cp = remote(src.at[:, cols], out.at[own + (slice(None), cols)], send.at[p, 0], recv.at[p, 0], ORDERS[p][0])
        cp.start(); links[p, 0] = cp
    keep = pltpu.make_async_copy(src, out.at[own], lsem)
    keep.start()
    sides = []
    for p, cols in enumerate(parts):
        cp = remote(src.at[:, cols], out.at[own + (slice(None), cols)], csend.at[p, 0], crecv.at[p, 0], "c")
        cp.start(); sides.append(cp)
    keep.wait()
    for k in range(3):
        for p, cols in enumerate(parts):
            order = ORDERS[p]
            links[p, k].wait_recv()
            if k < 2:
                at = box(w, order[: k + 1]) + (w["c"], slice(None), cols)
                cp = remote(out.at[at], out.at[at], send.at[p, k + 1], recv.at[p, k + 1], order[k + 1])
                cp.start(); links[p, k + 1] = cp
            at = box(w, order[:k], order[k]) + (w["c"], slice(None), cols)
            cp = remote(out.at[at], out.at[at], csend.at[p, k + 1], crecv.at[p, k + 1], "c")
            cp.start(); sides.append(cp)
    for cp in links.values():
        cp.wait_send()
    for cp in sides:
        cp.wait()

def cube_gather(own, name, cid):
    rows, width = own.shape
    return pl.pallas_call(
        gather_kernel,
        out_shape=jax.ShapeDtypeStruct((2, 2, 2, 2, rows, width), own.dtype),
        in_specs=[pl.BlockSpec(memory_space=pltpu.VMEM)],
        out_specs=pl.BlockSpec(memory_space=pltpu.VMEM),
        scratch_shapes=[pltpu.SemaphoreType.DMA((3, 3)), pltpu.SemaphoreType.DMA((3, 3)), pltpu.SemaphoreType.DMA((3, 4)), pltpu.SemaphoreType.DMA((3, 4)), pltpu.SemaphoreType.DMA],
        compiler_params=pltpu.CompilerParams(collective_id=cid, has_side_effects=True, vmem_limit_bytes=40 << 20),
        name=name,
    )(own)

def scatter_kernel(src, out, acc, side, r0, r1, r2, send, recv, csend, crecv, lsem):
    w = place()
    rows, width = out.shape
    parts = column_parts(width)
    greet([beside(w, q) for q in "cxyz"])
    def remote(a, b, ss, rs, dim):
        return pltpu.make_async_remote_copy(src_ref=a, dst_ref=b, send_sem=ss, recv_sem=rs, device_id=beside(w, dim), device_id_type=MESH)
    alls = (pl.ds(0, 2),) * 3
    first, local = [], []
    for p, cols in enumerate(parts):
        cp = remote(src.at[alls + (1 - w["c"], slice(None), cols)], side.at[alls + (slice(None), cols)], csend.at[p], crecv.at[p], "c")
        cp.start(); first.append(cp)
        lc = pltpu.make_async_copy(src.at[alls + (w["c"], slice(None), cols)], acc.at[alls + (slice(None), cols)], lsem.at[p])
        lc.start(); local.append(lc)
    land = (r0, r1, r2)
    def coords(order, k, fixed_k, a, b):
        left = [q for q in CANON if q in order[k + 1:]]
        vals = dict(zip(left, (a, b)))
        return tuple(vals[q] if q in vals else (w[q] if q != order[k] else (w[q] if fixed_k else 1 - w[q])) for q in CANON)
    links = {}
    def add_side(p, cols, fixed):
        order = ORDERS[p]
        @pl.loop(0, 4)
        def _(i):
            at = coords(order, 0, fixed, i // 2, i % 2) + (slice(None), cols)
            acc[at] = (acc[at].astype(jnp.float32) + side[at].astype(jnp.float32)).astype(acc.dtype)
    def push(p, cols, k):
        order = ORDERS[p]
        at = box(w, order[k + 1:], order[k]) + (slice(None), cols)
        n = 2 - k
        width_p = cols.size
        dst = land[k].at[(p,) + (pl.ds(0, 2),) * n + (slice(None), pl.ds(0, width_p))]
        cp = remote(acc.at[at], dst, send.at[p, k], recv.at[p, k], order[k])
        cp.start(); links[p, k] = cp
    for p, cols in enumerate(parts):
        first[p].wait_recv(); local[p].wait()
        add_side(p, cols, False)
        push(p, cols, 0)
        add_side(p, cols, True)
    for k in range(2):
        for p, cols in enumerate(parts):
            order = ORDERS[p]
            links[p, k].wait_recv()
            left = [q for q in CANON if q in order[k + 1:]]
            nxt = left.index(order[k + 1])
            def add(other):
                val = (1 - w[order[k + 1]]) if other else w[order[k + 1]]
                if k == 0:
                    @pl.loop(0, 2)
                    def _(i):
                        ab = (val, i) if nxt == 0 else (i, val)
                        at = coords(order, 0, True, *ab) + (slice(None), cols)
                        got = r0[(p,) + ab + (slice(None), pl.ds(0, cols.size))]
                        acc[at] = (acc[at].astype(jnp.float32) + got.astype(jnp.float32)).astype(acc.dtype)
                else:
                    at = coords(order, 1, True, val, val) + (slice(None), cols)
                    got = r1[(p, val, slice(None), pl.ds(0, cols.size))]
                    acc[at] = (acc[at].astype(jnp.float32) + got.astype(jnp.float32)).astype(acc.dtype)
            add(True)
            push(p, cols, k + 1)
            add(False)
    own = (w["z"], w["y"], w["x"])
    for p, cols in enumerate(parts):
        links[p, 2].wait_recv()
        out[:, cols] = acc[own + (slice(None), cols)].astype(jnp.float32) + r2[p, :, pl.ds(0, cols.size)].astype(jnp.float32)
    for cp in links.values():
        cp.wait_send()
    for cp in first:
        cp.wait_send()

def cube_scatter(partial, name, cid):
    rows, width = partial.shape[-2:]
    most = column_parts(width)[0].size
    dt = partial.dtype
    return pl.pallas_call(
        scatter_kernel,
        out_shape=jax.ShapeDtypeStruct((rows, width), jnp.float32),
        in_specs=[pl.BlockSpec(memory_space=pl.ANY)],
        out_specs=pl.BlockSpec(memory_space=pltpu.VMEM),
        scratch_shapes=[pltpu.VMEM((2, 2, 2, rows, width), dt), pltpu.VMEM((2, 2, 2, rows, width), dt),
            pltpu.VMEM((3, 2, 2, rows, most), dt), pltpu.VMEM((3, 2, rows, most), dt), pltpu.VMEM((3, rows, most), dt),
            pltpu.SemaphoreType.DMA((3, 3)), pltpu.SemaphoreType.DMA((3, 3)), pltpu.SemaphoreType.DMA((3,)), pltpu.SemaphoreType.DMA((3,)), pltpu.SemaphoreType.DMA((3,))],
        compiler_params=pltpu.CompilerParams(collective_id=cid, has_side_effects=True, vmem_limit_bytes=40 << 20),
        name=name,
    )(partial)

def peer(w, r):
    n = lax.axis_size("seq")
    e, s = r // n, r % n
    return (e + w["g"] * (lax.axis_size("dp") - 1 - 2 * e), s)

def anyone(w, i):
    n = lax.axis_size("seq")
    return (i // n, i % n)

def swap_kernel(device_of, row, src, out, send, recv, lsem):
    w = place()
    n = src.shape[0]
    me = w[row] * lax.axis_size("seq") + w["s"]
    others = [(me + k) % n for k in range(1, n)]
    greet([device_of(w, r) for r in others])
    cps = []
    for k, r in enumerate(others):
        cp = pltpu.make_async_remote_copy(src_ref=src.at[r], dst_ref=out.at[me], send_sem=send.at[k], recv_sem=recv.at[k], device_id=device_of(w, r), device_id_type=MESH)
        cp.start(); cps.append(cp)
    lc = pltpu.make_async_copy(src.at[me], out.at[me], lsem)
    lc.start(); lc.wait()
    for cp in cps:
        cp.wait()

def group_swap(blocks, name, cid):
    return swap(peer, "z", blocks, name, cid)


def world_swap(blocks, name, cid):
    return swap(anyone, "d", blocks, name, cid)


def swap(device_of, row, blocks, name, cid):
    n = blocks.shape[0]
    return pl.pallas_call(
        functools.partial(swap_kernel, device_of, row),
        out_shape=jax.ShapeDtypeStruct(blocks.shape, blocks.dtype),
        in_specs=[pl.BlockSpec(memory_space=pl.ANY)],
        out_specs=pl.BlockSpec(memory_space=pl.ANY),
        scratch_shapes=[pltpu.SemaphoreType.DMA((n - 1,)), pltpu.SemaphoreType.DMA((n - 1,)), pltpu.SemaphoreType.DMA],
        compiler_params=pltpu.CompilerParams(collective_id=cid, has_side_effects=True),
        name=name,
    )(blocks)


def head_lanes(width, head, size):
    lane = lax.broadcasted_iota(jnp.int32, (1, width), 1)
    return jnp.logical_and(lane >= head * size, lane < (head + 1) * size)


def used_pairs(key_seg, query_seg, first, length, block):
    key_pos = lax.broadcasted_iota(jnp.int32, (length, 1), 0)
    query_pos = first + lax.broadcasted_iota(jnp.int32, (1, block), 1)
    return jnp.logical_and(key_seg == query_seg, key_pos <= query_pos)


def across(left, right):
    return lax.dot_general(
        left, right, (((1,), (1,)), ((), ())), preferred_element_type=jnp.float32
    )


def attend_kernel(size, block, q_ref, k_ref, v_ref, key_seg_ref, query_seg_ref, mixed_ref, lse_ref):
    length, width = q_ref.shape[1:]
    heads = width // size
    scale = size**-0.5
    flipped = v_ref[0].T
    for first in range(0, length, block):
        upto = first + block
        rows = pl.ds(first, block)
        allowed = used_pairs(
            key_seg_ref[0, pl.ds(0, upto), :], query_seg_ref[0, :, rows], first, upto, block
        )
        keys = k_ref[0, pl.ds(0, upto), :]
        query = q_ref[0, rows, :] * jnp.asarray(scale, jnp.bfloat16)
        parts = []
        for head in range(heads):
            own = jnp.where(head_lanes(width, head, size), query, jnp.zeros_like(query))
            scores = jnp.where(allowed, across(keys, own), NEG)
            top = jnp.max(scores, axis=0, keepdims=True)
            weights = jnp.exp(scores - top)
            total = jnp.sum(weights, axis=0, keepdims=True)
            lse_ref[0, pl.ds(head, 1), rows] = top + jnp.log(total)
            probs = (weights * (1.0 / total)).astype(jnp.bfloat16)
            parts.append(
                jnp.dot(
                    flipped[head * size : (head + 1) * size, :upto],
                    probs,
                    preferred_element_type=jnp.float32,
                )
            )
        mixed_ref[0, rows, :] = jnp.concatenate(parts, axis=0).T


def attend(queries, keys, values, segs, size, name):
    count, length, width = queries.shape
    heads = width // size
    whole = pl.BlockSpec((1, length, width), lambda i: (i, 0, 0))
    return pl.pallas_call(
        functools.partial(attend_kernel, size, min(256, length)),
        grid=(count,),
        out_shape=(
            jax.ShapeDtypeStruct((count, length, width), jnp.float32),
            jax.ShapeDtypeStruct((count, heads, length), jnp.float32),
        ),
        in_specs=[
            whole,
            whole,
            whole,
            pl.BlockSpec((1, length, 1), lambda i: (i, 0, 0)),
            pl.BlockSpec((1, 1, length), lambda i: (i, 0, 0)),
        ],
        out_specs=(whole, pl.BlockSpec((1, heads, length), lambda i: (i, 0, 0))),
        compiler_params=pltpu.CompilerParams(vmem_limit_bytes=48 << 20),
        name=name,
    )(queries, keys, values, segs[:, :, None], segs[:, None, :])


def attend_back_kernel(
    size,
    block,
    q_ref,
    k_ref,
    v_ref,
    back_ref,
    mixed_ref,
    lse_ref,
    key_seg_ref,
    query_seg_ref,
    q_back_ref,
    k_back_ref,
    v_back_ref,
    k_sum,
    v_sum,
):
    length, width = q_ref.shape[1:]
    heads = width // size
    scale = size**-0.5
    flipped = k_ref[0].T
    k_sum[...] = jnp.zeros_like(k_sum)
    v_sum[...] = jnp.zeros_like(v_sum)
    for first in range(0, length, block):
        upto = first + block
        rows = pl.ds(first, block)
        before = pl.ds(0, upto)
        allowed = used_pairs(
            key_seg_ref[0, before, :], query_seg_ref[0, :, rows], first, upto, block
        )
        keys = k_ref[0, before, :]
        values = v_ref[0, before, :]
        query = q_ref[0, rows, :] * jnp.asarray(scale, jnp.bfloat16)
        back = back_ref[0, rows, :]
        product = (back.astype(jnp.float32) * mixed_ref[0, rows, :]).T
        parts = []
        for head in range(heads):
            lanes = head_lanes(width, head, size)
            own = jnp.where(lanes, query, jnp.zeros_like(query))
            own_back = jnp.where(lanes, back, jnp.zeros_like(back))
            delta = jnp.sum(product[head * size : (head + 1) * size, :], axis=0, keepdims=True)
            scores = across(keys, own) - lse_ref[0, pl.ds(head, 1), rows]
            probs = jnp.where(allowed, jnp.exp(jnp.where(allowed, scores, 0.0)), 0.0)
            score_back = (probs * (across(values, own_back) - delta)).astype(jnp.bfloat16)
            v_sum[before, :] += jnp.dot(
                probs.astype(jnp.bfloat16), own_back, preferred_element_type=jnp.float32
            )
            k_sum[before, :] += jnp.dot(score_back, own, preferred_element_type=jnp.float32)
            parts.append(
                jnp.dot(
                    flipped[head * size : (head + 1) * size, :upto],
                    score_back,
                    preferred_element_type=jnp.float32,
                )
            )
        q_back_ref[0, rows, :] = (jnp.concatenate(parts, axis=0).T * scale).astype(jnp.bfloat16)
    k_back_ref[0] = k_sum[...].astype(jnp.bfloat16)
    v_back_ref[0] = v_sum[...].astype(jnp.bfloat16)


def attend_back(queries, keys, values, back, mixed, lse, segs, size, name):
    count, length, width = queries.shape
    heads = width // size
    whole = pl.BlockSpec((1, length, width), lambda i: (i, 0, 0))
    shape = jax.ShapeDtypeStruct((count, length, width), jnp.bfloat16)
    return pl.pallas_call(
        functools.partial(attend_back_kernel, size, min(256, length)),
        grid=(count,),
        out_shape=(shape, shape, shape),
        in_specs=[whole] * 5
        + [
            pl.BlockSpec((1, heads, length), lambda i: (i, 0, 0)),
            pl.BlockSpec((1, length, 1), lambda i: (i, 0, 0)),
            pl.BlockSpec((1, 1, length), lambda i: (i, 0, 0)),
        ],
        out_specs=(whole, whole, whole),
        scratch_shapes=[pltpu.VMEM((length, width), jnp.float32)] * 2,
        compiler_params=pltpu.CompilerParams(vmem_limit_bytes=48 << 20),
        name=name,
    )(queries, keys, values, back, mixed, lse, segs[:, :, None], segs[:, None, :])


def near_half(blocks, ns, group):
    flip = blocks.reshape((2, ns) + blocks.shape[1:])[::-1].reshape(blocks.shape)
    return jnp.where(group == 0, blocks, flip)


def on_device_halves(
    tokens,
    segments,
    exit_layer,
    first_gain,
    first_shift,
    query_weight,
    query_bias,
    key_weight,
    value_weight,
    value_bias,
    output_weight,
    output_bias,
    second_gain,
    second_shift,
    up_weight,
    up_bias,
    down_weight,
    down_bias,
    cotangent,
):
    rows, width = tokens.shape[1:]
    nd, ns = lax.axis_size("dp"), lax.axis_size("seq")
    ndev, ranks = nd * ns, nd * ns // 2
    size = width // HEADS
    hidden_size = up_weight.shape[1]
    w = place()
    group = w["g"]
    me = w["z"] * ns + w["s"]
    mirror = [(d, nd - 1 - d) for d in range(nd)]

    def trade(value):
        return lax.ppermute(value, "dp", mirror)

    def pair(own, other):
        return jnp.where(group == 0, own, other), jnp.where(group == 0, other, own)

    def pieces(weight):
        cut = weight.reshape(weight.shape[0], 2, 2, ns, -1)
        low, high = cut[:, 0], cut[:, 1, ::-1]
        both = jnp.stack([low, high], axis=3)
        return both.transpose(1, 2, 0, 3, 4).reshape(ranks, weight.shape[0], -1)

    def whole_rows(swapped):
        mine, other = swapped, trade(swapped)
        low, high = pair(mine, other)
        flat = high.reshape((2, ns) + high.shape[1:])[::-1]
        return jnp.concatenate([low.reshape(-1, low.shape[-1]), flat.reshape(-1, low.shape[-1])])

    def own_rows(gradient):
        half = gradient.shape[0] // 2
        low, high = gradient[:half], gradient[half:]
        sent = jnp.where(group == 0, high, low).astype(jnp.bfloat16)
        kept = jnp.where(group == 0, low, high)
        total = (kept + trade(sent).astype(jnp.float32)).astype(jnp.bfloat16)
        return near_half(total.reshape(ranks, -1, total.shape[-1]), ns, group)

    def from_pieces(blocks, take):
        cut = blocks.reshape(2, ns, blocks.shape[1], 2, take)
        low, high = cut[:, :, :, 0], cut[::-1, :, :, 1]
        both = jnp.stack([low, high]).transpose(3, 0, 1, 2, 4)
        return both.reshape(blocks.shape[1], -1).astype(jnp.float32)

    def own_block(gradient):
        half = gradient.shape[0] // 2
        low, high = gradient[:half], gradient[half:]
        sent = jnp.where(group == 0, high, low).astype(jnp.bfloat16)
        return jnp.where(group == 0, low, high) + trade(sent).astype(jnp.float32)

    vector_parts = [
        first_gain,
        first_shift,
        query_bias,
        value_bias,
        output_bias,
        second_gain,
        second_shift,
        down_bias,
        up_bias,
    ]
    vectors = lax.all_gather(jnp.concatenate(vector_parts), ("dp", "seq"), axis=0)
    cuts, at = [], 0
    for part in vector_parts:
        cuts.append(vectors[:, at : at + part.shape[0]])
        at += part.shape[0]
    full = [cut.reshape(-1).astype(jnp.float32) for cut in cuts]
    gain_one, shift_one, _, _, output_shift, gain_two, shift_two, down_shift, _ = full
    low_at = me
    high_at = (nd - 1 - w["z"]) * ns + w["s"]

    def rank_vector(cut):
        return jnp.concatenate(
            [
                lax.dynamic_index_in_dim(cut, low_at, 0, keepdims=False),
                lax.dynamic_index_in_dim(cut, high_at, 0, keepdims=False),
            ]
        ).astype(jnp.float32)

    query_shift, value_shift, up_shift = (rank_vector(cuts[i]) for i in (2, 3, 8))
    attend_pieces = jnp.concatenate(
        [pieces(query_weight), pieces(key_weight), pieces(value_weight)], axis=2
    )
    attend_weight = whole_rows(group_swap(attend_pieces, "swap_attend", 0))
    output_rows = jnp.concatenate(pair(output_weight, trade(output_weight)))
    up_columns = whole_rows(group_swap(pieces(up_weight), "swap_up", 1))
    down_rows = jnp.concatenate(pair(down_weight, trade(down_weight)))

    beside_dp = [(d, d + 1 - 2 * (d % 2)) for d in range(nd)]
    other_segs = lax.ppermute(segments, "dp", beside_dp)
    segs = jnp.concatenate(
        [
            jnp.where(w["z"] == 0, segments, other_segs),
            jnp.where(w["z"] == 0, other_segs, segments),
        ]
    )

    keep = (exit_layer > LAYER).astype(jnp.float32).reshape(rows, 1)
    inputs = tokens.astype(jnp.float32).reshape(rows, width)
    upstream = cotangent.astype(jnp.float32).reshape(rows, width)
    branch_back_own = (keep * upstream).astype(jnp.bfloat16)

    def gathered(own, name, cid):
        return cube_gather(own, name, cid).reshape(-1, own.shape[1])

    def scattered(partial, name, cid):
        return cube_scatter(partial.reshape(2, 2, 2, 2, rows, -1), name, cid)

    normed_one = gathered(
        layer_norm(inputs, gain_one, shift_one).astype(jnp.bfloat16), "gather_one", 2
    )
    pre = jnp.dot(normed_one, attend_weight, preferred_element_type=jnp.float32)
    take = 2 * size
    queries = (pre[:, :take] + query_shift).astype(jnp.bfloat16).reshape(2, -1, take)
    keys = pre[:, take : 2 * take].astype(jnp.bfloat16).reshape(2, -1, take)
    values = (pre[:, 2 * take :] + value_shift).astype(jnp.bfloat16).reshape(2, -1, take)
    mixed_full, lse = attend(queries, keys, values, segs, size, "attend")
    mixed = mixed_full.reshape(-1, take).astype(jnp.bfloat16)
    attention = scattered(
        jnp.dot(mixed, output_rows, preferred_element_type=jnp.float32).astype(jnp.bfloat16),
        "scatter_attention",
        3,
    )
    middle = inputs + keep * (attention + output_shift)
    normed_two = gathered(
        layer_norm(middle, gain_two, shift_two).astype(jnp.bfloat16), "gather_two", 4
    )
    branch_back = gathered(branch_back_own, "gather_branch_back", 5)
    before = jnp.dot(normed_two, up_columns, preferred_element_type=jnp.float32) + up_shift
    active, pull_active = jax.vjp(activate, before)
    hidden = active.astype(jnp.bfloat16)
    hidden_back = transposed(branch_back, down_rows)
    pre_back = pull_active(hidden_back)[0].astype(jnp.bfloat16)
    normed_two_back = scattered(
        transposed(pre_back, up_columns).astype(jnp.bfloat16), "scatter_normed_two_back", 6
    )
    down_gradient = own_block(leading(hidden, branch_back))
    up_gradient = own_rows(leading(normed_two, pre_back))
    norm_result, pull_two = jax.vjp(layer_norm, middle, gain_two, shift_two)
    middle_part, gain_two_sum, shift_two_sum = pull_two(normed_two_back)
    middle_back = upstream + middle_part
    attention_back_own = (keep * middle_back).astype(jnp.bfloat16)
    attention_back = gathered(attention_back_own, "gather_attention_back", 7)
    mixed_back = transposed(attention_back, output_rows).astype(jnp.bfloat16)
    queries_back, keys_back, values_back = attend_back(
        queries, keys, values, mixed_back.reshape(2, -1, take), mixed_full, lse, segs, size, "attend_back"
    )
    stacked = jnp.concatenate([queries_back, keys_back, values_back], axis=2).reshape(-1, 3 * take)
    normed_one_back = scattered(
        transposed(stacked, attend_weight).astype(jnp.bfloat16), "scatter_normed_one_back", 8
    )
    branch = scattered(
        jnp.dot(hidden, down_rows, preferred_element_type=jnp.float32).astype(jnp.bfloat16),
        "scatter_branch",
        9,
    )
    layer_out = (middle + keep * (branch + down_shift)).astype(jnp.bfloat16)
    output_gradient = own_block(leading(mixed, attention_back))
    attend_gradient = own_rows(leading(normed_one, stacked))
    norm_first, pull_one = jax.vjp(layer_norm, inputs, gain_one, shift_one)
    inputs_part, gain_one_sum, shift_one_sum = pull_one(normed_one_back)
    tokens_gradient = (middle_back + inputs_part).astype(jnp.bfloat16)

    up_rows = from_pieces(group_swap(up_gradient, "swap_up_gradient", 10), hidden_size // ndev)
    attend_rows = group_swap(attend_gradient, "swap_attend_gradient", 11)
    matrix_rows = [
        from_pieces(attend_rows[:, :, i * take : (i + 1) * take], size) for i in range(3)
    ]

    def summed(value):
        return jnp.sum(value.astype(jnp.float32), axis=0)

    own_sums = [
        gain_one_sum,
        shift_one_sum,
        gain_two_sum,
        shift_two_sum,
        summed(attention_back_own),
        summed(branch_back_own),
    ]
    share = width // ndev
    dense = jnp.concatenate([value.reshape(ndev, share) for value in own_sums], axis=1)
    rank_sums = jnp.concatenate(
        [
            summed(queries_back.reshape(-1, take)).reshape(2, -1),
            summed(values_back.reshape(-1, take)).reshape(2, -1),
            summed(pre_back).reshape(2, -1),
        ],
        axis=1,
    )
    number = jnp.arange(ndev)[:, None]
    sparse = jnp.where(
        number == low_at, rank_sums[0], jnp.where(number == high_at, rank_sums[1], 0.0)
    )
    letter = jnp.concatenate([dense, sparse], axis=1)
    letter = jnp.pad(letter, ((0, 0), (0, -letter.shape[1] % 1024))).reshape(ndev, -1, 128)
    mail = jnp.sum(world_swap(letter, "swap_vectors", 12), axis=0).reshape(-1)
    vector_out, at = [], 0
    for part in (share,) * 6 + (size, size, hidden_size // ndev):
        vector_out.append(mail[at : at + part])
        at += part
    (
        gain_one_part,
        shift_one_part,
        gain_two_part,
        shift_two_part,
        output_shift_part,
        down_shift_part,
        query_shift_part,
        value_shift_part,
        up_shift_part,
    ) = vector_out
    return (
        layer_out.reshape(tokens.shape),
        tokens_gradient.reshape(tokens.shape),
        gain_one_part,
        shift_one_part,
        matrix_rows[0],
        query_shift_part,
        matrix_rows[1],
        matrix_rows[2],
        value_shift_part,
        output_gradient,
        output_shift_part,
        gain_two_part,
        shift_two_part,
        up_rows,
        up_shift_part,
        down_gradient,
        down_shift_part,
    )


def solution(mesh):
    placed = (
        P("dp", "seq", None),
        P("dp", None),
        P("dp", "seq"),
        P(("dp", "seq")),
        P(("dp", "seq")),
        P(("dp", "seq"), None),
        P(("dp", "seq")),
        P(("dp", "seq"), None),
        P(("dp", "seq"), None),
        P(("dp", "seq")),
        P(("dp", "seq"), None),
        P(("dp", "seq")),
        P(("dp", "seq")),
        P(("dp", "seq")),
        P(("dp", "seq"), None),
        P(("dp", "seq")),
        P(("dp", "seq"), None),
        P(("dp", "seq")),
        P("dp", "seq", None),
    )
    halves = mesh.shape["dp"] == 4 and mesh.shape["seq"] == 8
    return jax.shard_map(
        on_device_halves if halves else on_device,
        mesh=mesh,
        in_specs=placed,
        out_specs=(
            P("dp", "seq", None),
            P("dp", "seq", None),
            P(("dp", "seq")),
            P(("dp", "seq")),
            P(("dp", "seq"), None),
            P(("dp", "seq")),
            P(("dp", "seq"), None),
            P(("dp", "seq"), None),
            P(("dp", "seq")),
            P(("dp", "seq"), None),
            P(("dp", "seq")),
            P(("dp", "seq")),
            P(("dp", "seq")),
            P(("dp", "seq"), None),
            P(("dp", "seq")),
            P(("dp", "seq"), None),
            P(("dp", "seq")),
        ),
        check_vma=False,
    )
```

```python
import functools
import math

import jax
import jax.numpy as jnp
from jax import lax
from jax.experimental import pallas as pl
from jax.experimental.pallas import tpu as pltpu
from jax.sharding import PartitionSpec as P

HEADS = 32
LAYER = 12


EPS = 1e-05
NEG = -1e30


def activate(value):
    return jax.nn.gelu(value, approximate=True)


def layer_norm(value, gain, shift):
    mean = jnp.mean(value, axis=-1, keepdims=True)
    centred = value - mean
    spread = jnp.mean(centred * centred, axis=-1, keepdims=True)
    return centred * lax.rsqrt(spread + EPS) * gain + shift


def transposed(left, right):
    return lax.dot_general(
        left, right, (((1,), (1,)), ((), ())), preferred_element_type=jnp.float32
    )


def leading(left, right):
    return lax.dot_general(
        left, right, (((0,), (0,)), ((), ())), preferred_element_type=jnp.float32
    )


def visible(query_seg, query_pos, key_seg, key_pos):
    same = query_seg[:, :, None] == key_seg[:, None, :]
    return jnp.logical_and(same, key_pos[None, None, :] <= query_pos[None, :, None])


def by_blocks(step, carry, piece):
    length = jax.tree.leaves(piece)[0].shape[1]
    size = math.gcd(length, 128)

    def one(index, state):
        offset = index * size
        block = jax.tree.map(lambda part: lax.dynamic_slice_in_dim(part, offset, size, 1), piece)
        return step(state, block, offset)

    return lax.fori_loop(0, length // size, one, carry)


def on_device(
    tokens,
    segments,
    exit_layer,
    first_gain,
    first_shift,
    query_weight,
    query_bias,
    key_weight,
    value_weight,
    value_bias,
    output_weight,
    output_bias,
    second_gain,
    second_shift,
    up_weight,
    up_bias,
    down_weight,
    down_bias,
    cotangent,
):
    nseq, piece_len, width = tokens.shape
    head_count = HEADS
    head_size = width // head_count
    scale = head_size ** (-0.5)
    rows = nseq * piece_len
    own_first = lax.axis_index("seq") * piece_len
    own_pos = own_first + jnp.arange(piece_len, dtype=jnp.int32)
    own_seg = lax.dynamic_slice_in_dim(segments, own_first, piece_len, 1)
    keep = (exit_layer > LAYER).astype(jnp.float32).reshape(rows, 1)
    (
        gain_one,
        shift_one,
        query_full,
        query_shift,
        key_full,
        value_full,
        value_shift,
        output_full,
        output_shift,
        gain_two,
        shift_two,
        up_shift,
        down_shift,
    ) = (
        lax.all_gather(first_gain, ("dp", "seq"), axis=0, tiled=True),
        lax.all_gather(first_shift, ("dp", "seq"), axis=0, tiled=True),
        lax.all_gather(query_weight, ("dp", "seq"), axis=0, tiled=True),
        lax.all_gather(query_bias, ("dp", "seq"), axis=0, tiled=True),
        lax.all_gather(key_weight, ("dp", "seq"), axis=0, tiled=True),
        lax.all_gather(value_weight, ("dp", "seq"), axis=0, tiled=True),
        lax.all_gather(value_bias, ("dp", "seq"), axis=0, tiled=True),
        lax.all_gather(output_weight, ("dp", "seq"), axis=0, tiled=True),
        lax.all_gather(output_bias, ("dp", "seq"), axis=0, tiled=True),
        lax.all_gather(second_gain, ("dp", "seq"), axis=0, tiled=True),
        lax.all_gather(second_shift, ("dp", "seq"), axis=0, tiled=True),
        lax.all_gather(up_bias, ("dp", "seq"), axis=0, tiled=True),
        lax.all_gather(down_bias, ("dp", "seq"), axis=0, tiled=True),
    )
    gain_one = gain_one.astype(jnp.float32)
    shift_one = shift_one.astype(jnp.float32)
    gain_two = gain_two.astype(jnp.float32)
    shift_two = shift_two.astype(jnp.float32)
    inputs = tokens.astype(jnp.float32).reshape(rows, width)
    normed_one = layer_norm(inputs, gain_one, shift_one).astype(jnp.bfloat16)
    queries = (
        jnp.dot(normed_one, query_full, preferred_element_type=jnp.float32)
        + query_shift.astype(jnp.float32)
    ).astype(jnp.bfloat16)
    keys = jnp.dot(normed_one, key_full, preferred_element_type=jnp.float32).astype(jnp.bfloat16)
    values = (
        jnp.dot(normed_one, value_full, preferred_element_type=jnp.float32)
        + value_shift.astype(jnp.float32)
    ).astype(jnp.bfloat16)
    query_heads = queries.reshape(nseq, piece_len, head_count, head_size)
    key_heads = keys.reshape(nseq, piece_len, head_count, head_size)
    value_heads = values.reshape(nseq, piece_len, head_count, head_size)
    key_local = keys.reshape(nseq, piece_len, width)
    pair_local = jnp.concatenate([keys, values], axis=1).reshape(nseq, piece_len, 2 * width)

    def key_mask(start, length):
        key_pos = start + jnp.arange(length, dtype=jnp.int32)
        key_seg = lax.dynamic_slice_in_dim(segments, start, length, 1)
        return visible(own_seg, own_pos, key_seg, key_pos)[:, None]

    def local_scores(key_block):
        keyed = key_block.reshape(nseq, key_block.shape[1], head_count, head_size)
        return (
            jnp.einsum("sqhd,skhd->shqk", query_heads, keyed, preferred_element_type=jnp.float32)
            * scale
        )

    def norm_step(carry, block, start):
        top, total = carry
        allowed = key_mask(start, block.shape[1])
        scores = jnp.where(allowed, local_scores(block), NEG)
        new_top = jnp.maximum(top, jnp.max(scores, axis=-1))
        weights = jnp.where(allowed, jnp.exp(scores - new_top[..., None]), 0.0)
        return (new_top, total * jnp.exp(top - new_top) + jnp.sum(weights, axis=-1))

    start_norm = (
        jnp.full((nseq, head_count, piece_len), NEG, jnp.float32),
        jnp.zeros((nseq, head_count, piece_len), jnp.float32),
    )
    top, total = by_blocks(
        norm_step, start_norm, lax.all_gather(key_local, "seq", axis=1, tiled=True)
    )
    lse = top + jnp.log(total)

    def mix_step(acc, block, start):
        length = block.shape[1]
        allowed = key_mask(start, length)
        scores = local_scores(block[:, :, :width])
        probs = jnp.where(allowed, jnp.exp(scores - lse[..., None]), 0.0).astype(jnp.bfloat16)
        valued = block[:, :, width:].reshape(nseq, length, head_count, head_size)
        return acc + jnp.einsum(
            "shqk,skhd->sqhd", probs, valued, preferred_element_type=jnp.float32
        )

    empty_heads = jnp.zeros((nseq, piece_len, head_count, head_size), jnp.float32)
    mixed_heads = by_blocks(
        mix_step, empty_heads, lax.all_gather(pair_local, "seq", axis=1, tiled=True)
    )
    mixed = mixed_heads.reshape(rows, width).astype(jnp.bfloat16)
    attention = jnp.dot(
        mixed, output_full, preferred_element_type=jnp.float32
    ) + output_shift.astype(jnp.float32)
    middle = inputs + keep * attention
    normed_two = layer_norm(middle, gain_two, shift_two).astype(jnp.bfloat16)
    columns = normed_two
    before = jnp.dot(
        columns,
        lax.all_gather(up_weight, ("dp", "seq"), axis=0, tiled=True),
        preferred_element_type=jnp.float32,
    )
    pre_active = before + up_shift.astype(jnp.float32)
    hidden = activate(pre_active).astype(jnp.bfloat16)
    columns = hidden
    branch = jnp.dot(
        columns,
        lax.all_gather(down_weight, ("dp", "seq"), axis=0, tiled=True),
        preferred_element_type=jnp.float32,
    )
    branch = branch + down_shift.astype(jnp.float32)
    layer_out = (middle + keep * branch).astype(jnp.bfloat16).reshape(nseq, piece_len, width)
    upstream = cotangent.astype(jnp.float32).reshape(rows, width)
    branch_back = (keep * upstream).astype(jnp.bfloat16)
    down_shift_sum = jnp.sum(branch_back.astype(jnp.float32), axis=0)
    hidden_back = transposed(
        branch_back, lax.all_gather(down_weight, ("dp", "seq"), axis=0, tiled=True)
    )
    active_value, pull_active = jax.vjp(activate, pre_active)
    pre_back = pull_active(hidden_back)[0].astype(jnp.bfloat16)
    up_shift_sum = jnp.sum(pre_back.astype(jnp.float32), axis=0)
    down_gradient = lax.psum_scatter(
        leading(hidden, branch_back), ("dp", "seq"), scatter_dimension=0, tiled=True
    )
    normed_two_back = transposed(
        pre_back, lax.all_gather(up_weight, ("dp", "seq"), axis=0, tiled=True)
    )
    norm_result, pull_two = jax.vjp(layer_norm, middle, gain_two, shift_two)
    middle_part, gain_two_sum, shift_two_sum = pull_two(normed_two_back)
    middle_back = upstream + middle_part
    attention_back = (keep * middle_back).astype(jnp.bfloat16)
    output_shift_sum = jnp.sum(attention_back.astype(jnp.float32), axis=0)
    mixed_back = transposed(attention_back, output_full).astype(jnp.bfloat16)
    mixed_heads_back = mixed_back.reshape(nseq, piece_len, head_count, head_size)
    delta_rows = jnp.sum(mixed_heads_back.astype(jnp.float32) * mixed_heads, axis=-1)
    delta = delta_rows.transpose(0, 2, 1)
    lse_rows = lse.transpose(0, 2, 1)

    def query_step(acc, block, start):
        length = block.shape[1]
        allowed = key_mask(start, length)
        scores = local_scores(block[:, :, :width])
        probs = jnp.where(allowed, jnp.exp(scores - lse[..., None]), 0.0)
        valued = block[:, :, width:].reshape(nseq, length, head_count, head_size)
        keyed = block[:, :, :width].reshape(nseq, length, head_count, head_size)
        prob_back = jnp.einsum(
            "sqhd,skhd->shqk", mixed_heads_back, valued, preferred_element_type=jnp.float32
        )
        score_back = (probs * (prob_back - delta[..., None])).astype(jnp.bfloat16)
        return acc + jnp.einsum(
            "shqk,skhd->sqhd", score_back, keyed, preferred_element_type=jnp.float32
        )

    query_sum = by_blocks(
        query_step, empty_heads, lax.all_gather(pair_local, "seq", axis=1, tiled=True)
    )
    queries_back = (query_sum * scale).reshape(rows, width).astype(jnp.bfloat16)

    def key_step(carry, block, start):
        key_acc, value_acc = carry
        query_block, back_block, norm_block, delta_block = block
        length = query_block.shape[1]
        query_pos = start + jnp.arange(length, dtype=jnp.int32)
        query_seg = lax.dynamic_slice_in_dim(segments, start, length, 1)
        allowed = visible(query_seg, query_pos, own_seg, own_pos)[:, None]
        remote_query = query_block.astype(jnp.bfloat16).reshape(nseq, length, head_count, head_size)
        remote_back = back_block.astype(jnp.bfloat16).reshape(nseq, length, head_count, head_size)
        scores = (
            jnp.einsum(
                "sqhd,skhd->shqk", remote_query, key_heads, preferred_element_type=jnp.float32
            )
            * scale
        )
        probs = jnp.where(allowed, jnp.exp(scores - norm_block.transpose(0, 2, 1)[..., None]), 0.0)
        value_acc = value_acc + jnp.einsum(
            "shqk,sqhd->skhd",
            probs.astype(jnp.bfloat16),
            remote_back,
            preferred_element_type=jnp.float32,
        )
        prob_back = jnp.einsum(
            "sqhd,skhd->shqk", remote_back, value_heads, preferred_element_type=jnp.float32
        )
        score_back = (probs * (prob_back - delta_block.transpose(0, 2, 1)[..., None])).astype(
            jnp.bfloat16
        )
        key_acc = key_acc + jnp.einsum(
            "shqk,sqhd->skhd", score_back, remote_query, preferred_element_type=jnp.float32
        )
        return (key_acc, value_acc)

    query_send = queries.astype(jnp.float32).reshape(nseq, piece_len, width)
    back_send = mixed_back.astype(jnp.float32).reshape(nseq, piece_len, width)
    key_sum, value_sum = by_blocks(
        key_step,
        (empty_heads, empty_heads),
        (
            lax.all_gather(query_send.astype(jnp.bfloat16), "seq", axis=1, tiled=True).astype(
                jnp.float32
            ),
            lax.all_gather(back_send.astype(jnp.bfloat16), "seq", axis=1, tiled=True).astype(
                jnp.float32
            ),
            lax.all_gather(lse_rows.astype(jnp.bfloat16), "seq", axis=1, tiled=True).astype(
                jnp.float32
            ),
            lax.all_gather(delta_rows.astype(jnp.bfloat16), "seq", axis=1, tiled=True).astype(
                jnp.float32
            ),
        ),
    )
    keys_back = (key_sum * scale).reshape(rows, width).astype(jnp.bfloat16)
    values_back = value_sum.reshape(rows, width).astype(jnp.bfloat16)
    query_shift_sum = jnp.sum(queries_back.astype(jnp.float32), axis=0)
    value_shift_sum = jnp.sum(values_back.astype(jnp.float32), axis=0)
    normed_one_back = (
        transposed(queries_back, query_full)
        + transposed(keys_back, key_full)
        + transposed(values_back, value_full)
    )
    norm_first, pull_one = jax.vjp(layer_norm, inputs, gain_one, shift_one)
    inputs_part, gain_one_sum, shift_one_sum = pull_one(normed_one_back)
    tokens_gradient = (
        (middle_back + inputs_part).astype(jnp.bfloat16).reshape(nseq, piece_len, width)
    )
    stacked_back = jnp.concatenate([queries_back, keys_back, values_back], axis=1)
    row_gradient = lax.psum_scatter(
        jnp.concatenate(
            [
                leading(normed_one, stacked_back),
                leading(mixed, attention_back),
                leading(normed_two, pre_back),
            ],
            axis=1,
        ),
        ("dp", "seq"),
        scatter_dimension=0,
        tiled=True,
    )
    (
        gain_one_part,
        shift_one_part,
        query_shift_part,
        value_shift_part,
        output_shift_part,
        gain_two_part,
        shift_two_part,
        up_shift_part,
        down_shift_part,
    ) = (
        lax.psum_scatter(gain_one_sum, ("dp", "seq"), scatter_dimension=0, tiled=True),
        lax.psum_scatter(shift_one_sum, ("dp", "seq"), scatter_dimension=0, tiled=True),
        lax.psum_scatter(query_shift_sum, ("dp", "seq"), scatter_dimension=0, tiled=True),
        lax.psum_scatter(value_shift_sum, ("dp", "seq"), scatter_dimension=0, tiled=True),
        lax.psum_scatter(output_shift_sum, ("dp", "seq"), scatter_dimension=0, tiled=True),
        lax.psum_scatter(gain_two_sum, ("dp", "seq"), scatter_dimension=0, tiled=True),
        lax.psum_scatter(shift_two_sum, ("dp", "seq"), scatter_dimension=0, tiled=True),
        lax.psum_scatter(up_shift_sum, ("dp", "seq"), scatter_dimension=0, tiled=True),
        lax.psum_scatter(down_shift_sum, ("dp", "seq"), scatter_dimension=0, tiled=True),
    )
    return (
        layer_out,
        tokens_gradient,
        gain_one_part,
        shift_one_part,
        row_gradient[:, :width],
        query_shift_part,
        row_gradient[:, width : 2 * width],
        row_gradient[:, 2 * width : 3 * width],
        value_shift_part,
        row_gradient[:, 3 * width : 4 * width],
        output_shift_part,
        gain_two_part,
        shift_two_part,
        row_gradient[:, 4 * width :],
        up_shift_part,
        down_gradient,
        down_shift_part,
    )


MESH = pl.DeviceIdType.MESH
ORDERS = ("xyz", "yzx", "zxy")
CANON = "zyx"

def place():
    d = lax.axis_index("dp"); s = lax.axis_index("seq")
    half = lax.axis_size("dp") // 2
    far = d // half
    z = d + far * (2 * half - 1 - 2 * d)
    return dict(d=d, s=s, g=far, z=z, y=s // 4, x=(s // 2) % 2, c=s % 2)

def beside(w, dim):
    if dim == "z":
        return (w["d"] + 1 - 2 * (w["d"] % 2), w["s"])
    step = {"c": 1, "x": 2, "y": 4}[dim]
    return (w["d"], w["s"] + step * (1 - 2 * w[dim]))

def greet(ids):
    bar = pltpu.get_barrier_semaphore()
    for i in ids:
        pl.semaphore_signal(bar, inc=1, device_id=i, device_id_type=MESH)
    pl.semaphore_wait(bar, len(ids))

def column_parts(width):
    unit = width // 128
    cuts = [unit - 2 * (unit // 3), unit // 3, unit // 3]
    out, at = [], 0
    for c in cuts:
        out.append(pl.ds(at * 128, c * 128)); at += c
    return out

def box(w, open_dims, other=()):
    return tuple(pl.ds(0, 2) if q in open_dims else (1 - w[q] if q in other else w[q]) for q in CANON)

def gather_kernel(src, out, send, recv, csend, crecv, lsem):
    w = place()
    rows = src.shape[0]
    parts = column_parts(src.shape[1])
    greet([beside(w, q) for q in "cxyz"])
    def remote(a, b, ss, rs, dim):
        return pltpu.make_async_remote_copy(src_ref=a, dst_ref=b, send_sem=ss, recv_sem=rs, device_id=beside(w, dim), device_id_type=MESH)
    own = (w["z"], w["y"], w["x"], w["c"])
    everything = []
    links = {}
    for p, cols in enumerate(parts):
        cp = remote(src.at[:, cols], out.at[own + (slice(None), cols)], send.at[p, 0], recv.at[p, 0], ORDERS[p][0])
        cp.start(); links[p, 0] = cp
    keep = pltpu.make_async_copy(src, out.at[own], lsem)
    keep.start()
    sides = []
    for p, cols in enumerate(parts):
        cp = remote(src.at[:, cols], out.at[own + (slice(None), cols)], csend.at[p, 0], crecv.at[p, 0], "c")
        cp.start(); sides.append(cp)
    keep.wait()
    for k in range(3):
        for p, cols in enumerate(parts):
            order = ORDERS[p]
            links[p, k].wait_recv()
            if k < 2:
                at = box(w, order[: k + 1]) + (w["c"], slice(None), cols)
                cp = remote(out.at[at], out.at[at], send.at[p, k + 1], recv.at[p, k + 1], order[k + 1])
                cp.start(); links[p, k + 1] = cp
            at = box(w, order[:k], order[k]) + (w["c"], slice(None), cols)
            cp = remote(out.at[at], out.at[at], csend.at[p, k + 1], crecv.at[p, k + 1], "c")
            cp.start(); sides.append(cp)
    for cp in links.values():
        cp.wait_send()
    for cp in sides:
        cp.wait()

def cube_gather(own, name, cid):
    rows, width = own.shape
    return pl.pallas_call(
        gather_kernel,
        out_shape=jax.ShapeDtypeStruct((2, 2, 2, 2, rows, width), own.dtype),
        in_specs=[pl.BlockSpec(memory_space=pltpu.VMEM)],
        out_specs=pl.BlockSpec(memory_space=pltpu.VMEM),
        scratch_shapes=[pltpu.SemaphoreType.DMA((3, 3)), pltpu.SemaphoreType.DMA((3, 3)), pltpu.SemaphoreType.DMA((3, 4)), pltpu.SemaphoreType.DMA((3, 4)), pltpu.SemaphoreType.DMA],
        compiler_params=pltpu.CompilerParams(collective_id=cid, has_side_effects=True, vmem_limit_bytes=40 << 20),
        name=name,
    )(own)

def scatter_kernel(src, out, acc, side, r0, r1, r2, send, recv, csend, crecv, lsem):
    w = place()
    rows, width = out.shape
    parts = column_parts(width)
    greet([beside(w, q) for q in "cxyz"])
    def remote(a, b, ss, rs, dim):
        return pltpu.make_async_remote_copy(src_ref=a, dst_ref=b, send_sem=ss, recv_sem=rs, device_id=beside(w, dim), device_id_type=MESH)
    alls = (pl.ds(0, 2),) * 3
    first, local = [], []
    for p, cols in enumerate(parts):
        cp = remote(src.at[alls + (1 - w["c"], slice(None), cols)], side.at[alls + (slice(None), cols)], csend.at[p], crecv.at[p], "c")
        cp.start(); first.append(cp)
        lc = pltpu.make_async_copy(src.at[alls + (w["c"], slice(None), cols)], acc.at[alls + (slice(None), cols)], lsem.at[p])
        lc.start(); local.append(lc)
    land = (r0, r1, r2)
    def coords(order, k, fixed_k, a, b):
        left = [q for q in CANON if q in order[k + 1:]]
        vals = dict(zip(left, (a, b)))
        return tuple(vals[q] if q in vals else (w[q] if q != order[k] else (w[q] if fixed_k else 1 - w[q])) for q in CANON)
    links = {}
    def add_side(p, cols, fixed):
        order = ORDERS[p]
        @pl.loop(0, 4)
        def _(i):
            at = coords(order, 0, fixed, i // 2, i % 2) + (slice(None), cols)
            acc[at] = (acc[at].astype(jnp.float32) + side[at].astype(jnp.float32)).astype(acc.dtype)
    def push(p, cols, k):
        order = ORDERS[p]
        at = box(w, order[k + 1:], order[k]) + (slice(None), cols)
        n = 2 - k
        width_p = cols.size
        dst = land[k].at[(p,) + (pl.ds(0, 2),) * n + (slice(None), pl.ds(0, width_p))]
        cp = remote(acc.at[at], dst, send.at[p, k], recv.at[p, k], order[k])
        cp.start(); links[p, k] = cp
    for p, cols in enumerate(parts):
        first[p].wait_recv(); local[p].wait()
        add_side(p, cols, False)
        push(p, cols, 0)
        add_side(p, cols, True)
    for k in range(2):
        for p, cols in enumerate(parts):
            order = ORDERS[p]
            links[p, k].wait_recv()
            left = [q for q in CANON if q in order[k + 1:]]
            nxt = left.index(order[k + 1])
            def add(other):
                val = (1 - w[order[k + 1]]) if other else w[order[k + 1]]
                if k == 0:
                    @pl.loop(0, 2)
                    def _(i):
                        ab = (val, i) if nxt == 0 else (i, val)
                        at = coords(order, 0, True, *ab) + (slice(None), cols)
                        got = r0[(p,) + ab + (slice(None), pl.ds(0, cols.size))]
                        acc[at] = (acc[at].astype(jnp.float32) + got.astype(jnp.float32)).astype(acc.dtype)
                else:
                    at = coords(order, 1, True, val, val) + (slice(None), cols)
                    got = r1[(p, val, slice(None), pl.ds(0, cols.size))]
                    acc[at] = (acc[at].astype(jnp.float32) + got.astype(jnp.float32)).astype(acc.dtype)
            add(True)
            push(p, cols, k + 1)
            add(False)
    own = (w["z"], w["y"], w["x"])
    for p, cols in enumerate(parts):
        links[p, 2].wait_recv()
        out[:, cols] = acc[own + (slice(None), cols)].astype(jnp.float32) + r2[p, :, pl.ds(0, cols.size)].astype(jnp.float32)
    for cp in links.values():
        cp.wait_send()
    for cp in first:
        cp.wait_send()

def cube_scatter(partial, name, cid):
    rows, width = partial.shape[-2:]
    most = column_parts(width)[0].size
    dt = partial.dtype
    return pl.pallas_call(
        scatter_kernel,
        out_shape=jax.ShapeDtypeStruct((rows, width), jnp.float32),
        in_specs=[pl.BlockSpec(memory_space=pl.ANY)],
        out_specs=pl.BlockSpec(memory_space=pltpu.VMEM),
        scratch_shapes=[pltpu.VMEM((2, 2, 2, rows, width), dt), pltpu.VMEM((2, 2, 2, rows, width), dt),
            pltpu.VMEM((3, 2, 2, rows, most), dt), pltpu.VMEM((3, 2, rows, most), dt), pltpu.VMEM((3, rows, most), dt),
            pltpu.SemaphoreType.DMA((3, 3)), pltpu.SemaphoreType.DMA((3, 3)), pltpu.SemaphoreType.DMA((3,)), pltpu.SemaphoreType.DMA((3,)), pltpu.SemaphoreType.DMA((3,))],
        compiler_params=pltpu.CompilerParams(collective_id=cid, has_side_effects=True, vmem_limit_bytes=40 << 20),
        name=name,
    )(partial)

def peer(w, r):
    n = lax.axis_size("seq")
    e, s = r // n, r % n
    return (e + w["g"] * (lax.axis_size("dp") - 1 - 2 * e), s)


def anyone(w, i):
    n = lax.axis_size("seq")
    return (i // n, i % n)


HALF, WORLD, SPREAD = "half", "world", "spread"


def mail_order(w, kind, count):
    me = w["z" if kind == HALF else "d"] * lax.axis_size("seq") + w["s"]
    return me, [(me + k) % count for k in range(1, count)], peer if kind == HALF else anyone


def mail_copies(w, kind, src, out, send, recv, local):
    me, others, device_of = mail_order(w, kind, out.shape[0])
    copies = []
    for k, r in enumerate(others):
        copies.append(
            pltpu.make_async_remote_copy(
                src_ref=src if kind == SPREAD else src.at[r],
                dst_ref=out.at[me],
                send_sem=send.at[k],
                recv_sem=recv.at[k],
                device_id=device_of(w, r),
                device_id_type=MESH,
            )
        )
    own = pltpu.make_async_copy(src if kind == SPREAD else src.at[me], out.at[me], local)
    return copies + [own]


def mail(w, kind, src, out, send, recv, local):
    copies = mail_copies(w, kind, src, out, send, recv, local)
    for cp in copies:
        cp.start()
    return copies


def greet_mail(w, kinds_counts):
    counts = dict(kinds_counts)
    wide = max((n for kind, n in counts.items() if kind != HALF), default=0)
    if wide:
        _, others, device_of = mail_order(w, WORLD, wide)
    else:
        _, others, device_of = mail_order(w, HALF, counts[HALF])
    greet([device_of(w, r) for r in others])


def mail_kernel(kinds, *refs):
    n = len(kinds)
    srcs, outs, sems = refs[:n], refs[n : 2 * n], refs[2 * n :]
    w = place()
    greet_mail(w, [(kind, out.shape[0]) for kind, out in zip(kinds, outs)])
    copies = []
    for i, kind in enumerate(kinds):
        copies += mail(w, kind, srcs[i], outs[i], *sems[3 * i : 3 * i + 3])
    for cp in copies:
        cp.wait()


def mail_sems(count):
    return [
        pltpu.SemaphoreType.DMA((count - 1,)),
        pltpu.SemaphoreType.DMA((count - 1,)),
        pltpu.SemaphoreType.DMA,
    ]


def swap(items, name, cid):
    anywhere = pl.BlockSpec(memory_space=pl.ANY)
    kinds = [kind for _, kind in items]
    ndev = lax.axis_size("dp") * lax.axis_size("seq")
    shapes = [
        jax.ShapeDtypeStruct((ndev,) + x.shape if kind == SPREAD else x.shape, x.dtype)
        for x, kind in items
    ]
    return pl.pallas_call(
        functools.partial(mail_kernel, kinds),
        out_shape=tuple(shapes),
        in_specs=[anywhere] * len(items),
        out_specs=tuple([anywhere] * len(items)),
        scratch_shapes=[sem for shape in shapes for sem in mail_sems(shape.shape[0])],
        compiler_params=pltpu.CompilerParams(collective_id=cid, has_side_effects=True),
        name=name,
    )(*[x for x, _ in items])


def head_lanes(width, head, size):
    lane = lax.broadcasted_iota(jnp.int32, (1, width), 1)
    return jnp.logical_and(lane >= head * size, lane < (head + 1) * size)


def used_pairs(key_seg, query_seg, first, length, block):
    key_pos = lax.broadcasted_iota(jnp.int32, (length, 1), 0)
    query_pos = first + lax.broadcasted_iota(jnp.int32, (1, block), 1)
    return jnp.logical_and(key_seg == query_seg, key_pos <= query_pos)


def across(left, right):
    return lax.dot_general(
        left, right, (((1,), (1,)), ((), ())), preferred_element_type=jnp.float32
    )


def beside_mail(src, out, sems, work):
    w = place()

    @pl.when(pl.program_id(0) == 0)
    def _():
        greet_mail(w, [(HALF, out.shape[0])])
        mail(w, HALF, src, out, *sems)

    work()

    @pl.when(pl.program_id(0) == pl.num_programs(0) - 1)
    def _():
        for cp in mail_copies(w, HALF, src, out, *sems):
            cp.wait()


def attend_kernel(
    size,
    block,
    q_ref,
    k_ref,
    v_ref,
    key_seg_ref,
    query_seg_ref,
    mail_ref,
    mixed_ref,
    lse_ref,
    mailed_ref,
    *sems,
):
    beside_mail(
        mail_ref,
        mailed_ref,
        sems,
        lambda: attend_step(
            size, block, q_ref, k_ref, v_ref, key_seg_ref, query_seg_ref, mixed_ref, lse_ref
        ),
    )


def attend_step(size, block, q_ref, k_ref, v_ref, key_seg_ref, query_seg_ref, mixed_ref, lse_ref):
    length, width = q_ref.shape[1:]
    heads = width // size
    scale = size**-0.5
    flipped = v_ref[0].T
    for first in range(0, length, block):
        upto = first + block
        rows = pl.ds(first, block)
        allowed = used_pairs(
            key_seg_ref[0, pl.ds(0, upto), :], query_seg_ref[0, :, rows], first, upto, block
        )
        keys = k_ref[0, pl.ds(0, upto), :]
        query = q_ref[0, rows, :] * jnp.asarray(scale, jnp.bfloat16)
        parts = []
        for head in range(heads):
            own = jnp.where(head_lanes(width, head, size), query, jnp.zeros_like(query))
            scores = jnp.where(allowed, across(keys, own), NEG)
            top = jnp.max(scores, axis=0, keepdims=True)
            weights = jnp.exp(scores - top)
            total = jnp.sum(weights, axis=0, keepdims=True)
            lse_ref[0, pl.ds(head, 1), rows] = top + jnp.log(total)
            probs = (weights * (1.0 / total)).astype(jnp.bfloat16)
            parts.append(
                jnp.dot(
                    flipped[head * size : (head + 1) * size, :upto],
                    probs,
                    preferred_element_type=jnp.float32,
                )
            )
        mixed_ref[0, rows, :] = jnp.concatenate(parts, axis=0).T


def attend(queries, keys, values, segs, letters, size, name, cid):
    count, length, width = queries.shape
    heads = width // size
    whole = pl.BlockSpec((1, length, width), lambda i: (i, 0, 0))
    return pl.pallas_call(
        functools.partial(attend_kernel, size, min(256, length)),
        grid=(count,),
        out_shape=(
            jax.ShapeDtypeStruct((count, length, width), jnp.float32),
            jax.ShapeDtypeStruct((count, heads, length), jnp.float32),
            jax.ShapeDtypeStruct(letters.shape, letters.dtype),
        ),
        in_specs=[
            whole,
            whole,
            whole,
            pl.BlockSpec((1, length, 1), lambda i: (i, 0, 0)),
            pl.BlockSpec((1, 1, length), lambda i: (i, 0, 0)),
            pl.BlockSpec(memory_space=pl.ANY),
        ],
        out_specs=(
            whole,
            pl.BlockSpec((1, heads, length), lambda i: (i, 0, 0)),
            pl.BlockSpec(memory_space=pl.ANY),
        ),
        scratch_shapes=mail_sems(letters.shape[0]),
        compiler_params=pltpu.CompilerParams(
            collective_id=cid, has_side_effects=True, vmem_limit_bytes=48 << 20
        ),
        name=name,
    )(queries, keys, values, segs[:, :, None], segs[:, None, :], letters)


def attend_back_kernel(size, block, *refs):
    mail_ref, mailed_ref = refs[8], refs[12]
    kept = refs[:8] + refs[9:12] + refs[13:15]
    beside_mail(mail_ref, mailed_ref, refs[15:], lambda: attend_back_step(size, block, *kept))


def attend_back_step(
    size,
    block,
    q_ref,
    k_ref,
    v_ref,
    back_ref,
    mixed_ref,
    lse_ref,
    key_seg_ref,
    query_seg_ref,
    q_back_ref,
    k_back_ref,
    v_back_ref,
    k_sum,
    v_sum,
):
    length, width = q_ref.shape[1:]
    heads = width // size
    scale = size**-0.5
    flipped = k_ref[0].T
    k_sum[...] = jnp.zeros_like(k_sum)
    v_sum[...] = jnp.zeros_like(v_sum)
    for first in range(0, length, block):
        upto = first + block
        rows = pl.ds(first, block)
        before = pl.ds(0, upto)
        allowed = used_pairs(
            key_seg_ref[0, before, :], query_seg_ref[0, :, rows], first, upto, block
        )
        keys = k_ref[0, before, :]
        values = v_ref[0, before, :]
        query = q_ref[0, rows, :] * jnp.asarray(scale, jnp.bfloat16)
        back = back_ref[0, rows, :]
        product = (back.astype(jnp.float32) * mixed_ref[0, rows, :]).T
        parts = []
        for head in range(heads):
            lanes = head_lanes(width, head, size)
            own = jnp.where(lanes, query, jnp.zeros_like(query))
            own_back = jnp.where(lanes, back, jnp.zeros_like(back))
            delta = jnp.sum(product[head * size : (head + 1) * size, :], axis=0, keepdims=True)
            scores = across(keys, own) - lse_ref[0, pl.ds(head, 1), rows]
            probs = jnp.where(allowed, jnp.exp(jnp.where(allowed, scores, 0.0)), 0.0)
            score_back = (probs * (across(values, own_back) - delta)).astype(jnp.bfloat16)
            v_sum[before, :] += jnp.dot(
                probs.astype(jnp.bfloat16), own_back, preferred_element_type=jnp.float32
            )
            k_sum[before, :] += jnp.dot(score_back, own, preferred_element_type=jnp.float32)
            parts.append(
                jnp.dot(
                    flipped[head * size : (head + 1) * size, :upto],
                    score_back,
                    preferred_element_type=jnp.float32,
                )
            )
        q_back_ref[0, rows, :] = (jnp.concatenate(parts, axis=0).T * scale).astype(jnp.bfloat16)
    k_back_ref[0] = k_sum[...].astype(jnp.bfloat16)
    v_back_ref[0] = v_sum[...].astype(jnp.bfloat16)


def attend_back(queries, keys, values, back, mixed, lse, segs, letters, size, name, cid):
    count, length, width = queries.shape
    heads = width // size
    whole = pl.BlockSpec((1, length, width), lambda i: (i, 0, 0))
    shape = jax.ShapeDtypeStruct((count, length, width), jnp.bfloat16)
    return pl.pallas_call(
        functools.partial(attend_back_kernel, size, min(256, length)),
        grid=(count,),
        out_shape=(shape, shape, shape, jax.ShapeDtypeStruct(letters.shape, letters.dtype)),
        in_specs=[whole] * 5
        + [
            pl.BlockSpec((1, heads, length), lambda i: (i, 0, 0)),
            pl.BlockSpec((1, length, 1), lambda i: (i, 0, 0)),
            pl.BlockSpec((1, 1, length), lambda i: (i, 0, 0)),
            pl.BlockSpec(memory_space=pl.ANY),
        ],
        out_specs=(whole, whole, whole, pl.BlockSpec(memory_space=pl.ANY)),
        scratch_shapes=[pltpu.VMEM((length, width), jnp.float32)] * 2 + mail_sems(letters.shape[0]),
        compiler_params=pltpu.CompilerParams(
            collective_id=cid, has_side_effects=True, vmem_limit_bytes=48 << 20
        ),
        name=name,
    )(queries, keys, values, back, mixed, lse, segs[:, :, None], segs[:, None, :], letters)


def near_half(blocks, ns, group):
    flip = blocks.reshape((2, ns) + blocks.shape[1:])[::-1].reshape(blocks.shape)
    return jnp.where(group == 0, blocks, flip)


def on_device_halves(
    tokens,
    segments,
    exit_layer,
    first_gain,
    first_shift,
    query_weight,
    query_bias,
    key_weight,
    value_weight,
    value_bias,
    output_weight,
    output_bias,
    second_gain,
    second_shift,
    up_weight,
    up_bias,
    down_weight,
    down_bias,
    cotangent,
):
    rows, width = tokens.shape[1:]
    nd, ns = lax.axis_size("dp"), lax.axis_size("seq")
    ndev, ranks = nd * ns, nd * ns // 2
    size = width // HEADS
    hidden_size = up_weight.shape[1]
    w = place()
    group = w["g"]
    me = w["z"] * ns + w["s"]
    mirror = [(d, nd - 1 - d) for d in range(nd)]

    def trade(value):
        return lax.ppermute(value, "dp", mirror)

    def pair(own, other):
        return jnp.where(group == 0, own, other), jnp.where(group == 0, other, own)

    def pieces(weight):
        cut = weight.reshape(weight.shape[0], 2, 2, ns, -1)
        low, high = cut[:, 0], cut[:, 1, ::-1]
        both = jnp.stack([low, high], axis=3)
        return both.transpose(1, 2, 0, 3, 4).reshape(ranks, weight.shape[0], -1)

    def whole_rows(swapped):
        mine, other = swapped, trade(swapped)
        low, high = pair(mine, other)
        flat = high.reshape((2, ns) + high.shape[1:])[::-1]
        return jnp.concatenate([low.reshape(-1, low.shape[-1]), flat.reshape(-1, low.shape[-1])])

    def own_rows(gradient):
        half = gradient.shape[0] // 2
        low, high = gradient[:half], gradient[half:]
        sent = jnp.where(group == 0, high, low).astype(jnp.bfloat16)
        kept = jnp.where(group == 0, low, high)
        total = (kept + trade(sent).astype(jnp.float32)).astype(jnp.bfloat16)
        return near_half(total.reshape(ranks, -1, total.shape[-1]), ns, group)

    def from_pieces(blocks, take):
        cut = blocks.reshape(2, ns, blocks.shape[1], 2, take)
        low, high = cut[:, :, :, 0], cut[::-1, :, :, 1]
        both = jnp.stack([low, high]).transpose(3, 0, 1, 2, 4)
        return both.reshape(blocks.shape[1], -1).astype(jnp.float32)

    def own_block(gradient):
        half = gradient.shape[0] // 2
        low, high = gradient[:half], gradient[half:]
        sent = jnp.where(group == 0, high, low).astype(jnp.bfloat16)
        return jnp.where(group == 0, low, high) + trade(sent).astype(jnp.float32)

    vector_parts = [
        first_gain,
        first_shift,
        query_bias,
        value_bias,
        output_bias,
        second_gain,
        second_shift,
        down_bias,
        up_bias,
    ]
    attend_pieces = jnp.concatenate(
        [pieces(query_weight), pieces(key_weight), pieces(value_weight)], axis=2
    )
    letter = jnp.concatenate(vector_parts)
    letter = jnp.pad(letter, (0, -letter.shape[0] % 2048)).reshape(-1, 128)
    attend_blocks, vectors = swap([(attend_pieces, HALF), (letter, SPREAD)], "swap_attend", 0)
    vectors = vectors.reshape(ndev, -1)
    cuts, at = [], 0
    for part in vector_parts:
        cuts.append(vectors[:, at : at + part.shape[0]])
        at += part.shape[0]
    full = [cut.reshape(-1).astype(jnp.float32) for cut in cuts]
    gain_one, shift_one, _, _, output_shift, gain_two, shift_two, down_shift, _ = full
    low_at = me
    high_at = (nd - 1 - w["z"]) * ns + w["s"]

    def rank_vector(cut):
        return jnp.concatenate(
            [
                lax.dynamic_index_in_dim(cut, low_at, 0, keepdims=False),
                lax.dynamic_index_in_dim(cut, high_at, 0, keepdims=False),
            ]
        ).astype(jnp.float32)

    query_shift, value_shift, up_shift = (rank_vector(cuts[i]) for i in (2, 3, 8))
    attend_weight = whole_rows(attend_blocks)
    output_trade, down_trade, up_pieces, attend_weight = lax.optimization_barrier(
        (output_weight, down_weight, pieces(up_weight), attend_weight)
    )
    output_rows = jnp.concatenate(pair(output_weight, trade(output_trade)))
    down_rows = jnp.concatenate(pair(down_weight, trade(down_trade)))

    beside_dp = [(d, d + 1 - 2 * (d % 2)) for d in range(nd)]
    other_segs = lax.ppermute(segments, "dp", beside_dp)
    segs = jnp.concatenate(
        [
            jnp.where(w["z"] == 0, segments, other_segs),
            jnp.where(w["z"] == 0, other_segs, segments),
        ]
    )

    keep = (exit_layer > LAYER).astype(jnp.float32).reshape(rows, 1)
    inputs = tokens.astype(jnp.float32).reshape(rows, width)
    upstream = cotangent.astype(jnp.float32).reshape(rows, width)
    branch_back_own = (keep * upstream).astype(jnp.bfloat16)

    def gathered(own, name, cid):
        return cube_gather(own, name, cid).reshape(-1, own.shape[1])

    def scattered(partial, name, cid):
        return cube_scatter(partial.reshape(2, 2, 2, 2, rows, -1), name, cid)

    normed_one = gathered(
        layer_norm(inputs, gain_one, shift_one).astype(jnp.bfloat16), "gather_one", 2
    )
    pre = jnp.dot(normed_one, attend_weight, preferred_element_type=jnp.float32)
    take = 2 * size
    queries = (pre[:, :take] + query_shift).astype(jnp.bfloat16).reshape(2, -1, take)
    keys = pre[:, take : 2 * take].astype(jnp.bfloat16).reshape(2, -1, take)
    values = (pre[:, 2 * take :] + value_shift).astype(jnp.bfloat16).reshape(2, -1, take)
    mixed_full, lse, up_blocks = attend(
        queries, keys, values, segs, up_pieces, size, "attend", 1
    )
    up_columns = whole_rows(up_blocks)
    mixed = mixed_full.reshape(-1, take).astype(jnp.bfloat16)
    attention = scattered(
        jnp.dot(mixed, output_rows, preferred_element_type=jnp.float32).astype(jnp.bfloat16),
        "scatter_attention",
        3,
    )
    middle = inputs + keep * (attention + output_shift)
    normed_two = gathered(
        layer_norm(middle, gain_two, shift_two).astype(jnp.bfloat16), "gather_two", 4
    )
    branch_back = gathered(branch_back_own, "gather_branch_back", 5)
    before = jnp.dot(normed_two, up_columns, preferred_element_type=jnp.float32) + up_shift
    active, pull_active = jax.vjp(activate, before)
    hidden = active.astype(jnp.bfloat16)
    hidden_back = transposed(branch_back, down_rows)
    pre_back = pull_active(hidden_back)[0].astype(jnp.bfloat16)
    normed_two_back = scattered(
        transposed(pre_back, up_columns).astype(jnp.bfloat16), "scatter_normed_two_back", 6
    )
    down_gradient = own_block(leading(hidden, branch_back))
    up_gradient = own_rows(leading(normed_two, pre_back))
    norm_result, pull_two = jax.vjp(layer_norm, middle, gain_two, shift_two)
    middle_part, gain_two_sum, shift_two_sum = pull_two(normed_two_back)
    middle_back = upstream + middle_part
    attention_back_own = (keep * middle_back).astype(jnp.bfloat16)
    attention_back = gathered(attention_back_own, "gather_attention_back", 7)
    mixed_back = transposed(attention_back, output_rows).astype(jnp.bfloat16)
    queries_back, keys_back, values_back, up_blocks = attend_back(
        queries,
        keys,
        values,
        mixed_back.reshape(2, -1, take),
        mixed_full,
        lse,
        segs,
        up_gradient,
        size,
        "attend_back",
        10,
    )
    up_rows = from_pieces(up_blocks, hidden_size // ndev)
    stacked = jnp.concatenate([queries_back, keys_back, values_back], axis=2).reshape(-1, 3 * take)
    normed_one_back = scattered(
        transposed(stacked, attend_weight).astype(jnp.bfloat16), "scatter_normed_one_back", 8
    )
    branch = scattered(
        jnp.dot(hidden, down_rows, preferred_element_type=jnp.float32).astype(jnp.bfloat16),
        "scatter_branch",
        9,
    )
    layer_out = (middle + keep * (branch + down_shift)).astype(jnp.bfloat16)
    output_gradient = own_block(leading(mixed, attention_back))
    attend_gradient = own_rows(leading(normed_one, stacked))
    norm_first, pull_one = jax.vjp(layer_norm, inputs, gain_one, shift_one)
    inputs_part, gain_one_sum, shift_one_sum = pull_one(normed_one_back)
    tokens_gradient = (middle_back + inputs_part).astype(jnp.bfloat16)

    def summed(value):
        return jnp.sum(value.astype(jnp.float32), axis=0)

    own_sums = [
        gain_one_sum,
        shift_one_sum,
        gain_two_sum,
        shift_two_sum,
        summed(attention_back_own),
        summed(branch_back_own),
    ]
    share = width // ndev
    dense = jnp.concatenate([value.reshape(ndev, share) for value in own_sums], axis=1)
    rank_sums = jnp.concatenate(
        [
            summed(queries_back.reshape(-1, take)).reshape(2, -1),
            summed(values_back.reshape(-1, take)).reshape(2, -1),
            summed(pre_back).reshape(2, -1),
        ],
        axis=1,
    )
    number = jnp.arange(ndev)[:, None]
    sparse = jnp.where(
        number == low_at, rank_sums[0], jnp.where(number == high_at, rank_sums[1], 0.0)
    )
    letter = jnp.concatenate([dense, sparse], axis=1)
    letter = jnp.pad(letter, ((0, 0), (0, -letter.shape[1] % 1024))).reshape(ndev, -1, 128)
    attend_rows, mailed = swap([(attend_gradient, HALF), (letter, WORLD)], "swap_last", 11)
    matrix_rows = [
        from_pieces(attend_rows[:, :, i * take : (i + 1) * take], size) for i in range(3)
    ]
    mailed = jnp.sum(mailed, axis=0).reshape(-1)
    vector_out, at = [], 0
    for part in (share,) * 6 + (size, size, hidden_size // ndev):
        vector_out.append(mailed[at : at + part])
        at += part
    (
        gain_one_part,
        shift_one_part,
        gain_two_part,
        shift_two_part,
        output_shift_part,
        down_shift_part,
        query_shift_part,
        value_shift_part,
        up_shift_part,
    ) = vector_out
    return (
        layer_out.reshape(tokens.shape),
        tokens_gradient.reshape(tokens.shape),
        gain_one_part,
        shift_one_part,
        matrix_rows[0],
        query_shift_part,
        matrix_rows[1],
        matrix_rows[2],
        value_shift_part,
        output_gradient,
        output_shift_part,
        gain_two_part,
        shift_two_part,
        up_rows,
        up_shift_part,
        down_gradient,
        down_shift_part,
    )


def solution(mesh):
    placed = (
        P("dp", "seq", None),
        P("dp", None),
        P("dp", "seq"),
        P(("dp", "seq")),
        P(("dp", "seq")),
        P(("dp", "seq"), None),
        P(("dp", "seq")),
        P(("dp", "seq"), None),
        P(("dp", "seq"), None),
        P(("dp", "seq")),
        P(("dp", "seq"), None),
        P(("dp", "seq")),
        P(("dp", "seq")),
        P(("dp", "seq")),
        P(("dp", "seq"), None),
        P(("dp", "seq")),
        P(("dp", "seq"), None),
        P(("dp", "seq")),
        P("dp", "seq", None),
    )
    halves = mesh.shape["dp"] == 4 and mesh.shape["seq"] == 8
    return jax.shard_map(
        on_device_halves if halves else on_device,
        mesh=mesh,
        in_specs=placed,
        out_specs=(
            P("dp", "seq", None),
            P("dp", "seq", None),
            P(("dp", "seq")),
            P(("dp", "seq")),
            P(("dp", "seq"), None),
            P(("dp", "seq")),
            P(("dp", "seq"), None),
            P(("dp", "seq"), None),
            P(("dp", "seq")),
            P(("dp", "seq"), None),
            P(("dp", "seq")),
            P(("dp", "seq")),
            P(("dp", "seq")),
            P(("dp", "seq"), None),
            P(("dp", "seq")),
            P(("dp", "seq"), None),
            P(("dp", "seq")),
        ),
        check_vma=False,
    )
```

```python
import functools
import math

import jax
import jax.numpy as jnp
from jax import lax
from jax.experimental import pallas as pl
from jax.experimental.pallas import tpu as pltpu
from jax.sharding import PartitionSpec as P

HEADS = 32
LAYER = 12


EPS = 1e-05
NEG = -1e30


def activate(value):
    return jax.nn.gelu(value, approximate=True)


def layer_norm(value, gain, shift):
    mean = jnp.mean(value, axis=-1, keepdims=True)
    centred = value - mean
    spread = jnp.mean(centred * centred, axis=-1, keepdims=True)
    return centred * lax.rsqrt(spread + EPS) * gain + shift


def transposed(left, right):
    return lax.dot_general(
        left, right, (((1,), (1,)), ((), ())), preferred_element_type=jnp.float32
    )


def leading(left, right):
    return lax.dot_general(
        left, right, (((0,), (0,)), ((), ())), preferred_element_type=jnp.float32
    )


def visible(query_seg, query_pos, key_seg, key_pos):
    same = query_seg[:, :, None] == key_seg[:, None, :]
    return jnp.logical_and(same, key_pos[None, None, :] <= query_pos[None, :, None])


def by_blocks(step, carry, piece):
    length = jax.tree.leaves(piece)[0].shape[1]
    size = math.gcd(length, 128)

    def one(index, state):
        offset = index * size
        block = jax.tree.map(lambda part: lax.dynamic_slice_in_dim(part, offset, size, 1), piece)
        return step(state, block, offset)

    return lax.fori_loop(0, length // size, one, carry)


def on_device(
    tokens,
    segments,
    exit_layer,
    first_gain,
    first_shift,
    query_weight,
    query_bias,
    key_weight,
    value_weight,
    value_bias,
    output_weight,
    output_bias,
    second_gain,
    second_shift,
    up_weight,
    up_bias,
    down_weight,
    down_bias,
    cotangent,
):
    nseq, piece_len, width = tokens.shape
    head_count = HEADS
    head_size = width // head_count
    scale = head_size ** (-0.5)
    rows = nseq * piece_len
    own_first = lax.axis_index("seq") * piece_len
    own_pos = own_first + jnp.arange(piece_len, dtype=jnp.int32)
    own_seg = lax.dynamic_slice_in_dim(segments, own_first, piece_len, 1)
    keep = (exit_layer > LAYER).astype(jnp.float32).reshape(rows, 1)
    (
        gain_one,
        shift_one,
        query_full,
        query_shift,
        key_full,
        value_full,
        value_shift,
        output_full,
        output_shift,
        gain_two,
        shift_two,
        up_shift,
        down_shift,
    ) = (
        lax.all_gather(first_gain, ("dp", "seq"), axis=0, tiled=True),
        lax.all_gather(first_shift, ("dp", "seq"), axis=0, tiled=True),
        lax.all_gather(query_weight, ("dp", "seq"), axis=0, tiled=True),
        lax.all_gather(query_bias, ("dp", "seq"), axis=0, tiled=True),
        lax.all_gather(key_weight, ("dp", "seq"), axis=0, tiled=True),
        lax.all_gather(value_weight, ("dp", "seq"), axis=0, tiled=True),
        lax.all_gather(value_bias, ("dp", "seq"), axis=0, tiled=True),
        lax.all_gather(output_weight, ("dp", "seq"), axis=0, tiled=True),
        lax.all_gather(output_bias, ("dp", "seq"), axis=0, tiled=True),
        lax.all_gather(second_gain, ("dp", "seq"), axis=0, tiled=True),
        lax.all_gather(second_shift, ("dp", "seq"), axis=0, tiled=True),
        lax.all_gather(up_bias, ("dp", "seq"), axis=0, tiled=True),
        lax.all_gather(down_bias, ("dp", "seq"), axis=0, tiled=True),
    )
    gain_one = gain_one.astype(jnp.float32)
    shift_one = shift_one.astype(jnp.float32)
    gain_two = gain_two.astype(jnp.float32)
    shift_two = shift_two.astype(jnp.float32)
    inputs = tokens.astype(jnp.float32).reshape(rows, width)
    normed_one = layer_norm(inputs, gain_one, shift_one).astype(jnp.bfloat16)
    queries = (
        jnp.dot(normed_one, query_full, preferred_element_type=jnp.float32)
        + query_shift.astype(jnp.float32)
    ).astype(jnp.bfloat16)
    keys = jnp.dot(normed_one, key_full, preferred_element_type=jnp.float32).astype(jnp.bfloat16)
    values = (
        jnp.dot(normed_one, value_full, preferred_element_type=jnp.float32)
        + value_shift.astype(jnp.float32)
    ).astype(jnp.bfloat16)
    query_heads = queries.reshape(nseq, piece_len, head_count, head_size)
    key_heads = keys.reshape(nseq, piece_len, head_count, head_size)
    value_heads = values.reshape(nseq, piece_len, head_count, head_size)
    key_local = keys.reshape(nseq, piece_len, width)
    pair_local = jnp.concatenate([keys, values], axis=1).reshape(nseq, piece_len, 2 * width)

    def key_mask(start, length):
        key_pos = start + jnp.arange(length, dtype=jnp.int32)
        key_seg = lax.dynamic_slice_in_dim(segments, start, length, 1)
        return visible(own_seg, own_pos, key_seg, key_pos)[:, None]

    def local_scores(key_block):
        keyed = key_block.reshape(nseq, key_block.shape[1], head_count, head_size)
        return (
            jnp.einsum("sqhd,skhd->shqk", query_heads, keyed, preferred_element_type=jnp.float32)
            * scale
        )

    def norm_step(carry, block, start):
        top, total = carry
        allowed = key_mask(start, block.shape[1])
        scores = jnp.where(allowed, local_scores(block), NEG)
        new_top = jnp.maximum(top, jnp.max(scores, axis=-1))
        weights = jnp.where(allowed, jnp.exp(scores - new_top[..., None]), 0.0)
        return (new_top, total * jnp.exp(top - new_top) + jnp.sum(weights, axis=-1))

    start_norm = (
        jnp.full((nseq, head_count, piece_len), NEG, jnp.float32),
        jnp.zeros((nseq, head_count, piece_len), jnp.float32),
    )
    top, total = by_blocks(
        norm_step, start_norm, lax.all_gather(key_local, "seq", axis=1, tiled=True)
    )
    lse = top + jnp.log(total)

    def mix_step(acc, block, start):
        length = block.shape[1]
        allowed = key_mask(start, length)
        scores = local_scores(block[:, :, :width])
        probs = jnp.where(allowed, jnp.exp(scores - lse[..., None]), 0.0).astype(jnp.bfloat16)
        valued = block[:, :, width:].reshape(nseq, length, head_count, head_size)
        return acc + jnp.einsum(
            "shqk,skhd->sqhd", probs, valued, preferred_element_type=jnp.float32
        )

    empty_heads = jnp.zeros((nseq, piece_len, head_count, head_size), jnp.float32)
    mixed_heads = by_blocks(
        mix_step, empty_heads, lax.all_gather(pair_local, "seq", axis=1, tiled=True)
    )
    mixed = mixed_heads.reshape(rows, width).astype(jnp.bfloat16)
    attention = jnp.dot(
        mixed, output_full, preferred_element_type=jnp.float32
    ) + output_shift.astype(jnp.float32)
    middle = inputs + keep * attention
    normed_two = layer_norm(middle, gain_two, shift_two).astype(jnp.bfloat16)
    columns = normed_two
    before = jnp.dot(
        columns,
        lax.all_gather(up_weight, ("dp", "seq"), axis=0, tiled=True),
        preferred_element_type=jnp.float32,
    )
    pre_active = before + up_shift.astype(jnp.float32)
    hidden = activate(pre_active).astype(jnp.bfloat16)
    columns = hidden
    branch = jnp.dot(
        columns,
        lax.all_gather(down_weight, ("dp", "seq"), axis=0, tiled=True),
        preferred_element_type=jnp.float32,
    )
    branch = branch + down_shift.astype(jnp.float32)
    layer_out = (middle + keep * branch).astype(jnp.bfloat16).reshape(nseq, piece_len, width)
    upstream = cotangent.astype(jnp.float32).reshape(rows, width)
    branch_back = (keep * upstream).astype(jnp.bfloat16)
    down_shift_sum = jnp.sum(branch_back.astype(jnp.float32), axis=0)
    hidden_back = transposed(
        branch_back, lax.all_gather(down_weight, ("dp", "seq"), axis=0, tiled=True)
    )
    active_value, pull_active = jax.vjp(activate, pre_active)
    pre_back = pull_active(hidden_back)[0].astype(jnp.bfloat16)
    up_shift_sum = jnp.sum(pre_back.astype(jnp.float32), axis=0)
    down_gradient = lax.psum_scatter(
        leading(hidden, branch_back), ("dp", "seq"), scatter_dimension=0, tiled=True
    )
    normed_two_back = transposed(
        pre_back, lax.all_gather(up_weight, ("dp", "seq"), axis=0, tiled=True)
    )
    norm_result, pull_two = jax.vjp(layer_norm, middle, gain_two, shift_two)
    middle_part, gain_two_sum, shift_two_sum = pull_two(normed_two_back)
    middle_back = upstream + middle_part
    attention_back = (keep * middle_back).astype(jnp.bfloat16)
    output_shift_sum = jnp.sum(attention_back.astype(jnp.float32), axis=0)
    mixed_back = transposed(attention_back, output_full).astype(jnp.bfloat16)
    mixed_heads_back = mixed_back.reshape(nseq, piece_len, head_count, head_size)
    delta_rows = jnp.sum(mixed_heads_back.astype(jnp.float32) * mixed_heads, axis=-1)
    delta = delta_rows.transpose(0, 2, 1)
    lse_rows = lse.transpose(0, 2, 1)

    def query_step(acc, block, start):
        length = block.shape[1]
        allowed = key_mask(start, length)
        scores = local_scores(block[:, :, :width])
        probs = jnp.where(allowed, jnp.exp(scores - lse[..., None]), 0.0)
        valued = block[:, :, width:].reshape(nseq, length, head_count, head_size)
        keyed = block[:, :, :width].reshape(nseq, length, head_count, head_size)
        prob_back = jnp.einsum(
            "sqhd,skhd->shqk", mixed_heads_back, valued, preferred_element_type=jnp.float32
        )
        score_back = (probs * (prob_back - delta[..., None])).astype(jnp.bfloat16)
        return acc + jnp.einsum(
            "shqk,skhd->sqhd", score_back, keyed, preferred_element_type=jnp.float32
        )

    query_sum = by_blocks(
        query_step, empty_heads, lax.all_gather(pair_local, "seq", axis=1, tiled=True)
    )
    queries_back = (query_sum * scale).reshape(rows, width).astype(jnp.bfloat16)

    def key_step(carry, block, start):
        key_acc, value_acc = carry
        query_block, back_block, norm_block, delta_block = block
        length = query_block.shape[1]
        query_pos = start + jnp.arange(length, dtype=jnp.int32)
        query_seg = lax.dynamic_slice_in_dim(segments, start, length, 1)
        allowed = visible(query_seg, query_pos, own_seg, own_pos)[:, None]
        remote_query = query_block.astype(jnp.bfloat16).reshape(nseq, length, head_count, head_size)
        remote_back = back_block.astype(jnp.bfloat16).reshape(nseq, length, head_count, head_size)
        scores = (
            jnp.einsum(
                "sqhd,skhd->shqk", remote_query, key_heads, preferred_element_type=jnp.float32
            )
            * scale
        )
        probs = jnp.where(allowed, jnp.exp(scores - norm_block.transpose(0, 2, 1)[..., None]), 0.0)
        value_acc = value_acc + jnp.einsum(
            "shqk,sqhd->skhd",
            probs.astype(jnp.bfloat16),
            remote_back,
            preferred_element_type=jnp.float32,
        )
        prob_back = jnp.einsum(
            "sqhd,skhd->shqk", remote_back, value_heads, preferred_element_type=jnp.float32
        )
        score_back = (probs * (prob_back - delta_block.transpose(0, 2, 1)[..., None])).astype(
            jnp.bfloat16
        )
        key_acc = key_acc + jnp.einsum(
            "shqk,sqhd->skhd", score_back, remote_query, preferred_element_type=jnp.float32
        )
        return (key_acc, value_acc)

    query_send = queries.astype(jnp.float32).reshape(nseq, piece_len, width)
    back_send = mixed_back.astype(jnp.float32).reshape(nseq, piece_len, width)
    key_sum, value_sum = by_blocks(
        key_step,
        (empty_heads, empty_heads),
        (
            lax.all_gather(query_send.astype(jnp.bfloat16), "seq", axis=1, tiled=True).astype(
                jnp.float32
            ),
            lax.all_gather(back_send.astype(jnp.bfloat16), "seq", axis=1, tiled=True).astype(
                jnp.float32
            ),
            lax.all_gather(lse_rows.astype(jnp.bfloat16), "seq", axis=1, tiled=True).astype(
                jnp.float32
            ),
            lax.all_gather(delta_rows.astype(jnp.bfloat16), "seq", axis=1, tiled=True).astype(
                jnp.float32
            ),
        ),
    )
    keys_back = (key_sum * scale).reshape(rows, width).astype(jnp.bfloat16)
    values_back = value_sum.reshape(rows, width).astype(jnp.bfloat16)
    query_shift_sum = jnp.sum(queries_back.astype(jnp.float32), axis=0)
    value_shift_sum = jnp.sum(values_back.astype(jnp.float32), axis=0)
    normed_one_back = (
        transposed(queries_back, query_full)
        + transposed(keys_back, key_full)
        + transposed(values_back, value_full)
    )
    norm_first, pull_one = jax.vjp(layer_norm, inputs, gain_one, shift_one)
    inputs_part, gain_one_sum, shift_one_sum = pull_one(normed_one_back)
    tokens_gradient = (
        (middle_back + inputs_part).astype(jnp.bfloat16).reshape(nseq, piece_len, width)
    )
    stacked_back = jnp.concatenate([queries_back, keys_back, values_back], axis=1)
    row_gradient = lax.psum_scatter(
        jnp.concatenate(
            [
                leading(normed_one, stacked_back),
                leading(mixed, attention_back),
                leading(normed_two, pre_back),
            ],
            axis=1,
        ),
        ("dp", "seq"),
        scatter_dimension=0,
        tiled=True,
    )
    (
        gain_one_part,
        shift_one_part,
        query_shift_part,
        value_shift_part,
        output_shift_part,
        gain_two_part,
        shift_two_part,
        up_shift_part,
        down_shift_part,
    ) = (
        lax.psum_scatter(gain_one_sum, ("dp", "seq"), scatter_dimension=0, tiled=True),
        lax.psum_scatter(shift_one_sum, ("dp", "seq"), scatter_dimension=0, tiled=True),
        lax.psum_scatter(query_shift_sum, ("dp", "seq"), scatter_dimension=0, tiled=True),
        lax.psum_scatter(value_shift_sum, ("dp", "seq"), scatter_dimension=0, tiled=True),
        lax.psum_scatter(output_shift_sum, ("dp", "seq"), scatter_dimension=0, tiled=True),
        lax.psum_scatter(gain_two_sum, ("dp", "seq"), scatter_dimension=0, tiled=True),
        lax.psum_scatter(shift_two_sum, ("dp", "seq"), scatter_dimension=0, tiled=True),
        lax.psum_scatter(up_shift_sum, ("dp", "seq"), scatter_dimension=0, tiled=True),
        lax.psum_scatter(down_shift_sum, ("dp", "seq"), scatter_dimension=0, tiled=True),
    )
    return (
        layer_out,
        tokens_gradient,
        gain_one_part,
        shift_one_part,
        row_gradient[:, :width],
        query_shift_part,
        row_gradient[:, width : 2 * width],
        row_gradient[:, 2 * width : 3 * width],
        value_shift_part,
        row_gradient[:, 3 * width : 4 * width],
        output_shift_part,
        gain_two_part,
        shift_two_part,
        row_gradient[:, 4 * width :],
        up_shift_part,
        down_gradient,
        down_shift_part,
    )


MESH = pl.DeviceIdType.MESH
ORDERS = ("xyz", "yzx", "zxy")
CANON = "zyx"
ALL = (pl.ds(0, 2),) * 3
SLICE_IN, SLICE_OUT, WORLD, SPREAD, PAIR, NEAR = range(6)
VMEM_BYTES = 56 << 20


def place():
    d, s = lax.axis_index("dp"), lax.axis_index("seq")
    half = lax.axis_size("dp") // 2
    far = d // half
    z = d + far * (2 * half - 1 - 2 * d)
    return dict(d=d, s=s, g=far, z=z, y=s // 4, x=(s // 2) % 2, c=s % 2)


def beside(w, dim):
    if dim == "z":
        return (w["d"] + 1 - 2 * (w["d"] % 2), w["s"])
    step = {"c": 1, "x": 2, "y": 4}[dim]
    return (w["d"], w["s"] + step * (1 - 2 * w[dim]))


def partner(w):
    return (lax.axis_size("dp") - 1 - w["d"], w["s"])


def peer(w, r):
    n = lax.axis_size("seq")
    e, s = r // n, r % n
    return (e + w["g"] * (lax.axis_size("dp") - 1 - 2 * e), s)


def row_block(w, r):
    n = lax.axis_size("seq")
    e, s = r // n, r % n
    return (e + w["g"] * (1 - 2 * e)) * n + s


def anyone(i):
    n = lax.axis_size("seq")
    return (i // n, i % n)


def half_peers(w):
    count = lax.axis_size("dp") * lax.axis_size("seq") // 2
    me = w["z"] * lax.axis_size("seq") + w["s"]
    return me, [(me + k) % count for k in range(1, count)]


def world_peers(w):
    count = lax.axis_size("dp") * lax.axis_size("seq")
    me = w["d"] * lax.axis_size("seq") + w["s"]
    return me, [(me + k) % count for k in range(1, count)]


def greet(ids):
    bar = pltpu.get_barrier_semaphore()
    for i in ids:
        pl.semaphore_signal(bar, inc=1, device_id=i, device_id_type=MESH)
    pl.semaphore_wait(bar, len(ids))


def greet_half(w):
    greet([peer(w, r) for r in half_peers(w)[1]] + [partner(w)])


def greet_world(w):
    greet([anyone(i) for i in world_peers(w)[1]])


def remote(src, dst, send, recv, device):
    return pltpu.make_async_remote_copy(
        src_ref=src,
        dst_ref=dst,
        send_sem=send,
        recv_sem=recv,
        device_id=device,
        device_id_type=MESH,
    )


def mail(w, kind, src, out, send, recv, local):
    if kind == SLICE_IN:
        me, others = half_peers(w)
        todo = [(src.at[r], peer(w, r)) for r in others]
        own, to = src.at[me], out.at[row_block(w, me)]
    elif kind == SLICE_OUT:
        me, others = half_peers(w)
        todo = [(src.at[row_block(w, r)], peer(w, r)) for r in others]
        own, to = src.at[row_block(w, me)], out.at[me]
    elif kind == WORLD:
        me, others = world_peers(w)
        todo = [(src.at[i], anyone(i)) for i in others]
        own, to = src.at[me], out.at[me]
    elif kind == SPREAD:
        me, others = world_peers(w)
        todo = [(src, anyone(i)) for i in others]
        own, to = src, out.at[me]
    elif kind == PAIR:
        todo, own, to = [(src, partner(w))], src, out.at[w["g"]]
    else:
        todo, own, to = [(src, beside(w, "z"))], src, out.at[w["z"]]
    copies = [
        remote(part, to, send.at[k], recv.at[k], device) for k, (part, device) in enumerate(todo)
    ]
    return copies + [pltpu.make_async_copy(own, to, local)]


def start_all(copies):
    for cp in copies:
        cp.start()


def wait_all(copies):
    for cp in copies:
        cp.wait()


def mail_count(kind):
    count = lax.axis_size("dp") * lax.axis_size("seq")
    return {SLICE_IN: count // 2, SLICE_OUT: count // 2, WORLD: count, SPREAD: count}.get(kind, 2)


def mail_sems(kind):
    n = mail_count(kind) - 1
    dma = pltpu.SemaphoreType.DMA
    return [dma((n,)), dma((n,)), dma]


def mail_shape(kind, x):
    if kind in (SPREAD, PAIR, NEAR):
        return jax.ShapeDtypeStruct((mail_count(kind),) + x.shape, x.dtype)
    return jax.ShapeDtypeStruct(x.shape, x.dtype)


def mail_kernel(kinds, *refs):
    n = len(kinds)
    srcs, outs, sems = refs[:n], refs[n : 2 * n], refs[2 * n :]
    w = place()
    greet_world(w)
    copies = []
    for i, kind in enumerate(kinds):
        copies += mail(w, kind, srcs[i], outs[i], *sems[3 * i : 3 * i + 3])
    start_all(copies)
    wait_all(copies)


def exchange(items, name, cid):
    anywhere = pl.BlockSpec(memory_space=pl.ANY)
    kinds = [kind for _, kind in items]
    return pl.pallas_call(
        functools.partial(mail_kernel, kinds),
        out_shape=tuple(mail_shape(kind, x) for x, kind in items),
        in_specs=[anywhere] * len(items),
        out_specs=tuple([anywhere] * len(items)),
        scratch_shapes=[sem for kind in kinds for sem in mail_sems(kind)],
        compiler_params=pltpu.CompilerParams(collective_id=cid, has_side_effects=True),
        name=name,
    )(*[x for x, _ in items])


def column_parts(width):
    unit = width // 128
    third = unit // 3
    parts, at = [], 0
    for count in (unit - 2 * third, third, third):
        parts.append(pl.ds(at * 128, count * 128))
        at += count
    return parts


def box(w, both, other=()):
    return tuple(
        pl.ds(0, 2) if q in both else (1 - w[q] if q in other else w[q]) for q in CANON
    )


class Gather:
    def __init__(self, w, src, out, send, recv, side_send, side_recv, local):
        self.w, self.src, self.out = w, src, out
        self.send, self.recv, self.side_send, self.side_recv = send, recv, side_send, side_recv
        self.parts = column_parts(src.shape[1])
        self.own = (w["z"], w["y"], w["x"], w["c"])
        self.keep = pltpu.make_async_copy(src, out.at[self.own], local)
        self.links, self.sides = {}, []

    @staticmethod
    def sems():
        dma = pltpu.SemaphoreType.DMA
        return [dma((3, 3)), dma((3, 3)), dma((3, 4)), dma((3, 4)), dma]

    def push(self, p, k, src, dst):
        cp = remote(
            src, dst, self.send.at[p, k], self.recv.at[p, k], beside(self.w, ORDERS[p][k])
        )
        cp.start()
        self.links[p, k] = cp

    def across(self, p, k, src, dst):
        cp = remote(
            src, dst, self.side_send.at[p, k], self.side_recv.at[p, k], beside(self.w, "c")
        )
        cp.start()
        self.sides.append(cp)

    def start(self):
        for p, cols in enumerate(self.parts):
            self.push(p, 0, self.src.at[:, cols], self.out.at[self.own + (slice(None), cols)])
        self.keep.start()
        for p, cols in enumerate(self.parts):
            self.across(p, 0, self.src.at[:, cols], self.out.at[self.own + (slice(None), cols)])

    def step(self, k):
        w = self.w
        if k == 0:
            self.keep.wait()
        for p, cols in enumerate(self.parts):
            order = ORDERS[p]
            self.links[p, k].wait_recv()
            tail = (w["c"], slice(None), cols)
            if k < 2:
                held = self.out.at[box(w, order[: k + 1]) + tail]
                self.push(p, k + 1, held, held)
            new = self.out.at[box(w, order[:k], order[k]) + tail]
            self.across(p, k + 1, new, new)

    def finish(self):
        for cp in self.links.values():
            cp.wait_send()
        wait_all(self.sides)


class Scatter:
    def __init__(self, w, acc, away, side, land, send, recv, side_send, side_recv):
        self.w, self.acc, self.away, self.side, self.land = w, acc, away, side, land
        self.send, self.recv, self.side_send, self.side_recv = send, recv, side_send, side_recv
        self.parts = column_parts(acc.shape[-1])
        self.links, self.sides = {}, {}

    @staticmethod
    def scratch(rows, width):
        most = column_parts(width)[0].size
        half = pltpu.VMEM((2, 2, 2, rows, width), jnp.bfloat16)
        dma = pltpu.SemaphoreType.DMA
        return [
            half,
            half,
            half,
            pltpu.VMEM((3, 2, 2, rows, most), jnp.bfloat16),
            pltpu.VMEM((3, 2, rows, most), jnp.bfloat16),
            pltpu.VMEM((3, rows, most), jnp.bfloat16),
            dma((3, 3)),
            dma((3, 3)),
            dma((3,)),
            dma((3,)),
        ]

    @staticmethod
    def over(w, refs):
        return Scatter(w, *refs[:3], refs[3:6], *refs[6:])

    def produce(self, p, product):
        w, cols = self.w, self.parts[p]
        rows = self.acc.shape[3]

        def fill(out, core):
            @pl.loop(0, 4)
            def _(i):
                block = product(i // 2, i % 2, core, cols)
                out[i // 2, i % 2, :, :, cols] = block.astype(out.dtype).reshape(2, rows, -1)

        fill(self.away, 1 - w["c"])
        at = ALL + (slice(None), cols)
        cp = remote(
            self.away.at[at],
            self.side.at[at],
            self.side_send.at[p],
            self.side_recv.at[p],
            beside(w, "c"),
        )
        cp.start()
        self.sides[p] = cp
        fill(self.acc, w["c"])

    def at(self, order, k, other, rest):
        w = self.w
        left = dict(zip([q for q in CANON if q in order[k + 1 :]], rest))
        here = {q: w[q] for q in order[:k]}
        here[order[k]] = 1 - w[order[k]] if other else w[order[k]]
        here.update(left)
        return tuple(here[q] for q in CANON)

    def add(self, at, got, cols):
        at = at + (slice(None), cols)
        total = self.acc[at].astype(jnp.float32) + got.astype(jnp.float32)
        self.acc[at] = total.astype(self.acc.dtype)

    def push(self, p, k):
        w, cols, order = self.w, self.parts[p], ORDERS[p]
        src = self.acc.at[box(w, order[k + 1 :], order[k]) + (slice(None), cols)]
        dst = self.land[k].at[
            (p,) + (pl.ds(0, 2),) * (2 - k) + (slice(None), pl.ds(0, cols.size))
        ]
        cp = remote(src, dst, self.send.at[p, k], self.recv.at[p, k], beside(w, order[k]))
        cp.start()
        self.links[p, k] = cp

    def fold(self, p):
        cols, order = self.parts[p], ORDERS[p]
        self.sides[p].wait_recv()

        def add(other):
            @pl.loop(0, 4)
            def _(i):
                at = self.at(order, 0, other, (i // 2, i % 2))
                self.add(at, self.side[at + (slice(None), cols)], cols)

        add(True)
        self.push(p, 0)
        add(False)

    def step(self, k):
        w = self.w
        for p, cols in enumerate(self.parts):
            order = ORDERS[p]
            self.links[p, k].wait_recv()
            left = [q for q in CANON if q in order[k + 1 :]]
            slot = left.index(order[k + 1])
            inner = (slice(None), pl.ds(0, cols.size))
            for other in (True, False):
                here = 1 - w[order[k + 1]] if other else w[order[k + 1]]
                if k == 0:

                    @pl.loop(0, 2)
                    def _(i):
                        rest = (here, i) if slot == 0 else (i, here)
                        got = self.land[0][(p,) + rest + inner]
                        self.add(self.at(order, 0, False, rest), got, cols)

                else:
                    got = self.land[1][(p, here) + inner]
                    self.add(self.at(order, 1, False, (here,)), got, cols)
                if other:
                    self.push(p, k + 1)

    def finish(self, out):
        w = self.w
        own = (w["z"], w["y"], w["x"])
        for p, cols in enumerate(self.parts):
            self.links[p, 2].wait_recv()
            got = self.land[2][p, :, pl.ds(0, cols.size)]
            out[:, cols] = self.acc[own + (slice(None), cols)].astype(jnp.float32) + got.astype(
                jnp.float32
            )
        for cp in self.links.values():
            cp.wait_send()
        for cp in self.sides.values():
            cp.wait_send()


def across(left, right):
    return lax.dot_general(
        left, right, (((1,), (1,)), ((), ())), preferred_element_type=jnp.float32
    )


def straight(left, right):
    return jnp.dot(left, right, preferred_element_type=jnp.float32)


def flat(block):
    return block.reshape(-1, block.shape[-1])


def head_lanes(width, head, size):
    lane = lax.broadcasted_iota(jnp.int32, (1, width), 1)
    return jnp.logical_and(lane >= head * size, lane < (head + 1) * size)


def used_pairs(key_seg, query_seg, first, length, block):
    key_pos = lax.broadcasted_iota(jnp.int32, (length, 1), 0)
    query_pos = first + lax.broadcasted_iota(jnp.int32, (1, block), 1)
    return jnp.logical_and(key_seg == query_seg, key_pos <= query_pos)


def attend_block(size, block, first, q, k, v_flip, key_seg, query_seg, mixed, mixed_low, lse):
    width = q.shape[2]
    upto, rows = first + block, pl.ds(first, block)

    @pl.loop(0, q.shape[0])
    def _(i):
        allowed = used_pairs(key_seg[i, pl.ds(0, upto), :], query_seg[i, :, rows], first, upto, block)
        keys = k[i, pl.ds(0, upto), :]
        query = q[i, rows, :] * jnp.asarray(size**-0.5, q.dtype)
        parts = []
        for head in range(width // size):
            own = jnp.where(head_lanes(width, head, size), query, jnp.zeros_like(query))
            scores = jnp.where(allowed, across(keys, own), NEG)
            top = jnp.max(scores, axis=0, keepdims=True)
            weights = jnp.exp(scores - top)
            total = jnp.sum(weights, axis=0, keepdims=True)
            lse[i, pl.ds(head, 1), rows] = top + jnp.log(total)
            probs = (weights * (1.0 / total)).astype(q.dtype)
            parts.append(straight(v_flip[i, pl.ds(head * size, size), pl.ds(0, upto)], probs))
        full = jnp.concatenate(parts, axis=0).T
        mixed[i, rows, :] = full
        at = first // block
        mixed_low[i, at // 2, at % 2] = full.astype(mixed_low.dtype).reshape(mixed_low.shape[3:])


def attend_back_block(
    size, block, first, q, k, k_flip, v, back, mixed, lse, key_seg, query_seg, q_back, k_sum, v_sum
):
    width = q.shape[2]
    upto, rows = first + block, pl.ds(first, block)
    before = pl.ds(0, upto)
    scale = size**-0.5

    @pl.loop(0, q.shape[0])
    def _(i):
        allowed = used_pairs(key_seg[i, before, :], query_seg[i, :, rows], first, upto, block)
        keys, values = k[i, before, :], v[i, before, :]
        query = q[i, rows, :] * jnp.asarray(scale, q.dtype)
        grad = back[i, rows, :]
        product = (grad.astype(jnp.float32) * mixed[i, rows, :]).T
        parts = []
        for head in range(width // size):
            lanes = head_lanes(width, head, size)
            own = jnp.where(lanes, query, jnp.zeros_like(query))
            own_grad = jnp.where(lanes, grad, jnp.zeros_like(grad))
            delta = jnp.sum(product[head * size : (head + 1) * size, :], axis=0, keepdims=True)
            scores = across(keys, own) - lse[i, pl.ds(head, 1), rows]
            probs = jnp.exp(jnp.where(allowed, scores, NEG))
            score_back = (probs * (across(values, own_grad) - delta)).astype(q.dtype)
            v_sum[i, before, :] += straight(probs.astype(q.dtype), own_grad)
            k_sum[i, before, :] += straight(score_back, own)
            parts.append(straight(k_flip[i, pl.ds(head * size, size), before], score_back))
        q_back[i, rows, :] = (jnp.concatenate(parts, axis=0).T * scale).astype(q_back.dtype)


class Refs:
    def __init__(self, refs):
        self.refs, self.used = refs, 0

    def take(self, count):
        self.used += count
        return self.refs[self.used - count : self.used]


def attend_kernel(size, *refs):
    refs = Refs(refs)
    (own, grad, shift, out_rows, key_seg, query_seg, blocks, pieces, down) = refs.take(9)
    (attention, q, k, v, mixed, lse, rows_all, grads_all, pair, columns, downs) = refs.take(11)
    rows, grads, weight, v_flip, mixed_low = refs.take(5)
    one = refs.take(5)
    two = refs.take(5)
    sums = refs.take(10)
    pair_sems, column_sems, down_sems = refs.take(3), refs.take(3), refs.take(3)
    load, flush = refs.take(2)
    w = place()
    greet_half(w)
    gather = Gather(w, own, rows, *one)
    second = Gather(w, grad, grads, *two)
    scatter = Scatter.over(w, sums)
    gather.start()
    pair_mail = mail(w, PAIR, blocks, pair, *pair_sems)
    start_all(pair_mail)
    gather.step(0)
    column_mail = mail(w, SLICE_IN, pieces, columns, *column_sems)
    start_all(column_mail)
    gather.step(1)
    gather.step(2)
    wait_all(pair_mail)
    fetch = [
        pltpu.make_async_copy(pair.at[i], weight.at[pl.ds(i * pair.shape[1], pair.shape[1])], load.at[i])
        for i in range(2)
    ]
    start_all(fetch)
    gather.finish()
    keep_rows = pltpu.make_async_copy(rows, rows_all, flush.at[0])
    keep_rows.start()
    down_mail = mail(w, PAIR, down, downs, *down_sems)
    start_all(down_mail)
    second.start()
    wait_all(fetch)
    length, take = q.shape[1:]

    @pl.loop(0, 4)
    def _(i):
        block = straight(flat(rows[i // 2, i % 2]), weight[...]) + shift[...]
        at = pl.ds(i % 2 * (length // 2), length // 2)
        for ref, n in ((q, 0), (k, 1), (v, 2)):
            ref[i // 2, at, :] = block[:, n * take : (n + 1) * take].astype(ref.dtype)
        v_flip[i // 2, :, at] = block[:, 2 * take :].astype(v_flip.dtype).T

    second.step(0)
    block = length // 4
    for first in range(0, length, block):
        attend_block(
            size, block, first, q, k, v_flip, key_seg, query_seg, mixed, mixed_low, lse
        )
        if first == block:
            second.step(1)

    def product(e, y, c, cols):
        return straight(flat(mixed_low[e, y, :, c]), out_rows[:, cols])

    for p in range(3):
        scatter.produce(p, product)
    second.step(2)
    for p in range(3):
        scatter.fold(p)
    second.finish()
    keep_grads = pltpu.make_async_copy(grads, grads_all, flush.at[1])
    keep_grads.start()
    scatter.step(0)
    scatter.step(1)
    scatter.finish(attention)
    wait_all(down_mail)
    wait_all(column_mail)
    keep_rows.wait()
    keep_grads.wait()


def attend(own, grad, shift, out_rows, segs, blocks, pieces, down, size, name, cid):
    rows, width = own.shape
    ns = lax.axis_size("seq")
    length = rows * ns
    take = out_rows.shape[0]
    low, f32 = own.dtype, jnp.float32
    vmem, anywhere = pl.BlockSpec(memory_space=pltpu.VMEM), pl.BlockSpec(memory_space=pl.ANY)
    shape, dma = jax.ShapeDtypeStruct, pltpu.SemaphoreType.DMA
    whole = (2, 2, 2, 2, rows, width)
    return pl.pallas_call(
        functools.partial(attend_kernel, size),
        out_shape=(
            shape((rows, width), f32),
            *[shape((2, length, take), low)] * 3,
            shape((2, length, take), f32),
            shape((2, take // size, length), f32),
            shape(whole, low),
            shape(whole, low),
            shape((2,) + blocks.shape, low),
            shape(pieces.shape, low),
            shape((2,) + down.shape, low),
        ),
        in_specs=[vmem] * 6 + [anywhere] * 3,
        out_specs=tuple([vmem] * 6 + [anywhere] * 5),
        scratch_shapes=[
            pltpu.VMEM(whole, low),
            pltpu.VMEM(whole, low),
            pltpu.VMEM((2 * blocks.shape[0], blocks.shape[1]), low),
            pltpu.VMEM((2, take, length), low),
            pltpu.VMEM((2, 2, 2, 2, rows, take), low),
            *Gather.sems(),
            *Gather.sems(),
            *Scatter.scratch(rows, width),
            *mail_sems(PAIR),
            *mail_sems(SLICE_IN),
            *mail_sems(PAIR),
            dma((2,)),
            dma((2,)),
        ],
        compiler_params=pltpu.CompilerParams(
            collective_id=cid, has_side_effects=True, vmem_limit_bytes=VMEM_BYTES
        ),
        name=name,
    )(own, grad, shift, out_rows, segs[:, :, None], segs[:, None, :], blocks, pieces, down)


def feed_kernel(*refs):
    refs = Refs(refs)
    own, shift, columns, grads_all, downs = refs.take(5)
    back, hidden, shift_sum, down_grad, up_grad = refs.take(5)
    rows, grads, up, down, hidden_flip, pre_flip, pre = refs.take(7)
    one = refs.take(5)
    sums = refs.take(10)
    up_send, up_recv, up_local = refs.take(3)
    (load,) = refs.take(1)
    w = place()
    greet_half(w)
    gather = Gather(w, own, rows, *one)
    scatter = Scatter.over(w, sums)
    gather.start()
    half = columns.shape[0]
    mine = up.at[pl.ds(w["g"] * half, half)]
    trade = remote(columns, mine, up_send, up_recv, partner(w))
    keep = pltpu.make_async_copy(columns, mine, up_local)
    fetch = [
        pltpu.make_async_copy(downs, down, load.at[0]),
        pltpu.make_async_copy(grads_all, grads, load.at[1]),
    ]
    start_all([trade, keep] + fetch)
    for k in range(3):
        gather.step(k)
    gather.finish()
    wait_all([trade, keep] + fetch)
    width = down.shape[1]
    span = rows.shape[2] * rows.shape[3] * rows.shape[4]
    shift_sum[...] = jnp.zeros_like(shift_sum)

    @pl.loop(0, 4)
    def _(i):
        before = straight(flat(rows[i // 2, i % 2]), up[...]) + shift[...]
        active, pull = jax.vjp(activate, before)
        at = pl.ds(i * span, span)
        low = active.astype(hidden.dtype)
        hidden[i // 2, i % 2] = low.reshape(hidden.shape[2:])
        hidden_flip[:, at] = low.T
        hidden_back = across(flat(grads[i // 2, i % 2]), down[...])
        pre_back = pull(hidden_back)[0].astype(pre.dtype)
        pre[i // 2, i % 2] = pre_back.reshape(pre.shape[2:])
        pre_flip[:, at] = pre_back.T
        shift_sum[...] += jnp.sum(pre_back.astype(jnp.float32), axis=0, keepdims=True)

    def product(e, y, c, cols):
        return across(flat(pre[e, y, :, c]), up[cols, :])

    for p in range(3):
        scatter.produce(p, product)
    for p in range(3):
        scatter.fold(p)
    chunk = 256

    @pl.loop(0, width // chunk)
    def _(i):
        cols = pl.ds(i * chunk, chunk)
        grad = straight(hidden_flip[...], grads[:, :, :, :, :, cols].reshape(-1, chunk))
        down_grad[:, cols] = grad.astype(down_grad.dtype)

    scatter.step(0)

    @pl.loop(0, width // chunk)
    def _(i):
        cols = pl.ds(i * chunk, chunk)
        grad = straight(pre_flip[...], rows[:, :, :, :, :, cols].reshape(-1, chunk))
        up_grad[cols, :] = grad.astype(up_grad.dtype).T

    scatter.step(1)
    scatter.finish(back)


def feed(own, shift, columns, grads_all, downs, name, cid):
    rows, width = own.shape
    take = columns.shape[1]
    low, f32 = own.dtype, jnp.float32
    vmem, anywhere = pl.BlockSpec(memory_space=pltpu.VMEM), pl.BlockSpec(memory_space=pl.ANY)
    shape, dma = jax.ShapeDtypeStruct, pltpu.SemaphoreType.DMA
    whole = (2, 2, 2, 2, rows, width)
    tokens = 16 * rows
    return pl.pallas_call(
        feed_kernel,
        out_shape=(
            shape((rows, width), f32),
            shape((2, 2, 2, 2, rows, take), low),
            shape((1, take), f32),
            shape((take, width), low),
            shape((width, take), low),
        ),
        in_specs=[vmem] * 2 + [anywhere] * 3,
        out_specs=tuple([vmem] * 5),
        scratch_shapes=[
            pltpu.VMEM(whole, low),
            pltpu.VMEM(whole, low),
            pltpu.VMEM((width, take), low),
            pltpu.VMEM((take, width), low),
            pltpu.VMEM((take, tokens), low),
            pltpu.VMEM((take, tokens), low),
            pltpu.VMEM((2, 2, 2, 2, rows, take), low),
            *Gather.sems(),
            *Scatter.scratch(rows, width),
            dma,
            dma,
            dma,
            dma((2,)),
        ],
        compiler_params=pltpu.CompilerParams(
            collective_id=cid, has_side_effects=True, vmem_limit_bytes=VMEM_BYTES
        ),
        name=name,
    )(own, shift, columns, grads_all, downs)


def attend_back_kernel(size, *refs):
    refs = Refs(refs)
    (own, out_rows, q, k, v, mixed, lse, key_seg, query_seg) = refs.take(9)
    rows_all, pair, down_sent, up_sent = refs.take(4)
    (back, out_grad, attend_grad, q_sum, v_bias_sum, down_got, up_got) = refs.take(7)
    (grads, rows, weight, k_flip, mixed_flip, grad_heads, q_back, k_sum, v_sum, stack, stack_flip) = (
        refs.take(11)
    )
    one = refs.take(5)
    sums = refs.take(10)
    down_send, down_recv, up_send, up_recv = refs.take(4)
    (load,) = refs.take(1)
    w = place()
    greet_half(w)
    gather = Gather(w, own, grads, *one)
    scatter = Scatter.over(w, sums)
    gather.start()
    down_trade = remote(down_sent.at[1 - w["g"]], down_got, down_send, down_recv, partner(w))
    up_trade = remote(up_sent.at[1 - w["g"]], up_got, up_send, up_recv, partner(w))
    down_trade.start()
    half = pair.shape[1]
    fetch = [
        pltpu.make_async_copy(pair.at[i], weight.at[pl.ds(i * half, half)], load.at[i])
        for i in range(2)
    ] + [pltpu.make_async_copy(rows_all, rows, load.at[2])]
    start_all(fetch)
    length, take = q.shape[1:]
    for i in range(2):
        k_flip[i] = k[i].T
        mixed_flip[:, pl.ds(i * length, length)] = mixed[i].astype(mixed_flip.dtype).T
    k_sum[...] = jnp.zeros_like(k_sum)
    v_sum[...] = jnp.zeros_like(v_sum)
    for step in range(3):
        gather.step(step)
    gather.finish()

    @pl.loop(0, 4)
    def _(i):
        at = pl.ds(i % 2 * (length // 2), length // 2)
        grad = across(flat(grads[i // 2, i % 2]), out_rows[...])
        grad_heads[i // 2, at, :] = grad.astype(grad_heads.dtype)

    block = length // 4
    for first in range(0, length, block):
        attend_back_block(
            size,
            block,
            first,
            q,
            k,
            k_flip,
            v,
            grad_heads,
            mixed,
            lse,
            key_seg,
            query_seg,
            q_back,
            k_sum,
            v_sum,
        )
    down_trade.wait()
    up_trade.start()
    q_sum[...] = jnp.zeros_like(q_sum)
    v_bias_sum[...] = jnp.zeros_like(v_bias_sum)

    @pl.loop(0, 4)
    def _(i):
        at = pl.ds(i % 2 * (length // 2), length // 2)
        parts = [
            ref[i // 2, at, :].astype(stack.dtype) for ref in (q_back, k_sum, v_sum)
        ]
        for n, part in enumerate(parts):
            stack[i // 2, i % 2, :, :, :, pl.ds(n * take, take)] = part.reshape(
                stack.shape[2:5] + (take,)
            )
            stack_flip[pl.ds(n * take, take), pl.ds(i * (length // 2), length // 2)] = part.T
        q_sum[...] += jnp.sum(parts[0].astype(jnp.float32), axis=0, keepdims=True)
        v_bias_sum[...] += jnp.sum(parts[2].astype(jnp.float32), axis=0, keepdims=True)

    wait_all(fetch)

    def product(e, y, c, cols):
        return across(flat(stack[e, y, :, c]), weight[cols, :])

    for p in range(3):
        scatter.produce(p, product)
    for p in range(3):
        scatter.fold(p)
    chunk = 256

    @pl.loop(0, weight.shape[0] // chunk)
    def _(i):
        cols = pl.ds(i * chunk, chunk)
        grad = straight(stack_flip[...], rows[:, :, :, :, :, cols].reshape(-1, chunk))
        attend_grad[cols, :] = grad.astype(attend_grad.dtype).T
        grad = straight(mixed_flip[...], grads[:, :, :, :, :, cols].reshape(-1, chunk))
        out_grad[:, cols] = grad.astype(out_grad.dtype)

    scatter.step(0)
    scatter.step(1)
    scatter.finish(back)
    up_trade.wait()


def attend_back(
    own, out_rows, q, k, v, mixed, lse, segs, rows_all, pair, down_sent, up_sent, size, name, cid
):
    rows, width = own.shape
    length, take = q.shape[1:]
    low, f32 = own.dtype, jnp.float32
    vmem, anywhere = pl.BlockSpec(memory_space=pltpu.VMEM), pl.BlockSpec(memory_space=pl.ANY)
    shape, dma = jax.ShapeDtypeStruct, pltpu.SemaphoreType.DMA
    whole = (2, 2, 2, 2, rows, width)
    heads = (2, length, take)
    return pl.pallas_call(
        functools.partial(attend_back_kernel, size),
        out_shape=(
            shape((rows, width), f32),
            shape((take, width), low),
            shape((width, 3 * take), low),
            shape((1, take), f32),
            shape((1, take), f32),
            shape(down_sent.shape[1:], low),
            shape(up_sent.shape[1:], low),
        ),
        in_specs=[vmem] * 9 + [anywhere] * 4,
        out_specs=tuple([vmem] * 5 + [anywhere] * 2),
        scratch_shapes=[
            pltpu.VMEM(whole, low),
            pltpu.VMEM(whole, low),
            pltpu.VMEM((width, 3 * take), low),
            pltpu.VMEM((2, take, length), low),
            pltpu.VMEM((take, 2 * length), low),
            pltpu.VMEM(heads, low),
            pltpu.VMEM(heads, low),
            pltpu.VMEM(heads, f32),
            pltpu.VMEM(heads, f32),
            pltpu.VMEM((2, 2, 2, 2, rows, 3 * take), low),
            pltpu.VMEM((3 * take, 2 * length), low),
            *Gather.sems(),
            *Scatter.scratch(rows, width),
            dma,
            dma,
            dma,
            dma,
            dma((3,)),
        ],
        compiler_params=pltpu.CompilerParams(
            collective_id=cid, has_side_effects=True, vmem_limit_bytes=VMEM_BYTES
        ),
        name=name,
    )(
        own,
        out_rows,
        q,
        k,
        v,
        mixed,
        lse,
        segs[:, :, None],
        segs[:, None, :],
        rows_all,
        pair,
        down_sent,
        up_sent,
    )


def branch_kernel(*refs):
    refs = Refs(refs)
    hidden, downs, blocks, attend_sent, out_sent = refs.take(5)
    branch, swapped, attend_got, out_got = refs.take(4)
    sums = refs.take(10)
    swap_sems = refs.take(3)
    attend_send, attend_recv, out_send, out_recv = refs.take(4)
    w = place()
    greet_half(w)
    scatter = Scatter.over(w, sums)
    attend_trade = remote(
        attend_sent.at[1 - w["g"]], attend_got, attend_send, attend_recv, partner(w)
    )
    out_trade = remote(out_sent.at[1 - w["g"]], out_got, out_send, out_recv, partner(w))
    attend_trade.start()

    def product(e, y, c, cols):
        return straight(flat(hidden[e, y, :, c]), downs[:, cols])

    for p in range(3):
        scatter.produce(p, product)
    for p in range(3):
        scatter.fold(p)
    copies = mail(w, SLICE_OUT, blocks, swapped, *swap_sems)
    start_all(copies)
    scatter.step(0)
    scatter.step(1)
    out_trade.start()
    scatter.finish(branch)
    attend_trade.wait()
    out_trade.wait()
    wait_all(copies)


def branch_sum(hidden, downs, blocks, attend_sent, out_sent, name, cid):
    rows, width = hidden.shape[4], downs.shape[1]
    vmem, anywhere = pl.BlockSpec(memory_space=pltpu.VMEM), pl.BlockSpec(memory_space=pl.ANY)
    shape, dma = jax.ShapeDtypeStruct, pltpu.SemaphoreType.DMA
    return pl.pallas_call(
        branch_kernel,
        out_shape=(
            shape((rows, width), jnp.float32),
            shape(blocks.shape, blocks.dtype),
            shape(attend_sent.shape[1:], attend_sent.dtype),
            shape(out_sent.shape[1:], out_sent.dtype),
        ),
        in_specs=[vmem] * 2 + [anywhere] * 3,
        out_specs=tuple([vmem] + [anywhere] * 3),
        scratch_shapes=[
            *Scatter.scratch(rows, width),
            *mail_sems(SLICE_OUT),
            dma,
            dma,
            dma,
            dma,
        ],
        compiler_params=pltpu.CompilerParams(
            collective_id=cid, has_side_effects=True, vmem_limit_bytes=VMEM_BYTES
        ),
        name=name,
    )(hidden, downs, blocks, attend_sent, out_sent)


def on_device_halves(
    tokens,
    segments,
    exit_layer,
    first_gain,
    first_shift,
    query_weight,
    query_bias,
    key_weight,
    value_weight,
    value_bias,
    output_weight,
    output_bias,
    second_gain,
    second_shift,
    up_weight,
    up_bias,
    down_weight,
    down_bias,
    cotangent,
):
    rows, width = tokens.shape[1:]
    nd, ns = lax.axis_size("dp"), lax.axis_size("seq")
    ndev, ranks = nd * ns, nd * ns // 2
    size = width // HEADS
    hidden_size = up_weight.shape[1]
    take = 2 * size
    w = place()
    group = w["g"]
    low_at = w["z"] * ns + w["s"]
    high_at = (nd - 1 - w["z"]) * ns + w["s"]

    def pieces(weight):
        cut = weight.reshape(weight.shape[0], 2, 2, ns, -1)
        both = jnp.stack([cut[:, 0], cut[:, 1, ::-1]], axis=3)
        return both.transpose(1, 2, 0, 3, 4).reshape(ranks, weight.shape[0], -1)

    def from_pieces(blocks, take):
        cut = blocks.reshape(2, ns, blocks.shape[1], 2, take)
        both = jnp.stack([cut[:, :, :, 0], cut[::-1, :, :, 1]]).transpose(3, 0, 1, 2, 4)
        return both.reshape(blocks.shape[1], -1).astype(jnp.float32)

    def own_half(pair):
        return lax.dynamic_index_in_dim(pair, group, 0, keepdims=False).astype(jnp.float32)

    def total(pair, got):
        return own_half(pair) + got.astype(jnp.float32)

    vector_parts = [
        first_gain,
        first_shift,
        query_bias,
        value_bias,
        output_bias,
        second_gain,
        second_shift,
        down_bias,
        up_bias,
    ]
    attend_pieces = jnp.concatenate(
        [pieces(query_weight), pieces(key_weight), pieces(value_weight)], axis=2
    )
    letter = jnp.concatenate(vector_parts)
    letter = jnp.pad(letter, (0, -letter.shape[0] % 2048)).reshape(-1, 128)
    attend_blocks, vectors, output_rows, segs = exchange(
        [
            (attend_pieces, SLICE_IN),
            (letter, SPREAD),
            (output_weight, PAIR),
            (segments.reshape(-1, 128), NEAR),
        ],
        "exchange_first",
        0,
    )
    vectors = vectors.reshape(ndev, -1)
    output_rows = output_rows.reshape(-1, width)
    segs = segs.reshape(2, -1)
    cuts, at = [], 0
    for part in vector_parts:
        cuts.append(vectors[:, at : at + part.shape[0]])
        at += part.shape[0]
    full = [cut.reshape(-1).astype(jnp.float32) for cut in cuts]
    gain_one, shift_one, _, _, output_shift, gain_two, shift_two, down_shift, _ = full

    def rank_vector(cut):
        return jnp.concatenate(
            [
                lax.dynamic_index_in_dim(cut, low_at, 0, keepdims=False),
                lax.dynamic_index_in_dim(cut, high_at, 0, keepdims=False),
            ]
        ).astype(jnp.float32)

    query_shift, value_shift, up_shift = (rank_vector(cuts[i]) for i in (2, 3, 8))
    attend_shift = jnp.concatenate([query_shift, jnp.zeros_like(query_shift), value_shift])[None]

    keep = (exit_layer > LAYER).astype(jnp.float32).reshape(rows, 1)
    inputs = tokens.astype(jnp.float32).reshape(rows, width)
    upstream = cotangent.astype(jnp.float32).reshape(rows, width)
    branch_back = (keep * upstream).astype(jnp.bfloat16)
    normed_one = layer_norm(inputs, gain_one, shift_one).astype(jnp.bfloat16)
    (
        attention,
        queries,
        keys,
        values,
        mixed,
        lse,
        normed_all,
        branch_back_all,
        attend_pair,
        up_blocks,
        down_pair,
    ) = attend(
        normed_one,
        branch_back,
        attend_shift,
        output_rows,
        segs,
        attend_blocks.reshape(-1, 3 * take),
        pieces(up_weight),
        down_weight,
        size,
        "attend",
        1,
    )
    middle = inputs + keep * (attention + output_shift)
    normed_two = layer_norm(middle, gain_two, shift_two).astype(jnp.bfloat16)
    down_rows = down_pair.reshape(-1, width)
    normed_two_back, hidden, up_shift_sum, down_grad, up_grad = feed(
        normed_two,
        up_shift[None],
        up_blocks.reshape(width // 2, -1),
        branch_back_all,
        down_rows,
        "feed",
        2,
    )
    norm_result, pull_two = jax.vjp(layer_norm, middle, gain_two, shift_two)
    middle_part, gain_two_sum, shift_two_sum = pull_two(normed_two_back)
    middle_back = upstream + middle_part
    attention_back = (keep * middle_back).astype(jnp.bfloat16)
    down_grad = down_grad.reshape(2, -1, width)
    up_grad = up_grad.reshape(2, width // 2, -1)
    normed_one_back, output_grad, attend_grad, query_sum, value_sum, down_got, up_got = attend_back(
        attention_back,
        output_rows,
        queries,
        keys,
        values,
        mixed,
        lse,
        segs,
        normed_all,
        attend_pair,
        down_grad,
        up_grad,
        size,
        "attend_back",
        3,
    )
    up_half = total(up_grad, up_got).astype(jnp.bfloat16).reshape(ranks, width // ndev, -1)
    attend_grad = attend_grad.reshape(2, width // 2, -1)
    output_grad = output_grad.reshape(2, -1, width)
    branch, up_swapped, attend_got, output_got = branch_sum(
        hidden, down_rows, up_half, attend_grad, output_grad, "branch_sum", 4
    )
    layer_out = (middle + keep * (branch + down_shift)).astype(jnp.bfloat16)
    attend_half = total(attend_grad, attend_got).astype(jnp.bfloat16)
    attend_half = attend_half.reshape(ranks, width // ndev, -1)
    norm_first, pull_one = jax.vjp(layer_norm, inputs, gain_one, shift_one)
    inputs_part, gain_one_sum, shift_one_sum = pull_one(normed_one_back)
    tokens_gradient = (middle_back + inputs_part).astype(jnp.bfloat16)

    def summed(value):
        return jnp.sum(value.astype(jnp.float32), axis=0)

    own_sums = [
        gain_one_sum,
        shift_one_sum,
        gain_two_sum,
        shift_two_sum,
        summed(attention_back),
        summed(branch_back),
    ]
    share = width // ndev
    dense = jnp.concatenate([value.reshape(ndev, share) for value in own_sums], axis=1)
    rank_sums = jnp.concatenate(
        [query_sum.reshape(2, -1), value_sum.reshape(2, -1), up_shift_sum.reshape(2, -1)], axis=1
    )
    number = jnp.arange(ndev)[:, None]
    sparse = jnp.where(
        number == low_at, rank_sums[0], jnp.where(number == high_at, rank_sums[1], 0.0)
    )
    letter = jnp.concatenate([dense, sparse], axis=1)
    letter = jnp.pad(letter, ((0, 0), (0, -letter.shape[1] % 1024))).reshape(ndev, -1, 128)
    attend_swapped, mailed = exchange(
        [(attend_half, SLICE_OUT), (letter, WORLD)], "exchange_last", 5
    )
    matrix_rows = [
        from_pieces(attend_swapped[:, :, i * take : (i + 1) * take], size) for i in range(3)
    ]
    mailed = jnp.sum(mailed, axis=0).reshape(-1)
    vector_out, at = [], 0
    for part in (share,) * 6 + (size, size, hidden_size // ndev):
        vector_out.append(mailed[at : at + part])
        at += part
    (
        gain_one_part,
        shift_one_part,
        gain_two_part,
        shift_two_part,
        output_shift_part,
        down_shift_part,
        query_shift_part,
        value_shift_part,
        up_shift_part,
    ) = vector_out
    return (
        layer_out.reshape(tokens.shape),
        tokens_gradient.reshape(tokens.shape),
        gain_one_part,
        shift_one_part,
        matrix_rows[0],
        query_shift_part,
        matrix_rows[1],
        matrix_rows[2],
        value_shift_part,
        total(output_grad, output_got),
        output_shift_part,
        gain_two_part,
        shift_two_part,
        from_pieces(up_swapped, hidden_size // ndev),
        up_shift_part,
        total(down_grad, down_got),
        down_shift_part,
    )


def solution(mesh):
    placed = (
        P("dp", "seq", None),
        P("dp", None),
        P("dp", "seq"),
        P(("dp", "seq")),
        P(("dp", "seq")),
        P(("dp", "seq"), None),
        P(("dp", "seq")),
        P(("dp", "seq"), None),
        P(("dp", "seq"), None),
        P(("dp", "seq")),
        P(("dp", "seq"), None),
        P(("dp", "seq")),
        P(("dp", "seq")),
        P(("dp", "seq")),
        P(("dp", "seq"), None),
        P(("dp", "seq")),
        P(("dp", "seq"), None),
        P(("dp", "seq")),
        P("dp", "seq", None),
    )
    halves = mesh.shape["dp"] == 4 and mesh.shape["seq"] == 8
    return jax.shard_map(
        on_device_halves if halves else on_device,
        mesh=mesh,
        in_specs=placed,
        out_specs=(
            P("dp", "seq", None),
            P("dp", "seq", None),
            P(("dp", "seq")),
            P(("dp", "seq")),
            P(("dp", "seq"), None),
            P(("dp", "seq")),
            P(("dp", "seq"), None),
            P(("dp", "seq"), None),
            P(("dp", "seq")),
            P(("dp", "seq"), None),
            P(("dp", "seq")),
            P(("dp", "seq")),
            P(("dp", "seq")),
            P(("dp", "seq"), None),
            P(("dp", "seq")),
            P(("dp", "seq"), None),
            P(("dp", "seq")),
        ),
        check_vma=False,
    )
```

```python
import functools
import math

import jax
import jax.numpy as jnp
from jax import lax
from jax.experimental import pallas as pl
from jax.experimental.pallas import tpu as pltpu
from jax.sharding import PartitionSpec as P

HEADS = 32
LAYER = 12


EPS = 1e-05
NEG = -1e30


def activate(value):
    return jax.nn.gelu(value, approximate=True)


def layer_norm(value, gain, shift):
    mean = jnp.mean(value, axis=-1, keepdims=True)
    centred = value - mean
    spread = jnp.mean(centred * centred, axis=-1, keepdims=True)
    return centred * lax.rsqrt(spread + EPS) * gain + shift


def transposed(left, right):
    return lax.dot_general(
        left, right, (((1,), (1,)), ((), ())), preferred_element_type=jnp.float32
    )


def leading(left, right):
    return lax.dot_general(
        left, right, (((0,), (0,)), ((), ())), preferred_element_type=jnp.float32
    )


def visible(query_seg, query_pos, key_seg, key_pos):
    same = query_seg[:, :, None] == key_seg[:, None, :]
    return jnp.logical_and(same, key_pos[None, None, :] <= query_pos[None, :, None])


def by_blocks(step, carry, piece):
    length = jax.tree.leaves(piece)[0].shape[1]
    size = math.gcd(length, 128)

    def one(index, state):
        offset = index * size
        block = jax.tree.map(lambda part: lax.dynamic_slice_in_dim(part, offset, size, 1), piece)
        return step(state, block, offset)

    return lax.fori_loop(0, length // size, one, carry)


def on_device(
    tokens,
    segments,
    exit_layer,
    first_gain,
    first_shift,
    query_weight,
    query_bias,
    key_weight,
    value_weight,
    value_bias,
    output_weight,
    output_bias,
    second_gain,
    second_shift,
    up_weight,
    up_bias,
    down_weight,
    down_bias,
    cotangent,
):
    nseq, piece_len, width = tokens.shape
    head_count = HEADS
    head_size = width // head_count
    scale = head_size ** (-0.5)
    rows = nseq * piece_len
    own_first = lax.axis_index("seq") * piece_len
    own_pos = own_first + jnp.arange(piece_len, dtype=jnp.int32)
    own_seg = lax.dynamic_slice_in_dim(segments, own_first, piece_len, 1)
    keep = (exit_layer > LAYER).astype(jnp.float32).reshape(rows, 1)
    (
        gain_one,
        shift_one,
        query_full,
        query_shift,
        key_full,
        value_full,
        value_shift,
        output_full,
        output_shift,
        gain_two,
        shift_two,
        up_shift,
        down_shift,
    ) = (
        lax.all_gather(first_gain, ("dp", "seq"), axis=0, tiled=True),
        lax.all_gather(first_shift, ("dp", "seq"), axis=0, tiled=True),
        lax.all_gather(query_weight, ("dp", "seq"), axis=0, tiled=True),
        lax.all_gather(query_bias, ("dp", "seq"), axis=0, tiled=True),
        lax.all_gather(key_weight, ("dp", "seq"), axis=0, tiled=True),
        lax.all_gather(value_weight, ("dp", "seq"), axis=0, tiled=True),
        lax.all_gather(value_bias, ("dp", "seq"), axis=0, tiled=True),
        lax.all_gather(output_weight, ("dp", "seq"), axis=0, tiled=True),
        lax.all_gather(output_bias, ("dp", "seq"), axis=0, tiled=True),
        lax.all_gather(second_gain, ("dp", "seq"), axis=0, tiled=True),
        lax.all_gather(second_shift, ("dp", "seq"), axis=0, tiled=True),
        lax.all_gather(up_bias, ("dp", "seq"), axis=0, tiled=True),
        lax.all_gather(down_bias, ("dp", "seq"), axis=0, tiled=True),
    )
    gain_one = gain_one.astype(jnp.float32)
    shift_one = shift_one.astype(jnp.float32)
    gain_two = gain_two.astype(jnp.float32)
    shift_two = shift_two.astype(jnp.float32)
    inputs = tokens.astype(jnp.float32).reshape(rows, width)
    normed_one = layer_norm(inputs, gain_one, shift_one).astype(jnp.bfloat16)
    queries = (
        jnp.dot(normed_one, query_full, preferred_element_type=jnp.float32)
        + query_shift.astype(jnp.float32)
    ).astype(jnp.bfloat16)
    keys = jnp.dot(normed_one, key_full, preferred_element_type=jnp.float32).astype(jnp.bfloat16)
    values = (
        jnp.dot(normed_one, value_full, preferred_element_type=jnp.float32)
        + value_shift.astype(jnp.float32)
    ).astype(jnp.bfloat16)
    query_heads = queries.reshape(nseq, piece_len, head_count, head_size)
    key_heads = keys.reshape(nseq, piece_len, head_count, head_size)
    value_heads = values.reshape(nseq, piece_len, head_count, head_size)
    key_local = keys.reshape(nseq, piece_len, width)
    pair_local = jnp.concatenate([keys, values], axis=1).reshape(nseq, piece_len, 2 * width)

    def key_mask(start, length):
        key_pos = start + jnp.arange(length, dtype=jnp.int32)
        key_seg = lax.dynamic_slice_in_dim(segments, start, length, 1)
        return visible(own_seg, own_pos, key_seg, key_pos)[:, None]

    def local_scores(key_block):
        keyed = key_block.reshape(nseq, key_block.shape[1], head_count, head_size)
        return (
            jnp.einsum("sqhd,skhd->shqk", query_heads, keyed, preferred_element_type=jnp.float32)
            * scale
        )

    def norm_step(carry, block, start):
        top, total = carry
        allowed = key_mask(start, block.shape[1])
        scores = jnp.where(allowed, local_scores(block), NEG)
        new_top = jnp.maximum(top, jnp.max(scores, axis=-1))
        weights = jnp.where(allowed, jnp.exp(scores - new_top[..., None]), 0.0)
        return (new_top, total * jnp.exp(top - new_top) + jnp.sum(weights, axis=-1))

    start_norm = (
        jnp.full((nseq, head_count, piece_len), NEG, jnp.float32),
        jnp.zeros((nseq, head_count, piece_len), jnp.float32),
    )
    top, total = by_blocks(
        norm_step, start_norm, lax.all_gather(key_local, "seq", axis=1, tiled=True)
    )
    lse = top + jnp.log(total)

    def mix_step(acc, block, start):
        length = block.shape[1]
        allowed = key_mask(start, length)
        scores = local_scores(block[:, :, :width])
        probs = jnp.where(allowed, jnp.exp(scores - lse[..., None]), 0.0).astype(jnp.bfloat16)
        valued = block[:, :, width:].reshape(nseq, length, head_count, head_size)
        return acc + jnp.einsum(
            "shqk,skhd->sqhd", probs, valued, preferred_element_type=jnp.float32
        )

    empty_heads = jnp.zeros((nseq, piece_len, head_count, head_size), jnp.float32)
    mixed_heads = by_blocks(
        mix_step, empty_heads, lax.all_gather(pair_local, "seq", axis=1, tiled=True)
    )
    mixed = mixed_heads.reshape(rows, width).astype(jnp.bfloat16)
    attention = jnp.dot(
        mixed, output_full, preferred_element_type=jnp.float32
    ) + output_shift.astype(jnp.float32)
    middle = inputs + keep * attention
    normed_two = layer_norm(middle, gain_two, shift_two).astype(jnp.bfloat16)
    columns = normed_two
    before = jnp.dot(
        columns,
        lax.all_gather(up_weight, ("dp", "seq"), axis=0, tiled=True),
        preferred_element_type=jnp.float32,
    )
    pre_active = before + up_shift.astype(jnp.float32)
    hidden = activate(pre_active).astype(jnp.bfloat16)
    columns = hidden
    branch = jnp.dot(
        columns,
        lax.all_gather(down_weight, ("dp", "seq"), axis=0, tiled=True),
        preferred_element_type=jnp.float32,
    )
    branch = branch + down_shift.astype(jnp.float32)
    layer_out = (middle + keep * branch).astype(jnp.bfloat16).reshape(nseq, piece_len, width)
    upstream = cotangent.astype(jnp.float32).reshape(rows, width)
    branch_back = (keep * upstream).astype(jnp.bfloat16)
    down_shift_sum = jnp.sum(branch_back.astype(jnp.float32), axis=0)
    hidden_back = transposed(
        branch_back, lax.all_gather(down_weight, ("dp", "seq"), axis=0, tiled=True)
    )
    active_value, pull_active = jax.vjp(activate, pre_active)
    pre_back = pull_active(hidden_back)[0].astype(jnp.bfloat16)
    up_shift_sum = jnp.sum(pre_back.astype(jnp.float32), axis=0)
    down_gradient = lax.psum_scatter(
        leading(hidden, branch_back), ("dp", "seq"), scatter_dimension=0, tiled=True
    )
    normed_two_back = transposed(
        pre_back, lax.all_gather(up_weight, ("dp", "seq"), axis=0, tiled=True)
    )
    norm_result, pull_two = jax.vjp(layer_norm, middle, gain_two, shift_two)
    middle_part, gain_two_sum, shift_two_sum = pull_two(normed_two_back)
    middle_back = upstream + middle_part
    attention_back = (keep * middle_back).astype(jnp.bfloat16)
    output_shift_sum = jnp.sum(attention_back.astype(jnp.float32), axis=0)
    mixed_back = transposed(attention_back, output_full).astype(jnp.bfloat16)
    mixed_heads_back = mixed_back.reshape(nseq, piece_len, head_count, head_size)
    delta_rows = jnp.sum(mixed_heads_back.astype(jnp.float32) * mixed_heads, axis=-1)
    delta = delta_rows.transpose(0, 2, 1)
    lse_rows = lse.transpose(0, 2, 1)

    def query_step(acc, block, start):
        length = block.shape[1]
        allowed = key_mask(start, length)
        scores = local_scores(block[:, :, :width])
        probs = jnp.where(allowed, jnp.exp(scores - lse[..., None]), 0.0)
        valued = block[:, :, width:].reshape(nseq, length, head_count, head_size)
        keyed = block[:, :, :width].reshape(nseq, length, head_count, head_size)
        prob_back = jnp.einsum(
            "sqhd,skhd->shqk", mixed_heads_back, valued, preferred_element_type=jnp.float32
        )
        score_back = (probs * (prob_back - delta[..., None])).astype(jnp.bfloat16)
        return acc + jnp.einsum(
            "shqk,skhd->sqhd", score_back, keyed, preferred_element_type=jnp.float32
        )

    query_sum = by_blocks(
        query_step, empty_heads, lax.all_gather(pair_local, "seq", axis=1, tiled=True)
    )
    queries_back = (query_sum * scale).reshape(rows, width).astype(jnp.bfloat16)

    def key_step(carry, block, start):
        key_acc, value_acc = carry
        query_block, back_block, norm_block, delta_block = block
        length = query_block.shape[1]
        query_pos = start + jnp.arange(length, dtype=jnp.int32)
        query_seg = lax.dynamic_slice_in_dim(segments, start, length, 1)
        allowed = visible(query_seg, query_pos, own_seg, own_pos)[:, None]
        remote_query = query_block.astype(jnp.bfloat16).reshape(nseq, length, head_count, head_size)
        remote_back = back_block.astype(jnp.bfloat16).reshape(nseq, length, head_count, head_size)
        scores = (
            jnp.einsum(
                "sqhd,skhd->shqk", remote_query, key_heads, preferred_element_type=jnp.float32
            )
            * scale
        )
        probs = jnp.where(allowed, jnp.exp(scores - norm_block.transpose(0, 2, 1)[..., None]), 0.0)
        value_acc = value_acc + jnp.einsum(
            "shqk,sqhd->skhd",
            probs.astype(jnp.bfloat16),
            remote_back,
            preferred_element_type=jnp.float32,
        )
        prob_back = jnp.einsum(
            "sqhd,skhd->shqk", remote_back, value_heads, preferred_element_type=jnp.float32
        )
        score_back = (probs * (prob_back - delta_block.transpose(0, 2, 1)[..., None])).astype(
            jnp.bfloat16
        )
        key_acc = key_acc + jnp.einsum(
            "shqk,sqhd->skhd", score_back, remote_query, preferred_element_type=jnp.float32
        )
        return (key_acc, value_acc)

    query_send = queries.astype(jnp.float32).reshape(nseq, piece_len, width)
    back_send = mixed_back.astype(jnp.float32).reshape(nseq, piece_len, width)
    key_sum, value_sum = by_blocks(
        key_step,
        (empty_heads, empty_heads),
        (
            lax.all_gather(query_send.astype(jnp.bfloat16), "seq", axis=1, tiled=True).astype(
                jnp.float32
            ),
            lax.all_gather(back_send.astype(jnp.bfloat16), "seq", axis=1, tiled=True).astype(
                jnp.float32
            ),
            lax.all_gather(lse_rows.astype(jnp.bfloat16), "seq", axis=1, tiled=True).astype(
                jnp.float32
            ),
            lax.all_gather(delta_rows.astype(jnp.bfloat16), "seq", axis=1, tiled=True).astype(
                jnp.float32
            ),
        ),
    )
    keys_back = (key_sum * scale).reshape(rows, width).astype(jnp.bfloat16)
    values_back = value_sum.reshape(rows, width).astype(jnp.bfloat16)
    query_shift_sum = jnp.sum(queries_back.astype(jnp.float32), axis=0)
    value_shift_sum = jnp.sum(values_back.astype(jnp.float32), axis=0)
    normed_one_back = (
        transposed(queries_back, query_full)
        + transposed(keys_back, key_full)
        + transposed(values_back, value_full)
    )
    norm_first, pull_one = jax.vjp(layer_norm, inputs, gain_one, shift_one)
    inputs_part, gain_one_sum, shift_one_sum = pull_one(normed_one_back)
    tokens_gradient = (
        (middle_back + inputs_part).astype(jnp.bfloat16).reshape(nseq, piece_len, width)
    )
    stacked_back = jnp.concatenate([queries_back, keys_back, values_back], axis=1)
    row_gradient = lax.psum_scatter(
        jnp.concatenate(
            [
                leading(normed_one, stacked_back),
                leading(mixed, attention_back),
                leading(normed_two, pre_back),
            ],
            axis=1,
        ),
        ("dp", "seq"),
        scatter_dimension=0,
        tiled=True,
    )
    (
        gain_one_part,
        shift_one_part,
        query_shift_part,
        value_shift_part,
        output_shift_part,
        gain_two_part,
        shift_two_part,
        up_shift_part,
        down_shift_part,
    ) = (
        lax.psum_scatter(gain_one_sum, ("dp", "seq"), scatter_dimension=0, tiled=True),
        lax.psum_scatter(shift_one_sum, ("dp", "seq"), scatter_dimension=0, tiled=True),
        lax.psum_scatter(query_shift_sum, ("dp", "seq"), scatter_dimension=0, tiled=True),
        lax.psum_scatter(value_shift_sum, ("dp", "seq"), scatter_dimension=0, tiled=True),
        lax.psum_scatter(output_shift_sum, ("dp", "seq"), scatter_dimension=0, tiled=True),
        lax.psum_scatter(gain_two_sum, ("dp", "seq"), scatter_dimension=0, tiled=True),
        lax.psum_scatter(shift_two_sum, ("dp", "seq"), scatter_dimension=0, tiled=True),
        lax.psum_scatter(up_shift_sum, ("dp", "seq"), scatter_dimension=0, tiled=True),
        lax.psum_scatter(down_shift_sum, ("dp", "seq"), scatter_dimension=0, tiled=True),
    )
    return (
        layer_out,
        tokens_gradient,
        gain_one_part,
        shift_one_part,
        row_gradient[:, :width],
        query_shift_part,
        row_gradient[:, width : 2 * width],
        row_gradient[:, 2 * width : 3 * width],
        value_shift_part,
        row_gradient[:, 3 * width : 4 * width],
        output_shift_part,
        gain_two_part,
        shift_two_part,
        row_gradient[:, 4 * width :],
        up_shift_part,
        down_gradient,
        down_shift_part,
    )


MESH = pl.DeviceIdType.MESH
CANON = "zyx"
TURNS = ("xy", "yx")
SLICE_IN, SLICE_OUT, COLUMNS_IN, COLUMNS_OUT, LETTERS, SPREAD, PAIR, NEAR = range(8)
VMEM_BYTES = 60 << 20


def place():
    d, s = lax.axis_index("dp"), lax.axis_index("seq")
    half = lax.axis_size("dp") // 2
    far = d // half
    z = d + far * (2 * half - 1 - 2 * d)
    return dict(d=d, s=s, g=far, z=z, y=s // 4, x=(s // 2) % 2, c=s % 2)


def beside(w, dim):
    if dim == "z":
        return (w["d"] + 1 - 2 * (w["d"] % 2), w["s"])
    step = {"c": 1, "x": 2, "y": 4}[dim]
    return (w["d"], w["s"] + step * (1 - 2 * w[dim]))


def partner(w):
    return (lax.axis_size("dp") - 1 - w["d"], w["s"])


def peer(w, r):
    n = lax.axis_size("seq")
    e, s = r // n, r % n
    return (e + w["g"] * (lax.axis_size("dp") - 1 - 2 * e), s)


def row_block(w, r):
    n = lax.axis_size("seq")
    e, s = r // n, r % n
    return (e + w["g"] * (1 - 2 * e)) * n + s


def anyone(i):
    n = lax.axis_size("seq")
    return (i // n, i % n)


def half_peers(w):
    count = lax.axis_size("dp") * lax.axis_size("seq") // 2
    me = w["z"] * lax.axis_size("seq") + w["s"]
    return me, [(me + k) % count for k in range(1, count)]


def world_peers(w):
    count = lax.axis_size("dp") * lax.axis_size("seq")
    me = w["d"] * lax.axis_size("seq") + w["s"]
    return me, [(me + k) % count for k in range(1, count)]


def greet(ids):
    bar = pltpu.get_barrier_semaphore()
    for i in ids:
        pl.semaphore_signal(bar, inc=1, device_id=i, device_id_type=MESH)
    pl.semaphore_wait(bar, len(ids))


def greet_half(w):
    greet([peer(w, r) for r in half_peers(w)[1]] + [partner(w)])


def greet_world(w):
    greet([anyone(i) for i in world_peers(w)[1]])


def remote(src, dst, send, recv, device):
    return pltpu.make_async_remote_copy(
        src_ref=src,
        dst_ref=dst,
        send_sem=send,
        recv_sem=recv,
        device_id=device,
        device_id_type=MESH,
    )


def twice(w, r, size):
    count = lax.axis_size("dp") * lax.axis_size("seq") // 2
    other = count + (r + count // 2) % count
    return [pl.ds(pl.multiple_of(at * size, size), size) for at in (r, other)]


def mail(w, kind, src, out, send, recv, local):
    mine = None
    if kind == SLICE_IN:
        me, others = half_peers(w)
        to = out.at[row_block(w, me)]
        todo = [(src.at[r], to, peer(w, r)) for r in others]
        mine = [(src.at[me], to)]
    elif kind == SLICE_OUT:
        me, others = half_peers(w)
        to = out.at[me]
        todo = [(src.at[row_block(w, r)], to, peer(w, r)) for r in others]
        mine = [(src.at[row_block(w, me)], to)]
    elif kind == COLUMNS_IN:
        me, others = half_peers(w)
        size = out.shape[2] // 2
        to = [out.at[row_block(w, me), :, pl.ds(n * size, size)] for n in range(2)]
        todo = [
            (src.at[:, cols], to[n], peer(w, r))
            for r in others
            for n, cols in enumerate(twice(w, r, size))
        ]
        mine = [(src.at[:, cols], to[n]) for n, cols in enumerate(twice(w, me, size))]
    elif kind == COLUMNS_OUT:
        me, others = half_peers(w)
        size = src.shape[2] // 2
        to = [out.at[:, cols] for cols in twice(w, me, size)]
        todo = [
            (src.at[row_block(w, r), :, pl.ds(n * size, size)], to[n], peer(w, r))
            for r in others
            for n in range(2)
        ]
        mine = [
            (src.at[row_block(w, me), :, pl.ds(n * size, size)], to[n]) for n in range(2)
        ]
    elif kind == LETTERS:
        me, others = world_peers(w)
        to = out.at[me]
        todo = [(src.at[i // 2], to, anyone(i)) for i in others]
        mine = [(src.at[me // 2], to)]
    elif kind == SPREAD:
        me, others = world_peers(w)
        to = out.at[me]
        todo = [(src, to, anyone(i)) for i in others]
        mine = [(src, to)]
    elif kind == PAIR:
        to = out.at[w["g"]]
        todo = [(src, to, partner(w))]
        mine = [(src, to)]
    else:
        to = out.at[w["z"]]
        todo = [(src, to, beside(w, "z"))]
        mine = [(src, to)]
    copies = [
        remote(part, to, send.at[k], recv.at[k], device)
        for k, (part, to, device) in enumerate(todo)
    ]
    return copies + [
        pltpu.make_async_copy(part, to, local.at[k]) for k, (part, to) in enumerate(mine)
    ]


def start_all(copies):
    for cp in copies:
        cp.start()


def wait_all(copies):
    for cp in copies:
        cp.wait()


def mail_sems(kind):
    count = lax.axis_size("dp") * lax.axis_size("seq")
    half = count // 2 - 1
    n = {
        SLICE_IN: half,
        SLICE_OUT: half,
        COLUMNS_IN: 2 * half,
        COLUMNS_OUT: 2 * half,
        LETTERS: count - 1,
        SPREAD: count - 1,
    }.get(kind, 1)
    dma = pltpu.SemaphoreType.DMA
    return [dma((n,)), dma((n,)), dma((2,))]


def first_kernel(size, *refs):
    refs = Refs(refs)
    weights, (letter, out_rows, segs, grad) = refs.take(3), refs.take(4)
    blocks, letters, pair, near, grads, grad_far = refs.take(6)
    pieces, plane = refs.take(2)
    sems = [refs.take(3) for _ in range(4)]
    one = refs.take(5)
    cross_send, cross_recv, flush = refs.take(3)
    w = place()
    greet_world(w)
    copies = mail(w, SPREAD, letter, letters, *sems[1])
    start_all(copies)
    count = pieces.shape[0]
    for r in range(count):
        places = (r, count + (r + count // 2) % count)
        pieces[r] = jnp.concatenate(
            [ref[:, pl.ds(at * size, size)] for ref in weights for at in places], axis=1
        )
    copies += mail(w, SLICE_IN, pieces, blocks, *sems[0])
    start_all(copies[-count:])
    late = mail(w, PAIR, out_rows, pair, *sems[2]) + mail(w, NEAR, segs, near, *sems[3])
    start_all(late)
    gather = PlaneGather(w, grad, plane, *one)
    gather.start()
    cross = remote(grad, grad_far, cross_send, cross_recv, beside(w, "z"))
    cross.start()
    gather.turn()
    gather.land()
    gather.ready()
    keep = pltpu.make_async_copy(plane, grads, flush)
    keep.start()
    wait_all(copies + late + [cross])
    gather.finish()
    keep.wait()


def first(weights, letter, out_rows, segs, grad, size, name, cid):
    rows, width = weights[0].shape
    ndev = lax.axis_size("dp") * lax.axis_size("seq")
    shape, dma = jax.ShapeDtypeStruct, pltpu.SemaphoreType.DMA
    blocks = (ndev // 2, rows, 6 * size)
    vmem, anywhere = pl.BlockSpec(memory_space=pltpu.VMEM), pl.BlockSpec(memory_space=pl.ANY)
    return pl.pallas_call(
        functools.partial(first_kernel, size),
        out_shape=(
            shape(blocks, out_rows.dtype),
            shape((ndev,) + letter.shape, letter.dtype),
            shape((2,) + out_rows.shape, out_rows.dtype),
            shape((2,) + segs.shape, segs.dtype),
            shape((2, 2, 2) + grad.shape, grad.dtype),
            shape(grad.shape, grad.dtype),
        ),
        in_specs=[vmem] * 3 + [anywhere] * 3 + [vmem],
        out_specs=tuple([anywhere] * 6),
        scratch_shapes=[
            pltpu.VMEM(blocks, out_rows.dtype),
            pltpu.VMEM((2, 2, 2) + grad.shape, grad.dtype),
            *mail_sems(SLICE_IN),
            *mail_sems(SPREAD),
            *mail_sems(PAIR),
            *mail_sems(NEAR),
            *PlaneGather.sems(),
            dma,
            dma,
            dma,
        ],
        compiler_params=pltpu.CompilerParams(
            collective_id=cid, has_side_effects=True, vmem_limit_bytes=VMEM_BYTES
        ),
        name=name,
    )(*weights, letter, out_rows, segs, grad)


def box(w, **where):
    pick = {"other": lambda q: 1 - w[q], "both": lambda q: pl.ds(0, 2)}
    return tuple(pick[where[q]](q) if q in where else w[q] for q in CANON)


def halves(width):
    return [pl.ds(0, width // 2), pl.ds(width // 2, width // 2)]


class PlaneGather:
    def __init__(self, w, src, out, send, recv, side_send, side_recv, local):
        self.w, self.src, self.out = w, src, out
        self.send, self.recv, self.side_send, self.side_recv = send, recv, side_send, side_recv
        self.parts = halves(out.shape[-1])
        self.own = (w["y"], w["x"], w["c"])
        self.keep = None if src is None else pltpu.make_async_copy(src, out.at[self.own], local)
        self.links, self.sides = {}, []

    @staticmethod
    def sems():
        dma = pltpu.SemaphoreType.DMA
        return [dma((4,)), dma((4,)), dma((5,)), dma((5,)), dma]

    def push(self, p, k, src, dst):
        n = 2 * p + k
        cp = remote(src, dst, self.send.at[n], self.recv.at[n], beside(self.w, TURNS[p][k]))
        cp.start()
        self.links[p, k] = cp

    def over(self, src, dst):
        n = len(self.sides)
        cp = remote(src, dst, self.side_send.at[n], self.side_recv.at[n], beside(self.w, "c"))
        cp.start()
        self.sides.append(cp)

    def blocks(self, cols, **where):
        return self.out.at[box(self.w, **where)[1:] + (self.w["c"], slice(None), cols)]

    def start(self, before=lambda p: None):
        for p, cols in enumerate(self.parts):
            before(p)
            dst = self.out.at[self.own + (slice(None), cols)]
            self.push(p, 0, dst if self.src is None else self.src.at[:, cols], dst)
        dst = self.out.at[self.own]
        if self.keep is not None:
            self.keep.start()
        self.over(dst if self.src is None else self.src, dst)

    def turn(self):
        if self.keep is not None:
            self.keep.wait()
        for p, cols in enumerate(self.parts):
            a, b = TURNS[p]
            self.links[p, 0].wait_recv()
            held = self.blocks(cols, **{a: "both"})
            self.push(p, 1, held, held)
            new = self.blocks(cols, **{a: "other"})
            self.over(new, new)

    def land(self):
        for p, cols in enumerate(self.parts):
            a, b = TURNS[p]
            self.links[p, 1].wait_recv()
            new = self.blocks(cols, **{a: "both", b: "other"})
            self.over(new, new)

    def ready(self):
        for cp in self.sides:
            cp.wait_recv()

    def finish(self):
        for cp in list(self.links.values()) + self.sides:
            cp.wait_send()


class Gather:
    def __init__(self, w, src, out, *sems):
        self.w, self.src, self.out = w, src, out
        self.near = PlaneGather(w, src, out.at[w["z"]], *sems[:5])
        self.far = PlaneGather(w, None, out.at[1 - w["z"]], *sems[5:10])
        self.cross = []
        for p, cols in enumerate(halves(src.shape[1])):
            dst = out.at[box(w) + (w["c"], slice(None), cols)]
            self.cross.append(
                remote(src.at[:, cols], dst, sems[10].at[p], sems[11].at[p], beside(w, "z"))
            )

    @staticmethod
    def sems():
        dma = pltpu.SemaphoreType.DMA
        return [*PlaneGather.sems(), *PlaneGather.sems(), dma((2,)), dma((2,))]

    def start(self):
        self.near.start()
        start_all(self.cross)

    def turn(self):
        self.near.turn()

    def far_start(self):
        self.far.start(lambda p: self.cross[p].wait_recv())

    def near_ready(self):
        self.near.land()
        self.near.ready()

    def far_turn(self):
        self.far.turn()

    def far_ready(self):
        self.far.land()
        self.far.ready()

    def finish(self):
        self.near.finish()
        self.far.finish()
        for cp in self.cross:
            cp.wait_send()


class Scatter:
    def __init__(self, w, acc, away, side, land_two, land_one, land_z, send, recv, side_send, side_recv):
        self.w, self.acc, self.away, self.side = w, acc, away, side
        self.land_two, self.land_one, self.land_z = land_two, land_one, land_z
        self.send, self.recv, self.side_send, self.side_recv = send, recv, side_send, side_recv
        self.parts = halves(acc.shape[-1])
        self.links, self.sides = {}, {}

    @staticmethod
    def scratch(rows, width, wholes=3):
        whole = pltpu.VMEM((2, 2, 2, rows, width), jnp.bfloat16)
        dma = pltpu.SemaphoreType.DMA
        return [whole] * wholes + [
            pltpu.VMEM((2, 2, 2, rows, width // 2), jnp.bfloat16),
            pltpu.VMEM((2, 2, rows, width // 2), jnp.bfloat16),
            pltpu.VMEM((2, rows, width // 2), jnp.bfloat16),
            dma((10,)),
            dma((10,)),
            dma((4,)),
            dma((4,)),
        ]

    def plane(self, group):
        return 1 - self.w["z"] if group else self.w["z"]

    def produce(self, group, p, product):
        w, cols, z = self.w, self.parts[p], self.plane(group)
        rows = self.acc.shape[3]

        def fill(out, core):
            @pl.loop(0, 2)
            def _(y):
                block = product(z, y, core, cols)
                out[z, y, :, :, cols] = block.astype(out.dtype).reshape(2, rows, -1)

        fill(self.away, 1 - w["c"])
        at = (z, pl.ds(0, 2), pl.ds(0, 2), slice(None), cols)
        n = len(self.sides)
        cp = remote(
            self.away.at[at],
            self.side.at[at],
            self.side_send.at[n],
            self.side_recv.at[n],
            beside(w, "c"),
        )
        cp.start()
        self.sides[group, p] = cp
        fill(self.acc, w["c"])

    def push(self, key, dim, src, dst):
        n = len(self.links)
        cp = remote(src, dst, self.send.at[n], self.recv.at[n], beside(self.w, dim))
        cp.start()
        self.links[key] = cp

    def at(self, group, **where):
        index = box(self.w, **where)
        return (self.plane(group),) + index[1:]

    def add(self, at, got, cols):
        at = at + (slice(None), cols)
        total = self.acc[at].astype(jnp.float32) + got.astype(jnp.float32)
        self.acc[at] = total.astype(self.acc.dtype)

    def fold(self, group, p):
        cols, (b, a) = self.parts[p], TURNS[p]
        self.sides[group, p].wait_recv()

        def add(other):
            @pl.loop(0, 2)
            def _(i):
                here = dict(self.w)
                here[b] = i
                if other:
                    here[a] = 1 - self.w[a]
                at = (self.plane(group), here["y"], here["x"])
                self.add(at, self.side[at + (slice(None), cols)], cols)

        add(True)
        src = self.acc.at[self.at(group, **{a: "other", b: "both"}) + (slice(None), cols)]
        self.push((group, p, 0), a, src, self.land_two.at[group, p])
        add(False)

    def middle(self, group, p):
        w, cols, (b, a) = self.w, self.parts[p], TURNS[p]
        self.links[group, p, 0].wait_recv()
        there = self.at(group, **{b: "other"})
        self.add(there, self.land_two[group, p, 1 - w[b]], cols)
        src = self.acc.at[there + (slice(None), cols)]
        self.push((group, p, 1), b, src, self.land_one.at[group, p])
        self.add(self.at(group), self.land_two[group, p, w[b]], cols)

    def cross(self, p):
        cols = self.parts[p]
        self.links[1, p, 1].wait_recv()
        at = self.at(1)
        self.add(at, self.land_one[1, p], cols)
        self.push(("z", p), "z", self.acc.at[at + (slice(None), cols)], self.land_z.at[p])

    def finish(self, p, out):
        cols = self.parts[p]
        self.links[0, p, 1].wait_recv()
        self.links["z", p].wait_recv()
        total = self.acc[self.at(0) + (slice(None), cols)].astype(jnp.float32)
        total += self.land_one[0, p].astype(jnp.float32)
        out[:, cols] = total + self.land_z[p].astype(jnp.float32)

    def begin(self, product):
        self.produce(1, 0, product)
        self.produce(1, 1, product)
        self.fold(1, 0)
        self.fold(1, 1)
        self.produce(0, 0, product)
        self.produce(0, 1, product)

    def second(self):
        self.middle(1, 0)
        self.middle(1, 1)
        self.fold(0, 0)
        self.fold(0, 1)

    def third(self):
        self.cross(0)
        self.cross(1)

    def fourth(self):
        self.middle(0, 0)
        self.middle(0, 1)

    def end(self, out):
        self.finish(0, out)
        self.finish(1, out)
        for cp in list(self.links.values()) + list(self.sides.values()):
            cp.wait_send()


def across(left, right):
    return lax.dot_general(
        left, right, (((1,), (1,)), ((), ())), preferred_element_type=jnp.float32
    )


def straight(left, right):
    return jnp.dot(left, right, preferred_element_type=jnp.float32)


def flat(block):
    return block.reshape(-1, block.shape[-1])


def head_lanes(width, head, size):
    lane = lax.broadcasted_iota(jnp.int32, (1, width), 1)
    return jnp.logical_and(lane >= head * size, lane < (head + 1) * size)


def used_pairs(key_seg, query_seg, first, length, block):
    key_pos = lax.broadcasted_iota(jnp.int32, (length, 1), 0)
    query_pos = first + lax.broadcasted_iota(jnp.int32, (1, block), 1)
    return jnp.logical_and(key_seg == query_seg, key_pos <= query_pos)


def attend_block(i, size, block, first, q, k, v_flip, key_seg, query_seg, mixed, mixed_low, lse):
    width = q.shape[2]
    upto, rows = first + block, pl.ds(first, block)
    allowed = used_pairs(key_seg[i, pl.ds(0, upto), :], query_seg[i, :, rows], first, upto, block)
    keys = k[i, pl.ds(0, upto), :]
    query = q[i, rows, :] * jnp.asarray(size**-0.5, q.dtype)
    parts = []
    for head in range(width // size):
        own = jnp.where(head_lanes(width, head, size), query, jnp.zeros_like(query))
        scores = jnp.where(allowed, across(keys, own), NEG)
        top = jnp.max(scores, axis=0, keepdims=True)
        weights = jnp.exp(scores - top)
        total = jnp.sum(weights, axis=0, keepdims=True)
        lse[i, pl.ds(head, 1), rows] = top + jnp.log(total)
        probs = (weights * (1.0 / total)).astype(q.dtype)
        parts.append(straight(v_flip[i, pl.ds(head * size, size), pl.ds(0, upto)], probs))
    full = jnp.concatenate(parts, axis=0).T
    mixed[i, rows, :] = full
    at = first // block
    mixed_low[i, at // 2, at % 2] = full.astype(mixed_low.dtype).reshape(mixed_low.shape[3:])


def attend_back_block(
    i, size, block, first, q, k, k_flip, v, back, mixed, lse, key_seg, query_seg, q_back, k_sum, v_sum
):
    width = q.shape[2]
    upto, rows = first + block, pl.ds(first, block)
    before = pl.ds(0, upto)
    scale = size**-0.5
    allowed = used_pairs(key_seg[i, before, :], query_seg[i, :, rows], first, upto, block)
    keys, values = k[i, before, :], v[i, before, :]
    query = q[i, rows, :] * jnp.asarray(scale, q.dtype)
    grad = back[i, rows, :]
    product = (grad.astype(jnp.float32) * mixed[i, rows, :]).T
    parts = []
    for head in range(width // size):
        lanes = head_lanes(width, head, size)
        own = jnp.where(lanes, query, jnp.zeros_like(query))
        own_grad = jnp.where(lanes, grad, jnp.zeros_like(grad))
        delta = jnp.sum(product[head * size : (head + 1) * size, :], axis=0, keepdims=True)
        scores = across(keys, own) - lse[i, pl.ds(head, 1), rows]
        probs = jnp.exp(jnp.where(allowed, scores, NEG))
        score_back = (probs * (across(values, own_grad) - delta)).astype(q.dtype)
        v_sum[i, before, :] += straight(probs.astype(q.dtype), own_grad)
        k_sum[i, before, :] += straight(score_back, own)
        parts.append(straight(k_flip[i, pl.ds(head * size, size), before], score_back))
    q_back[i, rows, :] = (jnp.concatenate(parts, axis=0).T * scale).astype(q_back.dtype)


class Refs:
    def __init__(self, refs):
        self.refs, self.used = refs, 0

    def take(self, count):
        self.used += count
        return self.refs[self.used - count : self.used]


def attend_kernel(size, *refs):
    refs = Refs(refs)
    (own, shift, out_rows, key_seg, query_seg, grad_far, blocks, up, down) = refs.take(9)
    (attention, q, k, v, mixed, lse, rows_all, grads_all, pair, ups, downs) = refs.take(11)
    rows, grads, weight, v_flip, mixed_low, columns = refs.take(6)
    one = refs.take(12)
    two = refs.take(5)
    sums = refs.take(10)
    pair_sems, column_sems, up_sems, down_sems = [refs.take(3) for _ in range(4)]
    load, flush = refs.take(2)
    w = place()
    greet_half(w)
    gather = Gather(w, own, rows, *one)
    second = PlaneGather(w, grad_far, grads, *two)
    scatter = Scatter(w, *sums)
    length, take = q.shape[1:]
    block = length // 4
    gather.start()
    pair_mail = mail(w, PAIR, blocks, pair, *pair_sems)
    start_all(pair_mail)
    gather.turn()
    gather.far_start()
    gather.near_ready()
    gather.far_turn()
    wait_all(pair_mail)
    down_mail = mail(w, PAIR, down.at[pl.ds(0, downs.shape[1])], downs, *down_sems)
    start_all(down_mail)
    half = pair.shape[1]
    fetch = [
        pltpu.make_async_copy(pair.at[i], weight.at[pl.ds(i * half, half)], load.at[i])
        for i in range(2)
    ]
    start_all(fetch)
    wait_all(fetch)

    def project(i):
        @pl.loop(0, 2)
        def _(y):
            block = straight(flat(rows[i, y]), weight[...]) + shift[...]
            at = pl.ds(y * (length // 2), length // 2)
            for ref, n in ((q, 0), (k, 1), (v, 2)):
                ref[i, at, :] = block[:, n * take : (n + 1) * take].astype(ref.dtype)
            v_flip[i, :, at] = block[:, 2 * take :].astype(v_flip.dtype).T

    def mix(i):
        for first in range(0, length, block):
            attend_block(
                i, size, block, first, q, k, v_flip, key_seg, query_seg, mixed, mixed_low, lse
            )

    project(w["z"])
    gather.far_ready()
    column_mail = mail(w, COLUMNS_IN, up, columns, *column_sems)
    start_all(column_mail)
    second.start()
    gather.finish()
    keep_rows = pltpu.make_async_copy(rows, rows_all, flush.at[0])
    keep_rows.start()
    project(1 - w["z"])
    second.turn()
    mix(1 - w["z"])
    wait_all(column_mail)
    wait_all(down_mail)
    up_mail = mail(w, PAIR, columns, ups, *up_sems)
    start_all(up_mail)
    mix(w["z"])

    def product(z, y, c, cols):
        return straight(flat(mixed_low[z, y, :, c]), out_rows[:, cols])

    scatter.begin(product)
    second.land()
    scatter.second()
    second.ready()
    keep_grads = pltpu.make_async_copy(grads, grads_all, flush.at[1])
    keep_grads.start()
    scatter.third()
    scatter.fourth()
    scatter.end(attention)
    second.finish()
    wait_all(up_mail)
    keep_rows.wait()
    keep_grads.wait()


def attend(own, shift, out_rows, segs, grad_far, blocks, up, down, size, name, cid):
    rows, width = own.shape
    ns = lax.axis_size("seq")
    length = rows * ns
    take = out_rows.shape[0]
    low, f32 = own.dtype, jnp.float32
    vmem, anywhere = pl.BlockSpec(memory_space=pltpu.VMEM), pl.BlockSpec(memory_space=pl.ANY)
    shape, dma = jax.ShapeDtypeStruct, pltpu.SemaphoreType.DMA
    plane = (2, 2, 2, rows, width)
    columns = (2 * ns, up.shape[0], up.shape[1] // (2 * ns))
    return pl.pallas_call(
        functools.partial(attend_kernel, size),
        out_shape=(
            shape((rows, width), f32),
            *[shape((2, length, take), low)] * 3,
            shape((2, length, take), f32),
            shape((2, take // size, length), f32),
            shape((2,) + plane, low),
            shape(plane, low),
            shape((2,) + blocks.shape, low),
            shape((2,) + columns, low),
            shape((2, down.shape[0] // 2, down.shape[1]), low),
        ),
        in_specs=[vmem] * 6 + [anywhere, vmem, anywhere],
        out_specs=tuple([vmem] * 6 + [anywhere] * 5),
        scratch_shapes=[
            pltpu.VMEM((2,) + plane, low),
            pltpu.VMEM(plane, low),
            pltpu.VMEM((2 * blocks.shape[0], blocks.shape[1]), low),
            pltpu.VMEM((2, take, length), low),
            pltpu.VMEM((2, 2, 2, 2, rows, take), low),
            pltpu.VMEM(columns, low),
            *Gather.sems(),
            *PlaneGather.sems(),
            *Scatter.scratch(rows, width),
            *mail_sems(PAIR),
            *mail_sems(COLUMNS_IN),
            *mail_sems(PAIR),
            *mail_sems(PAIR),
            dma((2,)),
            dma((2,)),
        ],
        compiler_params=pltpu.CompilerParams(
            collective_id=cid, has_side_effects=True, vmem_limit_bytes=VMEM_BYTES
        ),
        name=name,
    )(own, shift, out_rows, segs[:, :, None], segs[:, None, :], grad_far, blocks, up, down)


def feed_kernel(*refs):
    refs = Refs(refs)
    own, shift, ups, grads_near, grads_far, downs, down_some = refs.take(7)
    back, branch, shift_sum, down_grad, up_grad, down_got = refs.take(6)
    rows, grads, up, down, slope, flip, hidden, stage = refs.take(8)
    pre = hidden
    one = refs.take(12)
    branch_sums = refs.take(10)
    sums = refs.take(8)
    down_sems = refs.take(3)
    grad_send, grad_recv, load, flush = refs.take(4)
    w = place()
    greet_half(w)
    gather = Gather(w, own, rows, *one)
    branch_scatter = Scatter(w, *branch_sums)
    core = lambda c: grads.at[pl.ds(0, 2), pl.ds(0, 2), pl.ds(0, 2), c]
    scatter = Scatter(w, core(0), core(1), *sums)
    gather.start()
    half = downs.shape[0]
    early = down_some.shape[1]
    rest = half - early
    place_down = pl.ds(w["g"] * half + early, rest)
    down_mail = [
        remote(
            downs.at[pl.ds(early, rest)],
            down.at[place_down],
            down_sems[0].at[0],
            down_sems[1].at[0],
            partner(w),
        ),
        pltpu.make_async_copy(downs.at[pl.ds(early, rest)], down.at[place_down], down_sems[2].at[0]),
    ]
    fetch = [
        pltpu.make_async_copy(ups, up, load.at[0]),
        pltpu.make_async_copy(grads_near, grads.at[w["z"]], load.at[1]),
        pltpu.make_async_copy(grads_far, grads.at[1 - w["z"]], load.at[2]),
        pltpu.make_async_copy(down_some.at[0], down.at[pl.ds(0, early)], load.at[3]),
        pltpu.make_async_copy(down_some.at[1], down.at[pl.ds(half, early)], load.at[4]),
    ]
    start_all(down_mail + fetch)
    width = rows.shape[5]
    span = rows.shape[2] * rows.shape[3] * rows.shape[4]
    chunk = 256
    shift_sum[...] = jnp.zeros_like(shift_sum)

    def forward(z):
        @pl.loop(0, 2)
        def _(y):
            before = straight(flat(rows[z, y]), up[...]) + shift[...]
            active, pull = jax.vjp(activate, before)
            at = pl.ds(z * (2 * span) + y * span, span)
            low = active.astype(hidden.dtype)
            hidden[z, y] = low.reshape(hidden.shape[2:])
            flip[:, at] = low.T
            slope[at, :] = pull(jnp.ones_like(before))[0].astype(slope.dtype)

    gather.turn()
    gather.far_start()
    gather.near_ready()
    wait_all(fetch)
    gather.far_turn()
    forward(w["z"])
    gather.far_ready()
    gather.finish()
    forward(1 - w["z"])
    wait_all(down_mail)

    def branch_product(z, y, c, cols):
        return straight(flat(hidden[z, y, :, c]), down[:, cols])

    branch_scatter.begin(branch_product)

    @pl.loop(0, width // chunk)
    def _(i):
        cols = pl.ds(i * chunk, chunk)
        grad = straight(flip[...], grads[:, :, :, :, :, cols].reshape(-1, chunk))
        down_grad[:, :, cols] = grad.astype(down_grad.dtype).reshape(2, -1, chunk)

    trade = remote(down_grad.at[1 - w["g"]], down_got, grad_send, grad_recv, partner(w))
    trade.start()
    branch_scatter.second()

    @pl.loop(0, 4)
    def _(i):
        at = pl.ds(i * span, span)
        hidden_back = across(flat(grads[i // 2, i % 2]), down[...])
        pre_back = (hidden_back * slope[at, :].astype(jnp.float32)).astype(pre.dtype)
        pre[i // 2, i % 2] = pre_back.reshape(pre.shape[2:])
        flip[:, at] = pre_back.T
        shift_sum[...] += jnp.sum(pre_back.astype(jnp.float32), axis=0, keepdims=True)

    def product(z, y, c, cols):
        return across(flat(pre[z, y, :, c]), up[cols, :])

    def store(i):
        at = up_grad.at[pl.ds(pl.multiple_of(i * chunk, chunk), chunk)]
        return pltpu.make_async_copy(stage.at[i % 2], at, flush.at[i % 2])

    scatter.begin(product)
    branch_scatter.third()

    @pl.loop(0, width // chunk)
    def _(i):
        cols = pl.ds(i * chunk, chunk)
        grad = straight(flip[...], rows[:, :, :, :, :, cols].reshape(-1, chunk))

        @pl.when(i >= 2)
        def _():
            store(i).wait()

        stage[i % 2] = grad.astype(stage.dtype).T
        store(i).start()

    store(0).wait()
    store(1).wait()
    scatter.second()
    branch_scatter.fourth()
    scatter.third()
    scatter.fourth()
    branch_scatter.end(branch)
    scatter.end(back)
    trade.wait()


def feed(own, shift, ups, grads_near, grads_far, downs, down_some, name, cid):
    rows, width = own.shape
    take = ups.shape[1]
    low, f32 = own.dtype, jnp.float32
    vmem, anywhere = pl.BlockSpec(memory_space=pltpu.VMEM), pl.BlockSpec(memory_space=pl.ANY)
    shape, dma = jax.ShapeDtypeStruct, pltpu.SemaphoreType.DMA
    whole = (2, 2, 2, 2, rows, width)
    tokens = 16 * rows
    return pl.pallas_call(
        feed_kernel,
        out_shape=(
            shape((rows, width), f32),
            shape((rows, width), f32),
            shape((1, take), f32),
            shape((2,) + downs.shape, low),
            shape((width, take), low),
            shape(downs.shape, low),
        ),
        in_specs=[vmem] * 2 + [anywhere] * 5,
        out_specs=(vmem, vmem, vmem, vmem, anywhere, anywhere),
        scratch_shapes=[
            pltpu.VMEM(whole, low),
            pltpu.VMEM(whole, low),
            pltpu.VMEM((width, take), low),
            pltpu.VMEM((take, width), low),
            pltpu.VMEM((tokens, take), low),
            pltpu.VMEM((take, tokens), low),
            pltpu.VMEM((2, 2, 2, 2, rows, take), low),
            pltpu.VMEM((2, 256, take), low),
            *Gather.sems(),
            *Scatter.scratch(rows, width),
            *Scatter.scratch(rows, width, 1),
            *mail_sems(PAIR),
            dma,
            dma,
            dma((5,)),
            dma((2,)),
        ],
        compiler_params=pltpu.CompilerParams(
            collective_id=cid, has_side_effects=True, vmem_limit_bytes=VMEM_BYTES
        ),
        name=name,
    )(own, shift, ups, grads_near, grads_far, downs, down_some)


def attend_back_kernel(size, *refs):
    refs = Refs(refs)
    (own, out_rows, q, k, v, mixed, lse, key_seg, query_seg) = refs.take(9)
    rows_all, pair, up_sent = refs.take(3)
    (back, out_grad, attend_grad, q_sum, v_bias_sum, up_got, out_got, attend_got) = refs.take(8)
    (grads, rows, weight, k_flip, mixed_flip, grad_heads, q_back, k_sum, v_sum, stack, stack_flip) = (
        refs.take(11)
    )
    one = refs.take(12)
    sums = refs.take(10)
    send, recv, load = refs.take(3)
    w = place()
    greet_half(w)
    gather = Gather(w, own, grads, *one)
    scatter = Scatter(w, *sums)
    gather.start()
    other = 1 - w["g"]
    up_trade = remote(up_sent.at[other], up_got, send.at[0], recv.at[0], partner(w))
    up_trade.start()
    half = pair.shape[1]
    fetch = [
        pltpu.make_async_copy(pair.at[i], weight.at[pl.ds(i * half, half)], load.at[i])
        for i in range(2)
    ] + [pltpu.make_async_copy(rows_all, rows, load.at[2])]
    start_all(fetch)
    length, take = q.shape[1:]
    for i in range(2):
        k_flip[i] = k[i].T
        mixed_flip[:, pl.ds(i * length, length)] = mixed[i].astype(mixed_flip.dtype).T
    k_sum[...] = jnp.zeros_like(k_sum)
    v_sum[...] = jnp.zeros_like(v_sum)
    q_sum[...] = jnp.zeros_like(q_sum)
    v_bias_sum[...] = jnp.zeros_like(v_bias_sum)
    block = length // 4

    def heads_back(i):
        @pl.loop(0, 2)
        def _(y):
            at = pl.ds(y * (length // 2), length // 2)
            grad = across(flat(grads[i, y]), out_rows[...])
            grad_heads[i, at, :] = grad.astype(grad_heads.dtype)

    def mix_back(i):
        for first in range(0, length, block):
            attend_back_block(
                i,
                size,
                block,
                first,
                q,
                k,
                k_flip,
                v,
                grad_heads,
                mixed,
                lse,
                key_seg,
                query_seg,
                q_back,
                k_sum,
                v_sum,
            )

        @pl.loop(0, 2)
        def _(y):
            at = pl.ds(y * (length // 2), length // 2)
            parts = [ref[i, at, :].astype(stack.dtype) for ref in (q_back, k_sum, v_sum)]
            for n, part in enumerate(parts):
                stack[i, y, :, :, :, pl.ds(n * take, take)] = part.reshape(
                    stack.shape[2:5] + (take,)
                )
                to = pl.ds(i * length + y * (length // 2), length // 2)
                stack_flip[pl.ds(n * take, take), to] = part.T
            q_sum[...] += jnp.sum(parts[0].astype(jnp.float32), axis=0, keepdims=True)
            v_bias_sum[...] += jnp.sum(parts[2].astype(jnp.float32), axis=0, keepdims=True)

    gather.turn()
    gather.far_start()
    gather.near_ready()
    gather.far_turn()
    heads_back(w["z"])
    mix_back(w["z"])
    gather.far_ready()
    gather.finish()
    heads_back(1 - w["z"])
    mix_back(1 - w["z"])
    wait_all(fetch)

    def product(z, y, c, cols):
        return across(flat(stack[z, y, :, c]), weight[cols, :])

    chunk = 256
    half_chunks = attend_grad.shape[1] // chunk
    attend_trade = remote(
        attend_grad.at[other], attend_got, send.at[1], recv.at[1], partner(w)
    )
    out_trade = remote(out_grad.at[other], out_got, send.at[2], recv.at[2], partner(w))

    @pl.loop(0, 2 * half_chunks)
    def _(i):
        cols = pl.ds(i * chunk, chunk)
        grad = straight(stack_flip[...], rows[:, :, :, :, :, cols].reshape(-1, chunk))
        attend_grad[i // half_chunks, pl.ds(i % half_chunks * chunk, chunk), :] = grad.astype(
            attend_grad.dtype
        ).T

    up_trade.wait()
    attend_trade.start()
    scatter.begin(product)

    @pl.loop(0, 2 * half_chunks)
    def _(i):
        cols = pl.ds(i * chunk, chunk)
        grad = straight(mixed_flip[...], grads[:, :, :, :, :, cols].reshape(-1, chunk))
        out_grad[:, :, cols] = grad.astype(out_grad.dtype).reshape(2, -1, chunk)

    scatter.second()
    scatter.third()
    scatter.fourth()
    attend_trade.wait()
    out_trade.start()
    scatter.end(back)
    out_trade.wait()


def attend_back(
    own, out_rows, q, k, v, mixed, lse, segs, rows_all, pair, up_sent, size, name, cid
):
    rows, width = own.shape
    length, take = q.shape[1:]
    low, f32 = own.dtype, jnp.float32
    vmem, anywhere = pl.BlockSpec(memory_space=pltpu.VMEM), pl.BlockSpec(memory_space=pl.ANY)
    shape, dma = jax.ShapeDtypeStruct, pltpu.SemaphoreType.DMA
    whole = (2, 2, 2, 2, rows, width)
    heads = (2, length, take)
    return pl.pallas_call(
        functools.partial(attend_back_kernel, size),
        out_shape=(
            shape((rows, width), f32),
            shape((2, take // 2, width), low),
            shape((2, width // 2, 3 * take), low),
            shape((1, take), f32),
            shape((1, take), f32),
            shape(up_sent.shape[1:], low),
            shape((take // 2, width), low),
            shape((width // 2, 3 * take), low),
        ),
        in_specs=[vmem] * 9 + [anywhere] * 3,
        out_specs=tuple([vmem] * 5 + [anywhere] * 3),
        scratch_shapes=[
            pltpu.VMEM(whole, low),
            pltpu.VMEM(whole, low),
            pltpu.VMEM((width, 3 * take), low),
            pltpu.VMEM((2, take, length), low),
            pltpu.VMEM((take, 2 * length), low),
            pltpu.VMEM(heads, low),
            pltpu.VMEM(heads, low),
            pltpu.VMEM(heads, f32),
            pltpu.VMEM(heads, f32),
            pltpu.VMEM((2, 2, 2, 2, rows, 3 * take), low),
            pltpu.VMEM((3 * take, 2 * length), low),
            *Gather.sems(),
            *Scatter.scratch(rows, width),
            dma((3,)),
            dma((3,)),
            dma((3,)),
        ],
        compiler_params=pltpu.CompilerParams(
            collective_id=cid, has_side_effects=True, vmem_limit_bytes=VMEM_BYTES
        ),
        name=name,
    )(
        own,
        out_rows,
        q,
        k,
        v,
        mixed,
        lse,
        segs[:, :, None],
        segs[:, None, :],
        rows_all,
        pair,
        up_sent,
    )


def last_kernel(size, *refs):
    refs = Refs(refs)
    attend_grad, attend_got, up_grad, up_got, letter, note = refs.take(6)
    q_rows, k_rows, v_rows, up_rows, letters, notes = refs.take(6)
    attend_parts, up_parts, swapped, low_letters = refs.take(4)
    sems = [refs.take(3) for _ in range(4)]
    (load,) = refs.take(1)
    w = place()
    mine = w["g"]
    fetch = [
        [
            pltpu.make_async_copy(ref, parts.at[i], load.at[n, i])
            for i, ref in enumerate((pair.at[mine], got))
        ]
        for n, (parts, pair, got) in enumerate(
            ((attend_parts, attend_grad, attend_got), (up_parts, up_grad, up_got))
        )
    ]
    start_all(fetch[0] + fetch[1])
    greet_world(w)
    count = attend_parts.shape[1]
    attend_mail = mail(w, SLICE_OUT, attend_parts.at[0], swapped, *sems[2])
    up_mail = mail(w, COLUMNS_OUT, up_parts.at[0], up_rows, *sems[3])
    letter_mail = mail(w, LETTERS, letter, low_letters, *sems[0])
    letter_mail += mail(w, PAIR, note, notes, *sems[1])
    for n, (parts, copies) in enumerate(((attend_parts, attend_mail), (up_parts, up_mail))):
        wait_all(fetch[n])

        @pl.loop(0, count)
        def _(i):
            total = parts[0, i].astype(jnp.float32) + parts[1, i].astype(jnp.float32)
            parts[0, i] = total.astype(parts.dtype)

        start_all(copies)
    start_all(letter_mail)
    wait_all(attend_mail)
    for n, out in enumerate((q_rows, k_rows, v_rows)):
        for high in range(2):
            for r in range(0, count, 2):
                at = high * count + (r + high * (count // 2)) % count
                lanes = pl.ds((2 * n + high) * size, size)
                both = jnp.concatenate([swapped[r, :, lanes], swapped[r + 1, :, lanes]], axis=1)
                out[:, pl.ds(at * size, 2 * size)] = both
    wait_all(letter_mail)
    letters[...] = jnp.sum(low_letters[...], axis=0)
    wait_all(up_mail)


def last(attend_grad, attend_got, up_grad, up_got, letter, note, size, name, cid):
    width = 2 * attend_got.shape[0]
    ndev = lax.axis_size("dp") * lax.axis_size("seq")
    low, f32 = up_got.dtype, jnp.float32
    vmem, anywhere = pl.BlockSpec(memory_space=pltpu.VMEM), pl.BlockSpec(memory_space=pl.ANY)
    shape, dma = jax.ShapeDtypeStruct, pltpu.SemaphoreType.DMA
    count = ndev // 2
    share = width // ndev

    def cut(x):
        return x.reshape(x.shape[:-2] + (count, share, x.shape[-1]))

    attend_grad, attend_got, up_grad, up_got = map(cut, (attend_grad, attend_got, up_grad, up_got))
    return pl.pallas_call(
        functools.partial(last_kernel, size),
        out_shape=(
            *[shape((share, width), low)] * 3,
            shape((share, count * up_got.shape[-1]), low),
            shape(letter.shape[1:], f32),
            shape((2,) + note.shape, f32),
        ),
        in_specs=[anywhere] * 6,
        out_specs=(vmem, vmem, vmem, vmem, vmem, anywhere),
        scratch_shapes=[
            pltpu.VMEM((2,) + attend_got.shape, low),
            pltpu.VMEM((2,) + up_got.shape, low),
            pltpu.VMEM(attend_got.shape, low),
            pltpu.VMEM((ndev,) + letter.shape[1:], f32),
            *mail_sems(LETTERS),
            *mail_sems(PAIR),
            *mail_sems(SLICE_OUT),
            *mail_sems(COLUMNS_OUT),
            dma((2, 2)),
        ],
        compiler_params=pltpu.CompilerParams(
            collective_id=cid, has_side_effects=True, vmem_limit_bytes=VMEM_BYTES
        ),
        name=name,
    )(attend_grad, attend_got, up_grad, up_got, letter, note)


def on_device_halves(
    tokens,
    segments,
    exit_layer,
    first_gain,
    first_shift,
    query_weight,
    query_bias,
    key_weight,
    value_weight,
    value_bias,
    output_weight,
    output_bias,
    second_gain,
    second_shift,
    up_weight,
    up_bias,
    down_weight,
    down_bias,
    cotangent,
):
    rows, width = tokens.shape[1:]
    nd, ns = lax.axis_size("dp"), lax.axis_size("seq")
    ndev = nd * ns
    size = width // HEADS
    hidden_size = up_weight.shape[1]
    take = 2 * size
    w = place()
    group = w["g"]
    low_at = w["z"] * ns + w["s"]
    high_at = (nd - 1 - w["z"]) * ns + w["s"]

    def own_half(pair):
        return lax.dynamic_index_in_dim(pair, group, 0, keepdims=False).astype(jnp.float32)

    def total(pair, got):
        return own_half(pair) + got.astype(jnp.float32)

    keep = (exit_layer > LAYER).astype(jnp.float32).reshape(rows, 1)
    inputs = tokens.astype(jnp.float32).reshape(rows, width)
    upstream = cotangent.astype(jnp.float32).reshape(rows, width)
    branch_back = (keep * upstream).astype(jnp.bfloat16)
    vector_parts = [
        first_gain,
        first_shift,
        query_bias,
        value_bias,
        output_bias,
        second_gain,
        second_shift,
        down_bias,
        up_bias,
    ]
    share = width // ndev
    letter = jnp.zeros((16, 128), jnp.bfloat16)
    at = 0
    for part in vector_parts:
        part = part.reshape(-1, share)
        count = part.shape[0]
        letter = letter + jnp.pad(part, ((at, 16 - at - count), (0, 128 - share)))
        at += count
    attend_blocks, vectors, output_rows, segs, grads_near, grad_far = first(
        (query_weight, key_weight, value_weight),
        letter,
        output_weight,
        segments.reshape(-1, 128),
        branch_back,
        size,
        "first",
        0,
    )
    output_rows = output_rows.reshape(-1, width)
    segs = segs.reshape(2, -1)
    cuts, at = [], 0
    for part in vector_parts:
        count = part.shape[0] // share
        cuts.append(vectors[:, at : at + count, :share].reshape(ndev, -1))
        at += count
    full = [cut.reshape(-1).astype(jnp.float32) for cut in cuts]
    gain_one, shift_one, _, _, output_shift, gain_two, shift_two, down_shift, _ = full

    def rank_vector(cut):
        return jnp.concatenate(
            [
                lax.dynamic_index_in_dim(cut, low_at, 0, keepdims=False),
                lax.dynamic_index_in_dim(cut, high_at, 0, keepdims=False),
            ]
        ).astype(jnp.float32)

    query_shift, value_shift, up_shift = (rank_vector(cuts[i]) for i in (2, 3, 8))
    attend_shift = jnp.concatenate([query_shift, jnp.zeros_like(query_shift), value_shift])[None]

    normed_one = layer_norm(inputs, gain_one, shift_one).astype(jnp.bfloat16)
    (
        attention,
        queries,
        keys,
        values,
        mixed,
        lse,
        normed_all,
        grads_far,
        attend_pair,
        up_pair,
        down_some,
    ) = attend(
        normed_one,
        attend_shift,
        output_rows,
        segs,
        grad_far,
        attend_blocks.reshape(-1, 3 * take),
        up_weight,
        down_weight,
        size,
        "attend",
        1,
    )
    middle = inputs + keep * (attention + output_shift)
    normed_two = layer_norm(middle, gain_two, shift_two).astype(jnp.bfloat16)
    normed_two_back, branch, up_shift_sum, down_grad, up_grad, down_got = feed(
        normed_two,
        up_shift[None],
        up_pair.reshape(width, -1),
        grads_near,
        grads_far,
        down_weight,
        down_some,
        "feed",
        2,
    )
    layer_out = (middle + keep * (branch + down_shift)).astype(jnp.bfloat16)
    norm_result, pull_two = jax.vjp(layer_norm, middle, gain_two, shift_two)
    middle_part, gain_two_sum, shift_two_sum = pull_two(normed_two_back)
    middle_back = upstream + middle_part
    attention_back = (keep * middle_back).astype(jnp.bfloat16)
    up_grad = up_grad.reshape(2, width // 2, -1)
    (
        normed_one_back,
        output_grad,
        attend_grad,
        query_sum,
        value_sum,
        up_got,
        output_got,
        attend_got,
    ) = attend_back(
        attention_back,
        output_rows,
        queries,
        keys,
        values,
        mixed,
        lse,
        segs,
        normed_all,
        attend_pair,
        up_grad,
        size,
        "attend_back",
        3,
    )
    norm_first, pull_one = jax.vjp(layer_norm, inputs, gain_one, shift_one)
    inputs_part, gain_one_sum, shift_one_sum = pull_one(normed_one_back)
    tokens_gradient = (middle_back + inputs_part).astype(jnp.bfloat16)

    def summed(value):
        return jnp.sum(value.astype(jnp.float32), axis=0)

    own_sums = [
        gain_one_sum,
        shift_one_sum,
        gain_two_sum,
        shift_two_sum,
        summed(attention_back),
        summed(branch_back),
    ]
    letter = jnp.stack([value.reshape(-1, 128) for value in own_sums], axis=1)
    letter = jnp.pad(letter, ((0, 0), (0, 2), (0, 0)))
    note = jnp.concatenate([query_sum, value_sum, up_shift_sum], axis=1)
    note = jnp.pad(note, ((0, 0), (0, -note.shape[1] % 1024))).reshape(-1, 128)
    query_rows, key_rows, value_rows, up_rows, letters, notes = last(
        attend_grad, attend_got, up_grad, up_got, letter, note, size, "last", 4
    )
    letters = lax.dynamic_slice_in_dim(letters, w["c"] * share, share, 1)
    notes = (notes[0] + notes[1]).reshape(-1)

    def own_part(at, length):
        return lax.dynamic_slice_in_dim(notes, at + group * length, length, 0)

    vector_out = [letters[i] for i in range(6)] + [
        own_part(0, size),
        own_part(take, size),
        own_part(2 * take, hidden_size // ndev),
    ]
    (
        gain_one_part,
        shift_one_part,
        gain_two_part,
        shift_two_part,
        output_shift_part,
        down_shift_part,
        query_shift_part,
        value_shift_part,
        up_shift_part,
    ) = vector_out
    return (
        layer_out.reshape(tokens.shape),
        tokens_gradient.reshape(tokens.shape),
        gain_one_part,
        shift_one_part,
        query_rows.astype(jnp.float32),
        query_shift_part,
        key_rows.astype(jnp.float32),
        value_rows.astype(jnp.float32),
        value_shift_part,
        total(output_grad, output_got),
        output_shift_part,
        gain_two_part,
        shift_two_part,
        up_rows.astype(jnp.float32),
        up_shift_part,
        total(down_grad, down_got),
        down_shift_part,
    )


def solution(mesh):
    placed = (
        P("dp", "seq", None),
        P("dp", None),
        P("dp", "seq"),
        P(("dp", "seq")),
        P(("dp", "seq")),
        P(("dp", "seq"), None),
        P(("dp", "seq")),
        P(("dp", "seq"), None),
        P(("dp", "seq"), None),
        P(("dp", "seq")),
        P(("dp", "seq"), None),
        P(("dp", "seq")),
        P(("dp", "seq")),
        P(("dp", "seq")),
        P(("dp", "seq"), None),
        P(("dp", "seq")),
        P(("dp", "seq"), None),
        P(("dp", "seq")),
        P("dp", "seq", None),
    )
    halves = mesh.shape["dp"] == 4 and mesh.shape["seq"] == 8
    return jax.shard_map(
        on_device_halves if halves else on_device,
        mesh=mesh,
        in_specs=placed,
        out_specs=(
            P("dp", "seq", None),
            P("dp", "seq", None),
            P(("dp", "seq")),
            P(("dp", "seq")),
            P(("dp", "seq"), None),
            P(("dp", "seq")),
            P(("dp", "seq"), None),
            P(("dp", "seq"), None),
            P(("dp", "seq")),
            P(("dp", "seq"), None),
            P(("dp", "seq")),
            P(("dp", "seq")),
            P(("dp", "seq")),
            P(("dp", "seq"), None),
            P(("dp", "seq")),
            P(("dp", "seq"), None),
            P(("dp", "seq")),
        ),
        check_vma=False,
    )
```

```python
import functools
import math

import jax
import jax.numpy as jnp
from jax import lax
from jax.experimental import pallas as pl
from jax.experimental.pallas import tpu as pltpu
from jax.sharding import PartitionSpec as P

HEADS = 32
LAYER = 12


EPS = 1e-05
NEG = -1e30


def activate(value):
    return jax.nn.gelu(value, approximate=True)


def layer_norm(value, gain, shift):
    mean = jnp.mean(value, axis=-1, keepdims=True)
    centred = value - mean
    spread = jnp.mean(centred * centred, axis=-1, keepdims=True)
    return centred * lax.rsqrt(spread + EPS) * gain + shift


def transposed(left, right):
    return lax.dot_general(
        left, right, (((1,), (1,)), ((), ())), preferred_element_type=jnp.float32
    )


def leading(left, right):
    return lax.dot_general(
        left, right, (((0,), (0,)), ((), ())), preferred_element_type=jnp.float32
    )


def visible(query_seg, query_pos, key_seg, key_pos):
    same = query_seg[:, :, None] == key_seg[:, None, :]
    return jnp.logical_and(same, key_pos[None, None, :] <= query_pos[None, :, None])


def by_blocks(step, carry, piece):
    length = jax.tree.leaves(piece)[0].shape[1]
    size = math.gcd(length, 128)

    def one(index, state):
        offset = index * size
        block = jax.tree.map(lambda part: lax.dynamic_slice_in_dim(part, offset, size, 1), piece)
        return step(state, block, offset)

    return lax.fori_loop(0, length // size, one, carry)


def on_device(
    tokens,
    segments,
    exit_layer,
    first_gain,
    first_shift,
    query_weight,
    query_bias,
    key_weight,
    value_weight,
    value_bias,
    output_weight,
    output_bias,
    second_gain,
    second_shift,
    up_weight,
    up_bias,
    down_weight,
    down_bias,
    cotangent,
):
    nseq, piece_len, width = tokens.shape
    head_count = HEADS
    head_size = width // head_count
    scale = head_size ** (-0.5)
    rows = nseq * piece_len
    own_first = lax.axis_index("seq") * piece_len
    own_pos = own_first + jnp.arange(piece_len, dtype=jnp.int32)
    own_seg = lax.dynamic_slice_in_dim(segments, own_first, piece_len, 1)
    keep = (exit_layer > LAYER).astype(jnp.float32).reshape(rows, 1)
    (
        gain_one,
        shift_one,
        query_full,
        query_shift,
        key_full,
        value_full,
        value_shift,
        output_full,
        output_shift,
        gain_two,
        shift_two,
        up_shift,
        down_shift,
    ) = (
        lax.all_gather(first_gain, ("dp", "seq"), axis=0, tiled=True),
        lax.all_gather(first_shift, ("dp", "seq"), axis=0, tiled=True),
        lax.all_gather(query_weight, ("dp", "seq"), axis=0, tiled=True),
        lax.all_gather(query_bias, ("dp", "seq"), axis=0, tiled=True),
        lax.all_gather(key_weight, ("dp", "seq"), axis=0, tiled=True),
        lax.all_gather(value_weight, ("dp", "seq"), axis=0, tiled=True),
        lax.all_gather(value_bias, ("dp", "seq"), axis=0, tiled=True),
        lax.all_gather(output_weight, ("dp", "seq"), axis=0, tiled=True),
        lax.all_gather(output_bias, ("dp", "seq"), axis=0, tiled=True),
        lax.all_gather(second_gain, ("dp", "seq"), axis=0, tiled=True),
        lax.all_gather(second_shift, ("dp", "seq"), axis=0, tiled=True),
        lax.all_gather(up_bias, ("dp", "seq"), axis=0, tiled=True),
        lax.all_gather(down_bias, ("dp", "seq"), axis=0, tiled=True),
    )
    gain_one = gain_one.astype(jnp.float32)
    shift_one = shift_one.astype(jnp.float32)
    gain_two = gain_two.astype(jnp.float32)
    shift_two = shift_two.astype(jnp.float32)
    inputs = tokens.astype(jnp.float32).reshape(rows, width)
    normed_one = layer_norm(inputs, gain_one, shift_one).astype(jnp.bfloat16)
    queries = (
        jnp.dot(normed_one, query_full, preferred_element_type=jnp.float32)
        + query_shift.astype(jnp.float32)
    ).astype(jnp.bfloat16)
    keys = jnp.dot(normed_one, key_full, preferred_element_type=jnp.float32).astype(jnp.bfloat16)
    values = (
        jnp.dot(normed_one, value_full, preferred_element_type=jnp.float32)
        + value_shift.astype(jnp.float32)
    ).astype(jnp.bfloat16)
    query_heads = queries.reshape(nseq, piece_len, head_count, head_size)
    key_heads = keys.reshape(nseq, piece_len, head_count, head_size)
    value_heads = values.reshape(nseq, piece_len, head_count, head_size)
    key_local = keys.reshape(nseq, piece_len, width)
    pair_local = jnp.concatenate([keys, values], axis=1).reshape(nseq, piece_len, 2 * width)

    def key_mask(start, length):
        key_pos = start + jnp.arange(length, dtype=jnp.int32)
        key_seg = lax.dynamic_slice_in_dim(segments, start, length, 1)
        return visible(own_seg, own_pos, key_seg, key_pos)[:, None]

    def local_scores(key_block):
        keyed = key_block.reshape(nseq, key_block.shape[1], head_count, head_size)
        return (
            jnp.einsum("sqhd,skhd->shqk", query_heads, keyed, preferred_element_type=jnp.float32)
            * scale
        )

    def norm_step(carry, block, start):
        top, total = carry
        allowed = key_mask(start, block.shape[1])
        scores = jnp.where(allowed, local_scores(block), NEG)
        new_top = jnp.maximum(top, jnp.max(scores, axis=-1))
        weights = jnp.where(allowed, jnp.exp(scores - new_top[..., None]), 0.0)
        return (new_top, total * jnp.exp(top - new_top) + jnp.sum(weights, axis=-1))

    start_norm = (
        jnp.full((nseq, head_count, piece_len), NEG, jnp.float32),
        jnp.zeros((nseq, head_count, piece_len), jnp.float32),
    )
    top, total = by_blocks(
        norm_step, start_norm, lax.all_gather(key_local, "seq", axis=1, tiled=True)
    )
    lse = top + jnp.log(total)

    def mix_step(acc, block, start):
        length = block.shape[1]
        allowed = key_mask(start, length)
        scores = local_scores(block[:, :, :width])
        probs = jnp.where(allowed, jnp.exp(scores - lse[..., None]), 0.0).astype(jnp.bfloat16)
        valued = block[:, :, width:].reshape(nseq, length, head_count, head_size)
        return acc + jnp.einsum(
            "shqk,skhd->sqhd", probs, valued, preferred_element_type=jnp.float32
        )

    empty_heads = jnp.zeros((nseq, piece_len, head_count, head_size), jnp.float32)
    mixed_heads = by_blocks(
        mix_step, empty_heads, lax.all_gather(pair_local, "seq", axis=1, tiled=True)
    )
    mixed = mixed_heads.reshape(rows, width).astype(jnp.bfloat16)
    attention = jnp.dot(
        mixed, output_full, preferred_element_type=jnp.float32
    ) + output_shift.astype(jnp.float32)
    middle = inputs + keep * attention
    normed_two = layer_norm(middle, gain_two, shift_two).astype(jnp.bfloat16)
    columns = normed_two
    before = jnp.dot(
        columns,
        lax.all_gather(up_weight, ("dp", "seq"), axis=0, tiled=True),
        preferred_element_type=jnp.float32,
    )
    pre_active = before + up_shift.astype(jnp.float32)
    hidden = activate(pre_active).astype(jnp.bfloat16)
    columns = hidden
    branch = jnp.dot(
        columns,
        lax.all_gather(down_weight, ("dp", "seq"), axis=0, tiled=True),
        preferred_element_type=jnp.float32,
    )
    branch = branch + down_shift.astype(jnp.float32)
    layer_out = (middle + keep * branch).astype(jnp.bfloat16).reshape(nseq, piece_len, width)
    upstream = cotangent.astype(jnp.float32).reshape(rows, width)
    branch_back = (keep * upstream).astype(jnp.bfloat16)
    down_shift_sum = jnp.sum(branch_back.astype(jnp.float32), axis=0)
    hidden_back = transposed(
        branch_back, lax.all_gather(down_weight, ("dp", "seq"), axis=0, tiled=True)
    )
    active_value, pull_active = jax.vjp(activate, pre_active)
    pre_back = pull_active(hidden_back)[0].astype(jnp.bfloat16)
    up_shift_sum = jnp.sum(pre_back.astype(jnp.float32), axis=0)
    down_gradient = lax.psum_scatter(
        leading(hidden, branch_back), ("dp", "seq"), scatter_dimension=0, tiled=True
    )
    normed_two_back = transposed(
        pre_back, lax.all_gather(up_weight, ("dp", "seq"), axis=0, tiled=True)
    )
    norm_result, pull_two = jax.vjp(layer_norm, middle, gain_two, shift_two)
    middle_part, gain_two_sum, shift_two_sum = pull_two(normed_two_back)
    middle_back = upstream + middle_part
    attention_back = (keep * middle_back).astype(jnp.bfloat16)
    output_shift_sum = jnp.sum(attention_back.astype(jnp.float32), axis=0)
    mixed_back = transposed(attention_back, output_full).astype(jnp.bfloat16)
    mixed_heads_back = mixed_back.reshape(nseq, piece_len, head_count, head_size)
    delta_rows = jnp.sum(mixed_heads_back.astype(jnp.float32) * mixed_heads, axis=-1)
    delta = delta_rows.transpose(0, 2, 1)
    lse_rows = lse.transpose(0, 2, 1)

    def query_step(acc, block, start):
        length = block.shape[1]
        allowed = key_mask(start, length)
        scores = local_scores(block[:, :, :width])
        probs = jnp.where(allowed, jnp.exp(scores - lse[..., None]), 0.0)
        valued = block[:, :, width:].reshape(nseq, length, head_count, head_size)
        keyed = block[:, :, :width].reshape(nseq, length, head_count, head_size)
        prob_back = jnp.einsum(
            "sqhd,skhd->shqk", mixed_heads_back, valued, preferred_element_type=jnp.float32
        )
        score_back = (probs * (prob_back - delta[..., None])).astype(jnp.bfloat16)
        return acc + jnp.einsum(
            "shqk,skhd->sqhd", score_back, keyed, preferred_element_type=jnp.float32
        )

    query_sum = by_blocks(
        query_step, empty_heads, lax.all_gather(pair_local, "seq", axis=1, tiled=True)
    )
    queries_back = (query_sum * scale).reshape(rows, width).astype(jnp.bfloat16)

    def key_step(carry, block, start):
        key_acc, value_acc = carry
        query_block, back_block, norm_block, delta_block = block
        length = query_block.shape[1]
        query_pos = start + jnp.arange(length, dtype=jnp.int32)
        query_seg = lax.dynamic_slice_in_dim(segments, start, length, 1)
        allowed = visible(query_seg, query_pos, own_seg, own_pos)[:, None]
        remote_query = query_block.astype(jnp.bfloat16).reshape(nseq, length, head_count, head_size)
        remote_back = back_block.astype(jnp.bfloat16).reshape(nseq, length, head_count, head_size)
        scores = (
            jnp.einsum(
                "sqhd,skhd->shqk", remote_query, key_heads, preferred_element_type=jnp.float32
            )
            * scale
        )
        probs = jnp.where(allowed, jnp.exp(scores - norm_block.transpose(0, 2, 1)[..., None]), 0.0)
        value_acc = value_acc + jnp.einsum(
            "shqk,sqhd->skhd",
            probs.astype(jnp.bfloat16),
            remote_back,
            preferred_element_type=jnp.float32,
        )
        prob_back = jnp.einsum(
            "sqhd,skhd->shqk", remote_back, value_heads, preferred_element_type=jnp.float32
        )
        score_back = (probs * (prob_back - delta_block.transpose(0, 2, 1)[..., None])).astype(
            jnp.bfloat16
        )
        key_acc = key_acc + jnp.einsum(
            "shqk,sqhd->skhd", score_back, remote_query, preferred_element_type=jnp.float32
        )
        return (key_acc, value_acc)

    query_send = queries.astype(jnp.float32).reshape(nseq, piece_len, width)
    back_send = mixed_back.astype(jnp.float32).reshape(nseq, piece_len, width)
    key_sum, value_sum = by_blocks(
        key_step,
        (empty_heads, empty_heads),
        (
            lax.all_gather(query_send.astype(jnp.bfloat16), "seq", axis=1, tiled=True).astype(
                jnp.float32
            ),
            lax.all_gather(back_send.astype(jnp.bfloat16), "seq", axis=1, tiled=True).astype(
                jnp.float32
            ),
            lax.all_gather(lse_rows.astype(jnp.bfloat16), "seq", axis=1, tiled=True).astype(
                jnp.float32
            ),
            lax.all_gather(delta_rows.astype(jnp.bfloat16), "seq", axis=1, tiled=True).astype(
                jnp.float32
            ),
        ),
    )
    keys_back = (key_sum * scale).reshape(rows, width).astype(jnp.bfloat16)
    values_back = value_sum.reshape(rows, width).astype(jnp.bfloat16)
    query_shift_sum = jnp.sum(queries_back.astype(jnp.float32), axis=0)
    value_shift_sum = jnp.sum(values_back.astype(jnp.float32), axis=0)
    normed_one_back = (
        transposed(queries_back, query_full)
        + transposed(keys_back, key_full)
        + transposed(values_back, value_full)
    )
    norm_first, pull_one = jax.vjp(layer_norm, inputs, gain_one, shift_one)
    inputs_part, gain_one_sum, shift_one_sum = pull_one(normed_one_back)
    tokens_gradient = (
        (middle_back + inputs_part).astype(jnp.bfloat16).reshape(nseq, piece_len, width)
    )
    stacked_back = jnp.concatenate([queries_back, keys_back, values_back], axis=1)
    row_gradient = lax.psum_scatter(
        jnp.concatenate(
            [
                leading(normed_one, stacked_back),
                leading(mixed, attention_back),
                leading(normed_two, pre_back),
            ],
            axis=1,
        ),
        ("dp", "seq"),
        scatter_dimension=0,
        tiled=True,
    )
    (
        gain_one_part,
        shift_one_part,
        query_shift_part,
        value_shift_part,
        output_shift_part,
        gain_two_part,
        shift_two_part,
        up_shift_part,
        down_shift_part,
    ) = (
        lax.psum_scatter(gain_one_sum, ("dp", "seq"), scatter_dimension=0, tiled=True),
        lax.psum_scatter(shift_one_sum, ("dp", "seq"), scatter_dimension=0, tiled=True),
        lax.psum_scatter(query_shift_sum, ("dp", "seq"), scatter_dimension=0, tiled=True),
        lax.psum_scatter(value_shift_sum, ("dp", "seq"), scatter_dimension=0, tiled=True),
        lax.psum_scatter(output_shift_sum, ("dp", "seq"), scatter_dimension=0, tiled=True),
        lax.psum_scatter(gain_two_sum, ("dp", "seq"), scatter_dimension=0, tiled=True),
        lax.psum_scatter(shift_two_sum, ("dp", "seq"), scatter_dimension=0, tiled=True),
        lax.psum_scatter(up_shift_sum, ("dp", "seq"), scatter_dimension=0, tiled=True),
        lax.psum_scatter(down_shift_sum, ("dp", "seq"), scatter_dimension=0, tiled=True),
    )
    return (
        layer_out,
        tokens_gradient,
        gain_one_part,
        shift_one_part,
        row_gradient[:, :width],
        query_shift_part,
        row_gradient[:, width : 2 * width],
        row_gradient[:, 2 * width : 3 * width],
        value_shift_part,
        row_gradient[:, 3 * width : 4 * width],
        output_shift_part,
        gain_two_part,
        shift_two_part,
        row_gradient[:, 4 * width :],
        up_shift_part,
        down_gradient,
        down_shift_part,
    )


MESH = pl.DeviceIdType.MESH
CANON = "zyx"
TURNS = ("xy", "yx")
SLICE_IN, SLICE_OUT, COLUMNS_IN, COLUMNS_OUT, LETTERS, SPREAD, PAIR, NEAR = range(8)
VMEM_BYTES = 60 << 20


def place():
    d, s = lax.axis_index("dp"), lax.axis_index("seq")
    half = lax.axis_size("dp") // 2
    far = d // half
    z = d + far * (2 * half - 1 - 2 * d)
    return dict(d=d, s=s, g=far, z=z, y=s // 4, x=(s // 2) % 2, c=s % 2)


def beside(w, dim):
    if dim == "z":
        return (w["d"] + 1 - 2 * (w["d"] % 2), w["s"])
    step = {"c": 1, "x": 2, "y": 4}[dim]
    return (w["d"], w["s"] + step * (1 - 2 * w[dim]))


def partner(w):
    return (lax.axis_size("dp") - 1 - w["d"], w["s"])


def peer(w, r):
    n = lax.axis_size("seq")
    e, s = r // n, r % n
    return (e + w["g"] * (lax.axis_size("dp") - 1 - 2 * e), s)


def row_block(w, r):
    n = lax.axis_size("seq")
    e, s = r // n, r % n
    return (e + w["g"] * (1 - 2 * e)) * n + s


def anyone(i):
    n = lax.axis_size("seq")
    return (i // n, i % n)


def half_peers(w):
    count = lax.axis_size("dp") * lax.axis_size("seq") // 2
    me = w["z"] * lax.axis_size("seq") + w["s"]
    return me, [(me + k) % count for k in range(1, count)]


def world_peers(w):
    count = lax.axis_size("dp") * lax.axis_size("seq")
    me = w["d"] * lax.axis_size("seq") + w["s"]
    return me, [(me + k) % count for k in range(1, count)]


def greet(ids):
    bar = pltpu.get_barrier_semaphore()
    for i in ids:
        pl.semaphore_signal(bar, inc=1, device_id=i, device_id_type=MESH)
    pl.semaphore_wait(bar, len(ids))


def greet_half(w):
    greet([peer(w, r) for r in half_peers(w)[1]] + [partner(w)])


def greet_world(w):
    greet([anyone(i) for i in world_peers(w)[1]])


def remote(src, dst, send, recv, device):
    return pltpu.make_async_remote_copy(
        src_ref=src,
        dst_ref=dst,
        send_sem=send,
        recv_sem=recv,
        device_id=device,
        device_id_type=MESH,
    )


def twice(w, r, size):
    count = lax.axis_size("dp") * lax.axis_size("seq") // 2
    other = count + (r + count // 2) % count
    return [pl.ds(pl.multiple_of(at * size, size), size) for at in (r, other)]


def mail(w, kind, src, out, send, recv, local):
    mine = None
    if kind == SLICE_IN:
        me, others = half_peers(w)
        to = out.at[row_block(w, me)]
        todo = [(src.at[r], to, peer(w, r)) for r in others]
        mine = [(src.at[me], to)]
    elif kind == SLICE_OUT:
        me, others = half_peers(w)
        to = out.at[me]
        todo = [(src.at[row_block(w, r)], to, peer(w, r)) for r in others]
        mine = [(src.at[row_block(w, me)], to)]
    elif kind == COLUMNS_IN:
        me, others = half_peers(w)
        size = out.shape[2] // 2
        to = [out.at[row_block(w, me), :, pl.ds(n * size, size)] for n in range(2)]
        todo = [
            (src.at[:, cols], to[n], peer(w, r))
            for r in others
            for n, cols in enumerate(twice(w, r, size))
        ]
        mine = [(src.at[:, cols], to[n]) for n, cols in enumerate(twice(w, me, size))]
    elif kind == COLUMNS_OUT:
        me, others = half_peers(w)
        size = src.shape[2] // 2
        to = [out.at[:, cols] for cols in twice(w, me, size)]
        todo = [
            (src.at[row_block(w, r), :, pl.ds(n * size, size)], to[n], peer(w, r))
            for r in others
            for n in range(2)
        ]
        mine = [
            (src.at[row_block(w, me), :, pl.ds(n * size, size)], to[n]) for n in range(2)
        ]
    elif kind == LETTERS:
        me, others = world_peers(w)
        to = out.at[me]
        todo = [(src.at[i // 2], to, anyone(i)) for i in others]
        mine = [(src.at[me // 2], to)]
    elif kind == SPREAD:
        me, others = world_peers(w)
        to = out.at[me]
        todo = [(src, to, anyone(i)) for i in others]
        mine = [(src, to)]
    elif kind == PAIR:
        to = out.at[w["g"]]
        todo = [(src, to, partner(w))]
        mine = [(src, to)]
    else:
        to = out.at[w["z"]]
        todo = [(src, to, beside(w, "z"))]
        mine = [(src, to)]
    copies = [
        remote(part, to, send.at[k], recv.at[k], device)
        for k, (part, to, device) in enumerate(todo)
    ]
    return copies + [
        pltpu.make_async_copy(part, to, local.at[k]) for k, (part, to) in enumerate(mine)
    ]


def start_all(copies):
    for cp in copies:
        cp.start()


def wait_all(copies):
    for cp in copies:
        cp.wait()


def mail_sems(kind):
    count = lax.axis_size("dp") * lax.axis_size("seq")
    half = count // 2 - 1
    n = {
        SLICE_IN: half,
        SLICE_OUT: half,
        COLUMNS_IN: 2 * half,
        COLUMNS_OUT: 2 * half,
        LETTERS: count - 1,
        SPREAD: count - 1,
    }.get(kind, 1)
    dma = pltpu.SemaphoreType.DMA
    return [dma((n,)), dma((n,)), dma((2,))]


def box(w, **where):
    pick = {"other": lambda q: 1 - w[q], "both": lambda q: pl.ds(0, 2)}
    return tuple(pick[where[q]](q) if q in where else w[q] for q in CANON)


def halves(width):
    return [pl.ds(0, width // 2), pl.ds(width // 2, width // 2)]


class PlaneGather:
    def __init__(self, w, src, out, send, recv, side_send, side_recv, local):
        self.w, self.src, self.out = w, src, out
        self.send, self.recv, self.side_send, self.side_recv = send, recv, side_send, side_recv
        self.parts = halves(out.shape[-1])
        self.own = (w["y"], w["x"], w["c"])
        self.keep = None if src is None else pltpu.make_async_copy(src, out.at[self.own], local)
        self.links, self.sides = {}, []

    @staticmethod
    def sems():
        dma = pltpu.SemaphoreType.DMA
        return [dma((4,)), dma((4,)), dma((5,)), dma((5,)), dma]

    def push(self, p, k, src, dst):
        n = 2 * p + k
        cp = remote(src, dst, self.send.at[n], self.recv.at[n], beside(self.w, TURNS[p][k]))
        cp.start()
        self.links[p, k] = cp

    def over(self, src, dst):
        n = len(self.sides)
        cp = remote(src, dst, self.side_send.at[n], self.side_recv.at[n], beside(self.w, "c"))
        cp.start()
        self.sides.append(cp)

    def blocks(self, cols, **where):
        return self.out.at[box(self.w, **where)[1:] + (self.w["c"], slice(None), cols)]

    def start(self, before=lambda p: None):
        for p, cols in enumerate(self.parts):
            before(p)
            dst = self.out.at[self.own + (slice(None), cols)]
            self.push(p, 0, dst if self.src is None else self.src.at[:, cols], dst)
        dst = self.out.at[self.own]
        if self.keep is not None:
            self.keep.start()
        self.over(dst if self.src is None else self.src, dst)

    def turn(self):
        if self.keep is not None:
            self.keep.wait()
        for p, cols in enumerate(self.parts):
            a, b = TURNS[p]
            self.links[p, 0].wait_recv()
            held = self.blocks(cols, **{a: "both"})
            self.push(p, 1, held, held)
            new = self.blocks(cols, **{a: "other"})
            self.over(new, new)

    def land(self):
        for p, cols in enumerate(self.parts):
            a, b = TURNS[p]
            self.links[p, 1].wait_recv()
            new = self.blocks(cols, **{a: "both", b: "other"})
            self.over(new, new)

    def ready(self):
        for cp in self.sides:
            cp.wait_recv()

    def finish(self):
        for cp in list(self.links.values()) + self.sides:
            cp.wait_send()


class Gather:
    def __init__(self, w, src, out, *sems):
        self.w, self.src, self.out = w, src, out
        self.near = PlaneGather(w, src, out.at[w["z"]], *sems[:5])
        self.far = PlaneGather(w, None, out.at[1 - w["z"]], *sems[5:10])
        self.cross = []
        for p, cols in enumerate(halves(src.shape[1])):
            dst = out.at[box(w) + (w["c"], slice(None), cols)]
            self.cross.append(
                remote(src.at[:, cols], dst, sems[10].at[p], sems[11].at[p], beside(w, "z"))
            )

    @staticmethod
    def sems():
        dma = pltpu.SemaphoreType.DMA
        return [*PlaneGather.sems(), *PlaneGather.sems(), dma((2,)), dma((2,))]

    def start(self):
        self.near.start()
        start_all(self.cross)

    def turn(self):
        self.near.turn()

    def far_start(self):
        self.far.start(lambda p: self.cross[p].wait_recv())

    def near_ready(self):
        self.near.land()
        self.near.ready()

    def far_turn(self):
        self.far.turn()

    def far_ready(self):
        self.far.land()
        self.far.ready()

    def finish(self):
        self.near.finish()
        self.far.finish()
        for cp in self.cross:
            cp.wait_send()


class Scatter:
    def __init__(self, w, acc, away, side, land_two, land_one, land_z, send, recv, side_send, side_recv):
        self.w, self.acc, self.away, self.side = w, acc, away, side
        self.land_two, self.land_one, self.land_z = land_two, land_one, land_z
        self.send, self.recv, self.side_send, self.side_recv = send, recv, side_send, side_recv
        self.parts = halves(acc.shape[-1])
        self.links, self.sides = {}, {}

    @staticmethod
    def scratch(rows, width, wholes=3):
        whole = pltpu.VMEM((2, 2, 2, rows, width), jnp.bfloat16)
        dma = pltpu.SemaphoreType.DMA
        return [whole] * wholes + [
            pltpu.VMEM((2, 2, 2, rows, width // 2), jnp.bfloat16),
            pltpu.VMEM((2, 2, rows, width // 2), jnp.bfloat16),
            pltpu.VMEM((2, rows, width // 2), jnp.bfloat16),
            dma((10,)),
            dma((10,)),
            dma((4,)),
            dma((4,)),
        ]

    def plane(self, group):
        return 1 - self.w["z"] if group else self.w["z"]

    def produce(self, group, p, product):
        w, cols, z = self.w, self.parts[p], self.plane(group)
        rows = self.acc.shape[3]

        def fill(out, core):
            @pl.loop(0, 2)
            def _(y):
                block = product(z, y, core, cols)
                out[z, y, :, :, cols] = block.astype(out.dtype).reshape(2, rows, -1)

        fill(self.away, 1 - w["c"])
        at = (z, pl.ds(0, 2), pl.ds(0, 2), slice(None), cols)
        n = len(self.sides)
        cp = remote(
            self.away.at[at],
            self.side.at[at],
            self.side_send.at[n],
            self.side_recv.at[n],
            beside(w, "c"),
        )
        cp.start()
        self.sides[group, p] = cp
        fill(self.acc, w["c"])

    def push(self, key, dim, src, dst):
        n = len(self.links)
        cp = remote(src, dst, self.send.at[n], self.recv.at[n], beside(self.w, dim))
        cp.start()
        self.links[key] = cp

    def at(self, group, **where):
        index = box(self.w, **where)
        return (self.plane(group),) + index[1:]

    def add(self, at, got, cols):
        at = at + (slice(None), cols)
        total = self.acc[at].astype(jnp.float32) + got.astype(jnp.float32)
        self.acc[at] = total.astype(self.acc.dtype)

    def fold(self, group, p):
        cols, (b, a) = self.parts[p], TURNS[p]
        self.sides[group, p].wait_recv()

        def add(other):
            @pl.loop(0, 2)
            def _(i):
                here = dict(self.w)
                here[b] = i
                if other:
                    here[a] = 1 - self.w[a]
                at = (self.plane(group), here["y"], here["x"])
                self.add(at, self.side[at + (slice(None), cols)], cols)

        add(True)
        src = self.acc.at[self.at(group, **{a: "other", b: "both"}) + (slice(None), cols)]
        self.push((group, p, 0), a, src, self.land_two.at[group, p])
        add(False)

    def middle(self, group, p):
        w, cols, (b, a) = self.w, self.parts[p], TURNS[p]
        self.links[group, p, 0].wait_recv()
        there = self.at(group, **{b: "other"})
        self.add(there, self.land_two[group, p, 1 - w[b]], cols)
        src = self.acc.at[there + (slice(None), cols)]
        self.push((group, p, 1), b, src, self.land_one.at[group, p])
        self.add(self.at(group), self.land_two[group, p, w[b]], cols)

    def cross(self, p):
        cols = self.parts[p]
        self.links[1, p, 1].wait_recv()
        at = self.at(1)
        self.add(at, self.land_one[1, p], cols)
        self.push(("z", p), "z", self.acc.at[at + (slice(None), cols)], self.land_z.at[p])

    def finish(self, p, out):
        cols = self.parts[p]
        self.links[0, p, 1].wait_recv()
        self.links["z", p].wait_recv()
        total = self.acc[self.at(0) + (slice(None), cols)].astype(jnp.float32)
        total += self.land_one[0, p].astype(jnp.float32)
        out[:, cols] = total + self.land_z[p].astype(jnp.float32)

    def begin(self, product):
        self.produce(1, 0, product)
        self.produce(1, 1, product)
        self.fold(1, 0)
        self.fold(1, 1)
        self.produce(0, 0, product)
        self.produce(0, 1, product)

    def second(self):
        self.middle(1, 0)
        self.middle(1, 1)
        self.fold(0, 0)
        self.fold(0, 1)

    def third(self):
        self.cross(0)
        self.cross(1)

    def fourth(self):
        self.middle(0, 0)
        self.middle(0, 1)

    def end(self, out):
        self.finish(0, out)
        self.finish(1, out)
        for cp in list(self.links.values()) + list(self.sides.values()):
            cp.wait_send()


def across(left, right):
    return lax.dot_general(
        left, right, (((1,), (1,)), ((), ())), preferred_element_type=jnp.float32
    )


def straight(left, right):
    return jnp.dot(left, right, preferred_element_type=jnp.float32)


def flat(block):
    return block.reshape(-1, block.shape[-1])


def head_lanes(width, head, size):
    lane = lax.broadcasted_iota(jnp.int32, (1, width), 1)
    return jnp.logical_and(lane >= head * size, lane < (head + 1) * size)


def used_pairs(key_seg, query_seg, first, length, block):
    key_pos = lax.broadcasted_iota(jnp.int32, (length, 1), 0)
    query_pos = first + lax.broadcasted_iota(jnp.int32, (1, block), 1)
    return jnp.logical_and(key_seg == query_seg, key_pos <= query_pos)


def attend_block(i, size, block, first, q, k, v_flip, key_seg, query_seg, mixed, mixed_low, lse):
    width = q.shape[2]
    upto, rows = first + block, pl.ds(first, block)
    allowed = used_pairs(key_seg[i, pl.ds(0, upto), :], query_seg[i, :, rows], first, upto, block)
    keys = k[i, pl.ds(0, upto), :]
    query = q[i, rows, :] * jnp.asarray(size**-0.5, q.dtype)
    parts = []
    for head in range(width // size):
        own = jnp.where(head_lanes(width, head, size), query, jnp.zeros_like(query))
        scores = jnp.where(allowed, across(keys, own), NEG)
        top = jnp.max(scores, axis=0, keepdims=True)
        weights = jnp.exp(scores - top)
        total = jnp.sum(weights, axis=0, keepdims=True)
        lse[i, pl.ds(head, 1), rows] = top + jnp.log(total)
        probs = (weights * (1.0 / total)).astype(q.dtype)
        parts.append(straight(v_flip[i, pl.ds(head * size, size), pl.ds(0, upto)], probs))
    full = jnp.concatenate(parts, axis=0).T
    mixed[i, rows, :] = full
    at = first // block
    mixed_low[i, at // 2, at % 2] = full.astype(mixed_low.dtype).reshape(mixed_low.shape[3:])


def attend_back_block(
    i, size, block, first, q, k, k_flip, v, back, mixed, lse, key_seg, query_seg, q_back, k_sum, v_sum
):
    width = q.shape[2]
    upto, rows = first + block, pl.ds(first, block)
    before = pl.ds(0, upto)
    scale = size**-0.5
    allowed = used_pairs(key_seg[i, before, :], query_seg[i, :, rows], first, upto, block)
    keys, values = k[i, before, :], v[i, before, :]
    query = q[i, rows, :] * jnp.asarray(scale, q.dtype)
    grad = back[i, rows, :]
    product = (grad.astype(jnp.float32) * mixed[i, rows, :]).T
    parts = []
    for head in range(width // size):
        lanes = head_lanes(width, head, size)
        own = jnp.where(lanes, query, jnp.zeros_like(query))
        own_grad = jnp.where(lanes, grad, jnp.zeros_like(grad))
        delta = jnp.sum(product[head * size : (head + 1) * size, :], axis=0, keepdims=True)
        scores = across(keys, own) - lse[i, pl.ds(head, 1), rows]
        probs = jnp.exp(jnp.where(allowed, scores, NEG))
        score_back = (probs * (across(values, own_grad) - delta)).astype(q.dtype)
        v_sum[i, before, :] += straight(probs.astype(q.dtype), own_grad)
        k_sum[i, before, :] += straight(score_back, own)
        parts.append(straight(k_flip[i, pl.ds(head * size, size), before], score_back))
    q_back[i, rows, :] = (jnp.concatenate(parts, axis=0).T * scale).astype(q_back.dtype)


class Refs:
    def __init__(self, refs):
        self.refs, self.used = refs, 0

    def take(self, count):
        self.used += count
        return self.refs[self.used - count : self.used]


def front_kernel(size, *refs):
    refs = Refs(refs)
    weights, (up, tokens, grad) = refs.take(3), refs.take(3)
    letter, out_own, segs, down = refs.take(4)
    attention, q, k, v, mixed, lse, key_seg, query_seg, letters, out_pair = refs.take(10)
    rows_all, grads_near, grads_far, pair, ups, downs = refs.take(6)
    pieces, blocks, columns, normed, vectors, near_segs = refs.take(6)
    rows, near_plane, far_plane, weight, v_flip, mixed_low = refs.take(6)
    one, two, three = refs.take(12), refs.take(5), refs.take(5)
    sums = refs.take(10)
    letter_sems, block_sems, seg_sems, out_sems, column_sems = [refs.take(3) for _ in range(5)]
    pair_sems, up_sems, down_sems, late_sems = [refs.take(3) for _ in range(4)]
    cross_send, cross_recv, load, flush = refs.take(4)
    w = place()
    length, take = q.shape[1:]
    block = length // 4
    width = tokens.shape[1]
    share = size
    greet_world(w)
    letter_mail = mail(w, SPREAD, letter, letters, *letter_sems)
    start_all(letter_mail)
    count = pieces.shape[0]
    for r in range(count):
        places = (r, count + (r + count // 2) % count)
        pieces[r] = jnp.concatenate(
            [ref[:, pl.ds(at * size, size)] for ref in weights for at in places], axis=1
        )
    block_mail = mail(w, SLICE_IN, pieces, blocks, *block_sems)
    start_all(block_mail)
    some = downs.shape[1] // 2
    down_parts = [
        mail(w, PAIR, down.at[part], downs.at[pl.ds(0, 2), part], *sems)
        for part, sems in ((pl.ds(0, some), down_sems), (pl.ds(some, some), late_sems))
    ]
    column_mail = mail(w, COLUMNS_IN, up, columns, *column_sems)
    start_all(column_mail)
    out_mail = mail(w, PAIR, out_own, out_pair, *out_sems)
    first = PlaneGather(w, grad, near_plane, *two)
    cross = remote(
        grad, far_plane.at[w["y"], w["x"], w["c"]], cross_send, cross_recv, beside(w, "z")
    )
    seg_mail = mail(w, NEAR, segs, near_segs, *seg_sems)
    start_all(seg_mail)
    value = tokens[...].astype(jnp.float32)
    centred = value - jnp.mean(value, axis=-1, keepdims=True)
    spread = jnp.mean(centred * centred, axis=-1, keepdims=True)
    centred = centred * lax.rsqrt(spread + EPS)
    wait_all(letter_mail)
    for n in range(2):
        for i in range(0, letters.shape[0], 2):
            vectors[pl.ds(n, 1), pl.ds(i * share, 2 * share)] = jnp.concatenate(
                [letters[j, pl.ds(n, 1), pl.ds(0, share)] for j in (i, i + 1)], axis=1
            ).astype(jnp.float32)
    normed[...] = (centred * vectors[pl.ds(0, 1), :] + vectors[pl.ds(1, 1), :]).astype(normed.dtype)
    gather = Gather(w, normed, rows, *one)
    second = PlaneGather(w, None, far_plane, *three)
    scatter = Scatter(w, *sums)
    gather.start()
    wait_all(block_mail)
    pair_mail = mail(w, PAIR, blocks, weight, *pair_sems)
    start_all(pair_mail)
    gather.turn()
    gather.far_start()
    gather.near_ready()
    gather.far_turn()
    first.start()
    cross.start()
    wait_all(seg_mail)
    for i in range(2):
        flipped = near_segs[i].T
        for n in range(near_segs.shape[1]):
            at = pl.ds(n * 128, 128)
            query_seg[i, :, at] = near_segs[i, pl.ds(n, 1), :]
            key_seg[i, at, :] = flipped[:, n : n + 1]
    count = lax.axis_size("dp") * lax.axis_size("seq")
    low_at = w["z"] * lax.axis_size("seq") + w["s"]
    high_at = (lax.axis_size("dp") - 1 - w["z"]) * lax.axis_size("seq") + w["s"]
    q_shift, v_shift = [
        jnp.concatenate(
            [letters[at, pl.ds(n, 1), pl.ds(0, share)] for at in (low_at, high_at)], axis=1
        ).astype(jnp.float32)
        for n in (2, 3)
    ]
    shift = jnp.concatenate([q_shift, jnp.zeros_like(q_shift), v_shift], axis=1)
    wait_all(column_mail)
    wait_all(pair_mail)
    up_mail = mail(w, PAIR, columns, ups, *up_sems)
    start_all(out_mail + up_mail)
    keep_pair = pltpu.make_async_copy(weight, pair, load)
    keep_pair.start()

    def project(i):
        @pl.loop(0, 2)
        def _(y):
            block = straight(flat(rows[i, y]), weight[...].reshape(width, -1)) + shift
            at = pl.ds(y * (length // 2), length // 2)
            for ref, n in ((q, 0), (k, 1), (v, 2)):
                ref[i, at, :] = block[:, n * take : (n + 1) * take].astype(ref.dtype)
            v_flip[i, :, at] = block[:, 2 * take :].astype(v_flip.dtype).T

    def mix(i):
        for first in range(0, length, block):
            attend_block(
                i, size, block, first, q, k, v_flip, key_seg, query_seg, mixed, mixed_low, lse
            )

    project(w["z"])
    gather.far_ready()
    gather.finish()
    keep_rows = pltpu.make_async_copy(rows, rows_all, flush.at[0])
    keep_rows.start()
    first.turn()
    mix(w["z"])
    first.land()
    cross.wait()
    second.start()
    project(1 - w["z"])
    mix(1 - w["z"])
    first.ready()
    keep_near = pltpu.make_async_copy(near_plane, grads_near, flush.at[2])
    keep_near.start()
    wait_all(out_mail)

    def product(z, y, c, cols):
        return straight(
            flat(mixed_low[z, y, :, c]), jnp.concatenate([out_pair[0, :, cols], out_pair[1, :, cols]])
        )

    second.turn()
    scatter.begin(product)
    scatter.second()
    second.land()
    wait_all(up_mail)
    start_all(down_parts[0] + down_parts[1])
    second.ready()
    keep_far = pltpu.make_async_copy(far_plane, grads_far, flush.at[1])
    keep_far.start()
    scatter.third()
    scatter.fourth()
    scatter.end(attention)
    first.finish()
    second.finish()
    wait_all(down_parts[0] + down_parts[1])
    keep_rows.wait()
    keep_near.wait()
    keep_far.wait()
    keep_pair.wait()


def front(weights, up, tokens, grad, letter, out_own, segs, down, size, early, name, cid):
    rows, width = tokens.shape
    ns = lax.axis_size("seq")
    ndev = lax.axis_size("dp") * ns
    length = rows * ns
    take = 2 * size
    low, f32 = tokens.dtype, jnp.float32
    vmem, anywhere = pl.BlockSpec(memory_space=pltpu.VMEM), pl.BlockSpec(memory_space=pl.ANY)
    shape, dma = jax.ShapeDtypeStruct, pltpu.SemaphoreType.DMA
    plane = (2, 2, 2, rows, width)
    share = weights[0].shape[0]
    blocks = (ndev // 2, share, 3 * take)
    columns = (ndev // 2, share, 2 * up.shape[1] // ndev)
    return pl.pallas_call(
        functools.partial(front_kernel, size),
        out_shape=(
            shape((rows, width), f32),
            *[shape((2, length, take), low)] * 3,
            shape((2, length, take), f32),
            shape((2, take // size, length), f32),
            shape((2, length, 1), segs.dtype),
            shape((2, 1, length), segs.dtype),
            shape((ndev,) + letter.shape, low),
            shape((2,) + out_own.shape, low),
            shape((2,) + plane, low),
            shape(plane, low),
            shape(plane, low),
            shape((2,) + blocks, low),
            shape((2,) + columns, low),
            shape((2, early, width), low),
        ),
        in_specs=[vmem] * 6 + [anywhere] * 4,
        out_specs=tuple([vmem] * 10 + [anywhere] * 6),
        scratch_shapes=[
            pltpu.VMEM(blocks, low),
            pltpu.VMEM(blocks, low),
            pltpu.VMEM(columns, low),
            pltpu.VMEM((rows, width), low),
            pltpu.VMEM((2, width), f32),
            pltpu.VMEM((2,) + segs.shape, segs.dtype),
            pltpu.VMEM((2,) + plane, low),
            pltpu.VMEM(plane, low),
            pltpu.VMEM(plane, low),
            pltpu.VMEM((2,) + blocks, low),
            pltpu.VMEM((2, take, length), low),
            pltpu.VMEM((2, 2, 2, 2, rows, take), low),
            *Gather.sems(),
            *PlaneGather.sems(),
            *PlaneGather.sems(),
            *Scatter.scratch(rows, width),
            *mail_sems(SPREAD),
            *mail_sems(SLICE_IN),
            *mail_sems(NEAR),
            *mail_sems(PAIR),
            *mail_sems(COLUMNS_IN),
            *mail_sems(PAIR),
            *mail_sems(PAIR),
            *mail_sems(PAIR),
            *mail_sems(PAIR),
            dma,
            dma,
            dma,
            dma((3,)),
        ],
        compiler_params=pltpu.CompilerParams(
            collective_id=cid, has_side_effects=True, vmem_limit_bytes=VMEM_BYTES
        ),
        name=name,
    )(*weights, up, tokens, grad, letter, out_own, segs, down)


def feed_kernel(*refs):
    refs = Refs(refs)
    own, shift, ups, grads_near, grads_far, downs, down_some = refs.take(7)
    back, branch, shift_sum, down_grad, up_grad, down_got = refs.take(6)
    rows, grads, up, down, slope, flip, hidden, stage = refs.take(8)
    pre = hidden
    one = refs.take(12)
    branch_sums = refs.take(10)
    sums = refs.take(8)
    down_sems = refs.take(3)
    grad_send, grad_recv, load, flush = refs.take(4)
    w = place()
    greet_half(w)
    gather = Gather(w, own, rows, *one)
    branch_scatter = Scatter(w, *branch_sums)
    core = lambda c: grads.at[pl.ds(0, 2), pl.ds(0, 2), pl.ds(0, 2), c]
    scatter = Scatter(w, core(0), core(1), *sums)
    gather.start()
    half = downs.shape[0]
    early = down_some.shape[1]
    rest = half - early
    place_down = pl.ds(w["g"] * half + early, rest)
    down_mail = [
        remote(
            downs.at[pl.ds(early, rest)],
            down.at[place_down],
            down_sems[0].at[0],
            down_sems[1].at[0],
            partner(w),
        ),
        pltpu.make_async_copy(downs.at[pl.ds(early, rest)], down.at[place_down], down_sems[2].at[0]),
    ]
    fetch = [
        pltpu.make_async_copy(ups, up, load.at[0]),
        pltpu.make_async_copy(grads_near, grads.at[w["z"]], load.at[1]),
        pltpu.make_async_copy(grads_far, grads.at[1 - w["z"]], load.at[2]),
        pltpu.make_async_copy(down_some.at[0], down.at[pl.ds(0, early)], load.at[3]),
        pltpu.make_async_copy(down_some.at[1], down.at[pl.ds(half, early)], load.at[4]),
    ]
    start_all(down_mail + fetch)
    width = rows.shape[5]
    span = rows.shape[2] * rows.shape[3] * rows.shape[4]
    chunk = 256
    shift_sum[...] = jnp.zeros_like(shift_sum)

    def forward(z):
        @pl.loop(0, 2)
        def _(y):
            before = straight(flat(rows[z, y]), up[...]) + shift[...]
            active, pull = jax.vjp(activate, before)
            at = pl.ds(z * (2 * span) + y * span, span)
            low = active.astype(hidden.dtype)
            hidden[z, y] = low.reshape(hidden.shape[2:])
            flip[:, at] = low.T
            slope[at, :] = pull(jnp.ones_like(before))[0].astype(slope.dtype)

    gather.turn()
    gather.far_start()
    gather.near_ready()
    wait_all(fetch)
    gather.far_turn()
    forward(w["z"])
    gather.far_ready()
    gather.finish()
    forward(1 - w["z"])
    wait_all(down_mail)

    def branch_product(z, y, c, cols):
        return straight(flat(hidden[z, y, :, c]), down[:, cols])

    branch_scatter.begin(branch_product)

    @pl.loop(0, width // chunk)
    def _(i):
        cols = pl.ds(i * chunk, chunk)
        grad = straight(flip[...], grads[:, :, :, :, :, cols].reshape(-1, chunk))
        down_grad[:, :, cols] = grad.astype(down_grad.dtype).reshape(2, -1, chunk)

    trade = remote(down_grad.at[1 - w["g"]], down_got, grad_send, grad_recv, partner(w))
    trade.start()
    branch_scatter.second()

    @pl.loop(0, 4)
    def _(i):
        at = pl.ds(i * span, span)
        hidden_back = across(flat(grads[i // 2, i % 2]), down[...])
        pre_back = (hidden_back * slope[at, :].astype(jnp.float32)).astype(pre.dtype)
        pre[i // 2, i % 2] = pre_back.reshape(pre.shape[2:])
        flip[:, at] = pre_back.T
        shift_sum[...] += jnp.sum(pre_back.astype(jnp.float32), axis=0, keepdims=True)

    def product(z, y, c, cols):
        return across(flat(pre[z, y, :, c]), up[cols, :])

    def store(i):
        at = up_grad.at[pl.ds(pl.multiple_of(i * chunk, chunk), chunk)]
        return pltpu.make_async_copy(stage.at[i % 2], at, flush.at[i % 2])

    scatter.begin(product)
    branch_scatter.third()

    @pl.loop(0, width // chunk)
    def _(i):
        cols = pl.ds(i * chunk, chunk)
        grad = straight(flip[...], rows[:, :, :, :, :, cols].reshape(-1, chunk))

        @pl.when(i >= 2)
        def _():
            store(i).wait()

        stage[i % 2] = grad.astype(stage.dtype).T
        store(i).start()

    store(0).wait()
    store(1).wait()
    scatter.second()
    branch_scatter.fourth()
    scatter.third()
    scatter.fourth()
    branch_scatter.end(branch)
    scatter.end(back)
    trade.wait()


def feed(own, shift, ups, grads_near, grads_far, downs, down_some, name, cid):
    rows, width = own.shape
    take = ups.shape[1]
    low, f32 = own.dtype, jnp.float32
    vmem, anywhere = pl.BlockSpec(memory_space=pltpu.VMEM), pl.BlockSpec(memory_space=pl.ANY)
    shape, dma = jax.ShapeDtypeStruct, pltpu.SemaphoreType.DMA
    whole = (2, 2, 2, 2, rows, width)
    tokens = 16 * rows
    return pl.pallas_call(
        feed_kernel,
        out_shape=(
            shape((rows, width), f32),
            shape((rows, width), f32),
            shape((1, take), f32),
            shape((2,) + downs.shape, low),
            shape((width, take), low),
            shape(downs.shape, low),
        ),
        in_specs=[vmem] * 2 + [anywhere] * 5,
        out_specs=(vmem, vmem, vmem, vmem, anywhere, anywhere),
        scratch_shapes=[
            pltpu.VMEM(whole, low),
            pltpu.VMEM(whole, low),
            pltpu.VMEM((width, take), low),
            pltpu.VMEM((take, width), low),
            pltpu.VMEM((tokens, take), low),
            pltpu.VMEM((take, tokens), low),
            pltpu.VMEM((2, 2, 2, 2, rows, take), low),
            pltpu.VMEM((2, 256, take), low),
            *Gather.sems(),
            *Scatter.scratch(rows, width),
            *Scatter.scratch(rows, width, 1),
            *mail_sems(PAIR),
            dma,
            dma,
            dma((5,)),
            dma((2,)),
        ],
        compiler_params=pltpu.CompilerParams(
            collective_id=cid, has_side_effects=True, vmem_limit_bytes=VMEM_BYTES
        ),
        name=name,
    )(own, shift, ups, grads_near, grads_far, downs, down_some)


def attend_back_kernel(size, *refs):
    refs = Refs(refs)
    (own, out_rows, q, k, v, mixed, lse, key_seg, query_seg) = refs.take(9)
    rows_all, pair, up_sent = refs.take(3)
    (back, out_grad, attend_grad, q_sum, v_bias_sum, up_rows, out_got, attend_got) = refs.take(8)
    (grads, rows, weight, k_flip, mixed_flip, grad_heads, q_back, k_sum, v_sum, stack, stack_flip) = (
        refs.take(11)
    )
    (up_parts,) = refs.take(1)
    one = refs.take(12)
    sums = refs.take(10)
    send, recv, load = refs.take(3)
    swap_sems = refs.take(3)
    w = place()
    greet_half(w)
    gather = Gather(w, own, grads, *one)
    scatter = Scatter(w, *sums)
    gather.start()
    other = 1 - w["g"]
    up_trade = remote(up_sent.at[other], up_parts.at[1], send.at[0], recv.at[0], partner(w))
    up_trade.start()
    fetch = [
        pltpu.make_async_copy(pair, weight, load.at[0]),
        pltpu.make_async_copy(rows_all, rows, load.at[1]),
        pltpu.make_async_copy(up_sent.at[w["g"]], up_parts.at[0], load.at[2]),
    ]
    start_all(fetch)
    length, take = q.shape[1:]
    for i in range(2):
        k_flip[i] = k[i].T
        mixed_flip[:, pl.ds(i * length, length)] = mixed[i].astype(mixed_flip.dtype).T
    k_sum[...] = jnp.zeros_like(k_sum)
    v_sum[...] = jnp.zeros_like(v_sum)
    q_sum[...] = jnp.zeros_like(q_sum)
    v_bias_sum[...] = jnp.zeros_like(v_bias_sum)
    block = length // 4

    def heads_back(i):
        @pl.loop(0, 2)
        def _(y):
            at = pl.ds(y * (length // 2), length // 2)
            grad = across(flat(grads[i, y]), out_rows[...])
            grad_heads[i, at, :] = grad.astype(grad_heads.dtype)

    def mix_back(i):
        for first in range(0, length, block):
            attend_back_block(
                i,
                size,
                block,
                first,
                q,
                k,
                k_flip,
                v,
                grad_heads,
                mixed,
                lse,
                key_seg,
                query_seg,
                q_back,
                k_sum,
                v_sum,
            )

        @pl.loop(0, 2)
        def _(y):
            at = pl.ds(y * (length // 2), length // 2)
            parts = [ref[i, at, :].astype(stack.dtype) for ref in (q_back, k_sum, v_sum)]
            for n, part in enumerate(parts):
                stack[i, y, :, :, :, pl.ds(n * take, take)] = part.reshape(
                    stack.shape[2:5] + (take,)
                )
                to = pl.ds(i * length + y * (length // 2), length // 2)
                stack_flip[pl.ds(n * take, take), to] = part.T
            q_sum[...] += jnp.sum(parts[0].astype(jnp.float32), axis=0, keepdims=True)
            v_bias_sum[...] += jnp.sum(parts[2].astype(jnp.float32), axis=0, keepdims=True)

    gather.turn()
    gather.far_start()
    gather.near_ready()
    gather.far_turn()
    heads_back(w["z"])
    mix_back(w["z"])
    gather.far_ready()
    gather.finish()
    chunk = 256
    half_chunks = attend_grad.shape[1] // chunk
    attend_trade = remote(
        attend_grad.at[other], attend_got, send.at[1], recv.at[1], partner(w)
    )
    out_trade = remote(out_grad.at[other], out_got, send.at[2], recv.at[2], partner(w))

    @pl.loop(0, 2 * half_chunks)
    def _(i):
        cols = pl.ds(i * chunk, chunk)
        grad = straight(mixed_flip[...], grads[:, :, :, :, :, cols].reshape(-1, chunk))
        out_grad[:, :, cols] = grad.astype(out_grad.dtype).reshape(2, -1, chunk)

    heads_back(1 - w["z"])
    up_trade.wait()
    out_trade.start()
    wait_all(fetch)

    @pl.loop(0, up_parts.shape[1])
    def _(i):
        total = up_parts[0, i].astype(jnp.float32) + up_parts[1, i].astype(jnp.float32)
        up_parts[0, i] = total.astype(up_parts.dtype)

    up_mail = mail(w, COLUMNS_OUT, up_parts.at[0], up_rows, *swap_sems)
    start_all(up_mail)
    mix_back(1 - w["z"])

    def product(z, y, c, cols):
        return across(flat(stack[z, y, :, c]), weight[cols, :])

    scatter.begin(product)

    @pl.loop(0, 2 * half_chunks)
    def _(i):
        cols = pl.ds(i * chunk, chunk)
        grad = straight(stack_flip[...], rows[:, :, :, :, :, cols].reshape(-1, chunk))
        attend_grad[i // half_chunks, pl.ds(i % half_chunks * chunk, chunk), :] = grad.astype(
            attend_grad.dtype
        ).T

    out_trade.wait()
    attend_trade.start()
    scatter.second()
    scatter.third()
    scatter.fourth()
    scatter.end(back)
    wait_all(up_mail)
    attend_trade.wait()


def attend_back(
    own, out_rows, q, k, v, mixed, lse, key_seg, query_seg, rows_all, pair, up_sent, size, name, cid
):
    rows, width = own.shape
    length, take = q.shape[1:]
    low, f32 = own.dtype, jnp.float32
    vmem, anywhere = pl.BlockSpec(memory_space=pltpu.VMEM), pl.BlockSpec(memory_space=pl.ANY)
    shape, dma = jax.ShapeDtypeStruct, pltpu.SemaphoreType.DMA
    whole = (2, 2, 2, 2, rows, width)
    heads = (2, length, take)
    return pl.pallas_call(
        functools.partial(attend_back_kernel, size),
        out_shape=(
            shape((rows, width), f32),
            shape((2, take // 2, width), low),
            shape((2, width // 2, 3 * take), low),
            shape((1, take), f32),
            shape((1, take), f32),
            shape((up_sent.shape[2], up_sent.shape[1] * up_sent.shape[3]), low),
            shape((take // 2, width), low),
            shape((width // 2, 3 * take), low),
        ),
        in_specs=[vmem] * 9 + [anywhere] * 3,
        out_specs=tuple([vmem] * 6 + [anywhere] * 2),
        scratch_shapes=[
            pltpu.VMEM(whole, low),
            pltpu.VMEM(whole, low),
            pltpu.VMEM((width, 3 * take), low),
            pltpu.VMEM((2, take, length), low),
            pltpu.VMEM((take, 2 * length), low),
            pltpu.VMEM(heads, low),
            pltpu.VMEM(heads, low),
            pltpu.VMEM(heads, f32),
            pltpu.VMEM(heads, f32),
            pltpu.VMEM((2, 2, 2, 2, rows, 3 * take), low),
            pltpu.VMEM((3 * take, 2 * length), low),
            pltpu.VMEM((2,) + up_sent.shape[1:], low),
            *Gather.sems(),
            *Scatter.scratch(rows, width),
            dma((3,)),
            dma((3,)),
            dma((3,)),
            *mail_sems(COLUMNS_OUT),
        ],
        compiler_params=pltpu.CompilerParams(
            collective_id=cid, has_side_effects=True, vmem_limit_bytes=VMEM_BYTES
        ),
        name=name,
    )(
        own,
        out_rows,
        q,
        k,
        v,
        mixed,
        lse,
        key_seg,
        query_seg,
        rows_all,
        pair,
        up_sent,
    )


def last_kernel(size, *refs):
    refs = Refs(refs)
    grad, got, letter, note = refs.take(4)
    q_rows, k_rows, v_rows, letters, notes = refs.take(5)
    parts, swapped, low_letters = refs.take(3)
    sems = [refs.take(3) for _ in range(3)]
    (load,) = refs.take(1)
    w = place()
    fetch = [
        pltpu.make_async_copy(grad.at[w["g"]], parts.at[0], load.at[0]),
        pltpu.make_async_copy(got, parts.at[1], load.at[1]),
    ]
    start_all(fetch)
    greet_world(w)
    letter_mail = mail(w, LETTERS, letter, low_letters, *sems[0])
    letter_mail += mail(w, PAIR, note, notes, *sems[1])
    wait_all(fetch)
    count = parts.shape[1]

    @pl.loop(0, count)
    def _(i):
        total = parts[0, i].astype(jnp.float32) + parts[1, i].astype(jnp.float32)
        parts[0, i] = total.astype(parts.dtype)

    swap_mail = mail(w, SLICE_OUT, parts.at[0], swapped, *sems[2])
    start_all(swap_mail + letter_mail)
    wait_all(swap_mail)
    for n, out in enumerate((q_rows, k_rows, v_rows)):
        for high in range(2):
            for r in range(0, count, 2):
                at = high * count + (r + high * (count // 2)) % count
                lanes = pl.ds((2 * n + high) * size, size)
                both = jnp.concatenate([swapped[r, :, lanes], swapped[r + 1, :, lanes]], axis=1)
                out[:, pl.ds(at * size, 2 * size)] = both.astype(out.dtype)
    wait_all(letter_mail)
    letters[...] = jnp.sum(low_letters[...], axis=0)


def last(grad, got, letter, note, size, name, cid):
    width = 2 * got.shape[0]
    ndev = lax.axis_size("dp") * lax.axis_size("seq")
    low, f32 = got.dtype, jnp.float32
    vmem, anywhere = pl.BlockSpec(memory_space=pltpu.VMEM), pl.BlockSpec(memory_space=pl.ANY)
    shape, dma = jax.ShapeDtypeStruct, pltpu.SemaphoreType.DMA
    share = width // ndev
    grad, got = [x.reshape(x.shape[:-2] + (ndev // 2, share, x.shape[-1])) for x in (grad, got)]
    return pl.pallas_call(
        functools.partial(last_kernel, size),
        out_shape=(
            *[shape((share, width), f32)] * 3,
            shape(letter.shape[1:], f32),
            shape((2,) + note.shape, f32),
        ),
        in_specs=[anywhere] * 4,
        out_specs=(vmem, vmem, vmem, vmem, anywhere),
        scratch_shapes=[
            pltpu.VMEM((2,) + got.shape, low),
            pltpu.VMEM(got.shape, low),
            pltpu.VMEM((ndev,) + letter.shape[1:], f32),
            *mail_sems(LETTERS),
            *mail_sems(PAIR),
            *mail_sems(SLICE_OUT),
            dma((2,)),
        ],
        compiler_params=pltpu.CompilerParams(
            collective_id=cid, has_side_effects=True, vmem_limit_bytes=VMEM_BYTES
        ),
        name=name,
    )(grad, got, letter, note)


def on_device_halves(
    tokens,
    segments,
    exit_layer,
    first_gain,
    first_shift,
    query_weight,
    query_bias,
    key_weight,
    value_weight,
    value_bias,
    output_weight,
    output_bias,
    second_gain,
    second_shift,
    up_weight,
    up_bias,
    down_weight,
    down_bias,
    cotangent,
):
    rows, width = tokens.shape[1:]
    nd, ns = lax.axis_size("dp"), lax.axis_size("seq")
    ndev = nd * ns
    size = width // HEADS
    hidden_size = up_weight.shape[1]
    take = 2 * size
    w = place()
    group = w["g"]
    low_at = w["z"] * ns + w["s"]
    high_at = (nd - 1 - w["z"]) * ns + w["s"]

    def own_half(pair):
        return lax.dynamic_index_in_dim(pair, group, 0, keepdims=False).astype(jnp.float32)

    def total(pair, got):
        return own_half(pair) + got.astype(jnp.float32)

    keep = (exit_layer > LAYER).astype(jnp.float32).reshape(rows, 1)
    inputs = tokens.astype(jnp.float32).reshape(rows, width)
    upstream = cotangent.astype(jnp.float32).reshape(rows, width)
    branch_back = (keep * upstream).astype(jnp.bfloat16)
    vector_parts = [
        first_gain,
        first_shift,
        query_bias,
        value_bias,
        output_bias,
        second_gain,
        second_shift,
        down_bias,
        up_bias,
    ]
    share = width // ndev
    letter = jnp.zeros((16, 128), jnp.bfloat16)
    at = 0
    for part in vector_parts:
        part = part.reshape(-1, share)
        count = part.shape[0]
        letter = letter + jnp.pad(part, ((at, 16 - at - count), (0, 128 - share)))
        at += count
    (
        attention,
        queries,
        keys,
        values,
        mixed,
        lse,
        key_seg,
        query_seg,
        vectors,
        output_rows,
        normed_all,
        grads_near,
        grads_far,
        attend_pair,
        up_pair,
        down_some,
    ) = front(
        (query_weight, key_weight, value_weight),
        up_weight,
        tokens.reshape(rows, width),
        branch_back,
        letter,
        output_weight,
        segments.reshape(-1, 128),
        down_weight,
        size,
        down_weight.shape[0] // 2,
        "front",
        0,
    )
    output_rows = output_rows.reshape(-1, width)
    cuts, at = [], 0
    for part in vector_parts:
        count = part.shape[0] // share
        cuts.append(vectors[:, at : at + count, :share].reshape(ndev, -1))
        at += count
    full = [cut.reshape(-1).astype(jnp.float32) for cut in cuts]
    gain_one, shift_one, _, _, output_shift, gain_two, shift_two, down_shift, _ = full

    def rank_vector(cut):
        return jnp.concatenate(
            [
                lax.dynamic_index_in_dim(cut, low_at, 0, keepdims=False),
                lax.dynamic_index_in_dim(cut, high_at, 0, keepdims=False),
            ]
        ).astype(jnp.float32)

    up_shift = rank_vector(cuts[8])
    middle = inputs + keep * (attention + output_shift)
    normed_two = layer_norm(middle, gain_two, shift_two).astype(jnp.bfloat16)
    normed_two_back, branch, up_shift_sum, down_grad, up_grad, down_got = feed(
        normed_two,
        up_shift[None],
        up_pair.reshape(width, -1),
        grads_near,
        grads_far,
        down_weight,
        down_some,
        "feed",
        1,
    )
    layer_out = (middle + keep * (branch + down_shift)).astype(jnp.bfloat16)
    norm_result, pull_two = jax.vjp(layer_norm, middle, gain_two, shift_two)
    middle_part, gain_two_sum, shift_two_sum = pull_two(normed_two_back)
    middle_back = upstream + middle_part
    attention_back = (keep * middle_back).astype(jnp.bfloat16)
    up_grad = up_grad.reshape(2, ndev // 2, width // ndev, -1)
    (
        normed_one_back,
        output_grad,
        attend_grad,
        query_sum,
        value_sum,
        up_rows,
        output_got,
        attend_got,
    ) = attend_back(
        attention_back,
        output_rows,
        queries,
        keys,
        values,
        mixed,
        lse,
        key_seg,
        query_seg,
        normed_all,
        attend_pair.reshape(width, -1),
        up_grad,
        size,
        "attend_back",
        2,
    )
    norm_first, pull_one = jax.vjp(layer_norm, inputs, gain_one, shift_one)
    inputs_part, gain_one_sum, shift_one_sum = pull_one(normed_one_back)
    tokens_gradient = (middle_back + inputs_part).astype(jnp.bfloat16)

    def summed(value):
        return jnp.sum(value.astype(jnp.float32), axis=0)

    own_sums = [
        gain_one_sum,
        shift_one_sum,
        gain_two_sum,
        shift_two_sum,
        summed(attention_back),
        summed(branch_back),
    ]
    letter = jnp.stack([value.reshape(-1, 128) for value in own_sums], axis=1)
    letter = jnp.pad(letter, ((0, 0), (0, 2), (0, 0)))
    note = jnp.concatenate([query_sum, value_sum, up_shift_sum], axis=1)
    note = jnp.pad(note, ((0, 0), (0, -note.shape[1] % 1024))).reshape(-1, 128)
    query_rows, key_rows, value_rows, letters, notes = last(
        attend_grad, attend_got, letter, note, size, "last", 3
    )
    letters = lax.dynamic_slice_in_dim(letters, w["c"] * share, share, 1)
    notes = (notes[0] + notes[1]).reshape(-1)

    def own_part(at, length):
        return lax.dynamic_slice_in_dim(notes, at + group * length, length, 0)

    vector_out = [letters[i] for i in range(6)] + [
        own_part(0, size),
        own_part(take, size),
        own_part(2 * take, hidden_size // ndev),
    ]
    (
        gain_one_part,
        shift_one_part,
        gain_two_part,
        shift_two_part,
        output_shift_part,
        down_shift_part,
        query_shift_part,
        value_shift_part,
        up_shift_part,
    ) = vector_out
    return (
        layer_out.reshape(tokens.shape),
        tokens_gradient.reshape(tokens.shape),
        gain_one_part,
        shift_one_part,
        query_rows,
        query_shift_part,
        key_rows,
        value_rows,
        value_shift_part,
        total(output_grad, output_got),
        output_shift_part,
        gain_two_part,
        shift_two_part,
        up_rows.astype(jnp.float32),
        up_shift_part,
        total(down_grad, down_got),
        down_shift_part,
    )


def solution(mesh):
    placed = (
        P("dp", "seq", None),
        P("dp", None),
        P("dp", "seq"),
        P(("dp", "seq")),
        P(("dp", "seq")),
        P(("dp", "seq"), None),
        P(("dp", "seq")),
        P(("dp", "seq"), None),
        P(("dp", "seq"), None),
        P(("dp", "seq")),
        P(("dp", "seq"), None),
        P(("dp", "seq")),
        P(("dp", "seq")),
        P(("dp", "seq")),
        P(("dp", "seq"), None),
        P(("dp", "seq")),
        P(("dp", "seq"), None),
        P(("dp", "seq")),
        P("dp", "seq", None),
    )
    halves = mesh.shape["dp"] == 4 and mesh.shape["seq"] == 8
    return jax.shard_map(
        on_device_halves if halves else on_device,
        mesh=mesh,
        in_specs=placed,
        out_specs=(
            P("dp", "seq", None),
            P("dp", "seq", None),
            P(("dp", "seq")),
            P(("dp", "seq")),
            P(("dp", "seq"), None),
            P(("dp", "seq")),
            P(("dp", "seq"), None),
            P(("dp", "seq"), None),
            P(("dp", "seq")),
            P(("dp", "seq"), None),
            P(("dp", "seq")),
            P(("dp", "seq")),
            P(("dp", "seq")),
            P(("dp", "seq"), None),
            P(("dp", "seq")),
            P(("dp", "seq"), None),
            P(("dp", "seq")),
        ),
        check_vma=False,
    )
```

```python
import functools
import math

import jax
import jax.numpy as jnp
from jax import lax
from jax.experimental import pallas as pl
from jax.experimental.pallas import tpu as pltpu
from jax.sharding import PartitionSpec as P

HEADS = 32
LAYER = 12


EPS = 1e-05
NEG = -1e30


def activate(value):
    return jax.nn.gelu(value, approximate=True)


def layer_norm(value, gain, shift):
    mean = jnp.mean(value, axis=-1, keepdims=True)
    centred = value - mean
    spread = jnp.mean(centred * centred, axis=-1, keepdims=True)
    return centred * lax.rsqrt(spread + EPS) * gain + shift


def transposed(left, right):
    return lax.dot_general(
        left, right, (((1,), (1,)), ((), ())), preferred_element_type=jnp.float32
    )


def leading(left, right):
    return lax.dot_general(
        left, right, (((0,), (0,)), ((), ())), preferred_element_type=jnp.float32
    )


def visible(query_seg, query_pos, key_seg, key_pos):
    same = query_seg[:, :, None] == key_seg[:, None, :]
    return jnp.logical_and(same, key_pos[None, None, :] <= query_pos[None, :, None])


def by_blocks(step, carry, piece):
    length = jax.tree.leaves(piece)[0].shape[1]
    size = math.gcd(length, 128)

    def one(index, state):
        offset = index * size
        block = jax.tree.map(lambda part: lax.dynamic_slice_in_dim(part, offset, size, 1), piece)
        return step(state, block, offset)

    return lax.fori_loop(0, length // size, one, carry)


def on_device(
    tokens,
    segments,
    exit_layer,
    first_gain,
    first_shift,
    query_weight,
    query_bias,
    key_weight,
    value_weight,
    value_bias,
    output_weight,
    output_bias,
    second_gain,
    second_shift,
    up_weight,
    up_bias,
    down_weight,
    down_bias,
    cotangent,
):
    nseq, piece_len, width = tokens.shape
    head_count = HEADS
    head_size = width // head_count
    scale = head_size ** (-0.5)
    rows = nseq * piece_len
    own_first = lax.axis_index("seq") * piece_len
    own_pos = own_first + jnp.arange(piece_len, dtype=jnp.int32)
    own_seg = lax.dynamic_slice_in_dim(segments, own_first, piece_len, 1)
    keep = (exit_layer > LAYER).astype(jnp.float32).reshape(rows, 1)
    (
        gain_one,
        shift_one,
        query_full,
        query_shift,
        key_full,
        value_full,
        value_shift,
        output_full,
        output_shift,
        gain_two,
        shift_two,
        up_shift,
        down_shift,
    ) = (
        lax.all_gather(first_gain, ("dp", "seq"), axis=0, tiled=True),
        lax.all_gather(first_shift, ("dp", "seq"), axis=0, tiled=True),
        lax.all_gather(query_weight, ("dp", "seq"), axis=0, tiled=True),
        lax.all_gather(query_bias, ("dp", "seq"), axis=0, tiled=True),
        lax.all_gather(key_weight, ("dp", "seq"), axis=0, tiled=True),
        lax.all_gather(value_weight, ("dp", "seq"), axis=0, tiled=True),
        lax.all_gather(value_bias, ("dp", "seq"), axis=0, tiled=True),
        lax.all_gather(output_weight, ("dp", "seq"), axis=0, tiled=True),
        lax.all_gather(output_bias, ("dp", "seq"), axis=0, tiled=True),
        lax.all_gather(second_gain, ("dp", "seq"), axis=0, tiled=True),
        lax.all_gather(second_shift, ("dp", "seq"), axis=0, tiled=True),
        lax.all_gather(up_bias, ("dp", "seq"), axis=0, tiled=True),
        lax.all_gather(down_bias, ("dp", "seq"), axis=0, tiled=True),
    )
    gain_one = gain_one.astype(jnp.float32)
    shift_one = shift_one.astype(jnp.float32)
    gain_two = gain_two.astype(jnp.float32)
    shift_two = shift_two.astype(jnp.float32)
    inputs = tokens.astype(jnp.float32).reshape(rows, width)
    normed_one = layer_norm(inputs, gain_one, shift_one).astype(jnp.bfloat16)
    queries = (
        jnp.dot(normed_one, query_full, preferred_element_type=jnp.float32)
        + query_shift.astype(jnp.float32)
    ).astype(jnp.bfloat16)
    keys = jnp.dot(normed_one, key_full, preferred_element_type=jnp.float32).astype(jnp.bfloat16)
    values = (
        jnp.dot(normed_one, value_full, preferred_element_type=jnp.float32)
        + value_shift.astype(jnp.float32)
    ).astype(jnp.bfloat16)
    query_heads = queries.reshape(nseq, piece_len, head_count, head_size)
    key_heads = keys.reshape(nseq, piece_len, head_count, head_size)
    value_heads = values.reshape(nseq, piece_len, head_count, head_size)
    key_local = keys.reshape(nseq, piece_len, width)
    pair_local = jnp.concatenate([keys, values], axis=1).reshape(nseq, piece_len, 2 * width)

    def key_mask(start, length):
        key_pos = start + jnp.arange(length, dtype=jnp.int32)
        key_seg = lax.dynamic_slice_in_dim(segments, start, length, 1)
        return visible(own_seg, own_pos, key_seg, key_pos)[:, None]

    def local_scores(key_block):
        keyed = key_block.reshape(nseq, key_block.shape[1], head_count, head_size)
        return (
            jnp.einsum("sqhd,skhd->shqk", query_heads, keyed, preferred_element_type=jnp.float32)
            * scale
        )

    def norm_step(carry, block, start):
        top, total = carry
        allowed = key_mask(start, block.shape[1])
        scores = jnp.where(allowed, local_scores(block), NEG)
        new_top = jnp.maximum(top, jnp.max(scores, axis=-1))
        weights = jnp.where(allowed, jnp.exp(scores - new_top[..., None]), 0.0)
        return (new_top, total * jnp.exp(top - new_top) + jnp.sum(weights, axis=-1))

    start_norm = (
        jnp.full((nseq, head_count, piece_len), NEG, jnp.float32),
        jnp.zeros((nseq, head_count, piece_len), jnp.float32),
    )
    top, total = by_blocks(
        norm_step, start_norm, lax.all_gather(key_local, "seq", axis=1, tiled=True)
    )
    lse = top + jnp.log(total)

    def mix_step(acc, block, start):
        length = block.shape[1]
        allowed = key_mask(start, length)
        scores = local_scores(block[:, :, :width])
        probs = jnp.where(allowed, jnp.exp(scores - lse[..., None]), 0.0).astype(jnp.bfloat16)
        valued = block[:, :, width:].reshape(nseq, length, head_count, head_size)
        return acc + jnp.einsum(
            "shqk,skhd->sqhd", probs, valued, preferred_element_type=jnp.float32
        )

    empty_heads = jnp.zeros((nseq, piece_len, head_count, head_size), jnp.float32)
    mixed_heads = by_blocks(
        mix_step, empty_heads, lax.all_gather(pair_local, "seq", axis=1, tiled=True)
    )
    mixed = mixed_heads.reshape(rows, width).astype(jnp.bfloat16)
    attention = jnp.dot(
        mixed, output_full, preferred_element_type=jnp.float32
    ) + output_shift.astype(jnp.float32)
    middle = inputs + keep * attention
    normed_two = layer_norm(middle, gain_two, shift_two).astype(jnp.bfloat16)
    columns = normed_two
    before = jnp.dot(
        columns,
        lax.all_gather(up_weight, ("dp", "seq"), axis=0, tiled=True),
        preferred_element_type=jnp.float32,
    )
    pre_active = before + up_shift.astype(jnp.float32)
    hidden = activate(pre_active).astype(jnp.bfloat16)
    columns = hidden
    branch = jnp.dot(
        columns,
        lax.all_gather(down_weight, ("dp", "seq"), axis=0, tiled=True),
        preferred_element_type=jnp.float32,
    )
    branch = branch + down_shift.astype(jnp.float32)
    layer_out = (middle + keep * branch).astype(jnp.bfloat16).reshape(nseq, piece_len, width)
    upstream = cotangent.astype(jnp.float32).reshape(rows, width)
    branch_back = (keep * upstream).astype(jnp.bfloat16)
    down_shift_sum = jnp.sum(branch_back.astype(jnp.float32), axis=0)
    hidden_back = transposed(
        branch_back, lax.all_gather(down_weight, ("dp", "seq"), axis=0, tiled=True)
    )
    active_value, pull_active = jax.vjp(activate, pre_active)
    pre_back = pull_active(hidden_back)[0].astype(jnp.bfloat16)
    up_shift_sum = jnp.sum(pre_back.astype(jnp.float32), axis=0)
    down_gradient = lax.psum_scatter(
        leading(hidden, branch_back), ("dp", "seq"), scatter_dimension=0, tiled=True
    )
    normed_two_back = transposed(
        pre_back, lax.all_gather(up_weight, ("dp", "seq"), axis=0, tiled=True)
    )
    norm_result, pull_two = jax.vjp(layer_norm, middle, gain_two, shift_two)
    middle_part, gain_two_sum, shift_two_sum = pull_two(normed_two_back)
    middle_back = upstream + middle_part
    attention_back = (keep * middle_back).astype(jnp.bfloat16)
    output_shift_sum = jnp.sum(attention_back.astype(jnp.float32), axis=0)
    mixed_back = transposed(attention_back, output_full).astype(jnp.bfloat16)
    mixed_heads_back = mixed_back.reshape(nseq, piece_len, head_count, head_size)
    delta_rows = jnp.sum(mixed_heads_back.astype(jnp.float32) * mixed_heads, axis=-1)
    delta = delta_rows.transpose(0, 2, 1)
    lse_rows = lse.transpose(0, 2, 1)

    def query_step(acc, block, start):
        length = block.shape[1]
        allowed = key_mask(start, length)
        scores = local_scores(block[:, :, :width])
        probs = jnp.where(allowed, jnp.exp(scores - lse[..., None]), 0.0)
        valued = block[:, :, width:].reshape(nseq, length, head_count, head_size)
        keyed = block[:, :, :width].reshape(nseq, length, head_count, head_size)
        prob_back = jnp.einsum(
            "sqhd,skhd->shqk", mixed_heads_back, valued, preferred_element_type=jnp.float32
        )
        score_back = (probs * (prob_back - delta[..., None])).astype(jnp.bfloat16)
        return acc + jnp.einsum(
            "shqk,skhd->sqhd", score_back, keyed, preferred_element_type=jnp.float32
        )

    query_sum = by_blocks(
        query_step, empty_heads, lax.all_gather(pair_local, "seq", axis=1, tiled=True)
    )
    queries_back = (query_sum * scale).reshape(rows, width).astype(jnp.bfloat16)

    def key_step(carry, block, start):
        key_acc, value_acc = carry
        query_block, back_block, norm_block, delta_block = block
        length = query_block.shape[1]
        query_pos = start + jnp.arange(length, dtype=jnp.int32)
        query_seg = lax.dynamic_slice_in_dim(segments, start, length, 1)
        allowed = visible(query_seg, query_pos, own_seg, own_pos)[:, None]
        remote_query = query_block.astype(jnp.bfloat16).reshape(nseq, length, head_count, head_size)
        remote_back = back_block.astype(jnp.bfloat16).reshape(nseq, length, head_count, head_size)
        scores = (
            jnp.einsum(
                "sqhd,skhd->shqk", remote_query, key_heads, preferred_element_type=jnp.float32
            )
            * scale
        )
        probs = jnp.where(allowed, jnp.exp(scores - norm_block.transpose(0, 2, 1)[..., None]), 0.0)
        value_acc = value_acc + jnp.einsum(
            "shqk,sqhd->skhd",
            probs.astype(jnp.bfloat16),
            remote_back,
            preferred_element_type=jnp.float32,
        )
        prob_back = jnp.einsum(
            "sqhd,skhd->shqk", remote_back, value_heads, preferred_element_type=jnp.float32
        )
        score_back = (probs * (prob_back - delta_block.transpose(0, 2, 1)[..., None])).astype(
            jnp.bfloat16
        )
        key_acc = key_acc + jnp.einsum(
            "shqk,sqhd->skhd", score_back, remote_query, preferred_element_type=jnp.float32
        )
        return (key_acc, value_acc)

    query_send = queries.astype(jnp.float32).reshape(nseq, piece_len, width)
    back_send = mixed_back.astype(jnp.float32).reshape(nseq, piece_len, width)
    key_sum, value_sum = by_blocks(
        key_step,
        (empty_heads, empty_heads),
        (
            lax.all_gather(query_send.astype(jnp.bfloat16), "seq", axis=1, tiled=True).astype(
                jnp.float32
            ),
            lax.all_gather(back_send.astype(jnp.bfloat16), "seq", axis=1, tiled=True).astype(
                jnp.float32
            ),
            lax.all_gather(lse_rows.astype(jnp.bfloat16), "seq", axis=1, tiled=True).astype(
                jnp.float32
            ),
            lax.all_gather(delta_rows.astype(jnp.bfloat16), "seq", axis=1, tiled=True).astype(
                jnp.float32
            ),
        ),
    )
    keys_back = (key_sum * scale).reshape(rows, width).astype(jnp.bfloat16)
    values_back = value_sum.reshape(rows, width).astype(jnp.bfloat16)
    query_shift_sum = jnp.sum(queries_back.astype(jnp.float32), axis=0)
    value_shift_sum = jnp.sum(values_back.astype(jnp.float32), axis=0)
    normed_one_back = (
        transposed(queries_back, query_full)
        + transposed(keys_back, key_full)
        + transposed(values_back, value_full)
    )
    norm_first, pull_one = jax.vjp(layer_norm, inputs, gain_one, shift_one)
    inputs_part, gain_one_sum, shift_one_sum = pull_one(normed_one_back)
    tokens_gradient = (
        (middle_back + inputs_part).astype(jnp.bfloat16).reshape(nseq, piece_len, width)
    )
    stacked_back = jnp.concatenate([queries_back, keys_back, values_back], axis=1)
    row_gradient = lax.psum_scatter(
        jnp.concatenate(
            [
                leading(normed_one, stacked_back),
                leading(mixed, attention_back),
                leading(normed_two, pre_back),
            ],
            axis=1,
        ),
        ("dp", "seq"),
        scatter_dimension=0,
        tiled=True,
    )
    (
        gain_one_part,
        shift_one_part,
        query_shift_part,
        value_shift_part,
        output_shift_part,
        gain_two_part,
        shift_two_part,
        up_shift_part,
        down_shift_part,
    ) = (
        lax.psum_scatter(gain_one_sum, ("dp", "seq"), scatter_dimension=0, tiled=True),
        lax.psum_scatter(shift_one_sum, ("dp", "seq"), scatter_dimension=0, tiled=True),
        lax.psum_scatter(query_shift_sum, ("dp", "seq"), scatter_dimension=0, tiled=True),
        lax.psum_scatter(value_shift_sum, ("dp", "seq"), scatter_dimension=0, tiled=True),
        lax.psum_scatter(output_shift_sum, ("dp", "seq"), scatter_dimension=0, tiled=True),
        lax.psum_scatter(gain_two_sum, ("dp", "seq"), scatter_dimension=0, tiled=True),
        lax.psum_scatter(shift_two_sum, ("dp", "seq"), scatter_dimension=0, tiled=True),
        lax.psum_scatter(up_shift_sum, ("dp", "seq"), scatter_dimension=0, tiled=True),
        lax.psum_scatter(down_shift_sum, ("dp", "seq"), scatter_dimension=0, tiled=True),
    )
    return (
        layer_out,
        tokens_gradient,
        gain_one_part,
        shift_one_part,
        row_gradient[:, :width],
        query_shift_part,
        row_gradient[:, width : 2 * width],
        row_gradient[:, 2 * width : 3 * width],
        value_shift_part,
        row_gradient[:, 3 * width : 4 * width],
        output_shift_part,
        gain_two_part,
        shift_two_part,
        row_gradient[:, 4 * width :],
        up_shift_part,
        down_gradient,
        down_shift_part,
    )


MESH = pl.DeviceIdType.MESH
CANON = "zyx"
TURNS = ("xy", "yx")
SLICE_IN, SLICE_OUT, COLUMNS_IN, COLUMNS_OUT, LETTERS, SPREAD, PAIR, NEAR = range(8)
VMEM_BYTES = 60 << 20


def place():
    d, s = lax.axis_index("dp"), lax.axis_index("seq")
    half = lax.axis_size("dp") // 2
    far = d // half
    z = d + far * (2 * half - 1 - 2 * d)
    return dict(d=d, s=s, g=far, z=z, y=s // 4, x=(s // 2) % 2, c=s % 2)


def beside(w, dim):
    if dim == "z":
        return (w["d"] + 1 - 2 * (w["d"] % 2), w["s"])
    step = {"c": 1, "x": 2, "y": 4}[dim]
    return (w["d"], w["s"] + step * (1 - 2 * w[dim]))


def partner(w):
    return (lax.axis_size("dp") - 1 - w["d"], w["s"])


def peer(w, r):
    n = lax.axis_size("seq")
    e, s = r // n, r % n
    return (e + w["g"] * (lax.axis_size("dp") - 1 - 2 * e), s)


def row_block(w, r):
    n = lax.axis_size("seq")
    e, s = r // n, r % n
    return (e + w["g"] * (1 - 2 * e)) * n + s


def anyone(i):
    n = lax.axis_size("seq")
    return (i // n, i % n)


def half_peers(w):
    count = lax.axis_size("dp") * lax.axis_size("seq") // 2
    me = w["z"] * lax.axis_size("seq") + w["s"]
    return me, [(me + k) % count for k in range(1, count)]


def world_peers(w):
    count = lax.axis_size("dp") * lax.axis_size("seq")
    me = w["d"] * lax.axis_size("seq") + w["s"]
    return me, [(me + k) % count for k in range(1, count)]


def greet(ids):
    bar = pltpu.get_barrier_semaphore()
    for i in ids:
        pl.semaphore_signal(bar, inc=1, device_id=i, device_id_type=MESH)
    pl.semaphore_wait(bar, len(ids))


def greet_half(w):
    greet([peer(w, r) for r in half_peers(w)[1]] + [partner(w)])


def greet_world(w):
    greet([anyone(i) for i in world_peers(w)[1]])


def remote(src, dst, send, recv, device):
    return pltpu.make_async_remote_copy(
        src_ref=src,
        dst_ref=dst,
        send_sem=send,
        recv_sem=recv,
        device_id=device,
        device_id_type=MESH,
    )


def twice(w, r, size):
    count = lax.axis_size("dp") * lax.axis_size("seq") // 2
    other = count + (r + count // 2) % count
    return [pl.ds(pl.multiple_of(at * size, size), size) for at in (r, other)]


def mail(w, kind, src, out, send, recv, local):
    mine = None
    if kind == SLICE_IN:
        me, others = half_peers(w)
        to = out.at[row_block(w, me)]
        todo = [(src.at[r], to, peer(w, r)) for r in others]
        mine = [(src.at[me], to)]
    elif kind == SLICE_OUT:
        me, others = half_peers(w)
        to = out.at[me]
        todo = [(src.at[row_block(w, r)], to, peer(w, r)) for r in others]
        mine = [(src.at[row_block(w, me)], to)]
    elif kind == COLUMNS_IN:
        me, others = half_peers(w)
        size = out.shape[2] // 2
        to = [out.at[row_block(w, me), :, pl.ds(n * size, size)] for n in range(2)]
        todo = [
            (src.at[:, cols], to[n], peer(w, r))
            for r in others
            for n, cols in enumerate(twice(w, r, size))
        ]
        mine = [(src.at[:, cols], to[n]) for n, cols in enumerate(twice(w, me, size))]
    elif kind == COLUMNS_OUT:
        me, others = half_peers(w)
        size = src.shape[2] // 2
        to = [out.at[:, cols] for cols in twice(w, me, size)]
        todo = [
            (src.at[row_block(w, r), :, pl.ds(n * size, size)], to[n], peer(w, r))
            for r in others
            for n in range(2)
        ]
        mine = [
            (src.at[row_block(w, me), :, pl.ds(n * size, size)], to[n]) for n in range(2)
        ]
    elif kind == LETTERS:
        me, others = world_peers(w)
        to = out.at[me]
        todo = [(src.at[i // 2], to, anyone(i)) for i in others]
        mine = [(src.at[me // 2], to)]
    elif kind == SPREAD:
        me, others = world_peers(w)
        to = out.at[me]
        todo = [(src, to, anyone(i)) for i in others]
        mine = [(src, to)]
    elif kind == PAIR:
        to = out.at[w["g"]]
        todo = [(src, to, partner(w))]
        mine = [(src, to)]
    else:
        to = out.at[w["z"]]
        todo = [(src, to, beside(w, "z"))]
        mine = [(src, to)]
    copies = [
        remote(part, to, send.at[k], recv.at[k], device)
        for k, (part, to, device) in enumerate(todo)
    ]
    return copies + [
        pltpu.make_async_copy(part, to, local.at[k]) for k, (part, to) in enumerate(mine)
    ]


def start_all(copies):
    for cp in copies:
        cp.start()


def wait_all(copies):
    for cp in copies:
        cp.wait()


def mail_sems(kind):
    count = lax.axis_size("dp") * lax.axis_size("seq")
    half = count // 2 - 1
    n = {
        SLICE_IN: half,
        SLICE_OUT: half,
        COLUMNS_IN: 2 * half,
        COLUMNS_OUT: 2 * half,
        LETTERS: count - 1,
        SPREAD: count - 1,
    }.get(kind, 1)
    dma = pltpu.SemaphoreType.DMA
    return [dma((n,)), dma((n,)), dma((2,))]


def box(w, **where):
    pick = {"other": lambda q: 1 - w[q], "both": lambda q: pl.ds(0, 2)}
    return tuple(pick[where[q]](q) if q in where else w[q] for q in CANON)


def halves(width):
    return [pl.ds(0, width // 2), pl.ds(width // 2, width // 2)]


class PlaneGather:
    def __init__(self, w, src, out, send, recv, side_send, side_recv, local):
        self.w, self.src, self.out = w, src, out
        self.send, self.recv, self.side_send, self.side_recv = send, recv, side_send, side_recv
        self.parts = halves(out.shape[-1])
        self.own = (w["y"], w["x"], w["c"])
        self.keep = None if src is None else pltpu.make_async_copy(src, out.at[self.own], local)
        self.links, self.sides = {}, []

    @staticmethod
    def sems():
        dma = pltpu.SemaphoreType.DMA
        return [dma((4,)), dma((4,)), dma((5,)), dma((5,)), dma]

    def push(self, p, k, src, dst):
        n = 2 * p + k
        cp = remote(src, dst, self.send.at[n], self.recv.at[n], beside(self.w, TURNS[p][k]))
        cp.start()
        self.links[p, k] = cp

    def over(self, src, dst):
        n = len(self.sides)
        cp = remote(src, dst, self.side_send.at[n], self.side_recv.at[n], beside(self.w, "c"))
        cp.start()
        self.sides.append(cp)

    def blocks(self, cols, **where):
        return self.out.at[box(self.w, **where)[1:] + (self.w["c"], slice(None), cols)]

    def start(self, before=lambda p: None):
        for p, cols in enumerate(self.parts):
            before(p)
            dst = self.out.at[self.own + (slice(None), cols)]
            self.push(p, 0, dst if self.src is None else self.src.at[:, cols], dst)
        dst = self.out.at[self.own]
        if self.keep is not None:
            self.keep.start()
        self.over(dst if self.src is None else self.src, dst)

    def turn(self):
        if self.keep is not None:
            self.keep.wait()
        for p, cols in enumerate(self.parts):
            a, b = TURNS[p]
            self.links[p, 0].wait_recv()
            held = self.blocks(cols, **{a: "both"})
            self.push(p, 1, held, held)
            new = self.blocks(cols, **{a: "other"})
            self.over(new, new)

    def land(self):
        for p, cols in enumerate(self.parts):
            a, b = TURNS[p]
            self.links[p, 1].wait_recv()
            new = self.blocks(cols, **{a: "both", b: "other"})
            self.over(new, new)

    def ready(self):
        for cp in self.sides:
            cp.wait_recv()

    def finish(self):
        for cp in list(self.links.values()) + self.sides:
            cp.wait_send()


class Gather:
    def __init__(self, w, src, out, *sems):
        self.w, self.src, self.out = w, src, out
        self.near = PlaneGather(w, src, out.at[w["z"]], *sems[:5])
        self.far = PlaneGather(w, None, out.at[1 - w["z"]], *sems[5:10])
        self.cross = []
        for p, cols in enumerate(halves(src.shape[1])):
            dst = out.at[box(w) + (w["c"], slice(None), cols)]
            self.cross.append(
                remote(src.at[:, cols], dst, sems[10].at[p], sems[11].at[p], beside(w, "z"))
            )

    @staticmethod
    def sems():
        dma = pltpu.SemaphoreType.DMA
        return [*PlaneGather.sems(), *PlaneGather.sems(), dma((2,)), dma((2,))]

    def start(self):
        self.near.start()
        start_all(self.cross)

    def turn(self):
        self.near.turn()

    def far_start(self):
        self.far.start(lambda p: self.cross[p].wait_recv())

    def near_ready(self):
        self.near.land()
        self.near.ready()

    def far_turn(self):
        self.far.turn()

    def far_ready(self):
        self.far.land()
        self.far.ready()

    def finish(self):
        self.near.finish()
        self.far.finish()
        for cp in self.cross:
            cp.wait_send()


class Scatter:
    def __init__(self, w, acc, away, side, land_two, land_one, land_z, send, recv, side_send, side_recv):
        self.w, self.acc, self.away, self.side = w, acc, away, side
        self.land_two, self.land_one, self.land_z = land_two, land_one, land_z
        self.send, self.recv, self.side_send, self.side_recv = send, recv, side_send, side_recv
        self.parts = halves(acc.shape[-1])
        self.links, self.sides = {}, {}

    @staticmethod
    def scratch(rows, width, wholes=3):
        whole = pltpu.VMEM((2, 2, 2, rows, width), jnp.bfloat16)
        dma = pltpu.SemaphoreType.DMA
        return [whole] * wholes + [
            pltpu.VMEM((2, 2, 2, rows, width // 2), jnp.bfloat16),
            pltpu.VMEM((2, 2, rows, width // 2), jnp.bfloat16),
            pltpu.VMEM((2, rows, width // 2), jnp.bfloat16),
            dma((10,)),
            dma((10,)),
            dma((4,)),
            dma((4,)),
        ]

    def plane(self, group):
        return 1 - self.w["z"] if group else self.w["z"]

    def produce(self, group, p, product):
        w, cols, z = self.w, self.parts[p], self.plane(group)
        rows = self.acc.shape[3]

        def fill(out, core):
            @pl.loop(0, 2)
            def _(y):
                block = product(z, y, core, cols)
                out[z, y, :, :, cols] = block.astype(out.dtype).reshape(2, rows, -1)

        fill(self.away, 1 - w["c"])
        at = (z, pl.ds(0, 2), pl.ds(0, 2), slice(None), cols)
        n = len(self.sides)
        cp = remote(
            self.away.at[at],
            self.side.at[at],
            self.side_send.at[n],
            self.side_recv.at[n],
            beside(w, "c"),
        )
        cp.start()
        self.sides[group, p] = cp
        fill(self.acc, w["c"])

    def push(self, key, dim, src, dst):
        n = len(self.links)
        cp = remote(src, dst, self.send.at[n], self.recv.at[n], beside(self.w, dim))
        cp.start()
        self.links[key] = cp

    def at(self, group, **where):
        index = box(self.w, **where)
        return (self.plane(group),) + index[1:]

    def add(self, at, got, cols):
        at = at + (slice(None), cols)
        total = self.acc[at].astype(jnp.float32) + got.astype(jnp.float32)
        self.acc[at] = total.astype(self.acc.dtype)

    def fold(self, group, p):
        cols, (b, a) = self.parts[p], TURNS[p]
        self.sides[group, p].wait_recv()

        def add(other):
            @pl.loop(0, 2)
            def _(i):
                here = dict(self.w)
                here[b] = i
                if other:
                    here[a] = 1 - self.w[a]
                at = (self.plane(group), here["y"], here["x"])
                self.add(at, self.side[at + (slice(None), cols)], cols)

        add(True)
        src = self.acc.at[self.at(group, **{a: "other", b: "both"}) + (slice(None), cols)]
        self.push((group, p, 0), a, src, self.land_two.at[group, p])
        add(False)

    def middle(self, group, p):
        w, cols, (b, a) = self.w, self.parts[p], TURNS[p]
        self.links[group, p, 0].wait_recv()
        there = self.at(group, **{b: "other"})
        self.add(there, self.land_two[group, p, 1 - w[b]], cols)
        src = self.acc.at[there + (slice(None), cols)]
        self.push((group, p, 1), b, src, self.land_one.at[group, p])
        self.add(self.at(group), self.land_two[group, p, w[b]], cols)

    def cross(self, p):
        cols = self.parts[p]
        self.links[1, p, 1].wait_recv()
        at = self.at(1)
        self.add(at, self.land_one[1, p], cols)
        self.push(("z", p), "z", self.acc.at[at + (slice(None), cols)], self.land_z.at[p])

    def finish(self, p, out):
        cols = self.parts[p]
        self.links[0, p, 1].wait_recv()
        self.links["z", p].wait_recv()
        total = self.acc[self.at(0) + (slice(None), cols)].astype(jnp.float32)
        total += self.land_one[0, p].astype(jnp.float32)
        out[:, cols] = total + self.land_z[p].astype(jnp.float32)

    def begin(self, product):
        self.produce(1, 0, product)
        self.produce(1, 1, product)
        self.fold(1, 0)
        self.fold(1, 1)
        self.produce(0, 0, product)
        self.produce(0, 1, product)

    def second(self):
        self.middle(1, 0)
        self.middle(1, 1)
        self.fold(0, 0)
        self.fold(0, 1)

    def third(self):
        self.cross(0)
        self.cross(1)

    def fourth(self):
        self.middle(0, 0)
        self.middle(0, 1)

    def end(self, out):
        self.finish(0, out)
        self.finish(1, out)
        for cp in list(self.links.values()) + list(self.sides.values()):
            cp.wait_send()


def across(left, right):
    return lax.dot_general(
        left, right, (((1,), (1,)), ((), ())), preferred_element_type=jnp.float32
    )


def straight(left, right):
    return jnp.dot(left, right, preferred_element_type=jnp.float32)


def flat(block):
    return block.reshape(-1, block.shape[-1])


def head_lanes(width, head, size):
    lane = lax.broadcasted_iota(jnp.int32, (1, width), 1)
    return jnp.logical_and(lane >= head * size, lane < (head + 1) * size)


def used_pairs(key_seg, query_seg, first, length, block):
    key_pos = lax.broadcasted_iota(jnp.int32, (length, 1), 0)
    query_pos = first + lax.broadcasted_iota(jnp.int32, (1, block), 1)
    return jnp.logical_and(key_seg == query_seg, key_pos <= query_pos)


def attend_block(i, size, block, first, q, k, v_flip, key_seg, query_seg, mixed, mixed_low, lse):
    width = q.shape[2]
    upto, rows = first + block, pl.ds(first, block)
    allowed = used_pairs(key_seg[i, pl.ds(0, upto), :], query_seg[i, :, rows], first, upto, block)
    keys = k[i, pl.ds(0, upto), :]
    query = q[i, rows, :] * jnp.asarray(size**-0.5, q.dtype)
    parts = []
    for head in range(width // size):
        own = jnp.where(head_lanes(width, head, size), query, jnp.zeros_like(query))
        scores = jnp.where(allowed, across(keys, own), NEG)
        top = jnp.max(scores, axis=0, keepdims=True)
        weights = jnp.exp(scores - top)
        total = jnp.sum(weights, axis=0, keepdims=True)
        lse[i, pl.ds(head, 1), rows] = top + jnp.log(total)
        probs = (weights * (1.0 / total)).astype(q.dtype)
        parts.append(straight(v_flip[i, pl.ds(head * size, size), pl.ds(0, upto)], probs))
    full = jnp.concatenate(parts, axis=0).T
    mixed[i, rows, :] = full
    at = first // block
    mixed_low[i, at // 2, at % 2] = full.astype(mixed_low.dtype).reshape(mixed_low.shape[3:])


def attend_back_block(
    i, size, block, first, q, k, k_flip, v, back, mixed, lse, key_seg, query_seg, q_back, k_sum, v_sum
):
    width = q.shape[2]
    upto, rows = first + block, pl.ds(first, block)
    before = pl.ds(0, upto)
    scale = size**-0.5
    allowed = used_pairs(key_seg[i, before, :], query_seg[i, :, rows], first, upto, block)
    keys, values = k[i, before, :], v[i, before, :]
    query = q[i, rows, :] * jnp.asarray(scale, q.dtype)
    grad = back[i, rows, :]
    product = (grad.astype(jnp.float32) * mixed[i, rows, :]).T
    parts = []
    for head in range(width // size):
        lanes = head_lanes(width, head, size)
        own = jnp.where(lanes, query, jnp.zeros_like(query))
        own_grad = jnp.where(lanes, grad, jnp.zeros_like(grad))
        delta = jnp.sum(product[head * size : (head + 1) * size, :], axis=0, keepdims=True)
        scores = across(keys, own) - lse[i, pl.ds(head, 1), rows]
        probs = jnp.exp(jnp.where(allowed, scores, NEG))
        score_back = (probs * (across(values, own_grad) - delta)).astype(q.dtype)
        v_sum[i, before, :] += straight(probs.astype(q.dtype), own_grad)
        k_sum[i, before, :] += straight(score_back, own)
        parts.append(straight(k_flip[i, pl.ds(head * size, size), before], score_back))
    q_back[i, rows, :] = (jnp.concatenate(parts, axis=0).T * scale).astype(q_back.dtype)


class Refs:
    def __init__(self, refs):
        self.refs, self.used = refs, 0

    def take(self, count):
        self.used += count
        return self.refs[self.used - count : self.used]


def front_kernel(size, *refs):
    refs = Refs(refs)
    weights, (up, tokens, grad, keep) = refs.take(3), refs.take(4)
    letter, out_own, segs, down = refs.take(4)
    middle, normed_two, up_shift = refs.take(3)
    q, k, v, mixed, lse, key_seg, query_seg, letters, out_pair = refs.take(9)
    rows_all, grads_near, grads_far, pair, ups, downs = refs.take(6)
    pieces, blocks, columns, normed, vectors, near_segs = refs.take(6)
    rows, near_plane, far_plane, weight, v_flip, mixed_low = refs.take(6)
    one, two, three = refs.take(12), refs.take(5), refs.take(5)
    sums = refs.take(10)
    letter_sems, block_sems, seg_sems, out_sems, column_sems = [refs.take(3) for _ in range(5)]
    pair_sems, up_sems, down_sems, late_sems = [refs.take(3) for _ in range(4)]
    cross_send, cross_recv, load, flush = refs.take(4)
    w = place()
    length, take = q.shape[1:]
    block = length // 4
    width = tokens.shape[1]
    share = size
    greet_world(w)
    letter_mail = mail(w, SPREAD, letter, letters, *letter_sems)
    start_all(letter_mail)
    count = pieces.shape[0]
    for r in range(count):
        places = (r, count + (r + count // 2) % count)
        pieces[r] = jnp.concatenate(
            [ref[:, pl.ds(at * size, size)] for ref in weights for at in places], axis=1
        )
    block_mail = mail(w, SLICE_IN, pieces, blocks, *block_sems)
    start_all(block_mail)
    some = downs.shape[1] // 2
    down_parts = [
        mail(w, PAIR, down.at[part], downs.at[pl.ds(0, 2), part], *sems)
        for part, sems in ((pl.ds(0, some), down_sems), (pl.ds(some, some), late_sems))
    ]
    column_mail = mail(w, COLUMNS_IN, up, columns, *column_sems)
    start_all(column_mail)
    out_mail = mail(w, PAIR, out_own, out_pair, *out_sems)
    first = PlaneGather(w, grad, near_plane, *two)
    cross = remote(
        grad, far_plane.at[w["y"], w["x"], w["c"]], cross_send, cross_recv, beside(w, "z")
    )
    seg_mail = mail(w, NEAR, segs, near_segs, *seg_sems)
    start_all(seg_mail)
    value = tokens[...].astype(jnp.float32)
    centred = value - jnp.mean(value, axis=-1, keepdims=True)
    spread = jnp.mean(centred * centred, axis=-1, keepdims=True)
    centred = centred * lax.rsqrt(spread + EPS)
    wait_all(letter_mail)

    def whole_vector(n):
        for i in range(0, letters.shape[0], 2):
            vectors[pl.ds(n, 1), pl.ds(i * share, 2 * share)] = jnp.concatenate(
                [letters[j, pl.ds(n, 1), pl.ds(0, share)] for j in (i, i + 1)], axis=1
            ).astype(jnp.float32)

    whole_vector(0)
    whole_vector(1)
    normed[...] = (centred * vectors[pl.ds(0, 1), :] + vectors[pl.ds(1, 1), :]).astype(normed.dtype)
    gather = Gather(w, normed, rows, *one)
    second = PlaneGather(w, None, far_plane, *three)
    scatter = Scatter(w, *sums)
    gather.start()
    wait_all(block_mail)
    pair_mail = mail(w, PAIR, blocks, weight, *pair_sems)
    start_all(pair_mail)
    gather.turn()
    gather.far_start()
    gather.near_ready()
    gather.far_turn()
    first.start()
    cross.start()
    wait_all(seg_mail)
    for i in range(2):
        flipped = near_segs[i].T
        for n in range(near_segs.shape[1]):
            at = pl.ds(n * 128, 128)
            query_seg[i, :, at] = near_segs[i, pl.ds(n, 1), :]
            key_seg[i, at, :] = flipped[:, n : n + 1]
    count = lax.axis_size("dp") * lax.axis_size("seq")
    low_at = w["z"] * lax.axis_size("seq") + w["s"]
    high_at = (lax.axis_size("dp") - 1 - w["z"]) * lax.axis_size("seq") + w["s"]
    q_shift, v_shift = [
        jnp.concatenate(
            [letters[at, pl.ds(n, 1), pl.ds(0, share)] for at in (low_at, high_at)], axis=1
        ).astype(jnp.float32)
        for n in (2, 3)
    ]
    shift = jnp.concatenate([q_shift, jnp.zeros_like(q_shift), v_shift], axis=1)
    for n in (4, 5, 6):
        whole_vector(n)
    up_rows = up_shift.shape[1] // (2 * share)
    up_shift[...] = jnp.concatenate(
        [
            letters[at, pl.ds(8 + n, 1), pl.ds(0, share)]
            for at in (low_at, high_at)
            for n in range(up_rows)
        ],
        axis=1,
    ).astype(jnp.float32)
    wait_all(column_mail)
    wait_all(pair_mail)
    up_mail = mail(w, PAIR, columns, ups, *up_sems)
    start_all(out_mail + up_mail)
    keep_pair = pltpu.make_async_copy(weight, pair, load)
    keep_pair.start()

    def project(i):
        @pl.loop(0, 2)
        def _(y):
            block = straight(flat(rows[i, y]), weight[...].reshape(width, -1)) + shift
            at = pl.ds(y * (length // 2), length // 2)
            for ref, n in ((q, 0), (k, 1), (v, 2)):
                ref[i, at, :] = block[:, n * take : (n + 1) * take].astype(ref.dtype)
            v_flip[i, :, at] = block[:, 2 * take :].astype(v_flip.dtype).T

    def mix(i):
        for first in range(0, length, block):
            attend_block(
                i, size, block, first, q, k, v_flip, key_seg, query_seg, mixed, mixed_low, lse
            )

    project(w["z"])
    gather.far_ready()
    gather.finish()
    keep_rows = pltpu.make_async_copy(rows, rows_all, flush.at[0])
    keep_rows.start()
    first.turn()
    mix(w["z"])
    first.land()
    cross.wait()
    second.start()
    project(1 - w["z"])
    mix(1 - w["z"])
    first.ready()
    keep_near = pltpu.make_async_copy(near_plane, grads_near, flush.at[2])
    keep_near.start()
    wait_all(out_mail)

    def product(z, y, c, cols):
        return straight(
            flat(mixed_low[z, y, :, c]), jnp.concatenate([out_pair[0, :, cols], out_pair[1, :, cols]])
        )

    second.turn()
    scatter.begin(product)
    scatter.second()
    second.land()
    wait_all(up_mail)
    start_all(down_parts[0] + down_parts[1])
    second.ready()
    keep_far = pltpu.make_async_copy(far_plane, grads_far, flush.at[1])
    keep_far.start()
    scatter.third()
    scatter.fourth()
    scatter.end(middle)
    value = tokens[...].astype(jnp.float32)
    value += keep[...] * (middle[...] + vectors[pl.ds(4, 1), :])
    middle[...] = value
    centred = value - jnp.mean(value, axis=-1, keepdims=True)
    spread = jnp.mean(centred * centred, axis=-1, keepdims=True)
    centred = centred * lax.rsqrt(spread + EPS)
    value = centred * vectors[pl.ds(5, 1), :] + vectors[pl.ds(6, 1), :]
    normed_two[...] = value.astype(normed_two.dtype)
    first.finish()
    second.finish()
    wait_all(down_parts[0] + down_parts[1])
    keep_rows.wait()
    keep_near.wait()
    keep_far.wait()
    keep_pair.wait()


def front(weights, up, tokens, grad, keep, letter, out_own, segs, down, size, early, name, cid):
    rows, width = tokens.shape
    ns = lax.axis_size("seq")
    ndev = lax.axis_size("dp") * ns
    length = rows * ns
    take = 2 * size
    low, f32 = tokens.dtype, jnp.float32
    vmem, anywhere = pl.BlockSpec(memory_space=pltpu.VMEM), pl.BlockSpec(memory_space=pl.ANY)
    shape, dma = jax.ShapeDtypeStruct, pltpu.SemaphoreType.DMA
    plane = (2, 2, 2, rows, width)
    share = weights[0].shape[0]
    blocks = (ndev // 2, share, 3 * take)
    columns = (ndev // 2, share, 2 * up.shape[1] // ndev)
    return pl.pallas_call(
        functools.partial(front_kernel, size),
        out_shape=(
            shape((rows, width), f32),
            shape((rows, width), low),
            shape((1, columns[2]), f32),
            *[shape((2, length, take), low)] * 3,
            shape((2, length, take), f32),
            shape((2, take // size, length), f32),
            shape((2, length, 1), segs.dtype),
            shape((2, 1, length), segs.dtype),
            shape((ndev,) + letter.shape, low),
            shape((2,) + out_own.shape, low),
            shape((2,) + plane, low),
            shape(plane, low),
            shape(plane, low),
            shape((2,) + blocks, low),
            shape((2,) + columns, low),
            shape((2, early, width), low),
        ),
        in_specs=[vmem] * 7 + [anywhere] * 4,
        out_specs=tuple([vmem] * 12 + [anywhere] * 6),
        scratch_shapes=[
            pltpu.VMEM(blocks, low),
            pltpu.VMEM(blocks, low),
            pltpu.VMEM(columns, low),
            pltpu.VMEM((rows, width), low),
            pltpu.VMEM((8, width), f32),
            pltpu.VMEM((2,) + segs.shape, segs.dtype),
            pltpu.VMEM((2,) + plane, low),
            pltpu.VMEM(plane, low),
            pltpu.VMEM(plane, low),
            pltpu.VMEM((2,) + blocks, low),
            pltpu.VMEM((2, take, length), low),
            pltpu.VMEM((2, 2, 2, 2, rows, take), low),
            *Gather.sems(),
            *PlaneGather.sems(),
            *PlaneGather.sems(),
            *Scatter.scratch(rows, width),
            *mail_sems(SPREAD),
            *mail_sems(SLICE_IN),
            *mail_sems(NEAR),
            *mail_sems(PAIR),
            *mail_sems(COLUMNS_IN),
            *mail_sems(PAIR),
            *mail_sems(PAIR),
            *mail_sems(PAIR),
            *mail_sems(PAIR),
            dma,
            dma,
            dma,
            dma((3,)),
        ],
        compiler_params=pltpu.CompilerParams(
            collective_id=cid, has_side_effects=True, vmem_limit_bytes=VMEM_BYTES
        ),
        name=name,
    )(*weights, up, tokens, grad, keep, letter, out_own, segs, down)


def feed_kernel(*refs):
    refs = Refs(refs)
    own, shift, ups, grads_near, grads_far, downs, down_some = refs.take(7)
    back, branch, shift_sum, down_grad, up_grad, down_got, up_some = refs.take(7)
    rows, grads, up, down, slope, flip, hidden, stage = refs.take(8)
    pre = hidden
    one = refs.take(12)
    branch_sums = refs.take(10)
    sums = refs.take(8)
    down_sems = refs.take(3)
    grad_send, grad_recv, load, flush = refs.take(4)
    w = place()
    greet_half(w)
    gather = Gather(w, own, rows, *one)
    branch_scatter = Scatter(w, *branch_sums)
    core = lambda c: grads.at[pl.ds(0, 2), pl.ds(0, 2), pl.ds(0, 2), c]
    scatter = Scatter(w, core(0), core(1), *sums)
    gather.start()
    half = downs.shape[0]
    early = down_some.shape[1]
    rest = half - early
    place_down = pl.ds(w["g"] * half + early, rest)
    down_mail = [
        remote(
            downs.at[pl.ds(early, rest)],
            down.at[place_down],
            down_sems[0].at[0],
            down_sems[1].at[0],
            partner(w),
        ),
        pltpu.make_async_copy(downs.at[pl.ds(early, rest)], down.at[place_down], down_sems[2].at[0]),
    ]
    fetch = [
        pltpu.make_async_copy(ups, up, load.at[0]),
        pltpu.make_async_copy(grads_near, grads.at[w["z"]], load.at[1]),
        pltpu.make_async_copy(grads_far, grads.at[1 - w["z"]], load.at[2]),
        pltpu.make_async_copy(down_some.at[0], down.at[pl.ds(0, early)], load.at[3]),
        pltpu.make_async_copy(down_some.at[1], down.at[pl.ds(half, early)], load.at[4]),
    ]
    start_all(down_mail + fetch)
    width = rows.shape[5]
    span = rows.shape[2] * rows.shape[3] * rows.shape[4]
    chunk = 256
    shift_sum[...] = jnp.zeros_like(shift_sum)

    def forward(z):
        @pl.loop(0, 2)
        def _(y):
            before = straight(flat(rows[z, y]), up[...]) + shift[...]
            active, pull = jax.vjp(activate, before)
            at = pl.ds(z * (2 * span) + y * span, span)
            low = active.astype(hidden.dtype)
            hidden[z, y] = low.reshape(hidden.shape[2:])
            flip[:, at] = low.T
            slope[at, :] = pull(jnp.ones_like(before))[0].astype(slope.dtype)

    gather.turn()
    gather.far_start()
    gather.near_ready()
    wait_all(fetch)
    gather.far_turn()
    forward(w["z"])
    gather.far_ready()
    gather.finish()
    forward(1 - w["z"])
    wait_all(down_mail)

    def branch_product(z, y, c, cols):
        return straight(flat(hidden[z, y, :, c]), down[:, cols])

    branch_scatter.begin(branch_product)

    @pl.loop(0, width // chunk)
    def _(i):
        cols = pl.ds(i * chunk, chunk)
        grad = straight(flip[...], grads[:, :, :, :, :, cols].reshape(-1, chunk))
        down_grad[:, :, cols] = grad.astype(down_grad.dtype).reshape(2, -1, chunk)

    trade = remote(
        down_grad.at[1 - w["g"]], down_got, grad_send.at[0], grad_recv.at[0], partner(w)
    )
    trade.start()
    branch_scatter.second()

    @pl.loop(0, 4)
    def _(i):
        at = pl.ds(i * span, span)
        hidden_back = across(flat(grads[i // 2, i % 2]), down[...])
        pre_back = (hidden_back * slope[at, :].astype(jnp.float32)).astype(pre.dtype)
        pre[i // 2, i % 2] = pre_back.reshape(pre.shape[2:])
        flip[:, at] = pre_back.T
        shift_sum[...] += jnp.sum(pre_back.astype(jnp.float32), axis=0, keepdims=True)

    def product(z, y, c, cols):
        return across(flat(pre[z, y, :, c]), up[cols, :])

    def store(i):
        at = up_grad.at[pl.ds(pl.multiple_of(i * chunk, chunk), chunk)]
        return pltpu.make_async_copy(stage.at[i % 2], at, flush.at[i % 2])

    scatter.begin(product)
    branch_scatter.third()

    @pl.loop(0, width // chunk)
    def _(i):
        cols = pl.ds(i * chunk, chunk)
        grad = straight(flip[...], rows[:, :, :, :, :, cols].reshape(-1, chunk))

        @pl.when(i >= 2)
        def _():
            store(i).wait()

        stage[i % 2] = grad.astype(stage.dtype).T
        store(i).start()

    store(0).wait()
    store(1).wait()
    sent = pl.ds((1 - w["g"]) * (width // 2), up_some.shape[0])
    up_trade = remote(up_grad.at[sent], up_some, grad_send.at[1], grad_recv.at[1], partner(w))
    up_trade.start()
    scatter.second()
    branch_scatter.fourth()
    scatter.third()
    scatter.fourth()
    branch_scatter.end(branch)
    scatter.end(back)
    trade.wait()
    up_trade.wait()


def feed(own, shift, ups, grads_near, grads_far, downs, down_some, name, cid):
    rows, width = own.shape
    take = ups.shape[1]
    low, f32 = own.dtype, jnp.float32
    vmem, anywhere = pl.BlockSpec(memory_space=pltpu.VMEM), pl.BlockSpec(memory_space=pl.ANY)
    shape, dma = jax.ShapeDtypeStruct, pltpu.SemaphoreType.DMA
    whole = (2, 2, 2, 2, rows, width)
    tokens = 16 * rows
    return pl.pallas_call(
        feed_kernel,
        out_shape=(
            shape((rows, width), f32),
            shape((rows, width), f32),
            shape((1, take), f32),
            shape((2,) + downs.shape, low),
            shape((width, take), low),
            shape(downs.shape, low),
            shape((width // 4, take), low),
        ),
        in_specs=[vmem] * 2 + [anywhere] * 5,
        out_specs=(vmem, vmem, vmem, vmem, anywhere, anywhere, anywhere),
        scratch_shapes=[
            pltpu.VMEM(whole, low),
            pltpu.VMEM(whole, low),
            pltpu.VMEM((width, take), low),
            pltpu.VMEM((take, width), low),
            pltpu.VMEM((tokens, take), low),
            pltpu.VMEM((take, tokens), low),
            pltpu.VMEM((2, 2, 2, 2, rows, take), low),
            pltpu.VMEM((2, 256, take), low),
            *Gather.sems(),
            *Scatter.scratch(rows, width),
            *Scatter.scratch(rows, width, 1),
            *mail_sems(PAIR),
            dma((2,)),
            dma((2,)),
            dma((5,)),
            dma((2,)),
        ],
        compiler_params=pltpu.CompilerParams(
            collective_id=cid, has_side_effects=True, vmem_limit_bytes=VMEM_BYTES
        ),
        name=name,
    )(own, shift, ups, grads_near, grads_far, downs, down_some)


def attend_back_kernel(size, *refs):
    refs = Refs(refs)
    (own, out_rows, q, k, v, mixed, lse, key_seg, query_seg) = refs.take(9)
    rows_all, pair, up_sent, up_some = refs.take(4)
    (back, out_grad, attend_grad, q_sum, v_bias_sum, up_rows, out_got, attend_got) = refs.take(8)
    (grads, rows, weight, k_flip, mixed_flip, grad_heads, q_back, k_sum, v_sum, stack, stack_flip) = (
        refs.take(11)
    )
    (up_parts,) = refs.take(1)
    one = refs.take(12)
    sums = refs.take(10)
    send, recv, load = refs.take(3)
    swap_sems = refs.take(3)
    w = place()
    greet_half(w)
    gather = Gather(w, own, grads, *one)
    scatter = Scatter(w, *sums)
    gather.start()
    other = 1 - w["g"]
    some = up_some.shape[0]
    rest = pl.ds(some, up_sent.shape[1] - some)
    up_trade = remote(
        up_sent.at[other, rest], up_parts.at[1, rest], send.at[0], recv.at[0], partner(w)
    )
    up_trade.start()
    fetch = [
        pltpu.make_async_copy(pair, weight, load.at[0]),
        pltpu.make_async_copy(rows_all, rows, load.at[1]),
        pltpu.make_async_copy(up_sent.at[w["g"]], up_parts.at[0], load.at[2]),
        pltpu.make_async_copy(up_some, up_parts.at[1, pl.ds(0, some)], load.at[3]),
    ]
    start_all(fetch)
    length, take = q.shape[1:]
    for i in range(2):
        k_flip[i] = k[i].T
        mixed_flip[:, pl.ds(i * length, length)] = mixed[i].astype(mixed_flip.dtype).T
    k_sum[...] = jnp.zeros_like(k_sum)
    v_sum[...] = jnp.zeros_like(v_sum)
    q_sum[...] = jnp.zeros_like(q_sum)
    v_bias_sum[...] = jnp.zeros_like(v_bias_sum)
    block = length // 4

    def heads_back(i):
        @pl.loop(0, 2)
        def _(y):
            at = pl.ds(y * (length // 2), length // 2)
            grad = across(flat(grads[i, y]), out_rows[...])
            grad_heads[i, at, :] = grad.astype(grad_heads.dtype)

    def mix_back(i):
        for first in range(0, length, block):
            attend_back_block(
                i,
                size,
                block,
                first,
                q,
                k,
                k_flip,
                v,
                grad_heads,
                mixed,
                lse,
                key_seg,
                query_seg,
                q_back,
                k_sum,
                v_sum,
            )

        @pl.loop(0, 2)
        def _(y):
            at = pl.ds(y * (length // 2), length // 2)
            parts = [ref[i, at, :].astype(stack.dtype) for ref in (q_back, k_sum, v_sum)]
            for n, part in enumerate(parts):
                stack[i, y, :, :, :, pl.ds(n * take, take)] = part.reshape(
                    stack.shape[2:5] + (take,)
                )
                to = pl.ds(i * length + y * (length // 2), length // 2)
                stack_flip[pl.ds(n * take, take), to] = part.T
            q_sum[...] += jnp.sum(parts[0].astype(jnp.float32), axis=0, keepdims=True)
            v_bias_sum[...] += jnp.sum(parts[2].astype(jnp.float32), axis=0, keepdims=True)

    gather.turn()
    gather.far_start()
    gather.near_ready()
    gather.far_turn()
    heads_back(w["z"])
    mix_back(w["z"])
    gather.far_ready()
    gather.finish()
    chunk = 256
    half_chunks = attend_grad.shape[1] // chunk
    attend_trade = remote(
        attend_grad.at[other], attend_got, send.at[1], recv.at[1], partner(w)
    )
    out_trade = remote(out_grad.at[other], out_got, send.at[2], recv.at[2], partner(w))

    @pl.loop(0, 2 * half_chunks)
    def _(i):
        cols = pl.ds(i * chunk, chunk)
        grad = straight(mixed_flip[...], grads[:, :, :, :, :, cols].reshape(-1, chunk))
        out_grad[:, :, cols] = grad.astype(out_grad.dtype).reshape(2, -1, chunk)

    heads_back(1 - w["z"])
    up_trade.wait()
    out_trade.start()
    wait_all(fetch)

    @pl.loop(0, up_parts.shape[1])
    def _(i):
        total = up_parts[0, i].astype(jnp.float32) + up_parts[1, i].astype(jnp.float32)
        up_parts[0, i] = total.astype(up_parts.dtype)

    up_mail = mail(w, COLUMNS_OUT, up_parts.at[0], up_rows, *swap_sems)
    start_all(up_mail)
    mix_back(1 - w["z"])

    def product(z, y, c, cols):
        return across(flat(stack[z, y, :, c]), weight[cols, :])

    scatter.begin(product)

    @pl.loop(0, 2 * half_chunks)
    def _(i):
        cols = pl.ds(i * chunk, chunk)
        grad = straight(stack_flip[...], rows[:, :, :, :, :, cols].reshape(-1, chunk))
        attend_grad[i // half_chunks, pl.ds(i % half_chunks * chunk, chunk), :] = grad.astype(
            attend_grad.dtype
        ).T

    out_trade.wait()
    attend_trade.start()
    scatter.second()
    scatter.third()
    scatter.fourth()
    scatter.end(back)
    wait_all(up_mail)
    attend_trade.wait()


def attend_back(
    own, out_rows, q, k, v, mixed, lse, key_seg, query_seg, rows_all, pair, up_sent, up_some,
    size, name, cid
):
    rows, width = own.shape
    length, take = q.shape[1:]
    low, f32 = own.dtype, jnp.float32
    vmem, anywhere = pl.BlockSpec(memory_space=pltpu.VMEM), pl.BlockSpec(memory_space=pl.ANY)
    shape, dma = jax.ShapeDtypeStruct, pltpu.SemaphoreType.DMA
    whole = (2, 2, 2, 2, rows, width)
    heads = (2, length, take)
    return pl.pallas_call(
        functools.partial(attend_back_kernel, size),
        out_shape=(
            shape((rows, width), f32),
            shape((2, take // 2, width), low),
            shape((2, width // 2, 3 * take), low),
            shape((1, take), f32),
            shape((1, take), f32),
            shape((up_sent.shape[2], up_sent.shape[1] * up_sent.shape[3]), low),
            shape((take // 2, width), low),
            shape((width // 2, 3 * take), low),
        ),
        in_specs=[vmem] * 9 + [anywhere] * 4,
        out_specs=tuple([vmem] * 6 + [anywhere] * 2),
        scratch_shapes=[
            pltpu.VMEM(whole, low),
            pltpu.VMEM(whole, low),
            pltpu.VMEM((width, 3 * take), low),
            pltpu.VMEM((2, take, length), low),
            pltpu.VMEM((take, 2 * length), low),
            pltpu.VMEM(heads, low),
            pltpu.VMEM(heads, low),
            pltpu.VMEM(heads, f32),
            pltpu.VMEM(heads, f32),
            pltpu.VMEM((2, 2, 2, 2, rows, 3 * take), low),
            pltpu.VMEM((3 * take, 2 * length), low),
            pltpu.VMEM((2,) + up_sent.shape[1:], low),
            *Gather.sems(),
            *Scatter.scratch(rows, width),
            dma((3,)),
            dma((3,)),
            dma((4,)),
            *mail_sems(COLUMNS_OUT),
        ],
        compiler_params=pltpu.CompilerParams(
            collective_id=cid, has_side_effects=True, vmem_limit_bytes=VMEM_BYTES
        ),
        name=name,
    )(
        own,
        out_rows,
        q,
        k,
        v,
        mixed,
        lse,
        key_seg,
        query_seg,
        rows_all,
        pair,
        up_sent,
        up_some,
    )


def last_kernel(size, *refs):
    refs = Refs(refs)
    grad, got, letter, note = refs.take(4)
    q_rows, k_rows, v_rows, letters, notes = refs.take(5)
    parts, swapped, low_letters = refs.take(3)
    sems = [refs.take(3) for _ in range(3)]
    (load,) = refs.take(1)
    w = place()
    fetch = [
        pltpu.make_async_copy(grad.at[w["g"]], parts.at[0], load.at[0]),
        pltpu.make_async_copy(got, parts.at[1], load.at[1]),
    ]
    start_all(fetch)
    greet_world(w)
    letter_mail = mail(w, LETTERS, letter, low_letters, *sems[0])
    letter_mail += mail(w, PAIR, note, notes, *sems[1])
    wait_all(fetch)
    count = parts.shape[1]

    @pl.loop(0, count)
    def _(i):
        total = parts[0, i].astype(jnp.float32) + parts[1, i].astype(jnp.float32)
        parts[0, i] = total.astype(parts.dtype)

    swap_mail = mail(w, SLICE_OUT, parts.at[0], swapped, *sems[2])
    start_all(swap_mail + letter_mail)
    wait_all(swap_mail)
    for n, out in enumerate((q_rows, k_rows, v_rows)):
        for high in range(2):
            for r in range(0, count, 2):
                at = high * count + (r + high * (count // 2)) % count
                lanes = pl.ds((2 * n + high) * size, size)
                both = jnp.concatenate([swapped[r, :, lanes], swapped[r + 1, :, lanes]], axis=1)
                out[:, pl.ds(at * size, 2 * size)] = both.astype(out.dtype)
    wait_all(letter_mail)
    letters[...] = jnp.sum(low_letters[...], axis=0)


def last(grad, got, letter, note, size, name, cid):
    width = 2 * got.shape[0]
    ndev = lax.axis_size("dp") * lax.axis_size("seq")
    low, f32 = got.dtype, jnp.float32
    vmem, anywhere = pl.BlockSpec(memory_space=pltpu.VMEM), pl.BlockSpec(memory_space=pl.ANY)
    shape, dma = jax.ShapeDtypeStruct, pltpu.SemaphoreType.DMA
    share = width // ndev
    grad, got = [x.reshape(x.shape[:-2] + (ndev // 2, share, x.shape[-1])) for x in (grad, got)]
    return pl.pallas_call(
        functools.partial(last_kernel, size),
        out_shape=(
            *[shape((share, width), f32)] * 3,
            shape(letter.shape[1:], f32),
            shape((2,) + note.shape, f32),
        ),
        in_specs=[anywhere] * 4,
        out_specs=(vmem, vmem, vmem, vmem, anywhere),
        scratch_shapes=[
            pltpu.VMEM((2,) + got.shape, low),
            pltpu.VMEM(got.shape, low),
            pltpu.VMEM((ndev,) + letter.shape[1:], f32),
            *mail_sems(LETTERS),
            *mail_sems(PAIR),
            *mail_sems(SLICE_OUT),
            dma((2,)),
        ],
        compiler_params=pltpu.CompilerParams(
            collective_id=cid, has_side_effects=True, vmem_limit_bytes=VMEM_BYTES
        ),
        name=name,
    )(grad, got, letter, note)


def on_device_halves(
    tokens,
    segments,
    exit_layer,
    first_gain,
    first_shift,
    query_weight,
    query_bias,
    key_weight,
    value_weight,
    value_bias,
    output_weight,
    output_bias,
    second_gain,
    second_shift,
    up_weight,
    up_bias,
    down_weight,
    down_bias,
    cotangent,
):
    rows, width = tokens.shape[1:]
    nd, ns = lax.axis_size("dp"), lax.axis_size("seq")
    ndev = nd * ns
    size = width // HEADS
    hidden_size = up_weight.shape[1]
    take = 2 * size
    w = place()
    group = w["g"]

    def own_half(pair):
        return lax.dynamic_index_in_dim(pair, group, 0, keepdims=False).astype(jnp.float32)

    def total(pair, got):
        return own_half(pair) + got.astype(jnp.float32)

    keep = (exit_layer > LAYER).astype(jnp.float32).reshape(rows, 1)
    inputs = tokens.astype(jnp.float32).reshape(rows, width)
    upstream = cotangent.astype(jnp.float32).reshape(rows, width)
    branch_back = (keep * upstream).astype(jnp.bfloat16)
    vector_parts = [
        first_gain,
        first_shift,
        query_bias,
        value_bias,
        output_bias,
        second_gain,
        second_shift,
        down_bias,
        up_bias,
    ]
    share = width // ndev
    letter = jnp.zeros((16, 128), jnp.bfloat16)
    at = 0
    for part in vector_parts:
        part = part.reshape(-1, share)
        count = part.shape[0]
        letter = letter + jnp.pad(part, ((at, 16 - at - count), (0, 128 - share)))
        at += count
    (
        middle,
        normed_two,
        up_shift,
        queries,
        keys,
        values,
        mixed,
        lse,
        key_seg,
        query_seg,
        vectors,
        output_rows,
        normed_all,
        grads_near,
        grads_far,
        attend_pair,
        up_pair,
        down_some,
    ) = front(
        (query_weight, key_weight, value_weight),
        up_weight,
        tokens.reshape(rows, width),
        branch_back,
        keep,
        letter,
        output_weight,
        segments.reshape(-1, 128),
        down_weight,
        size,
        down_weight.shape[0] // 2,
        "front",
        0,
    )
    output_rows = output_rows.reshape(-1, width)
    cuts, at = [], 0
    for part in vector_parts:
        count = part.shape[0] // share
        cuts.append(vectors[:, at : at + count, :share].reshape(ndev, -1))
        at += count
    full = [cut.reshape(-1).astype(jnp.float32) for cut in cuts]
    gain_one, shift_one, _, _, output_shift, gain_two, shift_two, down_shift, _ = full

    normed_two_back, branch, up_shift_sum, down_grad, up_grad, down_got, up_some = feed(
        normed_two,
        up_shift,
        up_pair.reshape(width, -1),
        grads_near,
        grads_far,
        down_weight,
        down_some,
        "feed",
        1,
    )
    layer_out = (middle + keep * (branch + down_shift)).astype(jnp.bfloat16)
    norm_result, pull_two = jax.vjp(layer_norm, middle, gain_two, shift_two)
    middle_part, gain_two_sum, shift_two_sum = pull_two(normed_two_back)
    middle_back = upstream + middle_part
    attention_back = (keep * middle_back).astype(jnp.bfloat16)
    up_grad = up_grad.reshape(2, ndev // 2, width // ndev, -1)
    (
        normed_one_back,
        output_grad,
        attend_grad,
        query_sum,
        value_sum,
        up_rows,
        output_got,
        attend_got,
    ) = attend_back(
        attention_back,
        output_rows,
        queries,
        keys,
        values,
        mixed,
        lse,
        key_seg,
        query_seg,
        normed_all,
        attend_pair.reshape(width, -1),
        up_grad,
        up_some.reshape(-1, width // ndev, up_some.shape[1]),
        size,
        "attend_back",
        2,
    )
    norm_first, pull_one = jax.vjp(layer_norm, inputs, gain_one, shift_one)
    inputs_part, gain_one_sum, shift_one_sum = pull_one(normed_one_back)
    tokens_gradient = (middle_back + inputs_part).astype(jnp.bfloat16)

    def summed(value):
        return jnp.sum(value.astype(jnp.float32), axis=0)

    own_sums = [
        gain_one_sum,
        shift_one_sum,
        gain_two_sum,
        shift_two_sum,
        summed(attention_back),
        summed(branch_back),
    ]
    letter = jnp.stack([value.reshape(-1, 128) for value in own_sums], axis=1)
    letter = jnp.pad(letter, ((0, 0), (0, 2), (0, 0)))
    note = jnp.concatenate([query_sum, value_sum, up_shift_sum], axis=1)
    note = jnp.pad(note, ((0, 0), (0, -note.shape[1] % 1024))).reshape(-1, 128)
    query_rows, key_rows, value_rows, letters, notes = last(
        attend_grad, attend_got, letter, note, size, "last", 3
    )
    letters = lax.dynamic_slice_in_dim(letters, w["c"] * share, share, 1)
    notes = (notes[0] + notes[1]).reshape(-1)

    def own_part(at, length):
        return lax.dynamic_slice_in_dim(notes, at + group * length, length, 0)

    vector_out = [letters[i] for i in range(6)] + [
        own_part(0, size),
        own_part(take, size),
        own_part(2 * take, hidden_size // ndev),
    ]
    (
        gain_one_part,
        shift_one_part,
        gain_two_part,
        shift_two_part,
        output_shift_part,
        down_shift_part,
        query_shift_part,
        value_shift_part,
        up_shift_part,
    ) = vector_out
    return (
        layer_out.reshape(tokens.shape),
        tokens_gradient.reshape(tokens.shape),
        gain_one_part,
        shift_one_part,
        query_rows,
        query_shift_part,
        key_rows,
        value_rows,
        value_shift_part,
        total(output_grad, output_got),
        output_shift_part,
        gain_two_part,
        shift_two_part,
        up_rows.astype(jnp.float32),
        up_shift_part,
        total(down_grad, down_got),
        down_shift_part,
    )


def solution(mesh):
    placed = (
        P("dp", "seq", None),
        P("dp", None),
        P("dp", "seq"),
        P(("dp", "seq")),
        P(("dp", "seq")),
        P(("dp", "seq"), None),
        P(("dp", "seq")),
        P(("dp", "seq"), None),
        P(("dp", "seq"), None),
        P(("dp", "seq")),
        P(("dp", "seq"), None),
        P(("dp", "seq")),
        P(("dp", "seq")),
        P(("dp", "seq")),
        P(("dp", "seq"), None),
        P(("dp", "seq")),
        P(("dp", "seq"), None),
        P(("dp", "seq")),
        P("dp", "seq", None),
    )
    halves = mesh.shape["dp"] == 4 and mesh.shape["seq"] == 8
    return jax.shard_map(
        on_device_halves if halves else on_device,
        mesh=mesh,
        in_specs=placed,
        out_specs=(
            P("dp", "seq", None),
            P("dp", "seq", None),
            P(("dp", "seq")),
            P(("dp", "seq")),
            P(("dp", "seq"), None),
            P(("dp", "seq")),
            P(("dp", "seq"), None),
            P(("dp", "seq"), None),
            P(("dp", "seq")),
            P(("dp", "seq"), None),
            P(("dp", "seq")),
            P(("dp", "seq")),
            P(("dp", "seq")),
            P(("dp", "seq"), None),
            P(("dp", "seq")),
            P(("dp", "seq"), None),
            P(("dp", "seq")),
        ),
        check_vma=False,
    )
```

```python
import functools
import math

import jax
import jax.numpy as jnp
from jax import lax
from jax.experimental import pallas as pl
from jax.experimental.pallas import tpu as pltpu
from jax.sharding import PartitionSpec as P

HEADS = 32
LAYER = 12


EPS = 1e-05
NEG = -1e30


def activate(value):
    return jax.nn.gelu(value, approximate=True)


def layer_norm(value, gain, shift):
    mean = jnp.mean(value, axis=-1, keepdims=True)
    centred = value - mean
    spread = jnp.mean(centred * centred, axis=-1, keepdims=True)
    return centred * lax.rsqrt(spread + EPS) * gain + shift


def transposed(left, right):
    return lax.dot_general(
        left, right, (((1,), (1,)), ((), ())), preferred_element_type=jnp.float32
    )


def leading(left, right):
    return lax.dot_general(
        left, right, (((0,), (0,)), ((), ())), preferred_element_type=jnp.float32
    )


def visible(query_seg, query_pos, key_seg, key_pos):
    same = query_seg[:, :, None] == key_seg[:, None, :]
    return jnp.logical_and(same, key_pos[None, None, :] <= query_pos[None, :, None])


def by_blocks(step, carry, piece):
    length = jax.tree.leaves(piece)[0].shape[1]
    size = math.gcd(length, 128)

    def one(index, state):
        offset = index * size
        block = jax.tree.map(lambda part: lax.dynamic_slice_in_dim(part, offset, size, 1), piece)
        return step(state, block, offset)

    return lax.fori_loop(0, length // size, one, carry)


def on_device(
    tokens,
    segments,
    exit_layer,
    first_gain,
    first_shift,
    query_weight,
    query_bias,
    key_weight,
    value_weight,
    value_bias,
    output_weight,
    output_bias,
    second_gain,
    second_shift,
    up_weight,
    up_bias,
    down_weight,
    down_bias,
    cotangent,
):
    nseq, piece_len, width = tokens.shape
    head_count = HEADS
    head_size = width // head_count
    scale = head_size ** (-0.5)
    rows = nseq * piece_len
    own_first = lax.axis_index("seq") * piece_len
    own_pos = own_first + jnp.arange(piece_len, dtype=jnp.int32)
    own_seg = lax.dynamic_slice_in_dim(segments, own_first, piece_len, 1)
    keep = (exit_layer > LAYER).astype(jnp.float32).reshape(rows, 1)
    (
        gain_one,
        shift_one,
        query_full,
        query_shift,
        key_full,
        value_full,
        value_shift,
        output_full,
        output_shift,
        gain_two,
        shift_two,
        up_shift,
        down_shift,
    ) = (
        lax.all_gather(first_gain, ("dp", "seq"), axis=0, tiled=True),
        lax.all_gather(first_shift, ("dp", "seq"), axis=0, tiled=True),
        lax.all_gather(query_weight, ("dp", "seq"), axis=0, tiled=True),
        lax.all_gather(query_bias, ("dp", "seq"), axis=0, tiled=True),
        lax.all_gather(key_weight, ("dp", "seq"), axis=0, tiled=True),
        lax.all_gather(value_weight, ("dp", "seq"), axis=0, tiled=True),
        lax.all_gather(value_bias, ("dp", "seq"), axis=0, tiled=True),
        lax.all_gather(output_weight, ("dp", "seq"), axis=0, tiled=True),
        lax.all_gather(output_bias, ("dp", "seq"), axis=0, tiled=True),
        lax.all_gather(second_gain, ("dp", "seq"), axis=0, tiled=True),
        lax.all_gather(second_shift, ("dp", "seq"), axis=0, tiled=True),
        lax.all_gather(up_bias, ("dp", "seq"), axis=0, tiled=True),
        lax.all_gather(down_bias, ("dp", "seq"), axis=0, tiled=True),
    )
    gain_one = gain_one.astype(jnp.float32)
    shift_one = shift_one.astype(jnp.float32)
    gain_two = gain_two.astype(jnp.float32)
    shift_two = shift_two.astype(jnp.float32)
    inputs = tokens.astype(jnp.float32).reshape(rows, width)
    normed_one = layer_norm(inputs, gain_one, shift_one).astype(jnp.bfloat16)
    queries = (
        jnp.dot(normed_one, query_full, preferred_element_type=jnp.float32)
        + query_shift.astype(jnp.float32)
    ).astype(jnp.bfloat16)
    keys = jnp.dot(normed_one, key_full, preferred_element_type=jnp.float32).astype(jnp.bfloat16)
    values = (
        jnp.dot(normed_one, value_full, preferred_element_type=jnp.float32)
        + value_shift.astype(jnp.float32)
    ).astype(jnp.bfloat16)
    query_heads = queries.reshape(nseq, piece_len, head_count, head_size)
    key_heads = keys.reshape(nseq, piece_len, head_count, head_size)
    value_heads = values.reshape(nseq, piece_len, head_count, head_size)
    key_local = keys.reshape(nseq, piece_len, width)
    pair_local = jnp.concatenate([keys, values], axis=1).reshape(nseq, piece_len, 2 * width)

    def key_mask(start, length):
        key_pos = start + jnp.arange(length, dtype=jnp.int32)
        key_seg = lax.dynamic_slice_in_dim(segments, start, length, 1)
        return visible(own_seg, own_pos, key_seg, key_pos)[:, None]

    def local_scores(key_block):
        keyed = key_block.reshape(nseq, key_block.shape[1], head_count, head_size)
        return (
            jnp.einsum("sqhd,skhd->shqk", query_heads, keyed, preferred_element_type=jnp.float32)
            * scale
        )

    def norm_step(carry, block, start):
        top, total = carry
        allowed = key_mask(start, block.shape[1])
        scores = jnp.where(allowed, local_scores(block), NEG)
        new_top = jnp.maximum(top, jnp.max(scores, axis=-1))
        weights = jnp.where(allowed, jnp.exp(scores - new_top[..., None]), 0.0)
        return (new_top, total * jnp.exp(top - new_top) + jnp.sum(weights, axis=-1))

    start_norm = (
        jnp.full((nseq, head_count, piece_len), NEG, jnp.float32),
        jnp.zeros((nseq, head_count, piece_len), jnp.float32),
    )
    top, total = by_blocks(
        norm_step, start_norm, lax.all_gather(key_local, "seq", axis=1, tiled=True)
    )
    lse = top + jnp.log(total)

    def mix_step(acc, block, start):
        length = block.shape[1]
        allowed = key_mask(start, length)
        scores = local_scores(block[:, :, :width])
        probs = jnp.where(allowed, jnp.exp(scores - lse[..., None]), 0.0).astype(jnp.bfloat16)
        valued = block[:, :, width:].reshape(nseq, length, head_count, head_size)
        return acc + jnp.einsum(
            "shqk,skhd->sqhd", probs, valued, preferred_element_type=jnp.float32
        )

    empty_heads = jnp.zeros((nseq, piece_len, head_count, head_size), jnp.float32)
    mixed_heads = by_blocks(
        mix_step, empty_heads, lax.all_gather(pair_local, "seq", axis=1, tiled=True)
    )
    mixed = mixed_heads.reshape(rows, width).astype(jnp.bfloat16)
    attention = jnp.dot(
        mixed, output_full, preferred_element_type=jnp.float32
    ) + output_shift.astype(jnp.float32)
    middle = inputs + keep * attention
    normed_two = layer_norm(middle, gain_two, shift_two).astype(jnp.bfloat16)
    columns = normed_two
    before = jnp.dot(
        columns,
        lax.all_gather(up_weight, ("dp", "seq"), axis=0, tiled=True),
        preferred_element_type=jnp.float32,
    )
    pre_active = before + up_shift.astype(jnp.float32)
    hidden = activate(pre_active).astype(jnp.bfloat16)
    columns = hidden
    branch = jnp.dot(
        columns,
        lax.all_gather(down_weight, ("dp", "seq"), axis=0, tiled=True),
        preferred_element_type=jnp.float32,
    )
    branch = branch + down_shift.astype(jnp.float32)
    layer_out = (middle + keep * branch).astype(jnp.bfloat16).reshape(nseq, piece_len, width)
    upstream = cotangent.astype(jnp.float32).reshape(rows, width)
    branch_back = (keep * upstream).astype(jnp.bfloat16)
    down_shift_sum = jnp.sum(branch_back.astype(jnp.float32), axis=0)
    hidden_back = transposed(
        branch_back, lax.all_gather(down_weight, ("dp", "seq"), axis=0, tiled=True)
    )
    active_value, pull_active = jax.vjp(activate, pre_active)
    pre_back = pull_active(hidden_back)[0].astype(jnp.bfloat16)
    up_shift_sum = jnp.sum(pre_back.astype(jnp.float32), axis=0)
    down_gradient = lax.psum_scatter(
        leading(hidden, branch_back), ("dp", "seq"), scatter_dimension=0, tiled=True
    )
    normed_two_back = transposed(
        pre_back, lax.all_gather(up_weight, ("dp", "seq"), axis=0, tiled=True)
    )
    norm_result, pull_two = jax.vjp(layer_norm, middle, gain_two, shift_two)
    middle_part, gain_two_sum, shift_two_sum = pull_two(normed_two_back)
    middle_back = upstream + middle_part
    attention_back = (keep * middle_back).astype(jnp.bfloat16)
    output_shift_sum = jnp.sum(attention_back.astype(jnp.float32), axis=0)
    mixed_back = transposed(attention_back, output_full).astype(jnp.bfloat16)
    mixed_heads_back = mixed_back.reshape(nseq, piece_len, head_count, head_size)
    delta_rows = jnp.sum(mixed_heads_back.astype(jnp.float32) * mixed_heads, axis=-1)
    delta = delta_rows.transpose(0, 2, 1)
    lse_rows = lse.transpose(0, 2, 1)

    def query_step(acc, block, start):
        length = block.shape[1]
        allowed = key_mask(start, length)
        scores = local_scores(block[:, :, :width])
        probs = jnp.where(allowed, jnp.exp(scores - lse[..., None]), 0.0)
        valued = block[:, :, width:].reshape(nseq, length, head_count, head_size)
        keyed = block[:, :, :width].reshape(nseq, length, head_count, head_size)
        prob_back = jnp.einsum(
            "sqhd,skhd->shqk", mixed_heads_back, valued, preferred_element_type=jnp.float32
        )
        score_back = (probs * (prob_back - delta[..., None])).astype(jnp.bfloat16)
        return acc + jnp.einsum(
            "shqk,skhd->sqhd", score_back, keyed, preferred_element_type=jnp.float32
        )

    query_sum = by_blocks(
        query_step, empty_heads, lax.all_gather(pair_local, "seq", axis=1, tiled=True)
    )
    queries_back = (query_sum * scale).reshape(rows, width).astype(jnp.bfloat16)

    def key_step(carry, block, start):
        key_acc, value_acc = carry
        query_block, back_block, norm_block, delta_block = block
        length = query_block.shape[1]
        query_pos = start + jnp.arange(length, dtype=jnp.int32)
        query_seg = lax.dynamic_slice_in_dim(segments, start, length, 1)
        allowed = visible(query_seg, query_pos, own_seg, own_pos)[:, None]
        remote_query = query_block.astype(jnp.bfloat16).reshape(nseq, length, head_count, head_size)
        remote_back = back_block.astype(jnp.bfloat16).reshape(nseq, length, head_count, head_size)
        scores = (
            jnp.einsum(
                "sqhd,skhd->shqk", remote_query, key_heads, preferred_element_type=jnp.float32
            )
            * scale
        )
        probs = jnp.where(allowed, jnp.exp(scores - norm_block.transpose(0, 2, 1)[..., None]), 0.0)
        value_acc = value_acc + jnp.einsum(
            "shqk,sqhd->skhd",
            probs.astype(jnp.bfloat16),
            remote_back,
            preferred_element_type=jnp.float32,
        )
        prob_back = jnp.einsum(
            "sqhd,skhd->shqk", remote_back, value_heads, preferred_element_type=jnp.float32
        )
        score_back = (probs * (prob_back - delta_block.transpose(0, 2, 1)[..., None])).astype(
            jnp.bfloat16
        )
        key_acc = key_acc + jnp.einsum(
            "shqk,sqhd->skhd", score_back, remote_query, preferred_element_type=jnp.float32
        )
        return (key_acc, value_acc)

    query_send = queries.astype(jnp.float32).reshape(nseq, piece_len, width)
    back_send = mixed_back.astype(jnp.float32).reshape(nseq, piece_len, width)
    key_sum, value_sum = by_blocks(
        key_step,
        (empty_heads, empty_heads),
        (
            lax.all_gather(query_send.astype(jnp.bfloat16), "seq", axis=1, tiled=True).astype(
                jnp.float32
            ),
            lax.all_gather(back_send.astype(jnp.bfloat16), "seq", axis=1, tiled=True).astype(
                jnp.float32
            ),
            lax.all_gather(lse_rows.astype(jnp.bfloat16), "seq", axis=1, tiled=True).astype(
                jnp.float32
            ),
            lax.all_gather(delta_rows.astype(jnp.bfloat16), "seq", axis=1, tiled=True).astype(
                jnp.float32
            ),
        ),
    )
    keys_back = (key_sum * scale).reshape(rows, width).astype(jnp.bfloat16)
    values_back = value_sum.reshape(rows, width).astype(jnp.bfloat16)
    query_shift_sum = jnp.sum(queries_back.astype(jnp.float32), axis=0)
    value_shift_sum = jnp.sum(values_back.astype(jnp.float32), axis=0)
    normed_one_back = (
        transposed(queries_back, query_full)
        + transposed(keys_back, key_full)
        + transposed(values_back, value_full)
    )
    norm_first, pull_one = jax.vjp(layer_norm, inputs, gain_one, shift_one)
    inputs_part, gain_one_sum, shift_one_sum = pull_one(normed_one_back)
    tokens_gradient = (
        (middle_back + inputs_part).astype(jnp.bfloat16).reshape(nseq, piece_len, width)
    )
    stacked_back = jnp.concatenate([queries_back, keys_back, values_back], axis=1)
    row_gradient = lax.psum_scatter(
        jnp.concatenate(
            [
                leading(normed_one, stacked_back),
                leading(mixed, attention_back),
                leading(normed_two, pre_back),
            ],
            axis=1,
        ),
        ("dp", "seq"),
        scatter_dimension=0,
        tiled=True,
    )
    (
        gain_one_part,
        shift_one_part,
        query_shift_part,
        value_shift_part,
        output_shift_part,
        gain_two_part,
        shift_two_part,
        up_shift_part,
        down_shift_part,
    ) = (
        lax.psum_scatter(gain_one_sum, ("dp", "seq"), scatter_dimension=0, tiled=True),
        lax.psum_scatter(shift_one_sum, ("dp", "seq"), scatter_dimension=0, tiled=True),
        lax.psum_scatter(query_shift_sum, ("dp", "seq"), scatter_dimension=0, tiled=True),
        lax.psum_scatter(value_shift_sum, ("dp", "seq"), scatter_dimension=0, tiled=True),
        lax.psum_scatter(output_shift_sum, ("dp", "seq"), scatter_dimension=0, tiled=True),
        lax.psum_scatter(gain_two_sum, ("dp", "seq"), scatter_dimension=0, tiled=True),
        lax.psum_scatter(shift_two_sum, ("dp", "seq"), scatter_dimension=0, tiled=True),
        lax.psum_scatter(up_shift_sum, ("dp", "seq"), scatter_dimension=0, tiled=True),
        lax.psum_scatter(down_shift_sum, ("dp", "seq"), scatter_dimension=0, tiled=True),
    )
    return (
        layer_out,
        tokens_gradient,
        gain_one_part,
        shift_one_part,
        row_gradient[:, :width],
        query_shift_part,
        row_gradient[:, width : 2 * width],
        row_gradient[:, 2 * width : 3 * width],
        value_shift_part,
        row_gradient[:, 3 * width : 4 * width],
        output_shift_part,
        gain_two_part,
        shift_two_part,
        row_gradient[:, 4 * width :],
        up_shift_part,
        down_gradient,
        down_shift_part,
    )


MESH = pl.DeviceIdType.MESH
CANON = "zyx"
TURNS = ("xy", "yx")
SLICE_IN, SLICE_OUT, COLUMNS_IN, COLUMNS_OUT, LETTERS, SPREAD, PAIR, NEAR = range(8)
VMEM_BYTES = 60 << 20


def place():
    d, s = lax.axis_index("dp"), lax.axis_index("seq")
    half = lax.axis_size("dp") // 2
    far = d // half
    z = d + far * (2 * half - 1 - 2 * d)
    return dict(d=d, s=s, g=far, z=z, y=s // 4, x=(s // 2) % 2, c=s % 2)


def beside(w, dim):
    if dim == "z":
        return (w["d"] + 1 - 2 * (w["d"] % 2), w["s"])
    step = {"c": 1, "x": 2, "y": 4}[dim]
    return (w["d"], w["s"] + step * (1 - 2 * w[dim]))


def partner(w):
    return (lax.axis_size("dp") - 1 - w["d"], w["s"])


def peer(w, r):
    n = lax.axis_size("seq")
    e, s = r // n, r % n
    return (e + w["g"] * (lax.axis_size("dp") - 1 - 2 * e), s)


def row_block(w, r):
    n = lax.axis_size("seq")
    e, s = r // n, r % n
    return (e + w["g"] * (1 - 2 * e)) * n + s


def anyone(i):
    n = lax.axis_size("seq")
    return (i // n, i % n)


def half_peers(w):
    count = lax.axis_size("dp") * lax.axis_size("seq") // 2
    me = w["z"] * lax.axis_size("seq") + w["s"]
    return me, [(me + k) % count for k in range(1, count)]


def world_peers(w):
    count = lax.axis_size("dp") * lax.axis_size("seq")
    me = w["d"] * lax.axis_size("seq") + w["s"]
    return me, [(me + k) % count for k in range(1, count)]


def greet(ids):
    bar = pltpu.get_barrier_semaphore()
    for i in ids:
        pl.semaphore_signal(bar, inc=1, device_id=i, device_id_type=MESH)
    pl.semaphore_wait(bar, len(ids))


def greet_half(w):
    greet([peer(w, r) for r in half_peers(w)[1]] + [partner(w)])


def greet_world(w):
    greet([anyone(i) for i in world_peers(w)[1]])


def remote(src, dst, send, recv, device):
    return pltpu.make_async_remote_copy(
        src_ref=src,
        dst_ref=dst,
        send_sem=send,
        recv_sem=recv,
        device_id=device,
        device_id_type=MESH,
    )


def twice(w, r, size):
    count = lax.axis_size("dp") * lax.axis_size("seq") // 2
    other = count + (r + count // 2) % count
    return [pl.ds(pl.multiple_of(at * size, size), size) for at in (r, other)]


def mail(w, kind, src, out, send, recv, local):
    mine = None
    if kind == SLICE_IN:
        me, others = half_peers(w)
        to = out.at[row_block(w, me)]
        todo = [(src.at[r], to, peer(w, r)) for r in others]
        mine = [(src.at[me], to)]
    elif kind == SLICE_OUT:
        me, others = half_peers(w)
        to = out.at[me]
        todo = [(src.at[row_block(w, r)], to, peer(w, r)) for r in others]
        mine = [(src.at[row_block(w, me)], to)]
    elif kind == COLUMNS_IN:
        me, others = half_peers(w)
        size = out.shape[2] // 2
        to = [out.at[row_block(w, me), :, pl.ds(n * size, size)] for n in range(2)]
        todo = [
            (src.at[:, cols], to[n], peer(w, r))
            for r in others
            for n, cols in enumerate(twice(w, r, size))
        ]
        mine = [(src.at[:, cols], to[n]) for n, cols in enumerate(twice(w, me, size))]
    elif kind == COLUMNS_OUT:
        me, others = half_peers(w)
        size = src.shape[2] // 2
        to = [out.at[:, cols] for cols in twice(w, me, size)]
        todo = [
            (src.at[row_block(w, r), :, pl.ds(n * size, size)], to[n], peer(w, r))
            for r in others
            for n in range(2)
        ]
        mine = [
            (src.at[row_block(w, me), :, pl.ds(n * size, size)], to[n]) for n in range(2)
        ]
    elif kind == LETTERS:
        me, others = world_peers(w)
        to = out.at[me]
        todo = [(src.at[i // 2], to, anyone(i)) for i in others]
        mine = [(src.at[me // 2], to)]
    elif kind == SPREAD:
        me, others = world_peers(w)
        to = out.at[me]
        todo = [(src, to, anyone(i)) for i in others]
        mine = [(src, to)]
    elif kind == PAIR:
        to = out.at[w["g"]]
        todo = [(src, to, partner(w))]
        mine = [(src, to)]
    else:
        to = out.at[w["z"]]
        todo = [(src, to, beside(w, "z"))]
        mine = [(src, to)]
    copies = [
        remote(part, to, send.at[k], recv.at[k], device)
        for k, (part, to, device) in enumerate(todo)
    ]
    return copies + [
        pltpu.make_async_copy(part, to, local.at[k]) for k, (part, to) in enumerate(mine)
    ]


def start_all(copies):
    for cp in copies:
        cp.start()


def wait_all(copies):
    for cp in copies:
        cp.wait()


def mail_sems(kind):
    count = lax.axis_size("dp") * lax.axis_size("seq")
    half = count // 2 - 1
    n = {
        SLICE_IN: half,
        SLICE_OUT: half,
        COLUMNS_IN: 2 * half,
        COLUMNS_OUT: 2 * half,
        LETTERS: count - 1,
        SPREAD: count - 1,
    }.get(kind, 1)
    dma = pltpu.SemaphoreType.DMA
    return [dma((n,)), dma((n,)), dma((2,))]


def box(w, **where):
    pick = {"other": lambda q: 1 - w[q], "both": lambda q: pl.ds(0, 2)}
    return tuple(pick[where[q]](q) if q in where else w[q] for q in CANON)


def halves(width):
    return [pl.ds(0, width // 2), pl.ds(width // 2, width // 2)]


class PlaneGather:
    def __init__(self, w, src, out, send, recv, side_send, side_recv, local):
        self.w, self.src, self.out = w, src, out
        self.send, self.recv, self.side_send, self.side_recv = send, recv, side_send, side_recv
        self.parts = halves(out.shape[-1])
        self.own = (w["y"], w["x"], w["c"])
        self.keep = None if src is None else pltpu.make_async_copy(src, out.at[self.own], local)
        self.links, self.sides = {}, []

    @staticmethod
    def sems():
        dma = pltpu.SemaphoreType.DMA
        return [dma((4,)), dma((4,)), dma((5,)), dma((5,)), dma]

    def push(self, p, k, src, dst):
        n = 2 * p + k
        cp = remote(src, dst, self.send.at[n], self.recv.at[n], beside(self.w, TURNS[p][k]))
        cp.start()
        self.links[p, k] = cp

    def over(self, src, dst):
        n = len(self.sides)
        cp = remote(src, dst, self.side_send.at[n], self.side_recv.at[n], beside(self.w, "c"))
        cp.start()
        self.sides.append(cp)

    def blocks(self, cols, **where):
        return self.out.at[box(self.w, **where)[1:] + (self.w["c"], slice(None), cols)]

    def start(self, before=lambda p: None):
        for p, cols in enumerate(self.parts):
            before(p)
            dst = self.out.at[self.own + (slice(None), cols)]
            self.push(p, 0, dst if self.src is None else self.src.at[:, cols], dst)
        dst = self.out.at[self.own]
        if self.keep is not None:
            self.keep.start()
        self.over(dst if self.src is None else self.src, dst)

    def turn(self):
        if self.keep is not None:
            self.keep.wait()
        for p, cols in enumerate(self.parts):
            a, b = TURNS[p]
            self.links[p, 0].wait_recv()
            held = self.blocks(cols, **{a: "both"})
            self.push(p, 1, held, held)
            new = self.blocks(cols, **{a: "other"})
            self.over(new, new)

    def land(self):
        for p, cols in enumerate(self.parts):
            a, b = TURNS[p]
            self.links[p, 1].wait_recv()
            new = self.blocks(cols, **{a: "both", b: "other"})
            self.over(new, new)

    def ready(self):
        for cp in self.sides:
            cp.wait_recv()

    def finish(self):
        for cp in list(self.links.values()) + self.sides:
            cp.wait_send()


class Gather:
    def __init__(self, w, src, out, *sems):
        self.w, self.src, self.out = w, src, out
        self.near = PlaneGather(w, src, out.at[w["z"]], *sems[:5])
        self.far = PlaneGather(w, None, out.at[1 - w["z"]], *sems[5:10])
        self.cross = []
        for p, cols in enumerate(halves(src.shape[1])):
            dst = out.at[box(w) + (w["c"], slice(None), cols)]
            self.cross.append(
                remote(src.at[:, cols], dst, sems[10].at[p], sems[11].at[p], beside(w, "z"))
            )

    @staticmethod
    def sems():
        dma = pltpu.SemaphoreType.DMA
        return [*PlaneGather.sems(), *PlaneGather.sems(), dma((2,)), dma((2,))]

    def start(self):
        self.near.start()
        start_all(self.cross)

    def turn(self):
        self.near.turn()

    def far_start(self):
        self.far.start(lambda p: self.cross[p].wait_recv())

    def near_ready(self):
        self.near.land()
        self.near.ready()

    def far_turn(self):
        self.far.turn()

    def far_ready(self):
        self.far.land()
        self.far.ready()

    def finish(self):
        self.near.finish()
        self.far.finish()
        for cp in self.cross:
            cp.wait_send()


class Scatter:
    def __init__(self, w, acc, away, side, land_two, land_one, land_z, send, recv, side_send, side_recv):
        self.w, self.acc, self.away, self.side = w, acc, away, side
        self.land_two, self.land_one, self.land_z = land_two, land_one, land_z
        self.send, self.recv, self.side_send, self.side_recv = send, recv, side_send, side_recv
        self.parts = halves(acc.shape[-1])
        self.links, self.sides = {}, {}

    @staticmethod
    def scratch(rows, width, wholes=3):
        whole = pltpu.VMEM((2, 2, 2, rows, width), jnp.bfloat16)
        dma = pltpu.SemaphoreType.DMA
        return [whole] * wholes + [
            pltpu.VMEM((2, 2, 2, rows, width // 2), jnp.bfloat16),
            pltpu.VMEM((2, 2, rows, width // 2), jnp.bfloat16),
            pltpu.VMEM((2, rows, width // 2), jnp.bfloat16),
            dma((10,)),
            dma((10,)),
            dma((4,)),
            dma((4,)),
        ]

    def plane(self, group):
        return 1 - self.w["z"] if group else self.w["z"]

    def produce(self, group, p, product):
        w, cols, z = self.w, self.parts[p], self.plane(group)
        rows = self.acc.shape[3]

        def fill(out, core):
            @pl.loop(0, 2)
            def _(y):
                block = product(z, y, core, cols)
                out[z, y, :, :, cols] = block.astype(out.dtype).reshape(2, rows, -1)

        fill(self.away, 1 - w["c"])
        at = (z, pl.ds(0, 2), pl.ds(0, 2), slice(None), cols)
        n = len(self.sides)
        cp = remote(
            self.away.at[at],
            self.side.at[at],
            self.side_send.at[n],
            self.side_recv.at[n],
            beside(w, "c"),
        )
        cp.start()
        self.sides[group, p] = cp
        fill(self.acc, w["c"])

    def push(self, key, dim, src, dst):
        n = len(self.links)
        cp = remote(src, dst, self.send.at[n], self.recv.at[n], beside(self.w, dim))
        cp.start()
        self.links[key] = cp

    def at(self, group, **where):
        index = box(self.w, **where)
        return (self.plane(group),) + index[1:]

    def add(self, at, got, cols):
        at = at + (slice(None), cols)
        total = self.acc[at].astype(jnp.float32) + got.astype(jnp.float32)
        self.acc[at] = total.astype(self.acc.dtype)

    def fold(self, group, p):
        cols, (b, a) = self.parts[p], TURNS[p]
        self.sides[group, p].wait_recv()

        def add(other):
            @pl.loop(0, 2)
            def _(i):
                here = dict(self.w)
                here[b] = i
                if other:
                    here[a] = 1 - self.w[a]
                at = (self.plane(group), here["y"], here["x"])
                self.add(at, self.side[at + (slice(None), cols)], cols)

        add(True)
        src = self.acc.at[self.at(group, **{a: "other", b: "both"}) + (slice(None), cols)]
        self.push((group, p, 0), a, src, self.land_two.at[group, p])
        add(False)

    def middle(self, group, p):
        w, cols, (b, a) = self.w, self.parts[p], TURNS[p]
        self.links[group, p, 0].wait_recv()
        there = self.at(group, **{b: "other"})
        self.add(there, self.land_two[group, p, 1 - w[b]], cols)
        src = self.acc.at[there + (slice(None), cols)]
        self.push((group, p, 1), b, src, self.land_one.at[group, p])
        self.add(self.at(group), self.land_two[group, p, w[b]], cols)

    def cross(self, p):
        cols = self.parts[p]
        self.links[1, p, 1].wait_recv()
        at = self.at(1)
        self.add(at, self.land_one[1, p], cols)
        self.push(("z", p), "z", self.acc.at[at + (slice(None), cols)], self.land_z.at[p])

    def finish(self, p, out):
        cols = self.parts[p]
        self.links[0, p, 1].wait_recv()
        self.links["z", p].wait_recv()
        total = self.acc[self.at(0) + (slice(None), cols)].astype(jnp.float32)
        total += self.land_one[0, p].astype(jnp.float32)
        out[:, cols] = total + self.land_z[p].astype(jnp.float32)

    def begin(self, product):
        self.produce(1, 0, product)
        self.produce(1, 1, product)
        self.fold(1, 0)
        self.fold(1, 1)
        self.produce(0, 0, product)
        self.produce(0, 1, product)

    def second(self):
        self.middle(1, 0)
        self.middle(1, 1)
        self.fold(0, 0)
        self.fold(0, 1)

    def third(self):
        self.cross(0)
        self.cross(1)

    def fourth(self):
        self.middle(0, 0)
        self.middle(0, 1)

    def end(self, out):
        self.finish(0, out)
        self.finish(1, out)
        for cp in list(self.links.values()) + list(self.sides.values()):
            cp.wait_send()


def across(left, right):
    return lax.dot_general(
        left, right, (((1,), (1,)), ((), ())), preferred_element_type=jnp.float32
    )


def straight(left, right):
    return jnp.dot(left, right, preferred_element_type=jnp.float32)


def flat(block):
    return block.reshape(-1, block.shape[-1])


def head_lanes(width, head, size):
    lane = lax.broadcasted_iota(jnp.int32, (1, width), 1)
    return jnp.logical_and(lane >= head * size, lane < (head + 1) * size)


def used_pairs(key_seg, query_seg, first, length, block):
    key_pos = lax.broadcasted_iota(jnp.int32, (length, 1), 0)
    query_pos = first + lax.broadcasted_iota(jnp.int32, (1, block), 1)
    return jnp.logical_and(key_seg == query_seg, key_pos <= query_pos)


def attend_block(i, size, block, first, q, k, v_flip, key_seg, query_seg, mixed, mixed_low, lse):
    width = q.shape[2]
    upto, rows = first + block, pl.ds(first, block)
    allowed = used_pairs(key_seg[i, pl.ds(0, upto), :], query_seg[i, :, rows], first, upto, block)
    keys = k[i, pl.ds(0, upto), :]
    query = q[i, rows, :] * jnp.asarray(size**-0.5, q.dtype)
    parts = []
    for head in range(width // size):
        own = jnp.where(head_lanes(width, head, size), query, jnp.zeros_like(query))
        scores = jnp.where(allowed, across(keys, own), NEG)
        top = jnp.max(scores, axis=0, keepdims=True)
        weights = jnp.exp(scores - top)
        total = jnp.sum(weights, axis=0, keepdims=True)
        lse[i, pl.ds(head, 1), rows] = top + jnp.log(total)
        probs = (weights * (1.0 / total)).astype(q.dtype)
        parts.append(straight(v_flip[i, pl.ds(head * size, size), pl.ds(0, upto)], probs))
    full = jnp.concatenate(parts, axis=0).T
    mixed[i, rows, :] = full
    at = first // block
    mixed_low[i, at // 2, at % 2] = full.astype(mixed_low.dtype).reshape(mixed_low.shape[3:])


def attend_back_block(
    i, size, block, first, q, k, k_flip, v, back, mixed, lse, key_seg, query_seg, q_back, k_sum, v_sum
):
    width = q.shape[2]
    upto, rows = first + block, pl.ds(first, block)
    before = pl.ds(0, upto)
    scale = size**-0.5
    allowed = used_pairs(key_seg[i, before, :], query_seg[i, :, rows], first, upto, block)
    keys, values = k[i, before, :], v[i, before, :]
    query = q[i, rows, :] * jnp.asarray(scale, q.dtype)
    grad = back[i, rows, :]
    product = (grad.astype(jnp.float32) * mixed[i, rows, :]).T
    parts = []
    for head in range(width // size):
        lanes = head_lanes(width, head, size)
        own = jnp.where(lanes, query, jnp.zeros_like(query))
        own_grad = jnp.where(lanes, grad, jnp.zeros_like(grad))
        delta = jnp.sum(product[head * size : (head + 1) * size, :], axis=0, keepdims=True)
        scores = across(keys, own) - lse[i, pl.ds(head, 1), rows]
        probs = jnp.exp(jnp.where(allowed, scores, NEG))
        score_back = (probs * (across(values, own_grad) - delta)).astype(q.dtype)
        v_sum[i, before, :] += straight(probs.astype(q.dtype), own_grad)
        k_sum[i, before, :] += straight(score_back, own)
        parts.append(straight(k_flip[i, pl.ds(head * size, size), before], score_back))
    q_back[i, rows, :] = (jnp.concatenate(parts, axis=0).T * scale).astype(q_back.dtype)


class Refs:
    def __init__(self, refs):
        self.refs, self.used = refs, 0

    def take(self, count):
        self.used += count
        return self.refs[self.used - count : self.used]


def front_kernel(size, *refs):
    refs = Refs(refs)
    weights, (up, tokens, grad, keep) = refs.take(3), refs.take(4)
    letter, out_own, segs, down = refs.take(4)
    middle, normed_two, up_shift = refs.take(3)
    q, k, v, mixed, lse, key_seg, query_seg, letters, out_pair = refs.take(9)
    rows_all, grads_near, grads_far, pair, ups, downs = refs.take(6)
    pieces, blocks, columns, normed, vectors, near_segs = refs.take(6)
    rows, near_plane, far_plane, weight, v_flip, mixed_low = refs.take(6)
    one, two, three = refs.take(12), refs.take(5), refs.take(5)
    sums = refs.take(10)
    letter_sems, block_sems, seg_sems, out_sems, column_sems = [refs.take(3) for _ in range(5)]
    pair_sems, up_sems, down_sems, late_sems = [refs.take(3) for _ in range(4)]
    cross_send, cross_recv, load, flush = refs.take(4)
    w = place()
    length, take = q.shape[1:]
    block = length // 4
    width = tokens.shape[1]
    share = size
    greet_world(w)
    letter_mail = mail(w, SPREAD, letter, letters, *letter_sems)
    start_all(letter_mail)
    count = pieces.shape[0]
    for r in range(count):
        places = (r, count + (r + count // 2) % count)
        pieces[r] = jnp.concatenate(
            [ref[:, pl.ds(at * size, size)] for ref in weights for at in places], axis=1
        )
    block_mail = mail(w, SLICE_IN, pieces, blocks, *block_sems)
    start_all(block_mail)
    some = downs.shape[1] // 2
    down_parts = [
        mail(w, PAIR, down.at[part], downs.at[pl.ds(0, 2), part], *sems)
        for part, sems in ((pl.ds(0, some), down_sems), (pl.ds(some, some), late_sems))
    ]
    column_mail = mail(w, COLUMNS_IN, up, columns, *column_sems)
    start_all(column_mail)
    out_mail = mail(w, PAIR, out_own, out_pair, *out_sems)
    first = PlaneGather(w, grad, near_plane, *two)
    cross = remote(
        grad, far_plane.at[w["y"], w["x"], w["c"]], cross_send, cross_recv, beside(w, "z")
    )
    seg_mail = mail(w, NEAR, segs, near_segs, *seg_sems)
    start_all(seg_mail)
    value = tokens[...].astype(jnp.float32)
    centred = value - jnp.mean(value, axis=-1, keepdims=True)
    spread = jnp.mean(centred * centred, axis=-1, keepdims=True)
    centred = centred * lax.rsqrt(spread + EPS)
    wait_all(letter_mail)

    def whole_vector(n):
        for i in range(0, letters.shape[0], 2):
            vectors[pl.ds(n, 1), pl.ds(i * share, 2 * share)] = jnp.concatenate(
                [letters[j, pl.ds(n, 1), pl.ds(0, share)] for j in (i, i + 1)], axis=1
            ).astype(jnp.float32)

    whole_vector(0)
    whole_vector(1)
    normed[...] = (centred * vectors[pl.ds(0, 1), :] + vectors[pl.ds(1, 1), :]).astype(normed.dtype)
    gather = Gather(w, normed, rows, *one)
    second = PlaneGather(w, None, far_plane, *three)
    scatter = Scatter(w, *sums)
    gather.start()
    wait_all(block_mail)
    pair_mail = mail(w, PAIR, blocks, weight, *pair_sems)
    start_all(pair_mail)
    gather.turn()
    gather.far_start()
    gather.near_ready()
    gather.far_turn()
    first.start()
    cross.start()
    wait_all(seg_mail)
    for i in range(2):
        flipped = near_segs[i].T
        for n in range(near_segs.shape[1]):
            at = pl.ds(n * 128, 128)
            query_seg[i, :, at] = near_segs[i, pl.ds(n, 1), :]
            key_seg[i, at, :] = flipped[:, n : n + 1]
    count = lax.axis_size("dp") * lax.axis_size("seq")
    low_at = w["z"] * lax.axis_size("seq") + w["s"]
    high_at = (lax.axis_size("dp") - 1 - w["z"]) * lax.axis_size("seq") + w["s"]
    q_shift, v_shift = [
        jnp.concatenate(
            [letters[at, pl.ds(n, 1), pl.ds(0, share)] for at in (low_at, high_at)], axis=1
        ).astype(jnp.float32)
        for n in (2, 3)
    ]
    shift = jnp.concatenate([q_shift, jnp.zeros_like(q_shift), v_shift], axis=1)
    for n in (4, 5, 6):
        whole_vector(n)
    up_rows = up_shift.shape[1] // (2 * share)
    up_shift[...] = jnp.concatenate(
        [
            letters[at, pl.ds(8 + n, 1), pl.ds(0, share)]
            for at in (low_at, high_at)
            for n in range(up_rows)
        ],
        axis=1,
    ).astype(jnp.float32)
    wait_all(column_mail)
    wait_all(pair_mail)
    up_mail = mail(w, PAIR, columns, ups, *up_sems)
    start_all(out_mail + up_mail)
    keep_pair = pltpu.make_async_copy(weight, pair, load)
    keep_pair.start()

    def project(i):
        @pl.loop(0, 2)
        def _(y):
            block = straight(flat(rows[i, y]), weight[...].reshape(width, -1)) + shift
            at = pl.ds(y * (length // 2), length // 2)
            for ref, n in ((q, 0), (k, 1), (v, 2)):
                ref[i, at, :] = block[:, n * take : (n + 1) * take].astype(ref.dtype)
            v_flip[i, :, at] = block[:, 2 * take :].astype(v_flip.dtype).T

    def mix(i):
        for first in range(0, length, block):
            attend_block(
                i, size, block, first, q, k, v_flip, key_seg, query_seg, mixed, mixed_low, lse
            )

    project(w["z"])
    gather.far_ready()
    gather.finish()
    keep_rows = pltpu.make_async_copy(rows, rows_all, flush.at[0])
    keep_rows.start()
    first.turn()
    mix(w["z"])
    first.land()
    cross.wait()
    second.start()
    project(1 - w["z"])
    mix(1 - w["z"])
    first.ready()
    keep_near = pltpu.make_async_copy(near_plane, grads_near, flush.at[2])
    keep_near.start()
    wait_all(out_mail)

    def product(z, y, c, cols):
        return straight(
            flat(mixed_low[z, y, :, c]), jnp.concatenate([out_pair[0, :, cols], out_pair[1, :, cols]])
        )

    second.turn()
    scatter.begin(product)
    scatter.second()
    second.land()
    wait_all(up_mail)
    start_all(down_parts[0] + down_parts[1])
    second.ready()
    keep_far = pltpu.make_async_copy(far_plane, grads_far, flush.at[1])
    keep_far.start()
    scatter.third()
    scatter.fourth()
    scatter.end(middle)
    value = tokens[...].astype(jnp.float32)
    value += keep[...] * (middle[...] + vectors[pl.ds(4, 1), :])
    middle[...] = value
    centred = value - jnp.mean(value, axis=-1, keepdims=True)
    spread = jnp.mean(centred * centred, axis=-1, keepdims=True)
    centred = centred * lax.rsqrt(spread + EPS)
    value = centred * vectors[pl.ds(5, 1), :] + vectors[pl.ds(6, 1), :]
    normed_two[...] = value.astype(normed_two.dtype)
    first.finish()
    second.finish()
    wait_all(down_parts[0] + down_parts[1])
    keep_rows.wait()
    keep_near.wait()
    keep_far.wait()
    keep_pair.wait()


def front(weights, up, tokens, grad, keep, letter, out_own, segs, down, size, early, name, cid):
    rows, width = tokens.shape
    ns = lax.axis_size("seq")
    ndev = lax.axis_size("dp") * ns
    length = rows * ns
    take = 2 * size
    low, f32 = tokens.dtype, jnp.float32
    vmem, anywhere = pl.BlockSpec(memory_space=pltpu.VMEM), pl.BlockSpec(memory_space=pl.ANY)
    shape, dma = jax.ShapeDtypeStruct, pltpu.SemaphoreType.DMA
    plane = (2, 2, 2, rows, width)
    share = weights[0].shape[0]
    blocks = (ndev // 2, share, 3 * take)
    columns = (ndev // 2, share, 2 * up.shape[1] // ndev)
    return pl.pallas_call(
        functools.partial(front_kernel, size),
        out_shape=(
            shape((rows, width), f32),
            shape((rows, width), low),
            shape((1, columns[2]), f32),
            *[shape((2, length, take), low)] * 3,
            shape((2, length, take), f32),
            shape((2, take // size, length), f32),
            shape((2, length, 1), segs.dtype),
            shape((2, 1, length), segs.dtype),
            shape((ndev,) + letter.shape, low),
            shape((2,) + out_own.shape, low),
            shape((2,) + plane, low),
            shape(plane, low),
            shape(plane, low),
            shape((2,) + blocks, low),
            shape((2,) + columns, low),
            shape((2, early, width), low),
        ),
        in_specs=[vmem] * 7 + [anywhere] * 4,
        out_specs=tuple([vmem] * 12 + [anywhere] * 6),
        scratch_shapes=[
            pltpu.VMEM(blocks, low),
            pltpu.VMEM(blocks, low),
            pltpu.VMEM(columns, low),
            pltpu.VMEM((rows, width), low),
            pltpu.VMEM((8, width), f32),
            pltpu.VMEM((2,) + segs.shape, segs.dtype),
            pltpu.VMEM((2,) + plane, low),
            pltpu.VMEM(plane, low),
            pltpu.VMEM(plane, low),
            pltpu.VMEM((2,) + blocks, low),
            pltpu.VMEM((2, take, length), low),
            pltpu.VMEM((2, 2, 2, 2, rows, take), low),
            *Gather.sems(),
            *PlaneGather.sems(),
            *PlaneGather.sems(),
            *Scatter.scratch(rows, width),
            *mail_sems(SPREAD),
            *mail_sems(SLICE_IN),
            *mail_sems(NEAR),
            *mail_sems(PAIR),
            *mail_sems(COLUMNS_IN),
            *mail_sems(PAIR),
            *mail_sems(PAIR),
            *mail_sems(PAIR),
            *mail_sems(PAIR),
            dma,
            dma,
            dma,
            dma((3,)),
        ],
        compiler_params=pltpu.CompilerParams(
            collective_id=cid, has_side_effects=True, vmem_limit_bytes=VMEM_BYTES
        ),
        name=name,
    )(*weights, up, tokens, grad, keep, letter, out_own, segs, down)


def feed_kernel(*refs):
    refs = Refs(refs)
    own, shift, ups, grads_near, grads_far, downs, down_some = refs.take(7)
    back, branch, shift_sum, down_grad, up_grad, down_got, up_some = refs.take(7)
    rows, grads, up, down, slope, flip, hidden, stage = refs.take(8)
    pre = hidden
    one = refs.take(12)
    branch_sums = refs.take(10)
    sums = refs.take(8)
    down_sems = refs.take(3)
    grad_send, grad_recv, load, flush = refs.take(4)
    w = place()
    greet_half(w)
    gather = Gather(w, own, rows, *one)
    branch_scatter = Scatter(w, *branch_sums)
    core = lambda c: grads.at[pl.ds(0, 2), pl.ds(0, 2), pl.ds(0, 2), c]
    scatter = Scatter(w, core(0), core(1), *sums)
    gather.start()
    half = downs.shape[0]
    early = down_some.shape[1]
    rest = half - early
    place_down = pl.ds(w["g"] * half + early, rest)
    down_mail = [
        remote(
            downs.at[pl.ds(early, rest)],
            down.at[place_down],
            down_sems[0].at[0],
            down_sems[1].at[0],
            partner(w),
        ),
        pltpu.make_async_copy(downs.at[pl.ds(early, rest)], down.at[place_down], down_sems[2].at[0]),
    ]
    fetch = [
        pltpu.make_async_copy(ups, up, load.at[0]),
        pltpu.make_async_copy(grads_near, grads.at[w["z"]], load.at[1]),
        pltpu.make_async_copy(grads_far, grads.at[1 - w["z"]], load.at[2]),
        pltpu.make_async_copy(down_some.at[0], down.at[pl.ds(0, early)], load.at[3]),
        pltpu.make_async_copy(down_some.at[1], down.at[pl.ds(half, early)], load.at[4]),
    ]
    start_all(down_mail + fetch)
    width = rows.shape[5]
    span = rows.shape[2] * rows.shape[3] * rows.shape[4]
    chunk = 256
    shift_sum[...] = jnp.zeros_like(shift_sum)

    def forward(z):
        @pl.loop(0, 2)
        def _(y):
            before = straight(flat(rows[z, y]), up[...]) + shift[...]
            active, pull = jax.vjp(activate, before)
            at = pl.ds(z * (2 * span) + y * span, span)
            low = active.astype(hidden.dtype)
            hidden[z, y] = low.reshape(hidden.shape[2:])
            flip[:, at] = low.T
            slope[at, :] = pull(jnp.ones_like(before))[0].astype(slope.dtype)

    gather.turn()
    gather.far_start()
    gather.near_ready()
    wait_all(fetch)
    gather.far_turn()
    forward(w["z"])
    gather.far_ready()
    gather.finish()
    forward(1 - w["z"])
    wait_all(down_mail)

    def branch_product(z, y, c, cols):
        return straight(flat(hidden[z, y, :, c]), down[:, cols])

    branch_scatter.begin(branch_product)

    @pl.loop(0, width // chunk)
    def _(i):
        cols = pl.ds(i * chunk, chunk)
        grad = straight(flip[...], grads[:, :, :, :, :, cols].reshape(-1, chunk))
        down_grad[:, :, cols] = grad.astype(down_grad.dtype).reshape(2, -1, chunk)

    trade = remote(
        down_grad.at[1 - w["g"]], down_got, grad_send.at[0], grad_recv.at[0], partner(w)
    )
    trade.start()
    branch_scatter.second()

    @pl.loop(0, 4)
    def _(i):
        at = pl.ds(i * span, span)
        hidden_back = across(flat(grads[i // 2, i % 2]), down[...])
        pre_back = (hidden_back * slope[at, :].astype(jnp.float32)).astype(pre.dtype)
        pre[i // 2, i % 2] = pre_back.reshape(pre.shape[2:])
        flip[:, at] = pre_back.T
        shift_sum[...] += jnp.sum(pre_back.astype(jnp.float32), axis=0, keepdims=True)

    def product(z, y, c, cols):
        return across(flat(pre[z, y, :, c]), up[cols, :])

    def store(i):
        at = up_grad.at[pl.ds(pl.multiple_of(i * chunk, chunk), chunk)]
        return pltpu.make_async_copy(stage.at[i % 2], at, flush.at[i % 2])

    scatter.begin(product)
    branch_scatter.third()

    @pl.loop(0, width // chunk)
    def _(i):
        cols = pl.ds(i * chunk, chunk)
        grad = straight(flip[...], rows[:, :, :, :, :, cols].reshape(-1, chunk))

        @pl.when(i >= 2)
        def _():
            store(i).wait()

        stage[i % 2] = grad.astype(stage.dtype).T
        store(i).start()

    store(0).wait()
    store(1).wait()
    sent = pl.ds((1 - w["g"]) * (width // 2), up_some.shape[0])
    up_trade = remote(up_grad.at[sent], up_some, grad_send.at[1], grad_recv.at[1], partner(w))
    up_trade.start()
    scatter.second()
    branch_scatter.fourth()
    scatter.third()
    scatter.fourth()
    branch_scatter.end(branch)
    scatter.end(back)
    trade.wait()
    up_trade.wait()


def feed(own, shift, ups, grads_near, grads_far, downs, down_some, name, cid):
    rows, width = own.shape
    take = ups.shape[1]
    low, f32 = own.dtype, jnp.float32
    vmem, anywhere = pl.BlockSpec(memory_space=pltpu.VMEM), pl.BlockSpec(memory_space=pl.ANY)
    shape, dma = jax.ShapeDtypeStruct, pltpu.SemaphoreType.DMA
    whole = (2, 2, 2, 2, rows, width)
    tokens = 16 * rows
    return pl.pallas_call(
        feed_kernel,
        out_shape=(
            shape((rows, width), f32),
            shape((rows, width), f32),
            shape((1, take), f32),
            shape((2,) + downs.shape, low),
            shape((width, take), low),
            shape(downs.shape, low),
            shape((width // 4, take), low),
        ),
        in_specs=[vmem] * 2 + [anywhere] * 5,
        out_specs=(vmem, vmem, vmem, vmem, anywhere, anywhere, anywhere),
        scratch_shapes=[
            pltpu.VMEM(whole, low),
            pltpu.VMEM(whole, low),
            pltpu.VMEM((width, take), low),
            pltpu.VMEM((take, width), low),
            pltpu.VMEM((tokens, take), low),
            pltpu.VMEM((take, tokens), low),
            pltpu.VMEM((2, 2, 2, 2, rows, take), low),
            pltpu.VMEM((2, 256, take), low),
            *Gather.sems(),
            *Scatter.scratch(rows, width),
            *Scatter.scratch(rows, width, 1),
            *mail_sems(PAIR),
            dma((2,)),
            dma((2,)),
            dma((5,)),
            dma((2,)),
        ],
        compiler_params=pltpu.CompilerParams(
            collective_id=cid, has_side_effects=True, vmem_limit_bytes=VMEM_BYTES
        ),
        name=name,
    )(own, shift, ups, grads_near, grads_far, downs, down_some)


def attend_back_kernel(size, *refs):
    refs = Refs(refs)
    (own, out_rows, q, k, v, mixed, lse, key_seg, query_seg) = refs.take(9)
    rows_all, pair, up_sent, up_some = refs.take(4)
    (back, out_grad, attend_grad, q_sum, v_bias_sum, up_rows, out_got, attend_got) = refs.take(8)
    (grads, rows, weight, k_flip, mixed_flip, grad_heads, q_back, k_sum, v_sum, stack, stack_flip) = (
        refs.take(11)
    )
    (up_parts,) = refs.take(1)
    one = refs.take(12)
    sums = refs.take(10)
    send, recv, load = refs.take(3)
    swap_sems = refs.take(3)
    w = place()
    greet_half(w)
    gather = Gather(w, own, grads, *one)
    scatter = Scatter(w, *sums)
    gather.start()
    other = 1 - w["g"]
    some = up_some.shape[0]
    rest = pl.ds(some, up_sent.shape[1] - some)
    up_trade = remote(
        up_sent.at[other, rest], up_parts.at[1, rest], send.at[0], recv.at[0], partner(w)
    )
    up_trade.start()
    fetch = [
        pltpu.make_async_copy(pair, weight, load.at[0]),
        pltpu.make_async_copy(rows_all, rows, load.at[1]),
        pltpu.make_async_copy(up_sent.at[w["g"]], up_parts.at[0], load.at[2]),
        pltpu.make_async_copy(up_some, up_parts.at[1, pl.ds(0, some)], load.at[3]),
    ]
    start_all(fetch)
    length, take = q.shape[1:]
    for i in range(2):
        k_flip[i] = k[i].T
        mixed_flip[:, pl.ds(i * length, length)] = mixed[i].astype(mixed_flip.dtype).T
    k_sum[...] = jnp.zeros_like(k_sum)
    v_sum[...] = jnp.zeros_like(v_sum)
    q_sum[...] = jnp.zeros_like(q_sum)
    v_bias_sum[...] = jnp.zeros_like(v_bias_sum)
    block = length // 4

    def heads_back(i):
        @pl.loop(0, 2)
        def _(y):
            at = pl.ds(y * (length // 2), length // 2)
            grad = across(flat(grads[i, y]), out_rows[...])
            grad_heads[i, at, :] = grad.astype(grad_heads.dtype)

    def mix_back(i):
        for first in range(0, length, block):
            attend_back_block(
                i,
                size,
                block,
                first,
                q,
                k,
                k_flip,
                v,
                grad_heads,
                mixed,
                lse,
                key_seg,
                query_seg,
                q_back,
                k_sum,
                v_sum,
            )

        @pl.loop(0, 2)
        def _(y):
            at = pl.ds(y * (length // 2), length // 2)
            parts = [ref[i, at, :].astype(stack.dtype) for ref in (q_back, k_sum, v_sum)]
            for n, part in enumerate(parts):
                stack[i, y, :, :, :, pl.ds(n * take, take)] = part.reshape(
                    stack.shape[2:5] + (take,)
                )
                to = pl.ds(i * length + y * (length // 2), length // 2)
                stack_flip[pl.ds(n * take, take), to] = part.T
            q_sum[...] += jnp.sum(parts[0].astype(jnp.float32), axis=0, keepdims=True)
            v_bias_sum[...] += jnp.sum(parts[2].astype(jnp.float32), axis=0, keepdims=True)

    gather.turn()
    gather.far_start()
    gather.near_ready()
    gather.far_turn()
    heads_back(w["z"])
    mix_back(w["z"])
    gather.far_ready()
    gather.finish()
    chunk = 256
    half_chunks = attend_grad.shape[1] // chunk
    attend_trade = remote(
        attend_grad.at[other], attend_got, send.at[1], recv.at[1], partner(w)
    )
    out_trade = remote(out_grad.at[other], out_got, send.at[2], recv.at[2], partner(w))

    @pl.loop(0, 2 * half_chunks)
    def _(i):
        cols = pl.ds(i * chunk, chunk)
        grad = straight(mixed_flip[...], grads[:, :, :, :, :, cols].reshape(-1, chunk))
        out_grad[:, :, cols] = grad.astype(out_grad.dtype).reshape(2, -1, chunk)

    heads_back(1 - w["z"])
    up_trade.wait()
    out_trade.start()
    wait_all(fetch)

    @pl.loop(0, up_parts.shape[1])
    def _(i):
        total = up_parts[0, i].astype(jnp.float32) + up_parts[1, i].astype(jnp.float32)
        up_parts[0, i] = total.astype(up_parts.dtype)

    up_mail = mail(w, COLUMNS_OUT, up_parts.at[0], up_rows, *swap_sems)
    mix_back(1 - w["z"])

    def product(z, y, c, cols):
        return across(flat(stack[z, y, :, c]), weight[cols, :])

    scatter.begin(product)
    start_all(up_mail)

    @pl.loop(0, 2 * half_chunks)
    def _(i):
        cols = pl.ds(i * chunk, chunk)
        grad = straight(stack_flip[...], rows[:, :, :, :, :, cols].reshape(-1, chunk))
        attend_grad[i // half_chunks, pl.ds(i % half_chunks * chunk, chunk), :] = grad.astype(
            attend_grad.dtype
        ).T

    out_trade.wait()
    attend_trade.start()
    scatter.second()
    scatter.third()
    scatter.fourth()
    scatter.end(back)
    wait_all(up_mail)
    attend_trade.wait()


def attend_back(
    own, out_rows, q, k, v, mixed, lse, key_seg, query_seg, rows_all, pair, up_sent, up_some,
    size, name, cid
):
    rows, width = own.shape
    length, take = q.shape[1:]
    low, f32 = own.dtype, jnp.float32
    vmem, anywhere = pl.BlockSpec(memory_space=pltpu.VMEM), pl.BlockSpec(memory_space=pl.ANY)
    shape, dma = jax.ShapeDtypeStruct, pltpu.SemaphoreType.DMA
    whole = (2, 2, 2, 2, rows, width)
    heads = (2, length, take)
    return pl.pallas_call(
        functools.partial(attend_back_kernel, size),
        out_shape=(
            shape((rows, width), f32),
            shape((2, take // 2, width), low),
            shape((2, width // 2, 3 * take), low),
            shape((1, take), f32),
            shape((1, take), f32),
            shape((up_sent.shape[2], up_sent.shape[1] * up_sent.shape[3]), low),
            shape((take // 2, width), low),
            shape((width // 2, 3 * take), low),
        ),
        in_specs=[vmem] * 9 + [anywhere] * 4,
        out_specs=tuple([vmem] * 6 + [anywhere] * 2),
        scratch_shapes=[
            pltpu.VMEM(whole, low),
            pltpu.VMEM(whole, low),
            pltpu.VMEM((width, 3 * take), low),
            pltpu.VMEM((2, take, length), low),
            pltpu.VMEM((take, 2 * length), low),
            pltpu.VMEM(heads, low),
            pltpu.VMEM(heads, low),
            pltpu.VMEM(heads, f32),
            pltpu.VMEM(heads, f32),
            pltpu.VMEM((2, 2, 2, 2, rows, 3 * take), low),
            pltpu.VMEM((3 * take, 2 * length), low),
            pltpu.VMEM((2,) + up_sent.shape[1:], low),
            *Gather.sems(),
            *Scatter.scratch(rows, width),
            dma((3,)),
            dma((3,)),
            dma((4,)),
            *mail_sems(COLUMNS_OUT),
        ],
        compiler_params=pltpu.CompilerParams(
            collective_id=cid, has_side_effects=True, vmem_limit_bytes=VMEM_BYTES
        ),
        name=name,
    )(
        own,
        out_rows,
        q,
        k,
        v,
        mixed,
        lse,
        key_seg,
        query_seg,
        rows_all,
        pair,
        up_sent,
        up_some,
    )


def last_kernel(size, *refs):
    refs = Refs(refs)
    grad, got, letter, note = refs.take(4)
    q_rows, k_rows, v_rows, letters, notes = refs.take(5)
    parts, swapped, low_letters = refs.take(3)
    sems = [refs.take(3) for _ in range(3)]
    (load,) = refs.take(1)
    w = place()
    fetch = [
        pltpu.make_async_copy(grad.at[w["g"]], parts.at[0], load.at[0]),
        pltpu.make_async_copy(got, parts.at[1], load.at[1]),
    ]
    start_all(fetch)
    greet_world(w)
    letter_mail = mail(w, LETTERS, letter, low_letters, *sems[0])
    letter_mail += mail(w, PAIR, note, notes, *sems[1])
    wait_all(fetch)
    count = parts.shape[1]

    @pl.loop(0, count)
    def _(i):
        total = parts[0, i].astype(jnp.float32) + parts[1, i].astype(jnp.float32)
        parts[0, i] = total.astype(parts.dtype)

    swap_mail = mail(w, SLICE_OUT, parts.at[0], swapped, *sems[2])
    start_all(swap_mail + letter_mail)
    wait_all(swap_mail)
    for n, out in enumerate((q_rows, k_rows, v_rows)):
        for high in range(2):
            for r in range(0, count, 2):
                at = high * count + (r + high * (count // 2)) % count
                lanes = pl.ds((2 * n + high) * size, size)
                both = jnp.concatenate([swapped[r, :, lanes], swapped[r + 1, :, lanes]], axis=1)
                out[:, pl.ds(at * size, 2 * size)] = both.astype(out.dtype)
    wait_all(letter_mail)
    letters[...] = jnp.sum(low_letters[...], axis=0)


def last(grad, got, letter, note, size, name, cid):
    width = 2 * got.shape[0]
    ndev = lax.axis_size("dp") * lax.axis_size("seq")
    low, f32 = got.dtype, jnp.float32
    vmem, anywhere = pl.BlockSpec(memory_space=pltpu.VMEM), pl.BlockSpec(memory_space=pl.ANY)
    shape, dma = jax.ShapeDtypeStruct, pltpu.SemaphoreType.DMA
    share = width // ndev
    grad, got = [x.reshape(x.shape[:-2] + (ndev // 2, share, x.shape[-1])) for x in (grad, got)]
    return pl.pallas_call(
        functools.partial(last_kernel, size),
        out_shape=(
            *[shape((share, width), f32)] * 3,
            shape(letter.shape[1:], f32),
            shape((2,) + note.shape, f32),
        ),
        in_specs=[anywhere] * 4,
        out_specs=(vmem, vmem, vmem, vmem, anywhere),
        scratch_shapes=[
            pltpu.VMEM((2,) + got.shape, low),
            pltpu.VMEM(got.shape, low),
            pltpu.VMEM((ndev,) + letter.shape[1:], f32),
            *mail_sems(LETTERS),
            *mail_sems(PAIR),
            *mail_sems(SLICE_OUT),
            dma((2,)),
        ],
        compiler_params=pltpu.CompilerParams(
            collective_id=cid, has_side_effects=True, vmem_limit_bytes=VMEM_BYTES
        ),
        name=name,
    )(grad, got, letter, note)


def on_device_halves(
    tokens,
    segments,
    exit_layer,
    first_gain,
    first_shift,
    query_weight,
    query_bias,
    key_weight,
    value_weight,
    value_bias,
    output_weight,
    output_bias,
    second_gain,
    second_shift,
    up_weight,
    up_bias,
    down_weight,
    down_bias,
    cotangent,
):
    rows, width = tokens.shape[1:]
    nd, ns = lax.axis_size("dp"), lax.axis_size("seq")
    ndev = nd * ns
    size = width // HEADS
    hidden_size = up_weight.shape[1]
    take = 2 * size
    w = place()
    group = w["g"]

    def own_half(pair):
        return lax.dynamic_index_in_dim(pair, group, 0, keepdims=False).astype(jnp.float32)

    def total(pair, got):
        return own_half(pair) + got.astype(jnp.float32)

    keep = (exit_layer > LAYER).astype(jnp.float32).reshape(rows, 1)
    inputs = tokens.astype(jnp.float32).reshape(rows, width)
    upstream = cotangent.astype(jnp.float32).reshape(rows, width)
    branch_back = (keep * upstream).astype(jnp.bfloat16)
    vector_parts = [
        first_gain,
        first_shift,
        query_bias,
        value_bias,
        output_bias,
        second_gain,
        second_shift,
        down_bias,
        up_bias,
    ]
    share = width // ndev
    letter = jnp.zeros((16, 128), jnp.bfloat16)
    at = 0
    for part in vector_parts:
        part = part.reshape(-1, share)
        count = part.shape[0]
        letter = letter + jnp.pad(part, ((at, 16 - at - count), (0, 128 - share)))
        at += count
    (
        middle,
        normed_two,
        up_shift,
        queries,
        keys,
        values,
        mixed,
        lse,
        key_seg,
        query_seg,
        vectors,
        output_rows,
        normed_all,
        grads_near,
        grads_far,
        attend_pair,
        up_pair,
        down_some,
    ) = front(
        (query_weight, key_weight, value_weight),
        up_weight,
        tokens.reshape(rows, width),
        branch_back,
        keep,
        letter,
        output_weight,
        segments.reshape(-1, 128),
        down_weight,
        size,
        down_weight.shape[0] // 2,
        "front",
        0,
    )
    output_rows = output_rows.reshape(-1, width)
    cuts, at = [], 0
    for part in vector_parts:
        count = part.shape[0] // share
        cuts.append(vectors[:, at : at + count, :share].reshape(ndev, -1))
        at += count
    full = [cut.reshape(-1).astype(jnp.float32) for cut in cuts]
    gain_one, shift_one, _, _, output_shift, gain_two, shift_two, down_shift, _ = full

    normed_two_back, branch, up_shift_sum, down_grad, up_grad, down_got, up_some = feed(
        normed_two,
        up_shift,
        up_pair.reshape(width, -1),
        grads_near,
        grads_far,
        down_weight,
        down_some,
        "feed",
        1,
    )
    layer_out = (middle + keep * (branch + down_shift)).astype(jnp.bfloat16)
    norm_result, pull_two = jax.vjp(layer_norm, middle, gain_two, shift_two)
    middle_part, gain_two_sum, shift_two_sum = pull_two(normed_two_back)
    middle_back = upstream + middle_part
    attention_back = (keep * middle_back).astype(jnp.bfloat16)
    up_grad = up_grad.reshape(2, ndev // 2, width // ndev, -1)
    (
        normed_one_back,
        output_grad,
        attend_grad,
        query_sum,
        value_sum,
        up_rows,
        output_got,
        attend_got,
    ) = attend_back(
        attention_back,
        output_rows,
        queries,
        keys,
        values,
        mixed,
        lse,
        key_seg,
        query_seg,
        normed_all,
        attend_pair.reshape(width, -1),
        up_grad,
        up_some.reshape(-1, width // ndev, up_some.shape[1]),
        size,
        "attend_back",
        2,
    )
    norm_first, pull_one = jax.vjp(layer_norm, inputs, gain_one, shift_one)
    inputs_part, gain_one_sum, shift_one_sum = pull_one(normed_one_back)
    tokens_gradient = (middle_back + inputs_part).astype(jnp.bfloat16)

    def summed(value):
        return jnp.sum(value.astype(jnp.float32), axis=0)

    own_sums = [
        gain_one_sum,
        shift_one_sum,
        gain_two_sum,
        shift_two_sum,
        summed(attention_back),
        summed(branch_back),
    ]
    letter = jnp.stack([value.reshape(-1, 128) for value in own_sums], axis=1)
    letter = jnp.pad(letter, ((0, 0), (0, 2), (0, 0)))
    note = jnp.concatenate([query_sum, value_sum, up_shift_sum], axis=1)
    note = jnp.pad(note, ((0, 0), (0, -note.shape[1] % 1024))).reshape(-1, 128)
    query_rows, key_rows, value_rows, letters, notes = last(
        attend_grad, attend_got, letter, note, size, "last", 3
    )
    letters = lax.dynamic_slice_in_dim(letters, w["c"] * share, share, 1)
    notes = (notes[0] + notes[1]).reshape(-1)

    def own_part(at, length):
        return lax.dynamic_slice_in_dim(notes, at + group * length, length, 0)

    vector_out = [letters[i] for i in range(6)] + [
        own_part(0, size),
        own_part(take, size),
        own_part(2 * take, hidden_size // ndev),
    ]
    (
        gain_one_part,
        shift_one_part,
        gain_two_part,
        shift_two_part,
        output_shift_part,
        down_shift_part,
        query_shift_part,
        value_shift_part,
        up_shift_part,
    ) = vector_out
    return (
        layer_out.reshape(tokens.shape),
        tokens_gradient.reshape(tokens.shape),
        gain_one_part,
        shift_one_part,
        query_rows,
        query_shift_part,
        key_rows,
        value_rows,
        value_shift_part,
        total(output_grad, output_got),
        output_shift_part,
        gain_two_part,
        shift_two_part,
        up_rows.astype(jnp.float32),
        up_shift_part,
        total(down_grad, down_got),
        down_shift_part,
    )


def solution(mesh):
    placed = (
        P("dp", "seq", None),
        P("dp", None),
        P("dp", "seq"),
        P(("dp", "seq")),
        P(("dp", "seq")),
        P(("dp", "seq"), None),
        P(("dp", "seq")),
        P(("dp", "seq"), None),
        P(("dp", "seq"), None),
        P(("dp", "seq")),
        P(("dp", "seq"), None),
        P(("dp", "seq")),
        P(("dp", "seq")),
        P(("dp", "seq")),
        P(("dp", "seq"), None),
        P(("dp", "seq")),
        P(("dp", "seq"), None),
        P(("dp", "seq")),
        P("dp", "seq", None),
    )
    halves = mesh.shape["dp"] == 4 and mesh.shape["seq"] == 8
    return jax.shard_map(
        on_device_halves if halves else on_device,
        mesh=mesh,
        in_specs=placed,
        out_specs=(
            P("dp", "seq", None),
            P("dp", "seq", None),
            P(("dp", "seq")),
            P(("dp", "seq")),
            P(("dp", "seq"), None),
            P(("dp", "seq")),
            P(("dp", "seq"), None),
            P(("dp", "seq"), None),
            P(("dp", "seq")),
            P(("dp", "seq"), None),
            P(("dp", "seq")),
            P(("dp", "seq")),
            P(("dp", "seq")),
            P(("dp", "seq"), None),
            P(("dp", "seq")),
            P(("dp", "seq"), None),
            P(("dp", "seq")),
        ),
        check_vma=False,
    )
```
